32 devices in a mesh: dp: 2 (over y), expert: 16 (over z, x, core).
Axes of the slice: x: 2, y: 2, z: 4, core: 2. Of those that a mesh axis runs over, the one named last changes fastest.
Arguments:
- tokens: bfloat16 [4096, 2048], P(('dp', 'expert')), may hold values from -6 to 6
- routes: int32 [4096, 2], P(('dp', 'expert')), may hold values from 0 to 15, all different within a row; in each aligned block of 128 rows (0 to 127, 128 to 255, ...) at most 24 rows name the same one
- gates: float32 [4096, 2], P(('dp', 'expert')), may hold values from 0.05 to 1
- grad_out: bfloat16 [4096, 2048], P(('dp', 'expert')), may hold values from -6 to 6
- w_gate: bfloat16 [16, 2048, 768], P('expert', 'dp'), may hold values from -0.125 to 0.125
- w_up: bfloat16 [16, 2048, 768], P('expert', 'dp'), may hold values from -0.125 to 0.125
- w_down: bfloat16 [16, 768, 2048], P('expert', None, 'dp'), may hold values from -0.21875 to 0.21875
Outputs:
- grad_tokens: bfloat16 [4096, 2048], P(('dp', 'expert'))
- grad_gates: float32 [4096, 2], P(('dp', 'expert'))
- grad_down: float32 [16, 768, 2048], P('expert', None, 'dp')
The draws below stay inside these ranges and needn't reach their ends.
Inputs may be any that keep to these rules, and one draw needn't show every extreme that they name: Within the rows of one device no expert is named by more than 24 routes, a bound that some block reaches; the 2 experts of a token differ.
All inputs are finite; a program needn't handle non-finite values.
Results may differ from the reference program's by a relative error of at most 0.015.
Values may be sent and summed in bfloat16 or wider, within the bound.
No kernel may reach another device: no remote copies, remote signals or barrier semaphores. Data moves between devices by JAX's collectives and lax.ppermute only.
A program may use at most 128 MiB of HBM per device.

```python
import math
import jax
import jax.numpy as jnp
import numpy as np
from jax import lax

D = 2048
H = 768
TOP = 2
TOK_DEV = 128
EXPERTS = 16
CAP = 24
TOKENS = 4096
N_DP = 2
N_EXPERT = 16


def steps_of(rng, extent, split, smallest, largest):
    gain = 1.0
    for dim, shards_of in split:
        draws = jax.random.uniform(jax.random.fold_in(jax.random.fold_in(rng, 6), dim), (shards_of,), jnp.float32, smallest / len(split), largest / len(split))
        gain = gain * jnp.repeat(jnp.exp(draws), extent[dim] // shards_of).reshape((-1,) + (1,) * (len(extent) - 1 - dim))
    return gain


def shared_out(own_key, own, number, rows, count, top, reach, skew):
    sequence = jax.random.permutation(own_key, count)
    heavy_load, usual = load_shares(count, rows * top, reach, skew, True), load_shares(count, rows * top, reach, skew, False)
    places = jnp.arange(count)

    def named(tallies, offset_by):
        used = int((tallies > 0).sum())
        fixed = max(1, used // 4)
        moved = fixed + (places - fixed + offset_by * (used - fixed)) % max(1, count - fixed)
        return jnp.zeros((count,), jnp.int32).at[sequence[jnp.where(places < fixed, places, moved)]].set(jnp.asarray(tallies, jnp.int32))

    tallies = jnp.where(number % 4 == 0, named(heavy_load, number // 4), named(usual, number - number // 4 - 1))
    mixed = jax.random.permutation(jax.random.fold_in(own, 3), count)
    donor, taker = mixed[0:count // 2 * 2:2], mixed[1:count // 2 * 2:2]
    room = jnp.minimum(tallies[donor] - 1, reach - tallies[taker]) // 2
    room = jnp.where((donor == sequence[0]) | (taker == sequence[0]) | (tallies[taker] == 0), 0, jnp.maximum(room, 0))
    moved = jax.random.randint(jax.random.fold_in(own, 4), (count // 2,), 0, 1 << 20) % (room + 1)
    tallies = tallies.at[donor].add(-moved).at[taker].add(moved)
    members = jnp.searchsorted(jnp.cumsum(tallies), jnp.arange(rows * top), side="right").astype(jnp.int32)
    listing = members.reshape(top, rows).T
    listing = listing[jax.random.permutation(jax.random.fold_in(own, 1), rows)]
    offset_by = jax.random.randint(jax.random.fold_in(own, 2), (rows, 1), 0, top)
    return jnp.take_along_axis(listing, (jnp.arange(top)[None, :] + offset_by) % top, axis=1)


def load_shares(count, total, bound, skew, full):
    weights = [(1 << 20) // math.isqrt(rank ** skew) + 1 for rank in range(1, count + 1)]
    largest = bound if full else min(bound, max(-(-total // count), total * weights[0] // sum(weights)))
    least = 1 if total - largest >= count - 1 else 0
    counts, spare = [largest] + [least] * (count - 1), total - largest - least * (count - 1)
    while spare > 0:
        candidates = [i for i in range(1, count) if counts[i] < largest] or [i for i in range(1, count) if counts[i] < bound]
        pool, left = sum([weights[i] for i in candidates]), spare
        for i in candidates:
            more = min(bound - counts[i], max(1, left * weights[i] // pool), spare)
            counts[i] = counts[i] + more
            spare = spare - more
    return np.array(counts)


def bell_draw(rng, extent, width, most, shards=(), held_as=jnp.bfloat16):
    array = jax.random.normal(rng, extent, jnp.float32) * width
    if len(shards) > 0:
        array = steps_of(rng, extent, shards, -0.22, 0.18) * array
    return jnp.clip(array, min=-most, max=most).astype(held_as)


def setup_inputs(seed: int = 0) -> dict:
    seeds = jax.random.split(jax.random.key(seed), 8)
    tokens = bell_draw(seeds[0], (TOKENS, D), 1.0, 6.0, ((0, 32),))
    routes_keys = jax.random.split(jax.random.fold_in(seeds[1], 1), TOKENS // TOK_DEV)
    routes_turns = jax.random.permutation(jax.random.fold_in(seeds[1], 3), TOKENS // TOK_DEV)
    routes = jax.vmap(lambda own, number: shared_out(jax.random.fold_in(seeds[1], 2), own, number, TOK_DEV, EXPERTS, TOP, CAP, 2))(routes_keys, routes_turns).reshape((TOKENS, TOP))
    gates = jnp.clip(jnp.exp(math.log(1.0) - 2.9957323 * jax.random.uniform(seeds[2], (TOKENS, TOP), jnp.float32) ** steps_of(seeds[2], (TOKENS, TOP), ((0, 32),), -0.2, 0.2)), 0.05, 1.0)
    grad_out = bell_draw(seeds[3], (TOKENS, D), 1.0, 6.0, ((0, 32),))
    w_gate = bell_draw(seeds[4], (EXPERTS, D, H), D ** -0.5, 0.125, ((0, 16), (1, 2)))
    w_up = bell_draw(seeds[5], (EXPERTS, D, H), D ** -0.5, 0.125, ((0, 16), (1, 2)))
    w_down = bell_draw(seeds[6], (EXPERTS, H, D), H ** -0.5, 0.21875, ((0, 16), (2, 2)))
    return {"tokens": tokens, "routes": routes, "gates": gates, "grad_out": grad_out, "w_gate": w_gate, "w_up": w_up, "w_down": w_down}


def silu_parts(pre):
    sig = jax.nn.sigmoid(pre)
    return pre * sig, sig * (1.0 + pre * (1.0 - sig))


def contract_last(left, right):
    return lax.dot_general(left, right, (((1,), (1,)), ((), ())), preferred_element_type=jnp.float32)


def reference(tokens, routes, gates, grad_out, w_gate, w_up, w_down):
    devices = N_DP * N_EXPERT
    flat = routes.reshape(-1).astype(jnp.int32)
    routed = TOKENS * TOP
    per_dev = TOK_DEV * TOP
    labels = jnp.arange(EXPERTS, dtype=jnp.int32)
    onehot = (flat[:, None] == labels[None, :]).astype(jnp.int32)
    blocked = onehot.reshape(devices, per_dev, EXPERTS)
    rank = (jnp.cumsum(blocked, axis=1) - blocked).reshape(routed, EXPERTS)
    rank = jnp.sum(rank * onehot, axis=1).astype(jnp.int32)
    device = (jnp.arange(routed, dtype=jnp.int32) // per_dev).astype(jnp.int32)
    position = device * CAP + rank
    table = jnp.full((EXPERTS, devices * CAP), routed, jnp.int32)
    table = table.at[flat, position].set(jnp.arange(routed, dtype=jnp.int32))
    padded_tokens = jnp.concatenate([tokens, jnp.zeros((1, D), jnp.bfloat16)], axis=0)
    padded_grads = jnp.concatenate([grad_out, jnp.zeros((1, D), jnp.bfloat16)], axis=0)
    padded_gates = jnp.concatenate([gates.reshape(-1), jnp.ones((1,), jnp.float32)], axis=0)

    def expert_step(carry, inputs):
        total, gate_grad = carry
        index, wg, wu, wd = inputs
        source = (index // TOP).astype(jnp.int32)
        x_rows = padded_tokens[source]
        scale = padded_gates[index]
        scaled = (scale[:, None] * padded_grads[source].astype(jnp.float32)).astype(jnp.bfloat16)
        pre_gate = jnp.dot(x_rows, wg, preferred_element_type=jnp.float32)
        pre_up = jnp.dot(x_rows, wu, preferred_element_type=jnp.float32)
        act, slope = silu_parts(pre_gate)
        hidden_f = act * pre_up
        hidden = hidden_f.astype(jnp.bfloat16)
        back = contract_last(scaled, wd)
        score = lax.optimization_barrier(jnp.sum(back * hidden_f, axis=1).astype(jnp.bfloat16)).astype(jnp.float32)
        d_gate = (back * pre_up * slope).astype(jnp.bfloat16)
        d_up = (back * act).astype(jnp.bfloat16)
        route_grad = (contract_last(d_gate, wg) + contract_last(d_up, wu)).astype(jnp.bfloat16)
        total = total.at[source].add(route_grad.astype(jnp.float32))
        gate_grad = gate_grad.at[index].set(score / scale)
        grouped_h = hidden.reshape(N_DP, N_EXPERT * CAP, H).astype(jnp.float32)
        grouped_s = scaled.reshape(N_DP, N_EXPERT * CAP, D).astype(jnp.float32)
        partial_value = jnp.einsum("gsh,gsd->ghd", grouped_h, grouped_s)
        summed = jnp.sum(lax.optimization_barrier(partial_value.astype(jnp.bfloat16)).astype(jnp.float32), axis=0)
        return (total, gate_grad), summed

    start = (jnp.zeros((TOKENS + 1, D), jnp.float32), jnp.zeros((routed + 1,), jnp.float32))
    (total, gate_grad), grad_down = lax.scan(expert_step, start, (table, w_gate, w_up, w_down))
    grad_tokens = total[:TOKENS].astype(jnp.bfloat16)
    grad_gates = gate_grad[:routed].reshape(TOKENS, TOP)
    return grad_tokens, grad_gates, grad_down
```

```python
import functools

import jax
import jax.numpy as jnp
from jax import lax
from jax.experimental import pallas as pl
from jax.experimental.pallas import tpu as pltpu
from jax.sharding import PartitionSpec as P

LANES = 128
VMEM_BYTES = 56 * 1024 * 1024


def contract_last(left, right):
    return lax.dot_general(
        left, right, (((1,), (1,)), ((), ())), preferred_element_type=jnp.float32
    )


def contract_first(left, right):
    return lax.dot_general(
        left, right, (((0,), (0,)), ((), ())), preferred_element_type=jnp.float32
    )


def tile_of(extent, most):
    return most if extent % most == 0 else extent


def slot_positions(routes, experts, stride, base):
    top, count = routes.shape
    labels = lax.broadcasted_iota(jnp.int32, (experts, count), 0)
    named = [labels == routes[k : k + 1, :] for k in range(top)]
    marks = sum(jnp.where(m, 1.0, 0.0) for m in named)
    earlier = lax.broadcasted_iota(jnp.int32, (count, count), 0) < lax.broadcasted_iota(
        jnp.int32, (count, count), 1
    )
    rank = jnp.dot(
        marks.astype(jnp.bfloat16),
        jnp.where(earlier, 1.0, 0.0).astype(jnp.bfloat16),
        preferred_element_type=jnp.float32,
    )
    slot = rank + (labels * stride + base).astype(jnp.float32)
    return [
        jnp.sum(jnp.where(m, slot, 0.0), axis=0, keepdims=True).astype(jnp.int32) for m in named
    ]


def dispatch_tokens(experts, cap, group_ref, routes_ref, tokens_ref, out_ref, pos_ref, pick_ref):
    @pl.when(pl.program_id(0) == 0)
    def _():
        pos = slot_positions(routes_ref[...], experts, cap, 0)
        slots, count = pick_ref.shape
        rows = lax.broadcasted_iota(jnp.int32, (slots, count), 0)
        pick_ref[...] = sum(jnp.where(rows == p, 1.0, 0.0) for p in pos).astype(jnp.bfloat16)
        for k, p in enumerate(pos):
            pos_ref[k : k + 1, :] = p

    out_ref[...] = jnp.dot(
        pick_ref[...], tokens_ref[...], preferred_element_type=jnp.float32
    ).astype(out_ref.dtype)


def dispatch_scaled(experts, cap, groups, group_ref, meta_ref, own_ref, *rest):
    others, (out_ref, pick_ref, scale_ref) = rest[: groups - 1], rest[groups - 1 :]
    count = own_ref.shape[0]
    slots = out_ref.shape[0]

    @pl.when(pl.program_id(0) == 0)
    def _():
        rows = lax.broadcasted_iota(jnp.int32, (slots, count), 0)
        total = jnp.zeros((slots, 1), jnp.float32)
        for q in range(groups):
            top = meta_ref.shape[1] // 2
            routes = meta_ref[q, :top, :].astype(jnp.int32)
            pos = slot_positions(routes, experts, groups * cap, q * cap)
            hit = jnp.zeros((slots, count), jnp.float32)
            weight = jnp.zeros((slots, count), jnp.float32)
            for k, p in enumerate(pos):
                here = rows == p
                hit = hit + jnp.where(here, 1.0, 0.0)
                weight = weight + jnp.where(here, meta_ref[q, top + k : top + k + 1, :], 0.0)
            pick_ref[:, q * count : (q + 1) * count] = hit.astype(jnp.bfloat16)
            total = total + jnp.sum(weight, axis=1, keepdims=True)
        scale_ref[...] = jnp.broadcast_to(total, scale_ref.shape)

    grads = jnp.concatenate([own_ref[...]] + [ref[...] for ref in others], axis=0)
    rows = jnp.dot(pick_ref[...], grads, preferred_element_type=jnp.float32)
    out_ref[...] = (scale_ref[:, :1] * rows).astype(out_ref.dtype)


def expert_kernel(groups, x_ref, *refs):
    gates, ups = refs[:groups], refs[groups : 2 * groups]
    parts = refs[2 * groups : 3 * groups]
    back_out, hidden_out, d_gate_ref, d_up_ref, score_ref = refs[3 * groups :]
    rows = x_ref.shape[0]
    share, hidden = gates[0].shape
    step = tile_of(hidden, 256)
    score_ref[...] = jnp.zeros_like(score_ref)

    @pl.loop(0, hidden // step)
    def _(j):
        cols = pl.ds(pl.multiple_of(j * step, step), step)
        pre_gate = jnp.zeros((rows, step), jnp.float32)
        pre_up = jnp.zeros((rows, step), jnp.float32)
        back = jnp.zeros((rows, step), jnp.float32)
        for k in range(groups):
            x = x_ref[:, k * share : (k + 1) * share]
            pre_gate += jnp.dot(x, gates[k][:, cols], preferred_element_type=jnp.float32)
            pre_up += jnp.dot(x, ups[k][:, cols], preferred_element_type=jnp.float32)
            back += parts[k][:, cols].astype(jnp.float32)
        sig = jax.nn.sigmoid(pre_gate)
        act = pre_gate * sig
        slope = sig * (1.0 + pre_gate * (1.0 - sig))
        hidden_f = act * pre_up
        hidden_out[:, cols] = hidden_f.astype(jnp.bfloat16)
        score_ref[...] += jnp.sum(back * hidden_f, axis=1, keepdims=True)
        d_gate_ref[:, cols] = (back * pre_up * slope).astype(jnp.bfloat16)
        d_up_ref[:, cols] = (back * act).astype(jnp.bfloat16)

    width = groups * share
    back_out[:, width:] = jnp.broadcast_to(score_ref[:, :1], (rows, LANES)).astype(jnp.bfloat16)
    block = tile_of(share, 256)
    for k in range(groups):

        @pl.loop(0, share // block)
        def _(c):
            at = pl.ds(pl.multiple_of(c * block, block), block)
            grad = contract_last(d_gate_ref[...], gates[k][at, :])
            grad += contract_last(d_up_ref[...], ups[k][at, :])
            out = pl.ds(pl.multiple_of(k * share + c * block, block), block)
            back_out[:, out] = grad.astype(jnp.bfloat16)


def combine_kernel(group_ref, pos_ref, gate_ref, rows_ref, score_ref, tokens_ref, gates_ref):
    count, top = pos_ref.shape
    slots = rows_ref.shape[0]
    lanes = lax.broadcasted_iota(jnp.int32, (count, slots), 1)
    picks = [
        jnp.where(lanes == pos_ref[:, k : k + 1], 1.0, 0.0).astype(jnp.bfloat16)
        for k in range(top)
    ]
    tokens_ref[...] = jnp.dot(
        sum(picks), rows_ref[...], preferred_element_type=jnp.float32
    ).astype(tokens_ref.dtype)

    @pl.when(pl.program_id(0) == 0)
    def _():
        for k in range(top):
            score = jnp.dot(picks[k], score_ref[...], preferred_element_type=jnp.float32)
            gates_ref[:, k : k + 1] = score[:, :1] / gate_ref[:, k : k + 1]


def per_device(tokens, routes, gates, grad_out, w_gate, w_up, w_down):
    experts = lax.axis_size("expert")
    groups = lax.axis_size("dp")
    group = lax.axis_index("dp")
    count, width = tokens.shape
    top = routes.shape[1]
    cap = 3 * count * top // (2 * experts)
    slots = experts * cap
    share = width // groups
    hidden = w_gate.shape[2]
    params = pltpu.CompilerParams(vmem_limit_bytes=VMEM_BYTES)
    here = group.astype(jnp.int32).reshape(1)

    def shifted(value, by):
        return lax.ppermute(value, "dp", [(i, (i + by) % groups) for i in range(groups)])

    def own_block(k, here_ref):
        return lax.rem(here_ref[0] - k + groups, groups)

    routes_t = jnp.transpose(routes)
    meta = jnp.concatenate([routes_t.astype(jnp.float32), jnp.transpose(gates)], axis=0)
    metas = [meta] + [shifted(meta, k) for k in range(1, groups)]
    grads = [
        shifted(
            lax.dynamic_slice(grad_out, (0, lax.rem(group + k, groups) * share), (count, share)), k
        )
        for k in range(1, groups)
    ]
    gate_parts = [w_gate[0]] + [shifted(w_gate[0], k) for k in range(1, groups)]
    up_parts = [w_up[0]] + [shifted(w_up[0], k) for k in range(1, groups)]

    block = tile_of(share, 512)
    scaled = pl.pallas_call(
        functools.partial(dispatch_scaled, experts, cap, groups),
        out_shape=jax.ShapeDtypeStruct((groups * slots, share), jnp.bfloat16),
        grid_spec=pltpu.PrefetchScalarGridSpec(
            num_scalar_prefetch=1,
            grid=(share // block,),
            in_specs=[
                pl.BlockSpec((groups, 2 * top, count), lambda c, g: (0, 0, 0)),
                pl.BlockSpec((count, block), lambda c, g: (0, g[0] * (share // block) + c)),
            ]
            + [pl.BlockSpec((count, block), lambda c, g: (0, c))] * (groups - 1),
            out_specs=pl.BlockSpec((groups * slots, block), lambda c, g: (0, c)),
            scratch_shapes=[
                pltpu.VMEM((groups * slots, groups * count), jnp.bfloat16),
                pltpu.VMEM((groups * slots, LANES), jnp.float32),
            ],
        ),
        compiler_params=params,
        name="dispatch_scaled",
    )(here, jnp.stack(metas), grad_out, *grads)
    scaled_rows = lax.all_to_all(
        scaled.reshape(experts, groups * cap, share), "expert", split_axis=0, concat_axis=0, tiled=True
    ).reshape(groups * slots, share)

    sent, pos = pl.pallas_call(
        functools.partial(dispatch_tokens, experts, cap),
        out_shape=(
            jax.ShapeDtypeStruct((slots, width), jnp.bfloat16),
            jax.ShapeDtypeStruct((top, count), jnp.int32),
        ),
        grid_spec=pltpu.PrefetchScalarGridSpec(
            num_scalar_prefetch=1,
            grid=(groups,),
            in_specs=[
                pl.BlockSpec((top, count), lambda k, g: (0, 0)),
                pl.BlockSpec((count, share), lambda k, g: (0, own_block(k, g))),
            ],
            out_specs=(
                pl.BlockSpec((slots, share), lambda k, g: (0, k)),
                pl.BlockSpec((top, count), lambda k, g: (0, 0)),
            ),
            scratch_shapes=[pltpu.VMEM((slots, count), jnp.bfloat16)],
        ),
        compiler_params=params,
        name="dispatch_tokens",
    )(here, routes_t, tokens)
    x_rows = lax.all_to_all(
        sent.reshape(experts, cap, width), "expert", split_axis=0, concat_axis=0, tiled=True
    ).reshape(slots, width)

    partial = contract_last(scaled_rows, w_down[0]).reshape(experts, groups, cap, hidden)
    back_parts = [partial[:, 0].reshape(slots, hidden)] + [
        shifted(partial[:, k].reshape(slots, hidden).astype(jnp.bfloat16), -k)
        for k in range(1, groups)
    ]

    returning, hidden_own = pl.pallas_call(
        functools.partial(expert_kernel, groups),
        out_shape=(
            jax.ShapeDtypeStruct((slots, width + LANES), jnp.bfloat16),
            jax.ShapeDtypeStruct((slots, hidden), jnp.bfloat16),
        ),
        scratch_shapes=[
            pltpu.VMEM((slots, hidden), jnp.bfloat16),
            pltpu.VMEM((slots, hidden), jnp.bfloat16),
            pltpu.VMEM((slots, LANES), jnp.float32),
        ],
        compiler_params=params,
        name="expert_rows",
    )(x_rows, *gate_parts, *up_parts, *back_parts)

    returned = lax.all_to_all(
        returning.reshape(experts, cap, width + LANES),
        "expert",
        split_axis=0,
        concat_axis=0,
        tiled=True,
    ).reshape(slots, width + LANES)

    hiddens = [hidden_own] + [shifted(hidden_own, k) for k in range(1, groups)]
    hidden_all = jnp.stack([h.reshape(experts, cap, hidden) for h in hiddens], axis=1)
    grad_down = contract_first(hidden_all.reshape(groups * slots, hidden), scaled_rows)[None]

    grad_tokens, grad_gates = pl.pallas_call(
        combine_kernel,
        out_shape=(
            jax.ShapeDtypeStruct((count, width), jnp.bfloat16),
            jax.ShapeDtypeStruct((count, top), jnp.float32),
        ),
        grid_spec=pltpu.PrefetchScalarGridSpec(
            num_scalar_prefetch=1,
            grid=(groups,),
            in_specs=[
                pl.BlockSpec((count, top), lambda k, g: (0, 0)),
                pl.BlockSpec((count, top), lambda k, g: (0, 0)),
                pl.BlockSpec((slots, share), lambda k, g: (0, k)),
                pl.BlockSpec((slots, LANES), lambda k, g: (0, width // LANES)),
            ],
            out_specs=(
                pl.BlockSpec((count, share), lambda k, g: (0, own_block(k, g))),
                pl.BlockSpec((count, top), lambda k, g: (0, 0)),
            ),
        ),
        compiler_params=params,
        name="combine",
    )(here, jnp.transpose(pos), gates, returned, returned)
    return (grad_tokens, grad_gates, grad_down)


def solution(mesh):
    placed = (
        P(("dp", "expert"), None),
        P(("dp", "expert"), None),
        P(("dp", "expert"), None),
        P(("dp", "expert"), None),
        P("expert", "dp", None),
        P("expert", "dp", None),
        P("expert", None, "dp"),
    )
    return jax.shard_map(
        per_device,
        mesh=mesh,
        in_specs=placed,
        out_specs=(P(("dp", "expert"), None), P(("dp", "expert"), None), P("expert", None, "dp")),
        check_vma=False,
    )
```

```python
import functools

import jax
import jax.numpy as jnp
from jax import lax
from jax.experimental import pallas as pl
from jax.experimental.pallas import tpu as pltpu
from jax.sharding import PartitionSpec as P

LANES = 128
VMEM_BYTES = 24 * 1024 * 1024


def contract_last(left, right):
    return lax.dot_general(
        left, right, (((1,), (1,)), ((), ())), preferred_element_type=jnp.float32
    )


def contract_first(left, right):
    return lax.dot_general(
        left, right, (((0,), (0,)), ((), ())), preferred_element_type=jnp.float32
    )


def tile_of(extent, most):
    return most if extent % most == 0 else extent


def slot_positions(routes, experts, stride, base):
    top, count = routes.shape
    labels = lax.broadcasted_iota(jnp.int32, (experts, count), 0)
    named = [labels == routes[k : k + 1, :] for k in range(top)]
    marks = sum(jnp.where(m, 1.0, 0.0) for m in named)
    earlier = lax.broadcasted_iota(jnp.int32, (count, count), 0) < lax.broadcasted_iota(
        jnp.int32, (count, count), 1
    )
    rank = jnp.dot(
        marks.astype(jnp.bfloat16),
        jnp.where(earlier, 1.0, 0.0).astype(jnp.bfloat16),
        preferred_element_type=jnp.float32,
    )
    slot = rank + (labels * stride + base).astype(jnp.float32)
    return [
        jnp.sum(jnp.where(m, slot, 0.0), axis=0, keepdims=True).astype(jnp.int32) for m in named
    ]


def dispatch_tokens(experts, cap, group_ref, routes_ref, tokens_ref, out_ref, pos_ref, pick_ref):
    @pl.when(pl.program_id(0) == 0)
    def _():
        pos = slot_positions(routes_ref[...], experts, cap, 0)
        slots, count = pick_ref.shape
        rows = lax.broadcasted_iota(jnp.int32, (slots, count), 0)
        pick_ref[...] = sum(jnp.where(rows == p, 1.0, 0.0) for p in pos).astype(jnp.bfloat16)
        for k, p in enumerate(pos):
            pos_ref[k : k + 1, :] = p

    out_ref[...] = jnp.dot(
        pick_ref[...], tokens_ref[...], preferred_element_type=jnp.float32
    ).astype(out_ref.dtype)


def dispatch_scaled(experts, cap, groups, group_ref, *rest):
    routes_refs, gate_refs = rest[:groups], rest[groups : 2 * groups]
    grad_refs, (out_ref, pick_ref, scale_ref) = rest[2 * groups : 3 * groups], rest[3 * groups :]
    count = grad_refs[0].shape[0]
    slots = out_ref.shape[0]

    @pl.when(pl.program_id(0) == 0)
    def _():
        rows = lax.broadcasted_iota(jnp.int32, (slots, count), 0)
        total = jnp.zeros((slots, 1), jnp.float32)
        for q in range(groups):
            pos = slot_positions(routes_refs[q][...], experts, groups * cap, q * cap)
            hit = jnp.zeros((slots, count), jnp.float32)
            weight = jnp.zeros((slots, count), jnp.float32)
            for k, p in enumerate(pos):
                here = rows == p
                hit = hit + jnp.where(here, 1.0, 0.0)
                weight = weight + jnp.where(here, gate_refs[q][k : k + 1, :], 0.0)
            pick_ref[:, q * count : (q + 1) * count] = hit.astype(jnp.bfloat16)
            total = total + jnp.sum(weight, axis=1, keepdims=True)
        scale_ref[...] = jnp.broadcast_to(total, scale_ref.shape)

    grads = jnp.concatenate([ref[...] for ref in grad_refs], axis=0)
    rows = jnp.dot(pick_ref[...], grads, preferred_element_type=jnp.float32)
    out_ref[...] = (scale_ref[:, :1] * rows).astype(out_ref.dtype)


def expert_kernel(groups, x_ref, *refs):
    gates, ups = refs[:groups], refs[groups : 3 * groups - 1]
    parts = refs[3 * groups - 1 : 4 * groups - 1]
    back_out, hidden_out, d_gate_ref, d_up_ref, score_ref = refs[4 * groups - 1 :]
    rows = x_ref.shape[0]
    hidden = gates[0].shape[1]
    step = tile_of(hidden, 256)
    score_ref[...] = jnp.zeros_like(score_ref)

    def against(weights, cols):
        total, at = jnp.zeros((rows, step), jnp.float32), 0
        for ref in weights:
            x = x_ref[:, at : at + ref.shape[0]]
            total += jnp.dot(x, ref[:, cols], preferred_element_type=jnp.float32)
            at += ref.shape[0]
        return total

    @pl.loop(0, hidden // step)
    def _(j):
        cols = pl.ds(pl.multiple_of(j * step, step), step)
        pre_gate = against(gates, cols)
        pre_up = against(ups, cols)
        back = sum(part[:, cols].astype(jnp.float32) for part in parts)
        sig = jax.nn.sigmoid(pre_gate)
        act = pre_gate * sig
        slope = sig * (1.0 + pre_gate * (1.0 - sig))
        hidden_f = act * pre_up
        hidden_out[:, cols] = hidden_f.astype(jnp.bfloat16)
        score_ref[...] += jnp.sum(back * hidden_f, axis=1, keepdims=True)
        d_gate_ref[:, cols] = (back * pre_up * slope).astype(jnp.bfloat16)
        d_up_ref[:, cols] = (back * act).astype(jnp.bfloat16)

    share = gates[0].shape[0]
    width = groups * share
    back_out[:, width:] = jnp.broadcast_to(score_ref[:, :1], (rows, LANES)).astype(jnp.bfloat16)
    at = 0
    for ref in ups:
        extent = ref.shape[0]
        gate = gates[at // share]
        block = tile_of(extent, 256)

        @pl.loop(0, extent // block)
        def _(c, ref=ref, gate=gate, at=at, block=block):
            rows_up = pl.ds(pl.multiple_of(c * block, block), block)
            rows_gate = pl.ds(pl.multiple_of(at % share + c * block, block), block)
            grad = contract_last(d_gate_ref[...], gate[rows_gate, :])
            grad += contract_last(d_up_ref[...], ref[rows_up, :])
            out = pl.ds(pl.multiple_of(at + c * block, block), block)
            back_out[:, out] = grad.astype(jnp.bfloat16)

        at += extent


def combine_kernel(group_ref, pos_ref, gate_ref, rows_ref, score_ref, tokens_ref, gates_ref):
    top, count = pos_ref.shape
    slots = rows_ref.shape[0]
    places = lax.broadcasted_iota(jnp.int32, (slots, count), 0)
    picks = [
        jnp.where(places == pos_ref[k : k + 1, :], 1.0, 0.0).astype(jnp.bfloat16)
        for k in range(top)
    ]
    tokens_ref[...] = contract_first(sum(picks), rows_ref[...]).astype(tokens_ref.dtype)

    @pl.when(pl.program_id(0) == 0)
    def _():
        for k in range(top):
            score = contract_first(score_ref[...], picks[k])
            gates_ref[k : k + 1, :] = score[:1, :] / gate_ref[k : k + 1, :]


def per_device(tokens, routes, gates, grad_out, w_gate, w_up, w_down):
    experts = lax.axis_size("expert")
    groups = lax.axis_size("dp")
    group = lax.axis_index("dp")
    count, width = tokens.shape
    top = routes.shape[1]
    cap = 3 * count * top // (2 * experts)
    slots = experts * cap
    share = width // groups
    hidden = w_gate.shape[2]
    params = pltpu.CompilerParams(vmem_limit_bytes=VMEM_BYTES)
    here = group.astype(jnp.int32).reshape(1)

    def shifted(value, by):
        return lax.ppermute(value, "dp", [(i, (i + by) % groups) for i in range(groups)])

    def own_block(k, here_ref):
        return lax.rem(here_ref[0] - k + groups, groups)

    routes_t = jnp.transpose(routes)
    gates_t = jnp.transpose(gates)
    routes_all = [routes_t] + [shifted(routes_t, k) for k in range(1, groups)]
    gates_all = [gates_t] + [shifted(gates_t, k) for k in range(1, groups)]
    grads = [
        shifted(
            lax.dynamic_slice(grad_out, (0, lax.rem(group + k, groups) * share), (count, share)), k
        )
        for k in range(1, groups)
    ]
    half = share // 2
    gate_parts = [shifted(w_gate[0], k) for k in range(1, groups)]
    up_first = [shifted(w_up[0, :half], k) for k in range(1, groups)]
    up_second = [shifted(w_up[0, half:], k) for k in range(1, groups)]

    block = tile_of(share, 512)
    scaled = pl.pallas_call(
        functools.partial(dispatch_scaled, experts, cap, groups),
        out_shape=jax.ShapeDtypeStruct((groups * slots, share), jnp.bfloat16),
        grid_spec=pltpu.PrefetchScalarGridSpec(
            num_scalar_prefetch=1,
            grid=(share // block,),
            in_specs=[
                pl.BlockSpec((top, count), lambda c, g: (0, 0)),
            ]
            * (2 * groups)
            + [pl.BlockSpec((count, block), lambda c, g: (0, g[0] * (share // block) + c))]
            + [pl.BlockSpec((count, block), lambda c, g: (0, c))] * (groups - 1),
            out_specs=pl.BlockSpec((groups * slots, block), lambda c, g: (0, c)),
            scratch_shapes=[
                pltpu.VMEM((groups * slots, groups * count), jnp.bfloat16),
                pltpu.VMEM((groups * slots, LANES), jnp.float32),
            ],
        ),
        compiler_params=params,
        name="dispatch_scaled",
    )(here, *routes_all, *gates_all, grad_out, *grads)
    scaled_rows = lax.all_to_all(
        scaled.reshape(experts, groups * cap, share), "expert", split_axis=0, concat_axis=0, tiled=True
    ).reshape(groups * slots, share)

    sent, pos = pl.pallas_call(
        functools.partial(dispatch_tokens, experts, cap),
        out_shape=(
            jax.ShapeDtypeStruct((slots, width), jnp.bfloat16),
            jax.ShapeDtypeStruct((top, count), jnp.int32),
        ),
        grid_spec=pltpu.PrefetchScalarGridSpec(
            num_scalar_prefetch=1,
            grid=(groups,),
            in_specs=[
                pl.BlockSpec((top, count), lambda k, g: (0, 0)),
                pl.BlockSpec((count, share), lambda k, g: (0, own_block(k, g))),
            ],
            out_specs=(
                pl.BlockSpec((slots, share), lambda k, g: (0, k)),
                pl.BlockSpec((top, count), lambda k, g: (0, 0)),
            ),
            scratch_shapes=[pltpu.VMEM((slots, count), jnp.bfloat16)],
        ),
        compiler_params=params,
        name="dispatch_tokens",
    )(here, routes_t, tokens)
    sent, *gate_parts = lax.optimization_barrier((sent, *gate_parts))
    x_rows = lax.all_to_all(
        sent.reshape(experts, cap, width), "expert", split_axis=0, concat_axis=0, tiled=True
    ).reshape(slots, width)

    partial = contract_last(scaled_rows, w_down[0]).reshape(experts, groups, cap, hidden)
    partial, *up_first = lax.optimization_barrier((partial, *up_first))
    back_parts = [partial[:, 0].reshape(slots, hidden)] + [
        shifted(partial[:, k].reshape(slots, hidden).astype(jnp.bfloat16), -k)
        for k in range(1, groups)
    ]

    returning, hidden_own = pl.pallas_call(
        functools.partial(expert_kernel, groups),
        out_shape=(
            jax.ShapeDtypeStruct((slots, width + LANES), jnp.bfloat16),
            jax.ShapeDtypeStruct((slots, hidden), jnp.bfloat16),
        ),
        scratch_shapes=[
            pltpu.VMEM((slots, hidden), jnp.bfloat16),
            pltpu.VMEM((slots, hidden), jnp.bfloat16),
            pltpu.VMEM((slots, LANES), jnp.float32),
        ],
        compiler_params=params,
        name="expert_rows",
    )(
        x_rows,
        w_gate[0],
        *gate_parts,
        w_up[0],
        *[part for pair in zip(up_first, up_second) for part in pair],
        *back_parts,
    )

    returned = lax.all_to_all(
        returning.reshape(experts, cap, width + LANES),
        "expert",
        split_axis=0,
        concat_axis=0,
        tiled=True,
    ).reshape(slots, width + LANES)

    hiddens = [hidden_own] + [shifted(hidden_own, k) for k in range(1, groups)]
    hidden_all = jnp.stack([h.reshape(experts, cap, hidden) for h in hiddens], axis=1)
    grad_down = contract_first(hidden_all.reshape(groups * slots, hidden), scaled_rows)[None]

    grad_tokens, grad_gates = pl.pallas_call(
        combine_kernel,
        out_shape=(
            jax.ShapeDtypeStruct((count, width), jnp.bfloat16),
            jax.ShapeDtypeStruct((top, count), jnp.float32),
        ),
        grid_spec=pltpu.PrefetchScalarGridSpec(
            num_scalar_prefetch=1,
            grid=(groups,),
            in_specs=[
                pl.BlockSpec((top, count), lambda k, g: (0, 0)),
                pl.BlockSpec((top, count), lambda k, g: (0, 0)),
                pl.BlockSpec((slots, share), lambda k, g: (0, k)),
                pl.BlockSpec((slots, LANES), lambda k, g: (0, width // LANES)),
            ],
            out_specs=(
                pl.BlockSpec((count, share), lambda k, g: (0, own_block(k, g))),
                pl.BlockSpec((top, count), lambda k, g: (0, 0)),
            ),
        ),
        compiler_params=params,
        name="combine",
    )(here, pos, gates_t, returned, returned)
    return (grad_tokens, jnp.transpose(grad_gates), grad_down)


def solution(mesh):
    placed = (
        P(("dp", "expert"), None),
        P(("dp", "expert"), None),
        P(("dp", "expert"), None),
        P(("dp", "expert"), None),
        P("expert", "dp", None),
        P("expert", "dp", None),
        P("expert", None, "dp"),
    )
    return jax.shard_map(
        per_device,
        mesh=mesh,
        in_specs=placed,
        out_specs=(P(("dp", "expert"), None), P(("dp", "expert"), None), P("expert", None, "dp")),
        check_vma=False,
    )
```

```python
import functools

import jax
import jax.numpy as jnp
from jax import lax
from jax.experimental import pallas as pl
from jax.experimental.pallas import tpu as pltpu
from jax.sharding import PartitionSpec as P

LANES = 128
VMEM_BYTES = 24 * 1024 * 1024


def contract_last(left, right):
    return lax.dot_general(
        left, right, (((1,), (1,)), ((), ())), preferred_element_type=jnp.float32
    )


def contract_first(left, right):
    return lax.dot_general(
        left, right, (((0,), (0,)), ((), ())), preferred_element_type=jnp.float32
    )


def tile_of(extent, most):
    return most if extent % most == 0 else extent


def slot_positions(labels_of, experts, stride, base):
    top, count = labels_of.shape
    labels = lax.broadcasted_iota(jnp.int32, (experts, count), 0)
    named = [labels == labels_of[k : k + 1, :] for k in range(top)]
    marks = sum(jnp.where(m, 1.0, 0.0) for m in named)
    earlier = lax.broadcasted_iota(jnp.int32, (count, count), 0) < lax.broadcasted_iota(
        jnp.int32, (count, count), 1
    )
    rank = jnp.dot(
        marks.astype(jnp.bfloat16),
        jnp.where(earlier, 1.0, 0.0).astype(jnp.bfloat16),
        preferred_element_type=jnp.float32,
    )
    slot = rank + (labels * stride + base).astype(jnp.float32)
    return [
        jnp.sum(jnp.where(m, slot, 0.0), axis=0, keepdims=True).astype(jnp.int32) for m in named
    ]


def gather_blocks(refs, part=slice(None), cols=slice(None)):
    if len(refs) == 1:
        return refs[0][part, cols]
    return jnp.concatenate(
        [ref[:, cols].astype(jnp.float32)[part] for ref in refs], axis=0
    ).astype(refs[0].dtype)


def scatter_blocks(refs, rows, cols=slice(None)):
    each = rows.shape[0] // len(refs)
    for i, ref in enumerate(refs):
        ref[:, cols] = rows[i * each : (i + 1) * each].astype(ref.dtype)


def dispatch_tokens(experts, cap, place_ref, routes_ref, tokens_ref, pos_ref, *refs):
    outs, pick_ref = refs[:-1], refs[-1]

    @pl.when(pl.program_id(0) == 0)
    def _():
        pos = slot_positions(routes_ref[...] ^ place_ref[1], experts, cap, 0)
        slots, count = pick_ref.shape
        rows = lax.broadcasted_iota(jnp.int32, (slots, count), 0)
        pick_ref[...] = sum(jnp.where(rows == p, 1.0, 0.0) for p in pos).astype(jnp.bfloat16)
        for k, p in enumerate(pos):
            pos_ref[k : k + 1, :] = p

    scatter_blocks(
        outs, jnp.dot(pick_ref[...], tokens_ref[...], preferred_element_type=jnp.float32)
    )


def dispatch_scaled(experts, cap, groups, place_ref, *refs):
    routes_refs, gate_refs = refs[:groups], refs[groups : 2 * groups]
    grad_refs, outs = refs[2 * groups : 3 * groups], refs[3 * groups : -2]
    pick_ref, scale_ref = refs[-2:]
    count = grad_refs[0].shape[0]
    slots = pick_ref.shape[0]

    @pl.when(pl.program_id(0) == 0)
    def _():
        rows = lax.broadcasted_iota(jnp.int32, (slots, count), 0)
        total = jnp.zeros((slots, 1), jnp.float32)
        for q in range(groups):
            labels = routes_refs[q][...] ^ place_ref[1]
            pos = slot_positions(labels, experts, groups * cap, q * cap)
            hit = jnp.zeros((slots, count), jnp.float32)
            weight = jnp.zeros((slots, count), jnp.float32)
            for k, p in enumerate(pos):
                here = rows == p
                hit = hit + jnp.where(here, 1.0, 0.0)
                weight = weight + jnp.where(here, gate_refs[q][k : k + 1, :], 0.0)
            pick_ref[:, q * count : (q + 1) * count] = hit.astype(jnp.bfloat16)
            total = total + jnp.sum(weight, axis=1, keepdims=True)
        scale_ref[...] = jnp.broadcast_to(total, scale_ref.shape)

    grads = jnp.concatenate([ref[...] for ref in grad_refs], axis=0)
    rows = jnp.dot(pick_ref[...], grads, preferred_element_type=jnp.float32)
    scatter_blocks(outs, scale_ref[:, :1] * rows)


def back_kernel(groups, cap, blocks, *refs):
    rows, (down_ref, own_ref), rest = refs[:blocks], refs[blocks : blocks + 2], refs[blocks + 2 :]
    others, all_ref = rest[: groups - 1], rest[groups - 1]
    slots = own_ref.shape[0]
    for q in range(groups):
        if blocks == 1:
            value = rows[0][...].reshape(slots // cap, groups, cap, -1)[:, q]
            value = value.reshape(slots, -1)
        else:
            value = gather_blocks(rows, slice(q * cap, (q + 1) * cap))
        all_ref[q * slots : (q + 1) * slots, :] = value
    hidden = down_ref.shape[0]
    step = tile_of(hidden, 256)

    @pl.loop(0, hidden // step)
    def _(j):
        cols = pl.ds(pl.multiple_of(j * step, step), step)
        for q, ref in enumerate((own_ref, *others)):
            part = contract_last(all_ref[q * slots : (q + 1) * slots, :], down_ref[cols, :])
            ref[:, cols] = part.astype(ref.dtype)


def forward_kernel(groups, blocks, *refs):
    rows, weights = refs[:blocks], refs[blocks : blocks + 2 * groups]
    pre_gate_ref, pre_up_ref, hidden_ref, x_ref = refs[blocks + 2 * groups :]
    gates, ups = weights[:groups], weights[groups:]
    share, hidden = gates[0].shape
    for k in range(groups):
        cols = slice(k * share, (k + 1) * share)
        x_ref[:, cols] = gather_blocks(rows, cols=cols)
    step = tile_of(hidden, 256)

    def against(parts, cols):
        return sum(
            jnp.dot(
                x_ref[:, k * share : (k + 1) * share],
                ref[:, cols],
                preferred_element_type=jnp.float32,
            )
            for k, ref in enumerate(parts)
        )

    @pl.loop(0, hidden // step)
    def _(j):
        cols = pl.ds(pl.multiple_of(j * step, step), step)
        pre_gate = against(gates, cols)
        pre_up = against(ups, cols)
        pre_gate_ref[:, cols] = pre_gate
        pre_up_ref[:, cols] = pre_up
        hidden_ref[:, cols] = (pre_gate * jax.nn.sigmoid(pre_gate) * pre_up).astype(jnp.bfloat16)


def backward_kernel(groups, blocks, pre_gate_ref, pre_up_ref, *refs):
    parts, weights = refs[:groups], refs[groups : 3 * groups]
    outs = refs[3 * groups : 3 * groups + blocks]
    d_gate_ref, d_up_ref = refs[3 * groups + blocks :]
    gates, ups = weights[:groups], weights[groups:]
    share, hidden = gates[0].shape
    pre_gate, pre_up = pre_gate_ref[...], pre_up_ref[...]
    back = sum(part[...].astype(jnp.float32) for part in parts)
    sig = jax.nn.sigmoid(pre_gate)
    act = pre_gate * sig
    slope = sig * (1.0 + pre_gate * (1.0 - sig))
    score = jnp.sum(back * (act * pre_up), axis=1, keepdims=True)
    d_gate_ref[...] = (back * pre_up * slope).astype(jnp.bfloat16)
    d_up_ref[...] = (back * act).astype(jnp.bfloat16)
    width = groups * share
    scatter_blocks(
        outs, jnp.broadcast_to(score, (score.shape[0], LANES)), slice(width, width + LANES)
    )
    block = tile_of(share, 256)
    for k in range(groups):

        @pl.loop(0, share // block)
        def _(c, k=k):
            at = pl.ds(pl.multiple_of(c * block, block), block)
            grad = contract_last(d_gate_ref[...], gates[k][at, :])
            grad += contract_last(d_up_ref[...], ups[k][at, :])
            scatter_blocks(
                outs, grad, pl.ds(pl.multiple_of(k * share + c * block, block), block)
            )


def combine_kernel(groups, place_ref, pos_ref, gate_ref, *refs):
    rows, (tokens_ref, gates_ref) = refs[:-2], refs[-2:]
    top, count = pos_ref.shape
    slots = sum(ref.shape[0] for ref in rows)
    width = tokens_ref.shape[1]
    share = width // groups
    places = lax.broadcasted_iota(jnp.int32, (slots, count), 0)
    picks = [
        jnp.where(places == pos_ref[k : k + 1, :], 1.0, 0.0).astype(jnp.bfloat16)
        for k in range(top)
    ]
    both = sum(picks)
    for k in range(groups):
        at = lax.rem(place_ref[0] - k + groups, groups) * share
        value = gather_blocks(rows, cols=slice(k * share, (k + 1) * share))
        tokens_ref[:, pl.ds(pl.multiple_of(at, share), share)] = contract_first(
            both, value
        ).astype(tokens_ref.dtype)
    scores = gather_blocks(rows, cols=slice(width, width + LANES))
    for k in range(top):
        score = contract_first(scores, picks[k])
        gates_ref[k : k + 1, :] = score[:1, :] / gate_ref[k : k + 1, :]


def per_device(tokens, routes, gates, grad_out, w_gate, w_up, w_down):
    experts = lax.axis_size("expert")
    groups = lax.axis_size("dp")
    group = lax.axis_index("dp")
    count, width = tokens.shape
    top = routes.shape[1]
    cap = 3 * count * top // (2 * experts)
    slots = experts * cap
    share = width // groups
    hidden = w_gate.shape[2]
    params = pltpu.CompilerParams(vmem_limit_bytes=VMEM_BYTES)
    paired = cap % 8 == 0 and experts & (experts - 1) == 0
    blocks = experts if paired else 1
    me = lax.axis_index("expert") if paired else 0
    place = jnp.stack([group, jnp.int32(0) + me]).astype(jnp.int32)

    def shifted(value, by):
        return lax.ppermute(value, "dp", [(i, (i + by) % groups) for i in range(groups)])

    def exchanged(pieces):
        if paired:
            return [pieces[0]] + [
                lax.ppermute(pieces[s], "expert", [(i, i ^ s) for i in range(experts)])
                for s in range(1, experts)
            ]
        (whole,) = pieces
        split = whole.reshape(experts, whole.shape[0] // experts, whole.shape[1])
        moved = lax.all_to_all(split, "expert", split_axis=0, concat_axis=0, tiled=True)
        return [moved.reshape(whole.shape)]

    def own_block(k, place_ref):
        return lax.rem(place_ref[0] - k + groups, groups)

    whole_spec = pl.BlockSpec(memory_space=pltpu.VMEM)
    small_spec = pl.BlockSpec((top, count), lambda k, g: (0, 0))
    routes_t, gates_t = jnp.transpose(routes), jnp.transpose(gates)

    routes_all = [routes_t] + [shifted(routes_t, k) for k in range(1, groups)]
    gates_all = [gates_t] + [shifted(gates_t, k) for k in range(1, groups)]
    grads = [
        shifted(
            lax.dynamic_slice(grad_out, (0, lax.rem(group + k, groups) * share), (count, share)), k
        )
        for k in range(1, groups)
    ]
    gate_parts = [w_gate[0]] + [shifted(w_gate[0], k) for k in range(1, groups)]
    up_parts = [w_up[0]] + [shifted(w_up[0], k) for k in range(1, groups)]

    pos, *sent = pl.pallas_call(
        functools.partial(dispatch_tokens, experts, cap),
        out_shape=[jax.ShapeDtypeStruct((top, count), jnp.int32)]
        + [jax.ShapeDtypeStruct((slots // blocks, width), jnp.bfloat16)] * blocks,
        grid_spec=pltpu.PrefetchScalarGridSpec(
            num_scalar_prefetch=1,
            grid=(groups,),
            in_specs=[
                small_spec,
                pl.BlockSpec((count, share), lambda k, g: (0, own_block(k, g))),
            ],
            out_specs=[small_spec]
            + [pl.BlockSpec((slots // blocks, share), lambda k, g: (0, k))] * blocks,
            scratch_shapes=[pltpu.VMEM((slots, count), jnp.bfloat16)],
        ),
        compiler_params=params,
        name="dispatch_tokens",
    )(place, routes_t, tokens)
    x_rows = exchanged(sent)

    block = tile_of(share, 512)
    scaled = pl.pallas_call(
        functools.partial(dispatch_scaled, experts, cap, groups),
        out_shape=[jax.ShapeDtypeStruct((groups * slots // blocks, share), jnp.bfloat16)] * blocks,
        grid_spec=pltpu.PrefetchScalarGridSpec(
            num_scalar_prefetch=1,
            grid=(share // block,),
            in_specs=[small_spec] * (2 * groups)
            + [pl.BlockSpec((count, block), lambda c, g: (0, g[0] * (share // block) + c))]
            + [pl.BlockSpec((count, block), lambda c, g: (0, c))] * (groups - 1),
            out_specs=[pl.BlockSpec((groups * slots // blocks, block), lambda c, g: (0, c))]
            * blocks,
            scratch_shapes=[
                pltpu.VMEM((groups * slots, groups * count), jnp.bfloat16),
                pltpu.VMEM((groups * slots, LANES), jnp.float32),
            ],
        ),
        compiler_params=params,
        name="dispatch_scaled",
    )(place, *routes_all, *gates_all, grad_out, *grads)
    scaled_rows = exchanged(scaled)

    scaled_rows, x_rows = lax.optimization_barrier((scaled_rows, x_rows))

    back_own, *rest = pl.pallas_call(
        functools.partial(back_kernel, groups, cap, blocks),
        out_shape=[jax.ShapeDtypeStruct((slots, hidden), jnp.float32)]
        + [jax.ShapeDtypeStruct((slots, hidden), jnp.bfloat16)] * (groups - 1)
        + [jax.ShapeDtypeStruct((groups * slots, share), jnp.bfloat16)],
        compiler_params=params,
        name="back",
    )(*scaled_rows, w_down[0])
    scaled_all = rest[-1]
    back_parts = [back_own] + [shifted(rest[k - 1], -k) for k in range(1, groups)]

    pre_gate, pre_up, hidden_own = pl.pallas_call(
        functools.partial(forward_kernel, groups, blocks),
        out_shape=[
            jax.ShapeDtypeStruct((slots, hidden), jnp.float32),
            jax.ShapeDtypeStruct((slots, hidden), jnp.float32),
            jax.ShapeDtypeStruct((slots, hidden), jnp.bfloat16),
        ],
        scratch_shapes=[pltpu.VMEM((slots, width), jnp.bfloat16)],
        compiler_params=params,
        name="forward",
    )(*x_rows, *gate_parts, *up_parts)

    returning = pl.pallas_call(
        functools.partial(backward_kernel, groups, blocks),
        out_shape=[jax.ShapeDtypeStruct((slots // blocks, width + LANES), jnp.bfloat16)] * blocks,
        scratch_shapes=[
            pltpu.VMEM((slots, hidden), jnp.bfloat16),
            pltpu.VMEM((slots, hidden), jnp.bfloat16),
        ],
        compiler_params=params,
        name="backward",
    )(pre_gate, pre_up, *back_parts, *gate_parts, *up_parts)
    returned = exchanged(returning)

    hiddens = [hidden_own] + [shifted(hidden_own, k) for k in range(1, groups)]
    grad_down = contract_first(jnp.concatenate(hiddens, axis=0), scaled_all)[None]

    grad_tokens, grad_gates = pl.pallas_call(
        functools.partial(combine_kernel, groups),
        out_shape=(
            jax.ShapeDtypeStruct((count, width), jnp.bfloat16),
            jax.ShapeDtypeStruct((top, count), jnp.float32),
        ),
        in_specs=[pl.BlockSpec(memory_space=pltpu.SMEM)] + [whole_spec] * (2 + blocks),
        compiler_params=params,
        name="combine",
    )(place, pos, gates_t, *returned)
    return (grad_tokens, jnp.transpose(grad_gates), grad_down)


def solution(mesh):
    placed = (
        P(("dp", "expert"), None),
        P(("dp", "expert"), None),
        P(("dp", "expert"), None),
        P(("dp", "expert"), None),
        P("expert", "dp", None),
        P("expert", "dp", None),
        P("expert", None, "dp"),
    )
    return jax.shard_map(
        per_device,
        mesh=mesh,
        in_specs=placed,
        out_specs=(P(("dp", "expert"), None), P(("dp", "expert"), None), P("expert", None, "dp")),
        check_vma=False,
    )
```

```python
import functools

import jax
import jax.numpy as jnp
from jax import lax
from jax.experimental import pallas as pl
from jax.experimental.pallas import tpu as pltpu
from jax.sharding import PartitionSpec as P

LANES = 128
VMEM_BYTES = 24 * 1024 * 1024


def contract_last(left, right):
    return lax.dot_general(
        left, right, (((1,), (1,)), ((), ())), preferred_element_type=jnp.float32
    )


def contract_first(left, right):
    return lax.dot_general(
        left, right, (((0,), (0,)), ((), ())), preferred_element_type=jnp.float32
    )


def tile_of(extent, most):
    return most if extent % most == 0 else extent


def slot_positions(routes, experts, stride, base):
    top, count = routes.shape
    labels = lax.broadcasted_iota(jnp.int32, (experts, count), 0)
    named = [labels == routes[k : k + 1, :] for k in range(top)]
    marks = sum(jnp.where(m, 1.0, 0.0) for m in named)
    earlier = lax.broadcasted_iota(jnp.int32, (count, count), 0) < lax.broadcasted_iota(
        jnp.int32, (count, count), 1
    )
    rank = jnp.dot(
        marks.astype(jnp.bfloat16),
        jnp.where(earlier, 1.0, 0.0).astype(jnp.bfloat16),
        preferred_element_type=jnp.float32,
    )
    slot = rank + (labels * stride + base).astype(jnp.float32)
    return [
        jnp.sum(jnp.where(m, slot, 0.0), axis=0, keepdims=True).astype(jnp.int32) for m in named
    ]


def rows_of(ref, cap, which, cols):
    value = ref[:, cols].astype(jnp.float32)
    count, width = value.shape
    value = value.reshape(count // (2 * cap), 2, cap, width)[:, which]
    return value.reshape(count // 2, width).astype(ref.dtype)


def dispatch_kernel(experts, cap, groups, place_ref, *refs):
    routes_refs, gate_refs = refs[:groups], refs[groups : 2 * groups]
    tokens_ref, grad_refs = refs[2 * groups], refs[2 * groups + 1 : 3 * groups + 1]
    out_ref, pos_ref, pick_ref, scale_ref = refs[3 * groups + 1 :]
    rows = pick_ref.shape[0]
    count = tokens_ref.shape[0]
    places = lax.broadcasted_iota(jnp.int32, (rows, count), 0)

    for g in range(groups):

        @pl.when((pl.program_id(0) == g) & (pl.program_id(1) == 0))
        def _(g=g):
            pos = slot_positions(routes_refs[g][...], experts, 2 * cap, 0)
            if g == 0:
                pick_ref[:, :count] = sum(jnp.where(places == p, 1.0, 0.0) for p in pos).astype(
                    jnp.bfloat16
                )
                for k, p in enumerate(slot_positions(routes_refs[0][...], experts, cap, 0)):
                    pos_ref[k : k + 1, :] = p
            hit = jnp.zeros((rows, count), jnp.float32)
            weight = pick_ref[:, :count].astype(jnp.float32)
            for k, p in enumerate(pos):
                here = places == p + cap
                hit = hit + jnp.where(here, 1.0, 0.0)
                weight = weight + jnp.where(here, gate_refs[g][k : k + 1, :], 0.0)
            pick_ref[:, count:] = hit.astype(jnp.bfloat16)
            scale_ref[...] = jnp.broadcast_to(
                jnp.sum(weight, axis=1, keepdims=True), scale_ref.shape
            )

        @pl.when(pl.program_id(0) == g)
        def _(g=g):
            values = jnp.concatenate([tokens_ref[...], grad_refs[g][...]], axis=0)
            picked = jnp.dot(pick_ref[...], values, preferred_element_type=jnp.float32)
            out_ref[...] = (scale_ref[:, :1] * picked).astype(out_ref.dtype)


def back_kernel(groups, cap, rows_ref, down_ref, own_ref, *rest):
    others, all_ref = rest[: groups - 1], rest[groups - 1]
    slots, hidden = own_ref.shape
    share = down_ref.shape[1]
    for q in range(groups):
        all_ref[q * slots : (q + 1) * slots, :] = rows_of(
            rows_ref, cap, 1, slice(q * share, (q + 1) * share)
        )
    step = tile_of(hidden, 256)

    @pl.loop(0, hidden // step)
    def _(j):
        cols = pl.ds(pl.multiple_of(j * step, step), step)
        for q, ref in enumerate((own_ref, *others)):
            part = contract_last(all_ref[q * slots : (q + 1) * slots, :], down_ref[cols, :])
            ref[:, cols] = part.astype(ref.dtype)


def forward_kernel(groups, cap, rows_ref, *refs):
    gates, ups = refs[:groups], refs[groups : 2 * groups]
    pre_gate_ref, pre_up_ref, hidden_ref, x_ref = refs[2 * groups :]
    share, hidden = gates[0].shape
    for k in range(groups):
        cols = slice(k * share, (k + 1) * share)
        x_ref[:, cols] = rows_of(rows_ref, cap, 0, cols)
    step = tile_of(hidden, 256)

    def against(parts, cols):
        return sum(
            jnp.dot(
                x_ref[:, k * share : (k + 1) * share],
                ref[:, cols],
                preferred_element_type=jnp.float32,
            )
            for k, ref in enumerate(parts)
        )

    @pl.loop(0, hidden // step)
    def _(j):
        cols = pl.ds(pl.multiple_of(j * step, step), step)
        pre_gate = against(gates, cols)
        pre_up = against(ups, cols)
        pre_gate_ref[:, cols] = pre_gate
        pre_up_ref[:, cols] = pre_up
        hidden_ref[:, cols] = (pre_gate * jax.nn.sigmoid(pre_gate) * pre_up).astype(jnp.bfloat16)


def backward_kernel(groups, pre_gate_ref, pre_up_ref, *refs):
    parts, weights = refs[:groups], refs[groups : 3 * groups]
    out_ref, d_gate_ref, d_up_ref = refs[3 * groups :]
    gates, ups = weights[:groups], weights[groups:]
    share, hidden = gates[0].shape
    pre_gate, pre_up = pre_gate_ref[...], pre_up_ref[...]
    back = sum(part[...].astype(jnp.float32) for part in parts)
    sig = jax.nn.sigmoid(pre_gate)
    act = pre_gate * sig
    slope = sig * (1.0 + pre_gate * (1.0 - sig))
    score = jnp.sum(back * (act * pre_up), axis=1, keepdims=True)
    d_gate_ref[...] = (back * pre_up * slope).astype(jnp.bfloat16)
    d_up_ref[...] = (back * act).astype(jnp.bfloat16)
    width = groups * share
    out_ref[:, width:] = jnp.broadcast_to(score, (score.shape[0], LANES)).astype(out_ref.dtype)
    block = tile_of(share, 256)
    for k in range(groups):

        @pl.loop(0, share // block)
        def _(c, k=k):
            at = pl.ds(pl.multiple_of(c * block, block), block)
            grad = contract_last(d_gate_ref[...], gates[k][at, :])
            grad += contract_last(d_up_ref[...], ups[k][at, :])
            out = pl.ds(pl.multiple_of(k * share + c * block, block), block)
            out_ref[:, out] = grad.astype(out_ref.dtype)


def combine_kernel(groups, place_ref, pos_ref, gate_ref, rows_ref, tokens_ref, gates_ref):
    top, count = pos_ref.shape
    slots = rows_ref.shape[0]
    width = tokens_ref.shape[1]
    share = width // groups
    places = lax.broadcasted_iota(jnp.int32, (slots, count), 0)
    picks = [
        jnp.where(places == pos_ref[k : k + 1, :], 1.0, 0.0).astype(jnp.bfloat16)
        for k in range(top)
    ]
    both = sum(picks)
    for k in range(groups):
        at = lax.rem(place_ref[0] - k + groups, groups) * share
        tokens_ref[:, pl.ds(pl.multiple_of(at, share), share)] = contract_first(
            both, rows_ref[:, k * share : (k + 1) * share]
        ).astype(tokens_ref.dtype)
    for k in range(top):
        score = contract_first(rows_ref[:, width:], picks[k])
        gates_ref[k : k + 1, :] = score[:1, :] / gate_ref[k : k + 1, :]


def per_device(tokens, routes, gates, grad_out, w_gate, w_up, w_down):
    experts = lax.axis_size("expert")
    groups = lax.axis_size("dp")
    group = lax.axis_index("dp")
    count, width = tokens.shape
    top = routes.shape[1]
    cap = 3 * count * top // (2 * experts)
    slots = experts * cap
    share = width // groups
    hidden = w_gate.shape[2]
    params = pltpu.CompilerParams(vmem_limit_bytes=VMEM_BYTES)
    place = group.astype(jnp.int32).reshape(1)

    def shifted(value, by):
        return lax.ppermute(value, "dp", [(i, (i + by) % groups) for i in range(groups)])

    def exchanged(rows):
        split = rows.reshape(experts, rows.shape[0] // experts, rows.shape[1])
        moved = lax.all_to_all(split, "expert", split_axis=0, concat_axis=0, tiled=True)
        return moved.reshape(rows.shape)

    routes_t, gates_t = jnp.transpose(routes), jnp.transpose(gates)
    routes_all = [routes_t] + [shifted(routes_t, k) for k in range(1, groups)]
    gates_all = [gates_t] + [shifted(gates_t, k) for k in range(1, groups)]
    grads = [
        shifted(
            lax.dynamic_slice(grad_out, (0, lax.rem(group + k, groups) * share), (count, share)), k
        )
        for k in range(1, groups)
    ]
    gate_parts = [w_gate[0]] + [shifted(w_gate[0], k) for k in range(1, groups)]
    up_parts = [w_up[0]] + [shifted(w_up[0], k) for k in range(1, groups)]

    block = tile_of(share, 512)
    steps = share // block
    small_spec = pl.BlockSpec((top, count), lambda q, c, g: (0, 0))
    sent, pos = pl.pallas_call(
        functools.partial(dispatch_kernel, experts, cap, groups),
        out_shape=(
            jax.ShapeDtypeStruct((2 * slots, width), jnp.bfloat16),
            jax.ShapeDtypeStruct((top, count), jnp.int32),
        ),
        grid_spec=pltpu.PrefetchScalarGridSpec(
            num_scalar_prefetch=1,
            grid=(groups, steps),
            in_specs=[small_spec] * (2 * groups)
            + [
                pl.BlockSpec(
                    (count, block),
                    lambda q, c, g: (0, lax.rem(g[0] - q + groups, groups) * steps + c),
                ),
                pl.BlockSpec(
                    (count, block),
                    lambda q, c, g: (0, g[0] * steps + jnp.where(q == 0, c, steps - 1)),
                ),
            ]
            + [
                pl.BlockSpec(
                    (count, block),
                    lambda q, c, g, k=k: (
                        0,
                        jnp.where(q == k, c, jnp.where(q < k, 0, steps - 1)),
                    ),
                )
                for k in range(1, groups)
            ],
            out_specs=(
                pl.BlockSpec((2 * slots, block), lambda q, c, g: (0, q * steps + c)),
                small_spec,
            ),
            scratch_shapes=[
                pltpu.VMEM((2 * slots, 2 * count), jnp.bfloat16),
                pltpu.VMEM((2 * slots, LANES), jnp.float32),
            ],
        ),
        compiler_params=params,
        name="dispatch",
    )(place, *routes_all, *gates_all, tokens, grad_out, *grads)
    rows = exchanged(sent)

    back_own, *rest = pl.pallas_call(
        functools.partial(back_kernel, groups, cap),
        out_shape=[jax.ShapeDtypeStruct((slots, hidden), jnp.float32)]
        + [jax.ShapeDtypeStruct((slots, hidden), jnp.bfloat16)] * (groups - 1)
        + [jax.ShapeDtypeStruct((groups * slots, share), jnp.bfloat16)],
        compiler_params=params,
        name="back",
    )(rows, w_down[0])
    scaled_all = rest[-1]
    back_parts = [back_own] + [shifted(rest[k - 1], -k) for k in range(1, groups)]

    pre_gate, pre_up, hidden_own = pl.pallas_call(
        functools.partial(forward_kernel, groups, cap),
        out_shape=[
            jax.ShapeDtypeStruct((slots, hidden), jnp.float32),
            jax.ShapeDtypeStruct((slots, hidden), jnp.float32),
            jax.ShapeDtypeStruct((slots, hidden), jnp.bfloat16),
        ],
        scratch_shapes=[pltpu.VMEM((slots, width), jnp.bfloat16)],
        compiler_params=params,
        name="forward",
    )(rows, *gate_parts, *up_parts)

    returning = pl.pallas_call(
        functools.partial(backward_kernel, groups),
        out_shape=jax.ShapeDtypeStruct((slots, width + LANES), jnp.bfloat16),
        scratch_shapes=[
            pltpu.VMEM((slots, hidden), jnp.bfloat16),
            pltpu.VMEM((slots, hidden), jnp.bfloat16),
        ],
        compiler_params=params,
        name="backward",
    )(pre_gate, pre_up, *back_parts, *gate_parts, *up_parts)
    returned = exchanged(returning)

    hiddens = [hidden_own] + [shifted(hidden_own, k) for k in range(1, groups)]
    grad_down = contract_first(jnp.concatenate(hiddens, axis=0), scaled_all)[None]

    whole_spec = pl.BlockSpec(memory_space=pltpu.VMEM)
    grad_tokens, grad_gates = pl.pallas_call(
        functools.partial(combine_kernel, groups),
        out_shape=(
            jax.ShapeDtypeStruct((count, width), jnp.bfloat16),
            jax.ShapeDtypeStruct((top, count), jnp.float32),
        ),
        in_specs=[pl.BlockSpec(memory_space=pltpu.SMEM)] + [whole_spec] * 3,
        compiler_params=params,
        name="combine",
    )(place, pos, gates_t, returned)
    return (grad_tokens, jnp.transpose(grad_gates), grad_down)


def solution(mesh):
    placed = (
        P(("dp", "expert"), None),
        P(("dp", "expert"), None),
        P(("dp", "expert"), None),
        P(("dp", "expert"), None),
        P("expert", "dp", None),
        P("expert", "dp", None),
        P("expert", None, "dp"),
    )
    return jax.shard_map(
        per_device,
        mesh=mesh,
        in_specs=placed,
        out_specs=(P(("dp", "expert"), None), P(("dp", "expert"), None), P("expert", None, "dp")),
        check_vma=False,
    )
```

```python
import functools

import jax
import jax.numpy as jnp
from jax import lax
from jax.experimental import pallas as pl
from jax.experimental.pallas import tpu as pltpu
from jax.sharding import PartitionSpec as P

LANES = 128
VMEM_BYTES = 24 * 1024 * 1024


def contract_last(left, right):
    return lax.dot_general(
        left, right, (((1,), (1,)), ((), ())), preferred_element_type=jnp.float32
    )


def contract_first(left, right):
    return lax.dot_general(
        left, right, (((0,), (0,)), ((), ())), preferred_element_type=jnp.float32
    )


def tile_of(extent, most):
    return most if extent % most == 0 else extent


def slot_positions(routes, experts, stride, base):
    top, count = routes.shape
    labels = lax.broadcasted_iota(jnp.int32, (experts, count), 0)
    named = [labels == routes[k : k + 1, :] for k in range(top)]
    marks = sum(jnp.where(m, 1.0, 0.0) for m in named)
    earlier = lax.broadcasted_iota(jnp.int32, (count, count), 0) < lax.broadcasted_iota(
        jnp.int32, (count, count), 1
    )
    rank = jnp.dot(
        marks.astype(jnp.bfloat16),
        jnp.where(earlier, 1.0, 0.0).astype(jnp.bfloat16),
        preferred_element_type=jnp.float32,
    )
    slot = rank + (labels * stride + base).astype(jnp.float32)
    return [
        jnp.sum(jnp.where(m, slot, 0.0), axis=0, keepdims=True).astype(jnp.int32) for m in named
    ]


def rows_of(ref, groups, cap, which):
    value = ref[...].astype(jnp.float32)
    count, width = value.shape
    value = value.reshape(count // (groups * cap), groups, cap, width)[:, which]
    return value.reshape(count // groups, width).astype(ref.dtype)


def dispatch_tokens(experts, cap, place_ref, routes_ref, tokens_ref, out_ref, pos_ref, pick_ref):
    @pl.when(pl.program_id(0) == 0)
    def _():
        pos = slot_positions(routes_ref[...], experts, cap, 0)
        rows = lax.broadcasted_iota(jnp.int32, pick_ref.shape, 0)
        pick_ref[...] = sum(jnp.where(rows == p, 1.0, 0.0) for p in pos).astype(jnp.bfloat16)
        for k, p in enumerate(pos):
            pos_ref[k : k + 1, :] = p

    out_ref[...] = jnp.dot(
        pick_ref[...], tokens_ref[...], preferred_element_type=jnp.float32
    ).astype(out_ref.dtype)


def dispatch_scaled(experts, cap, groups, place_ref, *refs):
    routes_refs, gate_refs = refs[:groups], refs[groups : 2 * groups]
    grad_refs, (out_ref, pick_ref, scale_ref) = refs[2 * groups : 3 * groups], refs[3 * groups :]
    count = grad_refs[0].shape[0]
    slots = out_ref.shape[0]

    @pl.when(pl.program_id(0) == 0)
    def _():
        rows = lax.broadcasted_iota(jnp.int32, (slots, count), 0)
        total = jnp.zeros((slots, 1), jnp.float32)
        for q in range(groups):
            pos = slot_positions(routes_refs[q][...], experts, groups * cap, q * cap)
            hit = jnp.zeros((slots, count), jnp.float32)
            weight = jnp.zeros((slots, count), jnp.float32)
            for k, p in enumerate(pos):
                here = rows == p
                hit = hit + jnp.where(here, 1.0, 0.0)
                weight = weight + jnp.where(here, gate_refs[q][k : k + 1, :], 0.0)
            pick_ref[:, q * count : (q + 1) * count] = hit.astype(jnp.bfloat16)
            total = total + jnp.sum(weight, axis=1, keepdims=True)
        scale_ref[...] = jnp.broadcast_to(total, scale_ref.shape)

    grads = jnp.concatenate([ref[...] for ref in grad_refs], axis=0)
    rows = jnp.dot(pick_ref[...], grads, preferred_element_type=jnp.float32)
    out_ref[...] = (scale_ref[:, :1] * rows).astype(out_ref.dtype)


def back_kernel(groups, cap, rows_ref, down_ref, own_ref, *rest):
    others, all_ref = rest[: groups - 1], rest[groups - 1]
    slots, hidden = own_ref.shape
    for q in range(groups):
        all_ref[q * slots : (q + 1) * slots, :] = rows_of(rows_ref, groups, cap, q)
    step = tile_of(hidden, 256)

    @pl.loop(0, hidden // step)
    def _(j):
        cols = pl.ds(pl.multiple_of(j * step, step), step)
        for q, ref in enumerate((own_ref, *others)):
            part = contract_last(all_ref[q * slots : (q + 1) * slots, :], down_ref[cols, :])
            ref[:, cols] = part.astype(ref.dtype)


def weight_views(refs):
    gates, ups = [refs[0]], [refs[1]]
    share = refs[0].shape[0]
    for ref in refs[2:]:
        gates.append(ref.at[:share])
        ups.append(ref.at[share:])
    return gates, ups


def forward_kernel(groups, x_ref, *refs):
    gates, ups = weight_views(refs[: groups + 1])
    pre_gate_ref, pre_up_ref, hidden_ref = refs[groups + 1 :]
    share, hidden = gates[0].shape
    step = tile_of(hidden, 256)

    def against(parts, cols):
        return sum(
            jnp.dot(
                x_ref[:, k * share : (k + 1) * share],
                ref[:, cols],
                preferred_element_type=jnp.float32,
            )
            for k, ref in enumerate(parts)
        )

    @pl.loop(0, hidden // step)
    def _(j):
        cols = pl.ds(pl.multiple_of(j * step, step), step)
        pre_gate = against(gates, cols)
        pre_up = against(ups, cols)
        pre_gate_ref[:, cols] = pre_gate
        pre_up_ref[:, cols] = pre_up
        hidden_ref[:, cols] = (pre_gate * jax.nn.sigmoid(pre_gate) * pre_up).astype(jnp.bfloat16)


def backward_kernel(groups, pre_gate_ref, pre_up_ref, *refs):
    parts, weights = refs[:groups], refs[groups : 2 * groups + 1]
    out_ref, d_gate_ref, d_up_ref = refs[2 * groups + 1 :]
    gates, ups = weight_views(weights)
    share, hidden = gates[0].shape
    pre_gate, pre_up = pre_gate_ref[...], pre_up_ref[...]
    back = sum(part[...].astype(jnp.float32) for part in parts)
    sig = jax.nn.sigmoid(pre_gate)
    act = pre_gate * sig
    slope = sig * (1.0 + pre_gate * (1.0 - sig))
    score = jnp.sum(back * (act * pre_up), axis=1, keepdims=True)
    d_gate_ref[...] = (back * pre_up * slope).astype(jnp.bfloat16)
    d_up_ref[...] = (back * act).astype(jnp.bfloat16)
    width = groups * share
    out_ref[:, width:] = jnp.broadcast_to(score, (score.shape[0], LANES)).astype(out_ref.dtype)
    block = tile_of(share, 256)
    for k in range(groups):

        @pl.loop(0, share // block)
        def _(c, k=k):
            at = pl.ds(pl.multiple_of(c * block, block), block)
            grad = contract_last(d_gate_ref[...], gates[k][at, :])
            grad += contract_last(d_up_ref[...], ups[k][at, :])
            out = pl.ds(pl.multiple_of(k * share + c * block, block), block)
            out_ref[:, out] = grad.astype(out_ref.dtype)


def combine_kernel(groups, place_ref, pos_ref, gate_ref, rows_ref, tokens_ref, gates_ref):
    top, count = pos_ref.shape
    slots = rows_ref.shape[0]
    width = tokens_ref.shape[1]
    share = width // groups
    places = lax.broadcasted_iota(jnp.int32, (slots, count), 0)
    picks = [
        jnp.where(places == pos_ref[k : k + 1, :], 1.0, 0.0).astype(jnp.bfloat16)
        for k in range(top)
    ]
    both = sum(picks)
    for k in range(groups):
        at = lax.rem(place_ref[0] - k + groups, groups) * share
        tokens_ref[:, pl.ds(pl.multiple_of(at, share), share)] = contract_first(
            both, rows_ref[:, k * share : (k + 1) * share]
        ).astype(tokens_ref.dtype)
    for k in range(top):
        score = contract_first(rows_ref[:, width:], picks[k])
        gates_ref[k : k + 1, :] = score[:1, :] / gate_ref[k : k + 1, :]


def per_device(tokens, routes, gates, grad_out, w_gate, w_up, w_down):
    experts = lax.axis_size("expert")
    groups = lax.axis_size("dp")
    group = lax.axis_index("dp")
    count, width = tokens.shape
    top = routes.shape[1]
    cap = 3 * count * top // (2 * experts)
    slots = experts * cap
    share = width // groups
    hidden = w_gate.shape[2]
    params = pltpu.CompilerParams(vmem_limit_bytes=VMEM_BYTES)
    place = group.astype(jnp.int32).reshape(1)

    def shifted(value, by):
        return lax.ppermute(value, "dp", [(i, (i + by) % groups) for i in range(groups)])

    def exchanged(rows):
        split = rows.reshape(experts, rows.shape[0] // experts, rows.shape[1])
        moved = lax.all_to_all(split, "expert", split_axis=0, concat_axis=0, tiled=True)
        return moved.reshape(rows.shape)

    routes_t, gates_t = jnp.transpose(routes), jnp.transpose(gates)
    routes_all = [routes_t] + [shifted(routes_t, k) for k in range(1, groups)]
    gates_all = [gates_t] + [shifted(gates_t, k) for k in range(1, groups)]
    grads = [
        shifted(
            lax.dynamic_slice(grad_out, (0, lax.rem(group + k, groups) * share), (count, share)), k
        )
        for k in range(1, groups)
    ]
    both = jnp.concatenate([w_gate[0], w_up[0]], axis=0)
    weights = [w_gate[0], w_up[0]] + [shifted(both, k) for k in range(1, groups)]

    def in_hbm(value):
        return pltpu.with_memory_space_constraint(value, pltpu.HBM)

    block = tile_of(share, 512)
    steps = share // block
    small_spec = pl.BlockSpec((top, count), lambda c, g: (0, 0))
    scaled = pl.pallas_call(
        functools.partial(dispatch_scaled, experts, cap, groups),
        out_shape=pltpu.HBM((groups * slots, share), jnp.bfloat16),
        grid_spec=pltpu.PrefetchScalarGridSpec(
            num_scalar_prefetch=1,
            grid=(steps,),
            in_specs=[small_spec] * (2 * groups)
            + [pl.BlockSpec((count, block), lambda c, g: (0, g[0] * steps + c))]
            + [pl.BlockSpec((count, block), lambda c, g: (0, c))] * (groups - 1),
            out_specs=pl.BlockSpec((groups * slots, block), lambda c, g: (0, c)),
            scratch_shapes=[
                pltpu.VMEM((groups * slots, groups * count), jnp.bfloat16),
                pltpu.VMEM((groups * slots, LANES), jnp.float32),
            ],
        ),
        compiler_params=params,
        name="dispatch_scaled",
    )(place, *routes_all, *gates_all, in_hbm(grad_out), *grads)
    scaled_rows = exchanged(scaled)

    sent, pos = pl.pallas_call(
        functools.partial(dispatch_tokens, experts, cap),
        out_shape=(
            pltpu.HBM((slots, width), jnp.bfloat16),
            jax.ShapeDtypeStruct((top, count), jnp.int32),
        ),
        grid_spec=pltpu.PrefetchScalarGridSpec(
            num_scalar_prefetch=1,
            grid=(groups,),
            in_specs=[
                small_spec,
                pl.BlockSpec(
                    (count, share), lambda k, g: (0, lax.rem(g[0] - k + groups, groups))
                ),
            ],
            out_specs=(pl.BlockSpec((slots, share), lambda k, g: (0, k)), small_spec),
            scratch_shapes=[pltpu.VMEM((slots, count), jnp.bfloat16)],
        ),
        compiler_params=params,
        name="dispatch_tokens",
    )(place, routes_t, in_hbm(tokens))
    x_rows = exchanged(sent)

    back_own, *rest = pl.pallas_call(
        functools.partial(back_kernel, groups, cap),
        out_shape=[jax.ShapeDtypeStruct((slots, hidden), jnp.float32)]
        + [jax.ShapeDtypeStruct((slots, hidden), jnp.bfloat16)] * (groups - 1)
        + [jax.ShapeDtypeStruct((groups * slots, share), jnp.bfloat16)],
        compiler_params=params,
        name="back",
    )(scaled_rows, w_down[0])
    scaled_all = rest[-1]
    back_parts = [back_own] + [shifted(rest[k - 1], -k) for k in range(1, groups)]

    pre_gate, pre_up, hidden_own = pl.pallas_call(
        functools.partial(forward_kernel, groups),
        out_shape=[
            jax.ShapeDtypeStruct((slots, hidden), jnp.float32),
            jax.ShapeDtypeStruct((slots, hidden), jnp.float32),
            jax.ShapeDtypeStruct((slots, hidden), jnp.bfloat16),
        ],
        compiler_params=params,
        name="forward",
    )(x_rows, *weights)

    returning = pl.pallas_call(
        functools.partial(backward_kernel, groups),
        out_shape=jax.ShapeDtypeStruct((slots, width + LANES), jnp.bfloat16),
        scratch_shapes=[
            pltpu.VMEM((slots, hidden), jnp.bfloat16),
            pltpu.VMEM((slots, hidden), jnp.bfloat16),
        ],
        compiler_params=params,
        name="backward",
    )(pre_gate, pre_up, *back_parts, *weights)
    returned = exchanged(returning)

    hiddens = [hidden_own] + [shifted(hidden_own, k) for k in range(1, groups)]
    grad_down = contract_first(jnp.concatenate(hiddens, axis=0), scaled_all)[None]

    whole_spec = pl.BlockSpec(memory_space=pltpu.VMEM)
    grad_tokens, grad_gates = pl.pallas_call(
        functools.partial(combine_kernel, groups),
        out_shape=(
            jax.ShapeDtypeStruct((count, width), jnp.bfloat16),
            jax.ShapeDtypeStruct((top, count), jnp.float32),
        ),
        in_specs=[pl.BlockSpec(memory_space=pltpu.SMEM)] + [whole_spec] * 3,
        compiler_params=params,
        name="combine",
    )(place, pos, gates_t, returned)
    return (grad_tokens, jnp.transpose(grad_gates), grad_down)


def solution(mesh):
    placed = (
        P(("dp", "expert"), None),
        P(("dp", "expert"), None),
        P(("dp", "expert"), None),
        P(("dp", "expert"), None),
        P("expert", "dp", None),
        P("expert", "dp", None),
        P("expert", None, "dp"),
    )
    return jax.shard_map(
        per_device,
        mesh=mesh,
        in_specs=placed,
        out_specs=(P(("dp", "expert"), None), P(("dp", "expert"), None), P("expert", None, "dp")),
        check_vma=False,
    )
```

```python
import functools

import jax
import jax.numpy as jnp
from jax import lax
from jax.experimental import pallas as pl
from jax.experimental.pallas import tpu as pltpu
from jax.sharding import PartitionSpec as P

LANES = 128
VMEM_BYTES = 24 * 1024 * 1024


def contract_last(left, right):
    return lax.dot_general(
        left, right, (((1,), (1,)), ((), ())), preferred_element_type=jnp.float32
    )


def contract_first(left, right):
    return lax.dot_general(
        left, right, (((0,), (0,)), ((), ())), preferred_element_type=jnp.float32
    )


def tile_of(extent, most):
    return most if extent % most == 0 else extent


def slot_positions(routes, experts, stride, base):
    top, count = routes.shape
    labels = lax.broadcasted_iota(jnp.int32, (experts, count), 0)
    named = [labels == routes[k : k + 1, :] for k in range(top)]
    marks = sum(jnp.where(m, 1.0, 0.0) for m in named)
    earlier = lax.broadcasted_iota(jnp.int32, (count, count), 0) < lax.broadcasted_iota(
        jnp.int32, (count, count), 1
    )
    rank = jnp.dot(
        marks.astype(jnp.bfloat16),
        jnp.where(earlier, 1.0, 0.0).astype(jnp.bfloat16),
        preferred_element_type=jnp.float32,
    )
    slot = rank + (labels * stride + base).astype(jnp.float32)
    return [
        jnp.sum(jnp.where(m, slot, 0.0), axis=0, keepdims=True).astype(jnp.int32) for m in named
    ]


def rows_of(ref, groups, cap, which):
    value = ref[...].astype(jnp.float32)
    count, width = value.shape
    value = value.reshape(count // (groups * cap), groups, cap, width)[:, which]
    return value.reshape(count // groups, width).astype(ref.dtype)


def dispatch_tokens(experts, cap, place_ref, routes_ref, tokens_ref, out_ref, pos_ref, pick_ref):
    @pl.when(pl.program_id(0) == 0)
    def _():
        pos = slot_positions(routes_ref[...], experts, cap, 0)
        rows = lax.broadcasted_iota(jnp.int32, pick_ref.shape, 0)
        pick_ref[...] = sum(jnp.where(rows == p, 1.0, 0.0) for p in pos).astype(jnp.bfloat16)
        for k, p in enumerate(pos):
            pos_ref[k : k + 1, :] = p

    out_ref[...] = jnp.dot(
        pick_ref[...], tokens_ref[...], preferred_element_type=jnp.float32
    ).astype(out_ref.dtype)


def dispatch_scaled(experts, cap, groups, place_ref, *refs):
    routes_refs, gate_refs = refs[:groups], refs[groups : 2 * groups]
    grad_refs, (out_ref, pick_ref, scale_ref) = refs[2 * groups : 3 * groups], refs[3 * groups :]
    count = grad_refs[0].shape[0]
    slots = out_ref.shape[0]

    @pl.when(pl.program_id(0) == 0)
    def _():
        rows = lax.broadcasted_iota(jnp.int32, (slots, count), 0)
        total = jnp.zeros((slots, 1), jnp.float32)
        for q in range(groups):
            pos = slot_positions(routes_refs[q][...], experts, groups * cap, q * cap)
            hit = jnp.zeros((slots, count), jnp.float32)
            weight = jnp.zeros((slots, count), jnp.float32)
            for k, p in enumerate(pos):
                here = rows == p
                hit = hit + jnp.where(here, 1.0, 0.0)
                weight = weight + jnp.where(here, gate_refs[q][k : k + 1, :], 0.0)
            pick_ref[:, q * count : (q + 1) * count] = hit.astype(jnp.bfloat16)
            total = total + jnp.sum(weight, axis=1, keepdims=True)
        scale_ref[...] = jnp.broadcast_to(total, scale_ref.shape)

    grads = jnp.concatenate([ref[...] for ref in grad_refs], axis=0)
    rows = jnp.dot(pick_ref[...], grads, preferred_element_type=jnp.float32)
    out_ref[...] = (scale_ref[:, :1] * rows).astype(out_ref.dtype)


def back_kernel(groups, cap, rows_ref, down_ref, own_ref, *rest):
    others, all_ref = rest[: groups - 1], rest[groups - 1]
    slots, hidden = own_ref.shape
    for q in range(groups):
        all_ref[q * slots : (q + 1) * slots, :] = rows_of(rows_ref, groups, cap, q)
    step = tile_of(hidden, 256)

    @pl.loop(0, hidden // step)
    def _(j):
        cols = pl.ds(pl.multiple_of(j * step, step), step)
        for q, ref in enumerate((own_ref, *others)):
            part = contract_last(all_ref[q * slots : (q + 1) * slots, :], down_ref[cols, :])
            ref[:, cols] = part.astype(ref.dtype)


def weight_views(refs):
    gates, ups = [refs[0]], [refs[1]]
    share = refs[0].shape[0]
    for ref in refs[2:]:
        gates.append(ref.at[:share])
        ups.append(ref.at[share:])
    return gates, ups


def forward_kernel(groups, x_ref, *refs):
    gates, ups = weight_views(refs[: groups + 1])
    pre_gate_ref, pre_up_ref, hidden_ref, held_ref, sems = refs[groups + 1 :]
    share, hidden = gates[0].shape
    step = tile_of(hidden, 256)
    spans = [slice(at, at + step) for at in range(0, hidden, step)]
    copies = [
        [
            pltpu.make_async_copy(ref.at[:, cols], held_ref.at[i, :, cols], sems.at[i, j])
            for i, ref in enumerate(gates + ups)
        ]
        for j, cols in enumerate(spans)
    ]
    for column in copies:
        for copy in column:
            copy.start()

    def against(first, cols):
        return sum(
            jnp.dot(
                x_ref[:, k * share : (k + 1) * share],
                held_ref[first + k, :, cols],
                preferred_element_type=jnp.float32,
            )
            for k in range(groups)
        )

    for column, cols in zip(copies, spans):
        for copy in column:
            copy.wait()
        pre_gate = against(0, cols)
        pre_up = against(groups, cols)
        pre_gate_ref[:, cols] = pre_gate
        pre_up_ref[:, cols] = pre_up
        hidden_ref[:, cols] = (pre_gate * jax.nn.sigmoid(pre_gate) * pre_up).astype(jnp.bfloat16)


def backward_kernel(groups, pre_gate_ref, pre_up_ref, *refs):
    parts, weights = refs[:groups], refs[groups : 2 * groups + 1]
    out_ref, d_gate_ref, d_up_ref, held_ref, rows_ref, sems, out_sems = refs[2 * groups + 1 :]
    gates, ups = weight_views(weights)
    share, hidden = gates[0].shape
    width = groups * share
    block = tile_of(share, 512)
    pieces = [(k, at) for k in range(groups) for at in range(0, share, block)]
    copies = [
        [
            pltpu.make_async_copy(
                ref.at[at : at + block], held_ref.at[i, at : at + block], sems.at[h, n]
            )
            for h, (i, ref) in enumerate(((k, gates[k]), (groups + k, ups[k])))
        ]
        for n, (k, at) in enumerate(pieces)
    ]
    for pair in copies:
        for copy in pair:
            copy.start()
    pre_gate, pre_up = pre_gate_ref[...], pre_up_ref[...]
    back = sum(part[...].astype(jnp.float32) for part in parts)
    sig = jax.nn.sigmoid(pre_gate)
    act = pre_gate * sig
    slope = sig * (1.0 + pre_gate * (1.0 - sig))
    score = jnp.sum(back * (act * pre_up), axis=1, keepdims=True)
    d_gate_ref[...] = (back * pre_up * slope).astype(jnp.bfloat16)
    d_up_ref[...] = (back * act).astype(jnp.bfloat16)
    rows_ref[:, width:] = jnp.broadcast_to(score, (score.shape[0], LANES)).astype(rows_ref.dtype)
    outs = []

    def send(cols):
        copy = pltpu.make_async_copy(
            rows_ref.at[:, cols], out_ref.at[:, cols], out_sems.at[len(outs)]
        )
        copy.start()
        outs.append(copy)

    send(slice(width, width + LANES))
    for (k, at), pair in zip(pieces, copies):
        for copy in pair:
            copy.wait()
        cols = slice(k * share + at, k * share + at + block)
        grad = contract_last(d_gate_ref[...], held_ref[k, at : at + block])
        grad += contract_last(d_up_ref[...], held_ref[groups + k, at : at + block])
        rows_ref[:, cols] = grad.astype(rows_ref.dtype)
        send(cols)
    for copy in outs:
        copy.wait()


def combine_kernel(groups, place_ref, pos_ref, gate_ref, rows_ref, tokens_ref, gates_ref):
    top, count = pos_ref.shape
    slots = rows_ref.shape[0]
    width = tokens_ref.shape[1]
    share = width // groups
    places = lax.broadcasted_iota(jnp.int32, (slots, count), 0)
    picks = [
        jnp.where(places == pos_ref[k : k + 1, :], 1.0, 0.0).astype(jnp.bfloat16)
        for k in range(top)
    ]
    both = sum(picks)
    for k in range(groups):
        at = lax.rem(place_ref[0] - k + groups, groups) * share
        tokens_ref[:, pl.ds(pl.multiple_of(at, share), share)] = contract_first(
            both, rows_ref[:, k * share : (k + 1) * share]
        ).astype(tokens_ref.dtype)
    for k in range(top):
        score = contract_first(rows_ref[:, width:], picks[k])
        gates_ref[k : k + 1, :] = score[:1, :] / gate_ref[k : k + 1, :]


def per_device(tokens, routes, gates, grad_out, w_gate, w_up, w_down):
    experts = lax.axis_size("expert")
    groups = lax.axis_size("dp")
    group = lax.axis_index("dp")
    count, width = tokens.shape
    top = routes.shape[1]
    cap = 3 * count * top // (2 * experts)
    slots = experts * cap
    share = width // groups
    hidden = w_gate.shape[2]
    params = pltpu.CompilerParams(vmem_limit_bytes=VMEM_BYTES)
    place = group.astype(jnp.int32).reshape(1)

    def shifted(value, by):
        return lax.ppermute(value, "dp", [(i, (i + by) % groups) for i in range(groups)])

    def exchanged(rows):
        split = rows.reshape(experts, rows.shape[0] // experts, rows.shape[1])
        moved = lax.all_to_all(split, "expert", split_axis=0, concat_axis=0, tiled=True)
        return moved.reshape(rows.shape)

    routes_t, gates_t = jnp.transpose(routes), jnp.transpose(gates)
    routes_all = [routes_t] + [shifted(routes_t, k) for k in range(1, groups)]
    gates_all = [gates_t] + [shifted(gates_t, k) for k in range(1, groups)]
    grads = [
        shifted(
            lax.dynamic_slice(grad_out, (0, lax.rem(group + k, groups) * share), (count, share)), k
        )
        for k in range(1, groups)
    ]
    both = jnp.concatenate([w_gate[0], w_up[0]], axis=0)
    weights = [w_gate[0], w_up[0]] + [shifted(both, k) for k in range(1, groups)]

    def in_hbm(value):
        return pltpu.with_memory_space_constraint(value, pltpu.HBM)

    block = tile_of(share, 512)
    steps = share // block
    small_spec = pl.BlockSpec((top, count), lambda c, g: (0, 0))
    scaled = pl.pallas_call(
        functools.partial(dispatch_scaled, experts, cap, groups),
        out_shape=pltpu.HBM((groups * slots, share), jnp.bfloat16),
        grid_spec=pltpu.PrefetchScalarGridSpec(
            num_scalar_prefetch=1,
            grid=(steps,),
            in_specs=[small_spec] * (2 * groups)
            + [pl.BlockSpec((count, block), lambda c, g: (0, g[0] * steps + c))]
            + [pl.BlockSpec((count, block), lambda c, g: (0, c))] * (groups - 1),
            out_specs=pl.BlockSpec((groups * slots, block), lambda c, g: (0, c)),
            scratch_shapes=[
                pltpu.VMEM((groups * slots, groups * count), jnp.bfloat16),
                pltpu.VMEM((groups * slots, LANES), jnp.float32),
            ],
        ),
        compiler_params=params,
        name="dispatch_scaled",
    )(place, in_hbm(routes_t), *routes_all[1:], in_hbm(gates_t), *gates_all[1:], in_hbm(grad_out), *grads)
    scaled_rows = exchanged(scaled)

    sent, pos = pl.pallas_call(
        functools.partial(dispatch_tokens, experts, cap),
        out_shape=(
            pltpu.HBM((slots, width), jnp.bfloat16),
            jax.ShapeDtypeStruct((top, count), jnp.int32),
        ),
        grid_spec=pltpu.PrefetchScalarGridSpec(
            num_scalar_prefetch=1,
            grid=(groups,),
            in_specs=[
                small_spec,
                pl.BlockSpec(
                    (count, share), lambda k, g: (0, lax.rem(g[0] - k + groups, groups))
                ),
            ],
            out_specs=(pl.BlockSpec((slots, share), lambda k, g: (0, k)), small_spec),
            scratch_shapes=[pltpu.VMEM((slots, count), jnp.bfloat16)],
        ),
        compiler_params=params,
        name="dispatch_tokens",
    )(place, in_hbm(routes_t), in_hbm(tokens))
    x_rows = exchanged(sent)

    back_own, *rest = pl.pallas_call(
        functools.partial(back_kernel, groups, cap),
        out_shape=[pltpu.HBM((slots, hidden), jnp.float32)]
        + [pltpu.HBM((slots, hidden), jnp.bfloat16)] * (groups - 1)
        + [pltpu.HBM((groups * slots, share), jnp.bfloat16)],
        compiler_params=params,
        name="back",
    )(scaled_rows, in_hbm(w_down[0]))
    scaled_all = rest[-1]
    back_parts = [back_own] + [shifted(rest[k - 1], -k) for k in range(1, groups)]

    whole_spec = pl.BlockSpec(memory_space=pltpu.VMEM)
    weight_spec = pl.BlockSpec(memory_space=pl.ANY)
    weights = [in_hbm(value) for value in weights]
    held = pltpu.VMEM((2 * groups, share, hidden), jnp.bfloat16)
    pre_gate, pre_up, hidden_own = pl.pallas_call(
        functools.partial(forward_kernel, groups),
        out_shape=[
            jax.ShapeDtypeStruct((slots, hidden), jnp.float32),
            jax.ShapeDtypeStruct((slots, hidden), jnp.float32),
            pltpu.HBM((slots, hidden), jnp.bfloat16),
        ],
        in_specs=[pl.BlockSpec()] + [weight_spec] * (groups + 1),
        scratch_shapes=[
            held,
            pltpu.SemaphoreType.DMA((2 * groups, hidden // tile_of(hidden, 256))),
        ],
        compiler_params=params,
        name="forward",
    )(x_rows, *weights)

    pieces = groups * (share // tile_of(share, 512))
    returning = pl.pallas_call(
        functools.partial(backward_kernel, groups),
        out_shape=pltpu.HBM((slots, width + LANES), jnp.bfloat16),
        in_specs=[pl.BlockSpec()] * (2 + groups) + [weight_spec] * (groups + 1),
        out_specs=pl.BlockSpec(memory_space=pl.ANY),
        scratch_shapes=[
            pltpu.VMEM((slots, hidden), jnp.bfloat16),
            pltpu.VMEM((slots, hidden), jnp.bfloat16),
            held,
            pltpu.VMEM((slots, width + LANES), jnp.bfloat16),
            pltpu.SemaphoreType.DMA((2, pieces)),
            pltpu.SemaphoreType.DMA((pieces + 1,)),
        ],
        compiler_params=params,
        name="backward",
    )(pre_gate, pre_up, *back_parts, *weights)
    returned = exchanged(returning)

    hiddens = [hidden_own] + [shifted(hidden_own, k) for k in range(1, groups)]
    grad_down = contract_first(jnp.concatenate(hiddens, axis=0), scaled_all)[None]

    grad_tokens, grad_gates = pl.pallas_call(
        functools.partial(combine_kernel, groups),
        out_shape=(
            jax.ShapeDtypeStruct((count, width), jnp.bfloat16),
            jax.ShapeDtypeStruct((top, count), jnp.float32),
        ),
        in_specs=[pl.BlockSpec(memory_space=pltpu.SMEM)] + [whole_spec] * 3,
        compiler_params=params,
        name="combine",
    )(place, pos, gates_t, returned)
    return (grad_tokens, jnp.transpose(grad_gates), grad_down)


def solution(mesh):
    placed = (
        P(("dp", "expert"), None),
        P(("dp", "expert"), None),
        P(("dp", "expert"), None),
        P(("dp", "expert"), None),
        P("expert", "dp", None),
        P("expert", "dp", None),
        P("expert", None, "dp"),
    )
    return jax.shard_map(
        per_device,
        mesh=mesh,
        in_specs=placed,
        out_specs=(P(("dp", "expert"), None), P(("dp", "expert"), None), P("expert", None, "dp")),
        check_vma=False,
    )
```

```python
import functools

import jax
import jax.numpy as jnp
from jax import lax
from jax.experimental import pallas as pl
from jax.experimental.pallas import tpu as pltpu
from jax.sharding import PartitionSpec as P

LANES = 128
VMEM_BYTES = 24 * 1024 * 1024


def contract_last(left, right):
    return lax.dot_general(
        left, right, (((1,), (1,)), ((), ())), preferred_element_type=jnp.float32
    )


def contract_first(left, right):
    return lax.dot_general(
        left, right, (((0,), (0,)), ((), ())), preferred_element_type=jnp.float32
    )


def tile_of(extent, most):
    return most if extent % most == 0 else extent


def slot_positions(routes, experts, stride, base):
    top, count = routes.shape
    labels = lax.broadcasted_iota(jnp.int32, (experts, count), 0)
    named = [labels == routes[k : k + 1, :] for k in range(top)]
    marks = sum(jnp.where(m, 1.0, 0.0) for m in named)
    earlier = lax.broadcasted_iota(jnp.int32, (count, count), 0) < lax.broadcasted_iota(
        jnp.int32, (count, count), 1
    )
    rank = jnp.dot(
        marks.astype(jnp.bfloat16),
        jnp.where(earlier, 1.0, 0.0).astype(jnp.bfloat16),
        preferred_element_type=jnp.float32,
    )
    slot = rank + (labels * stride + base + 1).astype(jnp.float32)
    return [
        jnp.sum(jnp.where(m, slot, 0.0), axis=0, keepdims=True).astype(jnp.int32) - 1
        for m in named
    ]


def by_half(value, cap, half, paired):
    count, width = value.shape
    if paired:
        value = value.reshape(count // (2 * cap), 2, cap, width)
        own, other = value[:, 0], value[:, 1]
    else:
        value = value.reshape(2, count // (2 * cap), cap, width)
        own, other = value[0], value[1]
    first = jnp.where(half == 0, own, other)
    second = jnp.where(half == 0, other, own)
    return jnp.stack([first, second], axis=0 if paired else 1).reshape(count, width)


def dispatch_tokens(experts, cap, place_ref, *refs):
    routes_refs, tokens_refs, (out_ref, pos_ref, pick_ref) = refs[:2], refs[2:4], refs[4:]
    count = tokens_refs[0].shape[0]

    @pl.when(pl.program_id(0) == 0)
    def _():
        rows = lax.broadcasted_iota(jnp.int32, (pick_ref.shape[0], count), 0)
        for c, ref in enumerate(routes_refs):
            near = ref[...] - place_ref[1] * (experts // 2)
            pos = slot_positions(near, experts // 2, 2 * cap, c * cap)
            pick_ref[:, c * count : (c + 1) * count] = sum(
                jnp.where(rows == p, 1.0, 0.0) for p in pos
            ).astype(jnp.bfloat16)
        for k, p in enumerate(slot_positions(routes_refs[0][...], experts, cap, 0)):
            pos_ref[k : k + 1, :] = p

    values = jnp.concatenate([ref[...] for ref in tokens_refs], axis=0)
    out_ref[...] = jnp.dot(
        pick_ref[...], values, preferred_element_type=jnp.float32
    ).astype(out_ref.dtype)


def dispatch_scaled(experts, cap, groups, place_ref, *refs):
    routes_refs, gate_refs = refs[:groups], refs[groups : 2 * groups]
    grad_refs, (out_ref, pick_ref, scale_ref) = refs[2 * groups : 3 * groups], refs[3 * groups :]
    count = grad_refs[0].shape[0]
    slots = out_ref.shape[0]

    @pl.when(pl.program_id(0) == 0)
    def _():
        rows = lax.broadcasted_iota(jnp.int32, (slots, count), 0)
        total = jnp.zeros((slots, 1), jnp.float32)
        for q in range(groups):
            pos = slot_positions(routes_refs[q][...], experts, groups * cap, q * cap)
            hit = jnp.zeros((slots, count), jnp.float32)
            weight = jnp.zeros((slots, count), jnp.float32)
            for k, p in enumerate(pos):
                here = rows == p
                hit = hit + jnp.where(here, 1.0, 0.0)
                weight = weight + jnp.where(here, gate_refs[q][k : k + 1, :], 0.0)
            pick_ref[:, q * count : (q + 1) * count] = hit.astype(jnp.bfloat16)
            total = total + jnp.sum(weight, axis=1, keepdims=True)
        scale_ref[...] = jnp.broadcast_to(total, scale_ref.shape)

    grads = jnp.concatenate([ref[...] for ref in grad_refs], axis=0)
    rows = jnp.dot(pick_ref[...], grads, preferred_element_type=jnp.float32)
    out_ref[...] = (scale_ref[:, :1] * rows).astype(out_ref.dtype)


def back_kernel(groups, cap, place_ref, rows_ref, down_ref, own_ref, *rest):
    others, all_ref = rest[: groups - 1], rest[groups - 1]
    slots, hidden = own_ref.shape
    count, share = rows_ref.shape
    rows = rows_ref[...].astype(jnp.float32).reshape(count // (groups * cap), groups, cap, share)
    for q in range(groups):
        ordered = by_half(rows[:, q].reshape(slots, share), cap, place_ref[1], False)
        all_ref[q * slots : (q + 1) * slots, :] = ordered.astype(all_ref.dtype)
    step = tile_of(hidden, 256)

    @pl.loop(0, hidden // step)
    def _(j):
        cols = pl.ds(pl.multiple_of(j * step, step), step)
        for q, ref in enumerate((own_ref, *others)):
            part = contract_last(all_ref[q * slots : (q + 1) * slots, :], down_ref[cols, :])
            ref[:, cols] = part.astype(ref.dtype)


def weight_views(groups, refs):
    share = refs[0].shape[0]
    early = refs[2].shape[0]
    views = [[(refs[0], 0, share)], [(refs[1], 0, share)]]
    for k in range(1, groups):
        first, second = refs[2 * k : 2 * k + 2]
        views.insert(k, [(first, 0, early), (second, 0, share - early)])
        views.append([(second, share - early, share)])
    return views


def forward_kernel(groups, x_ref, *refs):
    views = weight_views(groups, refs[: 2 * groups])
    act_ref, slope_ref, value_ref, hidden_ref, held_ref = refs[2 * groups : 2 * groups + 5]
    rows_ref, gate_sum_ref, up_sum_ref, sems, row_sems = refs[2 * groups + 5 :]
    share, hidden = held_ref.shape[1:]
    step = tile_of(hidden, 256)
    loads, copies = [], []
    for k in range(groups):
        cols = slice(k * share, (k + 1) * share)
        loads.append(
            [pltpu.make_async_copy(x_ref.at[:, cols], rows_ref.at[:, cols], row_sems.at[k])]
        )
        for i in (k, groups + k):
            to = 0
            for n, (ref, at, extent) in enumerate(views[i]):
                loads[k].append(
                    pltpu.make_async_copy(
                        ref.at[at : at + extent],
                        held_ref.at[i, to : to + extent],
                        sems.at[n, i],
                    )
                )
                to += extent
        for copy in loads[k]:
            copy.start()
    for k in range(groups):
        for copy in loads[k]:
            copy.wait()
        x = rows_ref[:, k * share : (k + 1) * share]
        for at in range(0, hidden, step):
            cols = slice(at, at + step)
            pre_gate = jnp.dot(x, held_ref[k, :, cols], preferred_element_type=jnp.float32)
            pre_up = jnp.dot(x, held_ref[groups + k, :, cols], preferred_element_type=jnp.float32)
            if k > 0:
                pre_gate += gate_sum_ref[:, cols]
                pre_up += up_sum_ref[:, cols]
            if k < groups - 1:
                gate_sum_ref[:, cols] = pre_gate
                up_sum_ref[:, cols] = pre_up
                continue
            sig = jax.nn.sigmoid(pre_gate)
            act = pre_gate * sig
            hidden_f = act * pre_up
            act_ref[:, cols] = act
            slope_ref[:, cols] = pre_up * (sig * (1.0 + pre_gate * (1.0 - sig)))
            value_ref[:, cols] = hidden_f
            hidden_ref[:, cols] = hidden_f.astype(hidden_ref.dtype)


def backward_kernel(groups, cap, place_ref, act_ref, slope_ref, value_ref, held_ref, *refs):
    parts, (out_ref, d_gate_ref, d_up_ref, rows_ref, out_sems) = refs[:groups], refs[groups:]
    share = held_ref.shape[1]
    width = groups * share
    block = tile_of(share, 512)
    half = place_ref[1]
    back = sum(part[...].astype(jnp.float32) for part in parts)
    score = jnp.sum(back * value_ref[...], axis=1, keepdims=True)
    d_gate_ref[...] = by_half(back * slope_ref[...], cap, half, True).astype(jnp.bfloat16)
    d_up_ref[...] = by_half(back * act_ref[...], cap, half, True).astype(jnp.bfloat16)
    score = by_half(jnp.broadcast_to(score, (score.shape[0], LANES)), cap, half, True)
    rows_ref[:, width:] = score.astype(rows_ref.dtype)
    outs = []

    def send(cols):
        copy = pltpu.make_async_copy(
            rows_ref.at[:, cols], out_ref.at[:, cols], out_sems.at[len(outs)]
        )
        copy.start()
        outs.append(copy)

    send(slice(width, width + LANES))
    for k in range(groups):
        for at in range(0, share, block):
            cols = slice(k * share + at, k * share + at + block)
            grad = contract_last(d_gate_ref[...], held_ref[k, at : at + block])
            grad += contract_last(d_up_ref[...], held_ref[groups + k, at : at + block])
            rows_ref[:, cols] = grad.astype(rows_ref.dtype)
            send(cols)
    for copy in outs:
        copy.wait()


def combine_kernel(groups, place_ref, pos_ref, gate_ref, rows_ref, tokens_ref, gates_ref):
    top, count = pos_ref.shape
    slots = rows_ref.shape[0]
    width = tokens_ref.shape[1]
    share = width // groups
    places = lax.broadcasted_iota(jnp.int32, (slots, count), 0)
    picks = [
        jnp.where(places == pos_ref[k : k + 1, :], 1.0, 0.0).astype(jnp.bfloat16)
        for k in range(top)
    ]
    both = sum(picks)
    for k in range(groups):
        at = lax.rem(place_ref[0] - k + groups, groups) * share
        tokens_ref[:, pl.ds(pl.multiple_of(at, share), share)] = contract_first(
            both, rows_ref[:, k * share : (k + 1) * share]
        ).astype(tokens_ref.dtype)
    for k in range(top):
        score = contract_first(rows_ref[:, width:], picks[k])
        gates_ref[k : k + 1, :] = score[:1, :] / gate_ref[k : k + 1, :]


def per_device(tokens, routes, gates, grad_out, w_gate, w_up, w_down):
    experts = lax.axis_size("expert")
    groups = lax.axis_size("dp")
    group = lax.axis_index("dp")
    count, width = tokens.shape
    top = routes.shape[1]
    cap = 3 * count * top // (2 * experts)
    slots = experts * cap
    share = width // groups
    hidden = w_gate.shape[2]
    params = pltpu.CompilerParams(vmem_limit_bytes=VMEM_BYTES)
    half = lax.div(lax.axis_index("expert"), experts // 2)
    place = jnp.stack([group, half]).astype(jnp.int32)
    halves = [list(range(experts // 2)), list(range(experts // 2, experts))]

    def shifted(value, by):
        return lax.ppermute(value, "dp", [(i, (i + by) % groups) for i in range(groups)])

    def across(value):
        pairs = [(i, (i + experts // 2) % experts) for i in range(experts)]
        return lax.ppermute(value, "expert", pairs)

    def exchanged(rows, among=None):
        count = experts if among is None else len(among[0])
        split = rows.reshape(count, rows.shape[0] // count, rows.shape[1])
        moved = lax.all_to_all(
            split, "expert", split_axis=0, concat_axis=0, axis_index_groups=among, tiled=True
        )
        return moved.reshape(rows.shape)

    routes_t, gates_t = jnp.transpose(routes), jnp.transpose(gates)
    routes_all = [routes_t] + [shifted(routes_t, k) for k in range(1, groups)]
    gates_all = [gates_t] + [shifted(gates_t, k) for k in range(1, groups)]
    grads = [
        shifted(
            lax.dynamic_slice(grad_out, (0, lax.rem(group + k, groups) * share), (count, share)), k
        )
        for k in range(1, groups)
    ]
    early = share // 2
    late = jnp.concatenate([w_gate[0, early:], w_up[0]], axis=0)
    first_parts = [shifted(w_gate[0, :early], k) for k in range(1, groups)]
    second_parts = [shifted(late, k) for k in range(1, groups)]
    tokens_across, routes_across = across(tokens), across(routes_t)

    def in_hbm(value):
        return pltpu.with_memory_space_constraint(value, pltpu.HBM)

    block = tile_of(share, 512)
    steps = share // block
    small_spec = pl.BlockSpec((top, count), lambda c, g: (0, 0))
    scaled = pl.pallas_call(
        functools.partial(dispatch_scaled, experts, cap, groups),
        out_shape=pltpu.HBM((groups * slots, share), jnp.bfloat16),
        grid_spec=pltpu.PrefetchScalarGridSpec(
            num_scalar_prefetch=1,
            grid=(steps,),
            in_specs=[small_spec] * (2 * groups)
            + [pl.BlockSpec((count, block), lambda c, g: (0, g[0] * steps + c))]
            + [pl.BlockSpec((count, block), lambda c, g: (0, c))] * (groups - 1),
            out_specs=pl.BlockSpec((groups * slots, block), lambda c, g: (0, c)),
            scratch_shapes=[
                pltpu.VMEM((groups * slots, groups * count), jnp.bfloat16),
                pltpu.VMEM((groups * slots, LANES), jnp.float32),
            ],
        ),
        compiler_params=params,
        name="dispatch_scaled",
    )(place, in_hbm(routes_t), *routes_all[1:], in_hbm(gates_t), *gates_all[1:], in_hbm(grad_out), *grads)
    scaled, tokens_across, *first_parts = lax.optimization_barrier(
        (scaled, tokens_across, *first_parts)
    )
    scaled_rows = exchanged(scaled)
    weights = [w_gate[0], w_up[0]]
    for pair in zip(first_parts, second_parts):
        weights.extend(pair)

    sent, pos = pl.pallas_call(
        functools.partial(dispatch_tokens, experts, cap),
        out_shape=(
            pltpu.HBM((slots, width), jnp.bfloat16),
            jax.ShapeDtypeStruct((top, count), jnp.int32),
        ),
        grid_spec=pltpu.PrefetchScalarGridSpec(
            num_scalar_prefetch=1,
            grid=(groups,),
            in_specs=[small_spec] * 2
            + [
                pl.BlockSpec(
                    (count, share), lambda k, g: (0, lax.rem(g[0] - k + groups, groups))
                )
            ]
            * 2,
            out_specs=(pl.BlockSpec((slots, share), lambda k, g: (0, k)), small_spec),
            scratch_shapes=[pltpu.VMEM((slots, 2 * count), jnp.bfloat16)],
        ),
        compiler_params=params,
        name="dispatch_tokens",
    )(place, in_hbm(routes_t), routes_across, in_hbm(tokens), in_hbm(tokens_across))
    x_rows = exchanged(sent, halves)

    place_spec = pl.BlockSpec(memory_space=pltpu.SMEM)

    back_own, *rest = pl.pallas_call(
        functools.partial(back_kernel, groups, cap),
        out_shape=[pltpu.HBM((slots, hidden), jnp.float32)]
        + [pltpu.HBM((slots, hidden), jnp.bfloat16)] * (groups - 1)
        + [pltpu.HBM((groups * slots, share), jnp.bfloat16)],
        in_specs=[place_spec, pl.BlockSpec(), pl.BlockSpec()],
        compiler_params=params,
        name="back",
    )(place, scaled_rows, in_hbm(w_down[0]))
    scaled_all = rest[-1]
    back_parts = [back_own] + [shifted(rest[k - 1], -k) for k in range(1, groups)]

    whole_spec = pl.BlockSpec(memory_space=pltpu.VMEM)
    any_spec = pl.BlockSpec(memory_space=pl.ANY)
    *factors, hidden_own, held = pl.pallas_call(
        functools.partial(forward_kernel, groups),
        out_shape=[pltpu.VMEM((slots, hidden), jnp.float32)] * 3
        + [
            pltpu.HBM((slots, hidden), jnp.bfloat16),
            pltpu.VMEM((2 * groups, share, hidden), jnp.bfloat16),
        ],
        in_specs=[any_spec] * (2 * groups + 1),
        scratch_shapes=[
            pltpu.VMEM((slots, width), jnp.bfloat16),
            pltpu.VMEM((slots, hidden), jnp.float32),
            pltpu.VMEM((slots, hidden), jnp.float32),
            pltpu.SemaphoreType.DMA((2, 2 * groups)),
            pltpu.SemaphoreType.DMA((groups,)),
        ],
        compiler_params=params,
        name="forward",
    )(in_hbm(x_rows), *[in_hbm(value) for value in weights])

    pieces = groups * (share // tile_of(share, 512))
    returning = pl.pallas_call(
        functools.partial(backward_kernel, groups, cap),
        out_shape=pltpu.HBM((slots, width + LANES), jnp.bfloat16),
        in_specs=[place_spec] + [whole_spec] * (4 + groups),
        out_specs=any_spec,
        scratch_shapes=[
            pltpu.VMEM((slots, hidden), jnp.bfloat16),
            pltpu.VMEM((slots, hidden), jnp.bfloat16),
            pltpu.VMEM((slots, width + LANES), jnp.bfloat16),
            pltpu.SemaphoreType.DMA((pieces + 1,)),
        ],
        compiler_params=params,
        name="backward",
    )(place, *factors, held, *back_parts)
    returned = exchanged(returning)

    hiddens = [hidden_own] + [shifted(hidden_own, k) for k in range(1, groups)]
    grad_down = contract_first(jnp.concatenate(hiddens, axis=0), scaled_all)[None]

    grad_tokens, grad_gates = pl.pallas_call(
        functools.partial(combine_kernel, groups),
        out_shape=(
            jax.ShapeDtypeStruct((count, width), jnp.bfloat16),
            jax.ShapeDtypeStruct((top, count), jnp.float32),
        ),
        in_specs=[pl.BlockSpec(memory_space=pltpu.SMEM)] + [whole_spec] * 3,
        compiler_params=params,
        name="combine",
    )(place, pos, gates_t, returned)
    return (grad_tokens, jnp.transpose(grad_gates), grad_down)


def solution(mesh):
    placed = (
        P(("dp", "expert"), None),
        P(("dp", "expert"), None),
        P(("dp", "expert"), None),
        P(("dp", "expert"), None),
        P("expert", "dp", None),
        P("expert", "dp", None),
        P("expert", None, "dp"),
    )
    return jax.shard_map(
        per_device,
        mesh=mesh,
        in_specs=placed,
        out_specs=(P(("dp", "expert"), None), P(("dp", "expert"), None), P("expert", None, "dp")),
        check_vma=False,
    )
```

```python
import functools

import jax
import jax.numpy as jnp
from jax import lax
from jax.experimental import pallas as pl
from jax.experimental.pallas import tpu as pltpu
from jax.sharding import PartitionSpec as P

LANES = 128
VMEM_BYTES = 24 * 1024 * 1024


def contract_last(left, right):
    return lax.dot_general(
        left, right, (((1,), (1,)), ((), ())), preferred_element_type=jnp.float32
    )


def contract_first(left, right):
    return lax.dot_general(
        left, right, (((0,), (0,)), ((), ())), preferred_element_type=jnp.float32
    )


def tile_of(extent, most):
    return most if extent % most == 0 else extent


def slot_positions(routes, experts, stride, base):
    top, count = routes.shape
    labels = lax.broadcasted_iota(jnp.int32, (experts, count), 0)
    named = [labels == routes[k : k + 1, :] for k in range(top)]
    marks = sum(jnp.where(m, 1.0, 0.0) for m in named)
    earlier = lax.broadcasted_iota(jnp.int32, (count, count), 0) < lax.broadcasted_iota(
        jnp.int32, (count, count), 1
    )
    rank = jnp.dot(
        marks.astype(jnp.bfloat16),
        jnp.where(earlier, 1.0, 0.0).astype(jnp.bfloat16),
        preferred_element_type=jnp.float32,
    )
    slot = rank + (labels * stride + base + 1).astype(jnp.float32)
    return [
        jnp.sum(jnp.where(m, slot, 0.0), axis=0, keepdims=True).astype(jnp.int32) - 1
        for m in named
    ]


def rows_of(ref, groups, cap, which):
    value = ref[...].astype(jnp.float32)
    count, width = value.shape
    value = value.reshape(count // (groups * cap), groups, cap, width)[:, which]
    return value.reshape(count // groups, width).astype(ref.dtype)


def dispatch_tokens(experts, cap, place_ref, routes_ref, tokens_ref, out_ref, pos_ref, pick_ref):
    @pl.when(pl.program_id(0) == 0)
    def _():
        pos = slot_positions(routes_ref[...], experts, cap, 0)
        rows = lax.broadcasted_iota(jnp.int32, pick_ref.shape, 0)
        pick_ref[...] = sum(jnp.where(rows == p, 1.0, 0.0) for p in pos).astype(jnp.bfloat16)
        for k, p in enumerate(pos):
            pos_ref[k : k + 1, :] = p

    out_ref[...] = jnp.dot(
        pick_ref[...], tokens_ref[...], preferred_element_type=jnp.float32
    ).astype(out_ref.dtype)


def dispatch_scaled(experts, cap, groups, place_ref, *refs):
    routes_refs, gate_refs = refs[:groups], refs[groups : 2 * groups]
    grad_refs, (out_ref, pick_ref, scale_ref) = refs[2 * groups : 3 * groups], refs[3 * groups :]
    count = grad_refs[0].shape[0]
    slots = out_ref.shape[0]

    @pl.when(pl.program_id(0) == 0)
    def _():
        rows = lax.broadcasted_iota(jnp.int32, (slots, count), 0)
        total = jnp.zeros((slots, 1), jnp.float32)
        for q in range(groups):
            pos = slot_positions(routes_refs[q][...], experts, groups * cap, q * cap)
            hit = jnp.zeros((slots, count), jnp.float32)
            weight = jnp.zeros((slots, count), jnp.float32)
            for k, p in enumerate(pos):
                here = rows == p
                hit = hit + jnp.where(here, 1.0, 0.0)
                weight = weight + jnp.where(here, gate_refs[q][k : k + 1, :], 0.0)
            pick_ref[:, q * count : (q + 1) * count] = hit.astype(jnp.bfloat16)
            total = total + jnp.sum(weight, axis=1, keepdims=True)
        scale_ref[...] = jnp.broadcast_to(total, scale_ref.shape)

    grads = jnp.concatenate([ref[...] for ref in grad_refs], axis=0)
    rows = jnp.dot(pick_ref[...], grads, preferred_element_type=jnp.float32)
    out_ref[...] = (scale_ref[:, :1] * rows).astype(out_ref.dtype)


def back_kernel(groups, cap, rows_ref, down_ref, own_ref, *rest):
    others, all_ref = rest[: groups - 1], rest[groups - 1]
    slots, hidden = own_ref.shape
    for q in range(groups):
        all_ref[q * slots : (q + 1) * slots, :] = rows_of(rows_ref, groups, cap, q)
    step = tile_of(hidden, 256)

    @pl.loop(0, hidden // step)
    def _(j):
        cols = pl.ds(pl.multiple_of(j * step, step), step)
        for q, ref in enumerate((own_ref, *others)):
            part = contract_last(all_ref[q * slots : (q + 1) * slots, :], down_ref[cols, :])
            ref[:, cols] = part.astype(ref.dtype)


def hold_kernel(groups, *refs):
    (own_gate, own_up), others = refs[:2], refs[2 : groups + 1]
    held_ref, sems = refs[groups + 1 :]
    share = own_gate.shape[0]
    sources = [own_gate, *[ref.at[:share] for ref in others]]
    sources += [own_up, *[ref.at[share:] for ref in others]]
    copies = [
        pltpu.make_async_copy(ref, held_ref.at[i], sems.at[i]) for i, ref in enumerate(sources)
    ]
    for copy in copies:
        copy.start()
    for copy in copies:
        copy.wait()


def forward_kernel(groups, x_ref, held_ref, *refs):
    act_ref, slope_ref, value_ref, hidden_ref, rows_ref, sems = refs
    share, hidden = held_ref.shape[1:]
    step = tile_of(hidden, 256)
    copies = []
    for k in range(groups):
        cols = slice(k * share, (k + 1) * share)
        copies.append(pltpu.make_async_copy(x_ref.at[:, cols], rows_ref.at[:, cols], sems.at[k]))
        copies[k].start()
    for copy in copies:
        copy.wait()

    def against(first, cols):
        return sum(
            jnp.dot(
                rows_ref[:, k * share : (k + 1) * share],
                held_ref[first + k, :, cols],
                preferred_element_type=jnp.float32,
            )
            for k in range(groups)
        )

    for at in range(0, hidden, step):
        cols = slice(at, at + step)
        pre_gate = against(0, cols)
        pre_up = against(groups, cols)
        sig = jax.nn.sigmoid(pre_gate)
        act = pre_gate * sig
        hidden_f = act * pre_up
        act_ref[:, cols] = act
        slope_ref[:, cols] = pre_up * (sig * (1.0 + pre_gate * (1.0 - sig)))
        value_ref[:, cols] = hidden_f
        hidden_ref[:, cols] = hidden_f.astype(hidden_ref.dtype)


def backward_kernel(groups, act_ref, slope_ref, value_ref, held_ref, *refs):
    parts, (out_ref, d_gate_ref, d_up_ref, rows_ref, out_sems) = refs[:groups], refs[groups:]
    share = held_ref.shape[1]
    width = groups * share
    block = tile_of(share, 512)
    back = sum(part[...].astype(jnp.float32) for part in parts)
    score = jnp.sum(back * value_ref[...], axis=1, keepdims=True)
    d_gate_ref[...] = (back * slope_ref[...]).astype(jnp.bfloat16)
    d_up_ref[...] = (back * act_ref[...]).astype(jnp.bfloat16)
    rows_ref[:, width:] = jnp.broadcast_to(score, (score.shape[0], LANES)).astype(rows_ref.dtype)
    outs = []

    def send(cols):
        copy = pltpu.make_async_copy(
            rows_ref.at[:, cols], out_ref.at[:, cols], out_sems.at[len(outs)]
        )
        copy.start()
        outs.append(copy)

    send(slice(width, width + LANES))
    for k in range(groups):
        for at in range(0, share, block):
            cols = slice(k * share + at, k * share + at + block)
            grad = contract_last(d_gate_ref[...], held_ref[k, at : at + block])
            grad += contract_last(d_up_ref[...], held_ref[groups + k, at : at + block])
            rows_ref[:, cols] = grad.astype(rows_ref.dtype)
            send(cols)
    for copy in outs:
        copy.wait()


def combine_kernel(groups, place_ref, pos_ref, gate_ref, rows_ref, tokens_ref, gates_ref):
    top, count = pos_ref.shape
    slots = rows_ref.shape[0]
    width = tokens_ref.shape[1]
    share = width // groups
    places = lax.broadcasted_iota(jnp.int32, (slots, count), 0)
    picks = [
        jnp.where(places == pos_ref[k : k + 1, :], 1.0, 0.0).astype(jnp.bfloat16)
        for k in range(top)
    ]
    both = sum(picks)
    for k in range(groups):
        at = lax.rem(place_ref[0] - k + groups, groups) * share
        tokens_ref[:, pl.ds(pl.multiple_of(at, share), share)] = contract_first(
            both, rows_ref[:, k * share : (k + 1) * share]
        ).astype(tokens_ref.dtype)
    for k in range(top):
        score = contract_first(rows_ref[:, width:], picks[k])
        gates_ref[k : k + 1, :] = score[:1, :] / gate_ref[k : k + 1, :]


def per_device(tokens, routes, gates, grad_out, w_gate, w_up, w_down):
    experts = lax.axis_size("expert")
    groups = lax.axis_size("dp")
    group = lax.axis_index("dp")
    count, width = tokens.shape
    top = routes.shape[1]
    cap = 3 * count * top // (2 * experts)
    slots = experts * cap
    share = width // groups
    hidden = w_gate.shape[2]
    params = pltpu.CompilerParams(vmem_limit_bytes=VMEM_BYTES)
    place = group.astype(jnp.int32).reshape(1)

    def shifted(value, by):
        return lax.ppermute(value, "dp", [(i, (i + by) % groups) for i in range(groups)])

    def exchanged(rows):
        split = rows.reshape(experts, rows.shape[0] // experts, rows.shape[1])
        moved = lax.all_to_all(split, "expert", split_axis=0, concat_axis=0, tiled=True)
        return moved.reshape(rows.shape)

    routes_t, gates_t = jnp.transpose(routes), jnp.transpose(gates)
    routes_all = [routes_t] + [shifted(routes_t, k) for k in range(1, groups)]
    gates_all = [gates_t] + [shifted(gates_t, k) for k in range(1, groups)]
    grads = [
        shifted(
            lax.dynamic_slice(grad_out, (0, lax.rem(group + k, groups) * share), (count, share)), k
        )
        for k in range(1, groups)
    ]
    both = jnp.concatenate([w_gate[0], w_up[0]], axis=0)
    both, gates_own = lax.optimization_barrier((both, gates_t))
    weights = [w_gate[0], w_up[0]] + [shifted(both, k) for k in range(1, groups)]

    def in_hbm(value):
        return pltpu.with_memory_space_constraint(value, pltpu.HBM)

    block = tile_of(share, 512)
    steps = share // block
    small_spec = pl.BlockSpec((top, count), lambda c, g: (0, 0))
    scaled = pl.pallas_call(
        functools.partial(dispatch_scaled, experts, cap, groups),
        out_shape=pltpu.HBM((groups * slots, share), jnp.bfloat16),
        grid_spec=pltpu.PrefetchScalarGridSpec(
            num_scalar_prefetch=1,
            grid=(steps,),
            in_specs=[small_spec] * (2 * groups)
            + [pl.BlockSpec((count, block), lambda c, g: (0, g[0] * steps + c))]
            + [pl.BlockSpec((count, block), lambda c, g: (0, c))] * (groups - 1),
            out_specs=pl.BlockSpec((groups * slots, block), lambda c, g: (0, c)),
            scratch_shapes=[
                pltpu.VMEM((groups * slots, groups * count), jnp.bfloat16),
                pltpu.VMEM((groups * slots, LANES), jnp.float32),
            ],
        ),
        compiler_params=params,
        name="dispatch_scaled",
    )(place, in_hbm(routes_t), *routes_all[1:], in_hbm(gates_own), *gates_all[1:], in_hbm(grad_out), *grads)
    scaled_rows = exchanged(scaled)

    sent, pos = pl.pallas_call(
        functools.partial(dispatch_tokens, experts, cap),
        out_shape=(
            pltpu.HBM((slots, width), jnp.bfloat16),
            jax.ShapeDtypeStruct((top, count), jnp.int32),
        ),
        grid_spec=pltpu.PrefetchScalarGridSpec(
            num_scalar_prefetch=1,
            grid=(groups,),
            in_specs=[
                small_spec,
                pl.BlockSpec(
                    (count, share), lambda k, g: (0, lax.rem(g[0] - k + groups, groups))
                ),
            ],
            out_specs=(pl.BlockSpec((slots, share), lambda k, g: (0, k)), small_spec),
            scratch_shapes=[pltpu.VMEM((slots, count), jnp.bfloat16)],
        ),
        compiler_params=params,
        name="dispatch_tokens",
    )(place, in_hbm(routes_t), in_hbm(tokens))
    x_rows = exchanged(sent)

    back_own, *rest = pl.pallas_call(
        functools.partial(back_kernel, groups, cap),
        out_shape=[pltpu.HBM((slots, hidden), jnp.float32)]
        + [pltpu.HBM((slots, hidden), jnp.bfloat16)] * (groups - 1)
        + [pltpu.HBM((groups * slots, share), jnp.bfloat16)],
        compiler_params=params,
        name="back",
    )(scaled_rows, in_hbm(w_down[0]))
    scaled_all = rest[-1]
    back_parts = [back_own] + [shifted(rest[k - 1], -k) for k in range(1, groups)]

    whole_spec = pl.BlockSpec(memory_space=pltpu.VMEM)
    any_spec = pl.BlockSpec(memory_space=pl.ANY)
    held = pl.pallas_call(
        functools.partial(hold_kernel, groups),
        out_shape=pltpu.VMEM((2 * groups, share, hidden), jnp.bfloat16),
        in_specs=[any_spec] * (groups + 1),
        scratch_shapes=[pltpu.SemaphoreType.DMA((2 * groups,))],
        compiler_params=params,
        name="hold",
    )(*[in_hbm(value) for value in weights])

    *factors, hidden_own = pl.pallas_call(
        functools.partial(forward_kernel, groups),
        out_shape=[pltpu.VMEM((slots, hidden), jnp.float32)] * 3
        + [pltpu.HBM((slots, hidden), jnp.bfloat16)],
        in_specs=[any_spec, whole_spec],
        scratch_shapes=[
            pltpu.VMEM((slots, width), jnp.bfloat16),
            pltpu.SemaphoreType.DMA((groups,)),
        ],
        compiler_params=params,
        name="forward",
    )(in_hbm(x_rows), held)

    pieces = groups * (share // tile_of(share, 512))
    returning = pl.pallas_call(
        functools.partial(backward_kernel, groups),
        out_shape=pltpu.HBM((slots, width + LANES), jnp.bfloat16),
        in_specs=[whole_spec] * (4 + groups),
        out_specs=any_spec,
        scratch_shapes=[
            pltpu.VMEM((slots, hidden), jnp.bfloat16),
            pltpu.VMEM((slots, hidden), jnp.bfloat16),
            pltpu.VMEM((slots, width + LANES), jnp.bfloat16),
            pltpu.SemaphoreType.DMA((pieces + 1,)),
        ],
        compiler_params=params,
        name="backward",
    )(*factors, held, *back_parts)
    returned = exchanged(returning)

    hiddens = [hidden_own] + [shifted(hidden_own, k) for k in range(1, groups)]
    grad_down = contract_first(jnp.concatenate(hiddens, axis=0), scaled_all)[None]

    grad_tokens, grad_gates = pl.pallas_call(
        functools.partial(combine_kernel, groups),
        out_shape=(
            jax.ShapeDtypeStruct((count, width), jnp.bfloat16),
            jax.ShapeDtypeStruct((top, count), jnp.float32),
        ),
        in_specs=[pl.BlockSpec(memory_space=pltpu.SMEM)] + [whole_spec] * 3,
        compiler_params=params,
        name="combine",
    )(place, pos, gates_t, returned)
    return (grad_tokens, jnp.transpose(grad_gates), grad_down)


def solution(mesh):
    placed = (
        P(("dp", "expert"), None),
        P(("dp", "expert"), None),
        P(("dp", "expert"), None),
        P(("dp", "expert"), None),
        P("expert", "dp", None),
        P("expert", "dp", None),
        P("expert", None, "dp"),
    )
    return jax.shard_map(
        per_device,
        mesh=mesh,
        in_specs=placed,
        out_specs=(P(("dp", "expert"), None), P(("dp", "expert"), None), P("expert", None, "dp")),
        check_vma=False,
    )
```

```python
import functools

import jax
import jax.numpy as jnp
from jax import lax
from jax.experimental import pallas as pl
from jax.experimental.pallas import tpu as pltpu
from jax.sharding import PartitionSpec as P

LANES = 128
VMEM_BYTES = 24 * 1024 * 1024


def contract_last(left, right):
    return lax.dot_general(
        left, right, (((1,), (1,)), ((), ())), preferred_element_type=jnp.float32
    )


def contract_first(left, right):
    return lax.dot_general(
        left, right, (((0,), (0,)), ((), ())), preferred_element_type=jnp.float32
    )


def tile_of(extent, most):
    return most if extent % most == 0 else extent


def slot_positions(routes, experts, stride, base):
    top, count = routes.shape
    labels = lax.broadcasted_iota(jnp.int32, (experts, count), 0)
    named = [labels == routes[k : k + 1, :] for k in range(top)]
    marks = sum(jnp.where(m, 1.0, 0.0) for m in named)
    earlier = lax.broadcasted_iota(jnp.int32, (count, count), 0) < lax.broadcasted_iota(
        jnp.int32, (count, count), 1
    )
    rank = jnp.dot(
        marks.astype(jnp.bfloat16),
        jnp.where(earlier, 1.0, 0.0).astype(jnp.bfloat16),
        preferred_element_type=jnp.float32,
    )
    slot = rank + (labels * stride + base + 1).astype(jnp.float32)
    return [
        jnp.sum(jnp.where(m, slot, 0.0), axis=0, keepdims=True).astype(jnp.int32) - 1
        for m in named
    ]


def rows_of(ref, groups, cap, which):
    value = ref[...].astype(jnp.float32)
    count, width = value.shape
    value = value.reshape(count // (groups * cap), groups, cap, width)[:, which]
    return value.reshape(count // groups, width).astype(ref.dtype)


def dispatch_tokens(experts, cap, place_ref, routes_ref, tokens_ref, out_ref, pos_ref, pick_ref):
    @pl.when(pl.program_id(0) == 0)
    def _():
        pos = slot_positions(routes_ref[...], experts, cap, 0)
        rows = lax.broadcasted_iota(jnp.int32, pick_ref.shape, 0)
        pick_ref[...] = sum(jnp.where(rows == p, 1.0, 0.0) for p in pos).astype(jnp.bfloat16)
        for k, p in enumerate(pos):
            pos_ref[k : k + 1, :] = p

    out_ref[...] = jnp.dot(
        pick_ref[...], tokens_ref[...], preferred_element_type=jnp.float32
    ).astype(out_ref.dtype)


def dispatch_scaled(experts, cap, groups, place_ref, *refs):
    routes_refs, gate_refs = refs[:groups], refs[groups : 2 * groups]
    grad_refs, (out_ref, pick_ref, scale_ref) = refs[2 * groups : 3 * groups], refs[3 * groups :]
    count = grad_refs[0].shape[0]
    slots = out_ref.shape[0]

    @pl.when(pl.program_id(0) == 0)
    def _():
        rows = lax.broadcasted_iota(jnp.int32, (slots, count), 0)
        total = jnp.zeros((slots, 1), jnp.float32)
        for q in range(groups):
            pos = slot_positions(routes_refs[q][...], experts, groups * cap, q * cap)
            hit = jnp.zeros((slots, count), jnp.float32)
            weight = jnp.zeros((slots, count), jnp.float32)
            for k, p in enumerate(pos):
                here = rows == p
                hit = hit + jnp.where(here, 1.0, 0.0)
                weight = weight + jnp.where(here, gate_refs[q][k : k + 1, :], 0.0)
            pick_ref[:, q * count : (q + 1) * count] = hit.astype(jnp.bfloat16)
            total = total + jnp.sum(weight, axis=1, keepdims=True)
        scale_ref[...] = jnp.broadcast_to(total, scale_ref.shape)

    grads = jnp.concatenate([ref[...] for ref in grad_refs], axis=0)
    rows = jnp.dot(pick_ref[...], grads, preferred_element_type=jnp.float32)
    out_ref[...] = (scale_ref[:, :1] * rows).astype(out_ref.dtype)


def back_kernel(groups, cap, rows_ref, down_ref, own_ref, *rest):
    others, all_ref = rest[: groups - 1], rest[groups - 1]
    slots, hidden = own_ref.shape
    for q in range(groups):
        all_ref[q * slots : (q + 1) * slots, :] = rows_of(rows_ref, groups, cap, q)
    step = tile_of(hidden, 256)

    @pl.loop(0, hidden // step)
    def _(j):
        cols = pl.ds(pl.multiple_of(j * step, step), step)
        for q, ref in enumerate((own_ref, *others)):
            part = contract_last(all_ref[q * slots : (q + 1) * slots, :], down_ref[cols, :])
            ref[:, cols] = part.astype(ref.dtype)


def forward_kernel(groups, x_ref, *refs):
    (own_gate, own_up), others = refs[:2], refs[2 : groups + 1]
    act_ref, slope_ref, value_ref, hidden_ref, held_ref = refs[groups + 1 : groups + 6]
    rows_ref, gate_sum_ref, up_sum_ref, sems, row_sems = refs[groups + 6 :]
    share, hidden = held_ref.shape[1:]
    step = tile_of(hidden, 384)
    gates = [own_gate, *[ref.at[:share] for ref in others]]
    ups = [own_up, *[ref.at[share:] for ref in others]]

    def load(ref, i):
        return pltpu.make_async_copy(ref, held_ref.at[i], sems.at[i])

    def columns(k):
        return slice(k * share, (k + 1) * share)

    stages = []
    for k in range(groups):
        cols = columns(k)
        rows = pltpu.make_async_copy(x_ref.at[:, cols], rows_ref.at[:, cols], row_sems.at[k])
        stages.append([rows, load(gates[k], k)])
        stages.append([load(ups[k], groups + k)])

    def start(n):
        for copy in stages[n] if n < len(stages) else ():
            copy.start()

    def finish(n):
        for copy in stages[n]:
            copy.wait()

    start(0)
    start(1)
    for k in range(groups):
        x = rows_ref.at[:, columns(k)]
        finish(2 * k)
        start(2 * k + 2)
        for at in range(0, hidden, step):
            cols = slice(at, at + step)
            part = jnp.dot(x[...], held_ref[k, :, cols], preferred_element_type=jnp.float32)
            gate_sum_ref[:, cols] = part if k == 0 else gate_sum_ref[:, cols] + part
        finish(2 * k + 1)
        start(2 * k + 3)
        for at in range(0, hidden, step):
            cols = slice(at, at + step)
            pre_up = jnp.dot(
                x[...], held_ref[groups + k, :, cols], preferred_element_type=jnp.float32
            )
            if k > 0:
                pre_up += up_sum_ref[:, cols]
            if k < groups - 1:
                up_sum_ref[:, cols] = pre_up
                continue
            pre_gate = gate_sum_ref[:, cols]
            sig = jax.nn.sigmoid(pre_gate)
            act = pre_gate * sig
            hidden_f = act * pre_up
            act_ref[:, cols] = act
            slope_ref[:, cols] = pre_up * (sig * (1.0 + pre_gate * (1.0 - sig)))
            value_ref[:, cols] = hidden_f
            hidden_ref[:, cols] = hidden_f.astype(hidden_ref.dtype)


def backward_kernel(groups, act_ref, slope_ref, value_ref, held_ref, *refs):
    parts, (out_ref, d_gate_ref, d_up_ref, rows_ref, out_sems) = refs[:groups], refs[groups:]
    share = held_ref.shape[1]
    width = groups * share
    block = tile_of(share, 512)
    back = sum(part[...].astype(jnp.float32) for part in parts)
    score = jnp.sum(back * value_ref[...], axis=1, keepdims=True)
    d_gate_ref[...] = (back * slope_ref[...]).astype(jnp.bfloat16)
    d_up_ref[...] = (back * act_ref[...]).astype(jnp.bfloat16)
    rows_ref[:, width:] = jnp.broadcast_to(score, (score.shape[0], LANES)).astype(rows_ref.dtype)
    outs = []

    def send(cols):
        copy = pltpu.make_async_copy(
            rows_ref.at[:, cols], out_ref.at[:, cols], out_sems.at[len(outs)]
        )
        copy.start()
        outs.append(copy)

    send(slice(width, width + LANES))
    for k in range(groups):
        for at in range(0, share, block):
            cols = slice(k * share + at, k * share + at + block)
            grad = contract_last(d_gate_ref[...], held_ref[k, at : at + block])
            grad += contract_last(d_up_ref[...], held_ref[groups + k, at : at + block])
            rows_ref[:, cols] = grad.astype(rows_ref.dtype)
            send(cols)
    for copy in outs:
        copy.wait()


def combine_kernel(groups, place_ref, pos_ref, gate_ref, rows_ref, tokens_ref, gates_ref):
    top, count = pos_ref.shape
    slots = rows_ref.shape[0]
    width = tokens_ref.shape[1]
    share = width // groups
    places = lax.broadcasted_iota(jnp.int32, (slots, count), 0)
    picks = [
        jnp.where(places == pos_ref[k : k + 1, :], 1.0, 0.0).astype(jnp.bfloat16)
        for k in range(top)
    ]
    both = sum(picks)
    for k in range(groups):
        at = lax.rem(place_ref[0] - k + groups, groups) * share
        tokens_ref[:, pl.ds(pl.multiple_of(at, share), share)] = contract_first(
            both, rows_ref[:, k * share : (k + 1) * share]
        ).astype(tokens_ref.dtype)
    for k in range(top):
        score = contract_first(rows_ref[:, width:], picks[k])
        gates_ref[k : k + 1, :] = score[:1, :] / gate_ref[k : k + 1, :]


def per_device(tokens, routes, gates, grad_out, w_gate, w_up, w_down):
    experts = lax.axis_size("expert")
    groups = lax.axis_size("dp")
    group = lax.axis_index("dp")
    count, width = tokens.shape
    top = routes.shape[1]
    cap = 3 * count * top // (2 * experts)
    slots = experts * cap
    share = width // groups
    hidden = w_gate.shape[2]
    params = pltpu.CompilerParams(vmem_limit_bytes=VMEM_BYTES)
    place = group.astype(jnp.int32).reshape(1)

    def shifted(value, by):
        return lax.ppermute(value, "dp", [(i, (i + by) % groups) for i in range(groups)])

    def exchanged(rows):
        split = rows.reshape(experts, rows.shape[0] // experts, rows.shape[1])
        moved = lax.all_to_all(split, "expert", split_axis=0, concat_axis=0, tiled=True)
        return moved.reshape(rows.shape)

    routes_t, gates_t = jnp.transpose(routes), jnp.transpose(gates)
    routes_all = [routes_t] + [shifted(routes_t, k) for k in range(1, groups)]
    gates_all = [gates_t] + [shifted(gates_t, k) for k in range(1, groups)]
    grads = [
        shifted(
            lax.dynamic_slice(grad_out, (0, lax.rem(group + k, groups) * share), (count, share)), k
        )
        for k in range(1, groups)
    ]
    both = jnp.concatenate([w_gate[0], w_up[0]], axis=0)
    both, gates_own = lax.optimization_barrier((both, gates_t))
    weights = [w_gate[0], w_up[0]] + [shifted(both, k) for k in range(1, groups)]

    def in_hbm(value):
        return pltpu.with_memory_space_constraint(value, pltpu.HBM)

    block = tile_of(share, 512)
    steps = share // block
    small_spec = pl.BlockSpec((top, count), lambda c, g: (0, 0))
    scaled = pl.pallas_call(
        functools.partial(dispatch_scaled, experts, cap, groups),
        out_shape=pltpu.HBM((groups * slots, share), jnp.bfloat16),
        grid_spec=pltpu.PrefetchScalarGridSpec(
            num_scalar_prefetch=1,
            grid=(steps,),
            in_specs=[small_spec] * (2 * groups)
            + [pl.BlockSpec((count, block), lambda c, g: (0, g[0] * steps + c))]
            + [pl.BlockSpec((count, block), lambda c, g: (0, c))] * (groups - 1),
            out_specs=pl.BlockSpec((groups * slots, block), lambda c, g: (0, c)),
            scratch_shapes=[
                pltpu.VMEM((groups * slots, groups * count), jnp.bfloat16),
                pltpu.VMEM((groups * slots, LANES), jnp.float32),
            ],
        ),
        compiler_params=params,
        name="dispatch_scaled",
    )(place, in_hbm(routes_t), *routes_all[1:], in_hbm(gates_own), *gates_all[1:], in_hbm(grad_out), *grads)
    scaled_rows = exchanged(scaled)

    sent, pos = pl.pallas_call(
        functools.partial(dispatch_tokens, experts, cap),
        out_shape=(
            pltpu.HBM((slots, width), jnp.bfloat16),
            jax.ShapeDtypeStruct((top, count), jnp.int32),
        ),
        grid_spec=pltpu.PrefetchScalarGridSpec(
            num_scalar_prefetch=1,
            grid=(groups,),
            in_specs=[
                small_spec,
                pl.BlockSpec(
                    (count, share), lambda k, g: (0, lax.rem(g[0] - k + groups, groups))
                ),
            ],
            out_specs=(pl.BlockSpec((slots, share), lambda k, g: (0, k)), small_spec),
            scratch_shapes=[pltpu.VMEM((slots, count), jnp.bfloat16)],
        ),
        compiler_params=params,
        name="dispatch_tokens",
    )(place, in_hbm(routes_t), in_hbm(tokens))
    x_rows = exchanged(sent)

    back_own, *rest = pl.pallas_call(
        functools.partial(back_kernel, groups, cap),
        out_shape=[pltpu.HBM((slots, hidden), jnp.float32)]
        + [pltpu.HBM((slots, hidden), jnp.bfloat16)] * (groups - 1)
        + [pltpu.HBM((groups * slots, share), jnp.bfloat16)],
        compiler_params=params,
        name="back",
    )(scaled_rows, in_hbm(w_down[0]))
    scaled_all = rest[-1]
    back_parts = [back_own] + [shifted(rest[k - 1], -k) for k in range(1, groups)]

    whole_spec = pl.BlockSpec(memory_space=pltpu.VMEM)
    any_spec = pl.BlockSpec(memory_space=pl.ANY)
    *factors, hidden_own, held = pl.pallas_call(
        functools.partial(forward_kernel, groups),
        out_shape=[pltpu.VMEM((slots, hidden), jnp.float32)] * 3
        + [
            pltpu.HBM((slots, hidden), jnp.bfloat16),
            pltpu.VMEM((2 * groups, share, hidden), jnp.bfloat16),
        ],
        in_specs=[any_spec] * (groups + 2),
        scratch_shapes=[
            pltpu.VMEM((slots, width), jnp.bfloat16),
            pltpu.VMEM((slots, hidden), jnp.float32),
            pltpu.VMEM((slots, hidden), jnp.float32),
            pltpu.SemaphoreType.DMA((2 * groups,)),
            pltpu.SemaphoreType.DMA((groups,)),
        ],
        compiler_params=params,
        name="forward",
    )(in_hbm(x_rows), *[in_hbm(value) for value in weights])

    pieces = groups * (share // tile_of(share, 512))
    returning = pl.pallas_call(
        functools.partial(backward_kernel, groups),
        out_shape=pltpu.HBM((slots, width + LANES), jnp.bfloat16),
        in_specs=[whole_spec] * (4 + groups),
        out_specs=any_spec,
        scratch_shapes=[
            pltpu.VMEM((slots, hidden), jnp.bfloat16),
            pltpu.VMEM((slots, hidden), jnp.bfloat16),
            pltpu.VMEM((slots, width + LANES), jnp.bfloat16),
            pltpu.SemaphoreType.DMA((pieces + 1,)),
        ],
        compiler_params=params,
        name="backward",
    )(*factors, held, *back_parts)
    returned = exchanged(returning)

    hiddens = [hidden_own] + [shifted(hidden_own, k) for k in range(1, groups)]
    grad_down = contract_first(jnp.concatenate(hiddens, axis=0), scaled_all)[None]

    grad_tokens, grad_gates = pl.pallas_call(
        functools.partial(combine_kernel, groups),
        out_shape=(
            jax.ShapeDtypeStruct((count, width), jnp.bfloat16),
            jax.ShapeDtypeStruct((top, count), jnp.float32),
        ),
        in_specs=[pl.BlockSpec(memory_space=pltpu.SMEM)] + [whole_spec] * 3,
        compiler_params=params,
        name="combine",
    )(place, pos, gates_t, returned)
    return (grad_tokens, jnp.transpose(grad_gates), grad_down)


def solution(mesh):
    placed = (
        P(("dp", "expert"), None),
        P(("dp", "expert"), None),
        P(("dp", "expert"), None),
        P(("dp", "expert"), None),
        P("expert", "dp", None),
        P("expert", "dp", None),
        P("expert", None, "dp"),
    )
    return jax.shard_map(
        per_device,
        mesh=mesh,
        in_specs=placed,
        out_specs=(P(("dp", "expert"), None), P(("dp", "expert"), None), P("expert", None, "dp")),
        check_vma=False,
    )
```

```python
import functools

import jax
import jax.numpy as jnp
from jax import lax
from jax.experimental import pallas as pl
from jax.experimental.pallas import tpu as pltpu
from jax.sharding import PartitionSpec as P

LANES = 128
VMEM_BYTES = 24 * 1024 * 1024


def contract_last(left, right):
    return lax.dot_general(
        left, right, (((1,), (1,)), ((), ())), preferred_element_type=jnp.float32
    )


def contract_first(left, right):
    return lax.dot_general(
        left, right, (((0,), (0,)), ((), ())), preferred_element_type=jnp.float32
    )


def tile_of(extent, most):
    return most if extent % most == 0 else extent


def slot_positions(routes, experts, stride, base):
    top, count = routes.shape
    labels = lax.broadcasted_iota(jnp.int32, (experts, count), 0)
    named = [labels == routes[k : k + 1, :] for k in range(top)]
    marks = sum(jnp.where(m, 1.0, 0.0) for m in named)
    earlier = lax.broadcasted_iota(jnp.int32, (count, count), 0) < lax.broadcasted_iota(
        jnp.int32, (count, count), 1
    )
    rank = jnp.dot(
        marks.astype(jnp.bfloat16),
        jnp.where(earlier, 1.0, 0.0).astype(jnp.bfloat16),
        preferred_element_type=jnp.float32,
    )
    slot = rank + (labels * stride + base + 1).astype(jnp.float32)
    return [
        jnp.sum(jnp.where(m, slot, 0.0), axis=0, keepdims=True).astype(jnp.int32) - 1
        for m in named
    ]


def rows_of(ref, groups, cap, which):
    value = ref[...].astype(jnp.float32)
    count, width = value.shape
    value = value.reshape(count // (groups * cap), groups, cap, width)[:, which]
    return value.reshape(count // groups, width).astype(ref.dtype)


def dispatch_tokens(experts, cap, place_ref, routes_ref, tokens_ref, out_ref, pos_ref, pick_ref):
    @pl.when(pl.program_id(0) == 0)
    def _():
        pos = slot_positions(routes_ref[...], experts, cap, 0)
        rows = lax.broadcasted_iota(jnp.int32, pick_ref.shape, 0)
        pick_ref[...] = sum(jnp.where(rows == p, 1.0, 0.0) for p in pos).astype(jnp.bfloat16)
        for k, p in enumerate(pos):
            pos_ref[k : k + 1, :] = p

    out_ref[...] = jnp.dot(
        pick_ref[...], tokens_ref[...], preferred_element_type=jnp.float32
    ).astype(out_ref.dtype)


def dispatch_scaled(experts, cap, groups, place_ref, *refs):
    routes_refs, gate_refs = refs[:groups], refs[groups : 2 * groups]
    grad_refs, (out_ref, pick_ref, scale_ref) = refs[2 * groups : 3 * groups], refs[3 * groups :]
    count = grad_refs[0].shape[0]
    slots = out_ref.shape[0]

    @pl.when(pl.program_id(0) == 0)
    def _():
        rows = lax.broadcasted_iota(jnp.int32, (slots, count), 0)
        total = jnp.zeros((slots, 1), jnp.float32)
        for q in range(groups):
            pos = slot_positions(routes_refs[q][...], experts, groups * cap, q * cap)
            hit = jnp.zeros((slots, count), jnp.float32)
            weight = jnp.zeros((slots, count), jnp.float32)
            for k, p in enumerate(pos):
                here = rows == p
                hit = hit + jnp.where(here, 1.0, 0.0)
                weight = weight + jnp.where(here, gate_refs[q][k : k + 1, :], 0.0)
            pick_ref[:, q * count : (q + 1) * count] = hit.astype(jnp.bfloat16)
            total = total + jnp.sum(weight, axis=1, keepdims=True)
        scale_ref[...] = jnp.broadcast_to(total, scale_ref.shape)

    grads = jnp.concatenate([ref[...] for ref in grad_refs], axis=0)
    rows = jnp.dot(pick_ref[...], grads, preferred_element_type=jnp.float32)
    out_ref[...] = (scale_ref[:, :1] * rows).astype(out_ref.dtype)


def back_kernel(groups, cap, mine_ref, rows_ref, down_ref, own_ref, *rest):
    others, all_ref = rest[: groups - 1], rest[groups - 1]
    slots, hidden = own_ref.shape
    all_ref[:slots, :] = mine_ref[...]
    for q in range(groups - 1):
        rows = rows_ref[...] if groups == 2 else rows_of(rows_ref, groups - 1, cap, q)
        all_ref[(q + 1) * slots : (q + 2) * slots, :] = rows
    step = tile_of(hidden, 256)

    @pl.loop(0, hidden // step)
    def _(j):
        cols = pl.ds(pl.multiple_of(j * step, step), step)
        for q, ref in enumerate((own_ref, *others)):
            part = contract_last(all_ref[q * slots : (q + 1) * slots, :], down_ref[cols, :])
            ref[:, cols] = part.astype(ref.dtype)


def forward_kernel(groups, x_ref, back_ref, *refs):
    gates, (own_up, *others) = refs[:groups], refs[groups : 3 * groups - 1]
    act_ref, slope_ref, value_ref, hidden_ref, held_ref, kept_ref = refs[
        3 * groups - 1 : 3 * groups + 5
    ]
    gate_sum_ref, up_sum_ref, sems, back_sem = refs[3 * groups + 5 :]
    share, hidden = held_ref.shape[1:]
    step = tile_of(hidden, 384)

    def load(ref, i, to=0, n=0):
        return pltpu.make_async_copy(ref, held_ref.at[i, to : to + ref.shape[0]], sems.at[n, i])

    stages = [[load(gates[0], 0)], [load(own_up, groups)]]
    for k in range(1, groups):
        first, second = others[2 * k - 2 : 2 * k]
        stages.append([load(gates[k], k)])
        stages.append(
            [load(first, groups + k), load(second, groups + k, first.shape[0], 1)]
        )
    kept = pltpu.make_async_copy(back_ref, kept_ref, back_sem.at[0])
    for copies in (*stages, [kept]):
        for copy in copies:
            copy.start()

    def against(i, cols):
        k = i % groups
        return jnp.dot(
            x_ref[:, k * share : (k + 1) * share],
            held_ref[i, :, cols],
            preferred_element_type=jnp.float32,
        )

    spans = [slice(at, at + step) for at in range(0, hidden, step)]
    for k in range(groups):
        for copy in stages[2 * k]:
            copy.wait()
        for cols in spans:
            part = against(k, cols)
            gate_sum_ref[:, cols] = part if k == 0 else gate_sum_ref[:, cols] + part
        for copy in stages[2 * k + 1]:
            copy.wait()
        for cols in spans:
            pre_up = against(groups + k, cols)
            if k > 0:
                pre_up += up_sum_ref[:, cols]
            if k < groups - 1:
                up_sum_ref[:, cols] = pre_up
                continue
            pre_gate = gate_sum_ref[:, cols]
            sig = jax.nn.sigmoid(pre_gate)
            act = pre_gate * sig
            hidden_f = act * pre_up
            act_ref[:, cols] = act
            slope_ref[:, cols] = pre_up * (sig * (1.0 + pre_gate * (1.0 - sig)))
            value_ref[:, cols] = hidden_f
            hidden_ref[:, cols] = hidden_f.astype(hidden_ref.dtype)
    kept.wait()


def backward_kernel(groups, act_ref, slope_ref, value_ref, held_ref, *refs):
    parts, (out_ref, d_gate_ref, d_up_ref, rows_ref, out_sems) = refs[:groups], refs[groups:]
    share = held_ref.shape[1]
    width = groups * share
    block = tile_of(share, 512)
    back = sum(part[...].astype(jnp.float32) for part in parts)
    score = jnp.sum(back * value_ref[...], axis=1, keepdims=True)
    d_gate_ref[...] = (back * slope_ref[...]).astype(jnp.bfloat16)
    d_up_ref[...] = (back * act_ref[...]).astype(jnp.bfloat16)
    rows_ref[:, width:] = jnp.broadcast_to(score, (score.shape[0], LANES)).astype(rows_ref.dtype)
    outs = []

    def send(cols):
        copy = pltpu.make_async_copy(
            rows_ref.at[:, cols], out_ref.at[:, cols], out_sems.at[len(outs)]
        )
        copy.start()
        outs.append(copy)

    send(slice(width, width + LANES))
    for k in range(groups):
        for at in range(0, share, block):
            cols = slice(k * share + at, k * share + at + block)
            grad = contract_last(d_gate_ref[...], held_ref[k, at : at + block])
            grad += contract_last(d_up_ref[...], held_ref[groups + k, at : at + block])
            rows_ref[:, cols] = grad.astype(rows_ref.dtype)
            send(cols)
    for copy in outs:
        copy.wait()


def combine_kernel(groups, place_ref, pos_ref, gate_ref, rows_ref, tokens_ref, gates_ref):
    top, count = pos_ref.shape
    slots = rows_ref.shape[0]
    width = tokens_ref.shape[1]
    share = width // groups
    places = lax.broadcasted_iota(jnp.int32, (slots, count), 0)
    picks = [
        jnp.where(places == pos_ref[k : k + 1, :], 1.0, 0.0).astype(jnp.bfloat16)
        for k in range(top)
    ]
    both = sum(picks)
    for k in range(groups):
        at = lax.rem(place_ref[0] - k + groups, groups) * share
        tokens_ref[:, pl.ds(pl.multiple_of(at, share), share)] = contract_first(
            both, rows_ref[:, k * share : (k + 1) * share]
        ).astype(tokens_ref.dtype)
    for k in range(top):
        score = contract_first(rows_ref[:, width:], picks[k])
        gates_ref[k : k + 1, :] = score[:1, :] / gate_ref[k : k + 1, :]


def per_device(tokens, routes, gates, grad_out, w_gate, w_up, w_down):
    experts = lax.axis_size("expert")
    groups = lax.axis_size("dp")
    group = lax.axis_index("dp")
    count, width = tokens.shape
    top = routes.shape[1]
    cap = 3 * count * top // (2 * experts)
    slots = experts * cap
    share = width // groups
    hidden = w_gate.shape[2]
    params = pltpu.CompilerParams(vmem_limit_bytes=VMEM_BYTES)
    place = group.astype(jnp.int32).reshape(1)

    def shifted(value, by):
        return lax.ppermute(value, "dp", [(i, (i + by) % groups) for i in range(groups)])

    def exchanged(rows):
        split = rows.reshape(experts, rows.shape[0] // experts, rows.shape[1])
        moved = lax.all_to_all(split, "expert", split_axis=0, concat_axis=0, tiled=True)
        return moved.reshape(rows.shape)

    routes_t, gates_t = jnp.transpose(routes), jnp.transpose(gates)
    routes_all = [routes_t] + [shifted(routes_t, k) for k in range(1, groups)]
    gates_all = [gates_t] + [shifted(gates_t, k) for k in range(1, groups)]
    grads = [
        shifted(
            lax.dynamic_slice(grad_out, (0, lax.rem(group + k, groups) * share), (count, share)), k
        )
        for k in range(1, groups)
    ]
    early = share * 3 // 16 if share % 256 == 0 else share // 2
    gates_moved = [shifted(w_gate[0], k) for k in range(1, groups)]
    ups_first = [shifted(w_up[0, :early], k) for k in range(1, groups)]
    ups_second = [shifted(w_up[0, early:], k) for k in range(1, groups)]

    def in_hbm(value):
        return pltpu.with_memory_space_constraint(value, pltpu.HBM)

    block = tile_of(share, 512)
    steps = share // block
    small_spec = pl.BlockSpec((top, count), lambda c, g: (0, 0))

    def dispatched(routes_of, gates_of, grads_of, grads_map):
        number = len(routes_of)
        return pl.pallas_call(
            functools.partial(dispatch_scaled, experts, cap, number),
            out_shape=pltpu.HBM((number * slots, share), jnp.bfloat16),
            grid_spec=pltpu.PrefetchScalarGridSpec(
                num_scalar_prefetch=1,
                grid=(steps,),
                in_specs=[small_spec] * (2 * number)
                + [pl.BlockSpec((count, block), grads_map)] * number,
                out_specs=pl.BlockSpec((number * slots, block), lambda c, g: (0, c)),
                scratch_shapes=[
                    pltpu.VMEM((number * slots, number * count), jnp.bfloat16),
                    pltpu.VMEM((number * slots, LANES), jnp.float32),
                ],
            ),
            compiler_params=params,
            name="dispatch_scaled",
        )(place, *routes_of, *gates_of, *grads_of)

    scaled_mine = dispatched(
        [in_hbm(routes_t)],
        [in_hbm(gates_t)],
        [in_hbm(grad_out)],
        lambda c, g: (0, g[0] * steps + c),
    )
    mine_rows = exchanged(scaled_mine)
    scaled = dispatched(routes_all[1:], gates_all[1:], grads, lambda c, g: (0, c))
    scaled, mine_rows = lax.optimization_barrier((scaled, mine_rows))
    scaled_rows = exchanged(scaled)

    sent, pos = pl.pallas_call(
        functools.partial(dispatch_tokens, experts, cap),
        out_shape=(
            pltpu.HBM((slots, width), jnp.bfloat16),
            jax.ShapeDtypeStruct((top, count), jnp.int32),
        ),
        grid_spec=pltpu.PrefetchScalarGridSpec(
            num_scalar_prefetch=1,
            grid=(groups,),
            in_specs=[
                small_spec,
                pl.BlockSpec(
                    (count, share), lambda k, g: (0, lax.rem(g[0] - k + groups, groups))
                ),
            ],
            out_specs=(pl.BlockSpec((slots, share), lambda k, g: (0, k)), small_spec),
            scratch_shapes=[pltpu.VMEM((slots, count), jnp.bfloat16)],
        ),
        compiler_params=params,
        name="dispatch_tokens",
    )(place, in_hbm(routes_t), in_hbm(tokens))
    sent, scaled_rows, gates_moved, ups_first = lax.optimization_barrier(
        (sent, scaled_rows, gates_moved, ups_first)
    )
    x_rows = exchanged(sent)

    back_own, *rest = pl.pallas_call(
        functools.partial(back_kernel, groups, cap),
        out_shape=[pltpu.HBM((slots, hidden), jnp.float32)]
        + [pltpu.HBM((slots, hidden), jnp.bfloat16)] * (groups - 1)
        + [pltpu.HBM((groups * slots, share), jnp.bfloat16)],
        compiler_params=params,
        name="back",
    )(mine_rows, scaled_rows, in_hbm(w_down[0]))
    scaled_all = rest[-1]
    back_parts = [shifted(rest[k - 1], -k) for k in range(1, groups)]

    whole_spec = pl.BlockSpec(memory_space=pltpu.VMEM)
    any_spec = pl.BlockSpec(memory_space=pl.ANY)
    weights = [w_gate[0], *gates_moved, w_up[0]]
    for pair in zip(ups_first, ups_second):
        weights.extend(pair)
    *factors, hidden_own, held, back_kept = pl.pallas_call(
        functools.partial(forward_kernel, groups),
        out_shape=[pltpu.VMEM((slots, hidden), jnp.float32)] * 3
        + [
            pltpu.HBM((slots, hidden), jnp.bfloat16),
            pltpu.VMEM((2 * groups, share, hidden), jnp.bfloat16),
            pltpu.VMEM((slots, hidden), jnp.float32),
        ],
        in_specs=[whole_spec] + [any_spec] * (3 * groups),
        scratch_shapes=[
            pltpu.VMEM((slots, hidden), jnp.float32),
            pltpu.VMEM((slots, hidden), jnp.float32),
            pltpu.SemaphoreType.DMA((2, 2 * groups)),
            pltpu.SemaphoreType.DMA((1,)),
        ],
        compiler_params=params,
        name="forward",
    )(x_rows, in_hbm(back_own), *[in_hbm(value) for value in weights])

    pieces = groups * (share // tile_of(share, 512))
    returning = pl.pallas_call(
        functools.partial(backward_kernel, groups),
        out_shape=pltpu.HBM((slots, width + LANES), jnp.bfloat16),
        in_specs=[whole_spec] * (4 + groups),
        out_specs=any_spec,
        scratch_shapes=[
            pltpu.VMEM((slots, hidden), jnp.bfloat16),
            pltpu.VMEM((slots, hidden), jnp.bfloat16),
            pltpu.VMEM((slots, width + LANES), jnp.bfloat16),
            pltpu.SemaphoreType.DMA((pieces + 1,)),
        ],
        compiler_params=params,
        name="backward",
    )(*factors, held, back_kept, *back_parts)
    returned = exchanged(returning)

    hiddens = [hidden_own] + [shifted(hidden_own, k) for k in range(1, groups)]
    grad_down = contract_first(jnp.concatenate(hiddens, axis=0), scaled_all)[None]

    grad_tokens, grad_gates = pl.pallas_call(
        functools.partial(combine_kernel, groups),
        out_shape=(
            jax.ShapeDtypeStruct((count, width), jnp.bfloat16),
            jax.ShapeDtypeStruct((top, count), jnp.float32),
        ),
        in_specs=[pl.BlockSpec(memory_space=pltpu.SMEM)] + [whole_spec] * 3,
        compiler_params=params,
        name="combine",
    )(place, pos, gates_t, returned)
    return (grad_tokens, jnp.transpose(grad_gates), grad_down)


def solution(mesh):
    placed = (
        P(("dp", "expert"), None),
        P(("dp", "expert"), None),
        P(("dp", "expert"), None),
        P(("dp", "expert"), None),
        P("expert", "dp", None),
        P("expert", "dp", None),
        P("expert", None, "dp"),
    )
    return jax.shard_map(
        per_device,
        mesh=mesh,
        in_specs=placed,
        out_specs=(P(("dp", "expert"), None), P(("dp", "expert"), None), P("expert", None, "dp")),
        check_vma=False,
    )
```

```python
import functools

import jax
import jax.numpy as jnp
from jax import lax
from jax.experimental import pallas as pl
from jax.experimental.pallas import tpu as pltpu
from jax.sharding import PartitionSpec as P

LANES = 128
VMEM_BYTES = 24 * 1024 * 1024
BACK_COST_US = 30


def contract_last(left, right):
    return lax.dot_general(
        left, right, (((1,), (1,)), ((), ())), preferred_element_type=jnp.float32
    )


def contract_first(left, right):
    return lax.dot_general(
        left, right, (((0,), (0,)), ((), ())), preferred_element_type=jnp.float32
    )


def tile_of(extent, most):
    return most if extent % most == 0 else extent


def slot_positions(routes, experts, stride, base):
    top, count = routes.shape
    labels = lax.broadcasted_iota(jnp.int32, (experts, count), 0)
    named = [labels == routes[k : k + 1, :] for k in range(top)]
    marks = sum(jnp.where(m, 1.0, 0.0) for m in named)
    earlier = lax.broadcasted_iota(jnp.int32, (count, count), 0) < lax.broadcasted_iota(
        jnp.int32, (count, count), 1
    )
    rank = jnp.dot(
        marks.astype(jnp.bfloat16),
        jnp.where(earlier, 1.0, 0.0).astype(jnp.bfloat16),
        preferred_element_type=jnp.float32,
    )
    slot = rank + (labels * stride + base + 1).astype(jnp.float32)
    return [
        jnp.sum(jnp.where(m, slot, 0.0), axis=0, keepdims=True).astype(jnp.int32) - 1
        for m in named
    ]


def rows_of(ref, groups, cap, which):
    value = ref[...].astype(jnp.float32)
    count, width = value.shape
    value = value.reshape(count // (groups * cap), groups, cap, width)[:, which]
    return value.reshape(count // groups, width).astype(ref.dtype)


def dispatch_tokens(experts, cap, place_ref, routes_ref, tokens_ref, out_ref, pos_ref, pick_ref):
    @pl.when(pl.program_id(0) == 0)
    def _():
        pos = slot_positions(routes_ref[...], experts, cap, 0)
        rows = lax.broadcasted_iota(jnp.int32, pick_ref.shape, 0)
        pick_ref[...] = sum(jnp.where(rows == p, 1.0, 0.0) for p in pos).astype(jnp.bfloat16)
        for k, p in enumerate(pos):
            pos_ref[k : k + 1, :] = p

    out_ref[...] = jnp.dot(
        pick_ref[...], tokens_ref[...], preferred_element_type=jnp.float32
    ).astype(out_ref.dtype)


def dispatch_scaled(experts, cap, groups, place_ref, *refs):
    routes_refs, gate_refs = refs[:groups], refs[groups : 2 * groups]
    grad_refs, (out_ref, pick_ref, scale_ref) = refs[2 * groups : 3 * groups], refs[3 * groups :]
    count = grad_refs[0].shape[0]
    slots = out_ref.shape[0]

    @pl.when(pl.program_id(0) == 0)
    def _():
        rows = lax.broadcasted_iota(jnp.int32, (slots, count), 0)
        total = jnp.zeros((slots, 1), jnp.float32)
        for q in range(groups):
            pos = slot_positions(routes_refs[q][...], experts, groups * cap, q * cap)
            hit = jnp.zeros((slots, count), jnp.float32)
            weight = jnp.zeros((slots, count), jnp.float32)
            for k, p in enumerate(pos):
                here = rows == p
                hit = hit + jnp.where(here, 1.0, 0.0)
                weight = weight + jnp.where(here, gate_refs[q][k : k + 1, :], 0.0)
            pick_ref[:, q * count : (q + 1) * count] = hit.astype(jnp.bfloat16)
            total = total + jnp.sum(weight, axis=1, keepdims=True)
        scale_ref[...] = jnp.broadcast_to(total, scale_ref.shape)

    grads = jnp.concatenate([ref[...] for ref in grad_refs], axis=0)
    rows = jnp.dot(pick_ref[...], grads, preferred_element_type=jnp.float32)
    out_ref[...] = (scale_ref[:, :1] * rows).astype(out_ref.dtype)


def back_kernel(groups, cap, rows_ref, down_ref, own_ref, *rest):
    others, all_ref = rest[: groups - 1], rest[groups - 1]
    slots, hidden = own_ref.shape
    for q in range(groups):
        all_ref[q * slots : (q + 1) * slots, :] = rows_of(rows_ref, groups, cap, q)
    step = tile_of(hidden, 256)

    @pl.loop(0, hidden // step)
    def _(j):
        cols = pl.ds(pl.multiple_of(j * step, step), step)
        for q, ref in enumerate((own_ref, *others)):
            part = contract_last(all_ref[q * slots : (q + 1) * slots, :], down_ref[cols, :])
            ref[:, cols] = part.astype(ref.dtype)


def forward_kernel(groups, x_ref, back_ref, *refs):
    (own_gate, own_up), others = refs[:2], refs[2 : groups + 1]
    act_ref, slope_ref, value_ref, hidden_ref, held_ref, kept_ref = refs[groups + 1 : groups + 7]
    gate_sum_ref, up_sum_ref, sems, back_sem = refs[groups + 7 :]
    share, hidden = held_ref.shape[1:]
    step = tile_of(hidden, 384)
    gates = [own_gate, *[ref.at[:share] for ref in others]]
    ups = [own_up, *[ref.at[share:] for ref in others]]
    spans = [slice(at, at + step) for at in range(0, hidden, step)]

    loads = []
    for k in range(groups):
        for ref, i in ((gates[k], k), (ups[k], groups + k)):
            for n, cols in enumerate(spans):
                loads.append(
                    pltpu.make_async_copy(
                        ref.at[:, cols], held_ref.at[i, :, cols], sems.at[n, i]
                    )
                )
    loads.append(pltpu.make_async_copy(back_ref, kept_ref, back_sem.at[0]))
    flying = 3
    for copy in loads[:flying]:
        copy.start()
    place = 0

    def arrived():
        nonlocal place
        loads[place].wait()
        if place + flying < len(loads):
            loads[place + flying].start()
        place += 1

    def against(k, i, cols):
        return jnp.dot(
            x_ref[:, k * share : (k + 1) * share],
            held_ref[i, :, cols],
            preferred_element_type=jnp.float32,
        )

    for k in range(groups):
        for cols in spans:
            arrived()
            part = against(k, k, cols)
            gate_sum_ref[:, cols] = part if k == 0 else gate_sum_ref[:, cols] + part
        for cols in spans:
            arrived()
            pre_up = against(k, groups + k, cols)
            if k > 0:
                pre_up += up_sum_ref[:, cols]
            if k < groups - 1:
                up_sum_ref[:, cols] = pre_up
                continue
            pre_gate = gate_sum_ref[:, cols]
            sig = jax.nn.sigmoid(pre_gate)
            act = pre_gate * sig
            hidden_f = act * pre_up
            act_ref[:, cols] = act
            slope_ref[:, cols] = pre_up * (sig * (1.0 + pre_gate * (1.0 - sig)))
            value_ref[:, cols] = hidden_f
            hidden_ref[:, cols] = hidden_f.astype(hidden_ref.dtype)
    arrived()


def backward_kernel(groups, act_ref, slope_ref, value_ref, held_ref, *refs):
    parts, (out_ref, d_gate_ref, d_up_ref, rows_ref, out_sems) = refs[:groups], refs[groups:]
    share = held_ref.shape[1]
    width = groups * share
    block = tile_of(share, 512)
    back = sum(part[...].astype(jnp.float32) for part in parts)
    score = jnp.sum(back * value_ref[...], axis=1, keepdims=True)
    d_gate_ref[...] = (back * slope_ref[...]).astype(jnp.bfloat16)
    d_up_ref[...] = (back * act_ref[...]).astype(jnp.bfloat16)
    rows_ref[:, width:] = jnp.broadcast_to(score, (score.shape[0], LANES)).astype(rows_ref.dtype)
    outs = []

    def send(cols):
        copy = pltpu.make_async_copy(
            rows_ref.at[:, cols], out_ref.at[:, cols], out_sems.at[len(outs)]
        )
        copy.start()
        outs.append(copy)

    send(slice(width, width + LANES))
    for k in range(groups):
        for at in range(0, share, block):
            cols = slice(k * share + at, k * share + at + block)
            grad = contract_last(d_gate_ref[...], held_ref[k, at : at + block])
            grad += contract_last(d_up_ref[...], held_ref[groups + k, at : at + block])
            rows_ref[:, cols] = grad.astype(rows_ref.dtype)
            send(cols)
    for copy in outs:
        copy.wait()


def combine_kernel(groups, place_ref, pos_ref, gate_ref, rows_ref, tokens_ref, gates_ref):
    top, count = pos_ref.shape
    slots = rows_ref.shape[0]
    width = tokens_ref.shape[1]
    share = width // groups
    places = lax.broadcasted_iota(jnp.int32, (slots, count), 0)
    picks = [
        jnp.where(places == pos_ref[k : k + 1, :], 1.0, 0.0).astype(jnp.bfloat16)
        for k in range(top)
    ]
    both = sum(picks)
    for k in range(groups):
        at = lax.rem(place_ref[0] - k + groups, groups) * share
        tokens_ref[:, pl.ds(pl.multiple_of(at, share), share)] = contract_first(
            both, rows_ref[:, k * share : (k + 1) * share]
        ).astype(tokens_ref.dtype)
    for k in range(top):
        score = contract_first(rows_ref[:, width:], picks[k])
        gates_ref[k : k + 1, :] = score[:1, :] / gate_ref[k : k + 1, :]


def per_device(tokens, routes, gates, grad_out, w_gate, w_up, w_down):
    experts = lax.axis_size("expert")
    groups = lax.axis_size("dp")
    group = lax.axis_index("dp")
    count, width = tokens.shape
    top = routes.shape[1]
    cap = 3 * count * top // (2 * experts)
    slots = experts * cap
    share = width // groups
    hidden = w_gate.shape[2]
    params = pltpu.CompilerParams(vmem_limit_bytes=VMEM_BYTES)
    place = group.astype(jnp.int32).reshape(1)

    def shifted(value, by):
        return lax.ppermute(value, "dp", [(i, (i + by) % groups) for i in range(groups)])

    def exchanged(rows):
        split = rows.reshape(experts, rows.shape[0] // experts, rows.shape[1])
        moved = lax.all_to_all(split, "expert", split_axis=0, concat_axis=0, tiled=True)
        return moved.reshape(rows.shape)

    routes_t, gates_t = jnp.transpose(routes), jnp.transpose(gates)
    routes_all = [routes_t] + [shifted(routes_t, k) for k in range(1, groups)]
    gates_all = [gates_t] + [shifted(gates_t, k) for k in range(1, groups)]
    grads = [
        shifted(
            lax.dynamic_slice(grad_out, (0, lax.rem(group + k, groups) * share), (count, share)), k
        )
        for k in range(1, groups)
    ]
    both = jnp.concatenate([w_gate[0], w_up[0]], axis=0)
    both, gates_own = lax.optimization_barrier((both, gates_t))
    both, grads = lax.optimization_barrier((both, grads))
    weights_moved = [shifted(both, k) for k in range(1, groups)]

    def in_hbm(value):
        return pltpu.with_memory_space_constraint(value, pltpu.HBM)

    block = tile_of(share, 512)
    steps = share // block
    small_spec = pl.BlockSpec((top, count), lambda c, g: (0, 0))
    scaled = pl.pallas_call(
        functools.partial(dispatch_scaled, experts, cap, groups),
        out_shape=pltpu.HBM((groups * slots, share), jnp.bfloat16),
        grid_spec=pltpu.PrefetchScalarGridSpec(
            num_scalar_prefetch=1,
            grid=(steps,),
            in_specs=[small_spec] * (2 * groups)
            + [pl.BlockSpec((count, block), lambda c, g: (0, g[0] * steps + c))]
            + [pl.BlockSpec((count, block), lambda c, g: (0, c))] * (groups - 1),
            out_specs=pl.BlockSpec((groups * slots, block), lambda c, g: (0, c)),
            scratch_shapes=[
                pltpu.VMEM((groups * slots, groups * count), jnp.bfloat16),
                pltpu.VMEM((groups * slots, LANES), jnp.float32),
            ],
        ),
        compiler_params=params,
        name="dispatch_scaled",
    )(place, in_hbm(routes_t), *routes_all[1:], in_hbm(gates_own), *gates_all[1:], in_hbm(grad_out), *grads)
    scaled_rows = exchanged(scaled)

    sent, pos = pl.pallas_call(
        functools.partial(dispatch_tokens, experts, cap),
        out_shape=(
            pltpu.HBM((slots, width), jnp.bfloat16),
            jax.ShapeDtypeStruct((top, count), jnp.int32),
        ),
        grid_spec=pltpu.PrefetchScalarGridSpec(
            num_scalar_prefetch=1,
            grid=(groups,),
            in_specs=[
                small_spec,
                pl.BlockSpec(
                    (count, share), lambda k, g: (0, lax.rem(g[0] - k + groups, groups))
                ),
            ],
            out_specs=(pl.BlockSpec((slots, share), lambda k, g: (0, k)), small_spec),
            scratch_shapes=[pltpu.VMEM((slots, count), jnp.bfloat16)],
        ),
        compiler_params=params,
        name="dispatch_tokens",
    )(place, in_hbm(routes_t), in_hbm(tokens))
    x_rows = exchanged(sent)

    scaled_rows, weights_moved = lax.optimization_barrier((scaled_rows, weights_moved))
    weights = [w_gate[0], w_up[0], *weights_moved]

    back_own, *rest = pl.pallas_call(
        functools.partial(back_kernel, groups, cap),
        out_shape=[pltpu.HBM((slots, hidden), jnp.float32)]
        + [pltpu.HBM((slots, hidden), jnp.bfloat16)] * (groups - 1)
        + [pltpu.HBM((groups * slots, share), jnp.bfloat16)],
        cost_estimate=pl.CostEstimate(
            flops=BACK_COST_US * 10**9, bytes_accessed=BACK_COST_US * 10**6, transcendentals=0
        ),
        compiler_params=params,
        name="back",
    )(scaled_rows, in_hbm(w_down[0]))
    scaled_all = rest[-1]
    back_parts = [shifted(rest[k - 1], -k) for k in range(1, groups)]

    whole_spec = pl.BlockSpec(memory_space=pltpu.VMEM)
    any_spec = pl.BlockSpec(memory_space=pl.ANY)
    *factors, hidden_own, held, back_kept = pl.pallas_call(
        functools.partial(forward_kernel, groups),
        out_shape=[pltpu.VMEM((slots, hidden), jnp.float32)] * 3
        + [
            pltpu.HBM((slots, hidden), jnp.bfloat16),
            pltpu.VMEM((2 * groups, share, hidden), jnp.bfloat16),
            pltpu.VMEM((slots, hidden), jnp.float32),
        ],
        in_specs=[whole_spec] + [any_spec] * (groups + 2),
        scratch_shapes=[
            pltpu.VMEM((slots, hidden), jnp.float32),
            pltpu.VMEM((slots, hidden), jnp.float32),
            pltpu.SemaphoreType.DMA((hidden // tile_of(hidden, 384), 2 * groups)),
            pltpu.SemaphoreType.DMA((1,)),
        ],
        compiler_params=params,
        name="forward",
    )(x_rows, in_hbm(back_own), *[in_hbm(value) for value in weights])

    pieces = groups * (share // tile_of(share, 512))
    returning = pl.pallas_call(
        functools.partial(backward_kernel, groups),
        out_shape=pltpu.HBM((slots, width + LANES), jnp.bfloat16),
        in_specs=[whole_spec] * (4 + groups),
        out_specs=any_spec,
        scratch_shapes=[
            pltpu.VMEM((slots, hidden), jnp.bfloat16),
            pltpu.VMEM((slots, hidden), jnp.bfloat16),
            pltpu.VMEM((slots, width + LANES), jnp.bfloat16),
            pltpu.SemaphoreType.DMA((pieces + 1,)),
        ],
        compiler_params=params,
        name="backward",
    )(*factors, held, back_kept, *back_parts)
    returned = exchanged(returning)

    hiddens = [hidden_own] + [shifted(hidden_own, k) for k in range(1, groups)]
    grad_down = contract_first(jnp.concatenate(hiddens, axis=0), scaled_all)[None]

    grad_tokens, grad_gates = pl.pallas_call(
        functools.partial(combine_kernel, groups),
        out_shape=(
            jax.ShapeDtypeStruct((count, width), jnp.bfloat16),
            jax.ShapeDtypeStruct((top, count), jnp.float32),
        ),
        in_specs=[pl.BlockSpec(memory_space=pltpu.SMEM)] + [whole_spec] * 3,
        compiler_params=params,
        name="combine",
    )(place, pos, gates_t, returned)
    return (grad_tokens, jnp.transpose(grad_gates), grad_down)


def solution(mesh):
    placed = (
        P(("dp", "expert"), None),
        P(("dp", "expert"), None),
        P(("dp", "expert"), None),
        P(("dp", "expert"), None),
        P("expert", "dp", None),
        P("expert", "dp", None),
        P("expert", None, "dp"),
    )
    return jax.shard_map(
        per_device,
        mesh=mesh,
        in_specs=placed,
        out_specs=(P(("dp", "expert"), None), P(("dp", "expert"), None), P("expert", None, "dp")),
        check_vma=False,
    )
```

```python
import functools

import jax
import jax.numpy as jnp
from jax import lax
from jax.experimental import pallas as pl
from jax.experimental.pallas import tpu as pltpu
from jax.sharding import PartitionSpec as P

LANES = 128
VMEM_BYTES = 24 * 1024 * 1024
BACK_COST_US = 30


def contract_last(left, right):
    return lax.dot_general(
        left, right, (((1,), (1,)), ((), ())), preferred_element_type=jnp.float32
    )


def contract_first(left, right):
    return lax.dot_general(
        left, right, (((0,), (0,)), ((), ())), preferred_element_type=jnp.float32
    )


def tile_of(extent, most):
    return most if extent % most == 0 else extent


def slot_positions(routes, experts, stride, base):
    top, count = routes.shape
    labels = lax.broadcasted_iota(jnp.int32, (experts, count), 0)
    named = [labels == routes[k : k + 1, :] for k in range(top)]
    marks = sum(jnp.where(m, 1.0, 0.0) for m in named)
    earlier = lax.broadcasted_iota(jnp.int32, (count, count), 0) < lax.broadcasted_iota(
        jnp.int32, (count, count), 1
    )
    rank = jnp.dot(
        marks.astype(jnp.bfloat16),
        jnp.where(earlier, 1.0, 0.0).astype(jnp.bfloat16),
        preferred_element_type=jnp.float32,
    )
    slot = rank + (labels * stride + base + 1).astype(jnp.float32)
    return [
        jnp.sum(jnp.where(m, slot, 0.0), axis=0, keepdims=True).astype(jnp.int32) - 1
        for m in named
    ]


def by_half(value, cap, half, paired):
    count, width = value.shape
    if paired:
        value = value.reshape(count // (2 * cap), 2, cap, width)
        own, other = value[:, 0], value[:, 1]
    else:
        value = value.reshape(2, count // (2 * cap), cap, width)
        own, other = value[0], value[1]
    first = jnp.where(half == 0, own, other)
    second = jnp.where(half == 0, other, own)
    return jnp.stack([first, second], axis=0 if paired else 1).reshape(count, width)


def dispatch_tokens(experts, cap, place_ref, *refs):
    routes_refs, tokens_refs, (out_ref, pos_ref, pick_ref) = refs[:2], refs[2:4], refs[4:]
    count = tokens_refs[0].shape[0]

    @pl.when(pl.program_id(0) == 0)
    def _():
        rows = lax.broadcasted_iota(jnp.int32, (pick_ref.shape[0], count), 0)
        for c, ref in enumerate(routes_refs):
            near = ref[...] - place_ref[1] * (experts // 2)
            pos = slot_positions(near, experts // 2, 2 * cap, c * cap)
            pick_ref[:, c * count : (c + 1) * count] = sum(
                jnp.where(rows == p, 1.0, 0.0) for p in pos
            ).astype(jnp.bfloat16)
        for k, p in enumerate(slot_positions(routes_refs[0][...], experts, cap, 0)):
            pos_ref[k : k + 1, :] = p

    values = jnp.concatenate([ref[...] for ref in tokens_refs], axis=0)
    out_ref[...] = jnp.dot(
        pick_ref[...], values, preferred_element_type=jnp.float32
    ).astype(out_ref.dtype)


def dispatch_scaled(experts, cap, groups, place_ref, *refs):
    routes_refs, gate_refs = refs[:groups], refs[groups : 2 * groups]
    grad_refs, (out_ref, pick_ref, scale_ref) = refs[2 * groups : 3 * groups], refs[3 * groups :]
    count = grad_refs[0].shape[0]
    slots = out_ref.shape[0]

    @pl.when(pl.program_id(0) == 0)
    def _():
        rows = lax.broadcasted_iota(jnp.int32, (slots, count), 0)
        total = jnp.zeros((slots, 1), jnp.float32)
        for q in range(groups):
            pos = slot_positions(routes_refs[q][...], experts, groups * cap, q * cap)
            hit = jnp.zeros((slots, count), jnp.float32)
            weight = jnp.zeros((slots, count), jnp.float32)
            for k, p in enumerate(pos):
                here = rows == p
                hit = hit + jnp.where(here, 1.0, 0.0)
                weight = weight + jnp.where(here, gate_refs[q][k : k + 1, :], 0.0)
            pick_ref[:, q * count : (q + 1) * count] = hit.astype(jnp.bfloat16)
            total = total + jnp.sum(weight, axis=1, keepdims=True)
        scale_ref[...] = jnp.broadcast_to(total, scale_ref.shape)

    grads = jnp.concatenate([ref[...] for ref in grad_refs], axis=0)
    rows = jnp.dot(pick_ref[...], grads, preferred_element_type=jnp.float32)
    out_ref[...] = (scale_ref[:, :1] * rows).astype(out_ref.dtype)


def back_kernel(groups, cap, place_ref, rows_ref, down_ref, own_ref, *rest):
    others, all_ref = rest[: groups - 1], rest[groups - 1]
    slots, hidden = own_ref.shape
    count, share = rows_ref.shape
    rows = rows_ref[...].astype(jnp.float32).reshape(count // (groups * cap), groups, cap, share)
    for q in range(groups):
        ordered = by_half(rows[:, q].reshape(slots, share), cap, place_ref[1], False)
        all_ref[q * slots : (q + 1) * slots, :] = ordered.astype(all_ref.dtype)
    step = tile_of(hidden, 256)

    @pl.loop(0, hidden // step)
    def _(j):
        cols = pl.ds(pl.multiple_of(j * step, step), step)
        for q, ref in enumerate((own_ref, *others)):
            part = contract_last(all_ref[q * slots : (q + 1) * slots, :], down_ref[cols, :])
            ref[:, cols] = part.astype(ref.dtype)


def forward_kernel(groups, x_ref, back_ref, *refs):
    (own_gate, own_up), others = refs[:2], refs[2 : groups + 1]
    act_ref, slope_ref, value_ref, hidden_ref, held_ref, kept_ref = refs[groups + 1 : groups + 7]
    gate_sum_ref, up_sum_ref, sems, back_sem = refs[groups + 7 :]
    share, hidden = held_ref.shape[1:]
    step = tile_of(hidden, 384)
    gates = [own_gate, *[ref.at[:share] for ref in others]]
    ups = [own_up, *[ref.at[share:] for ref in others]]
    spans = [slice(at, at + step) for at in range(0, hidden, step)]

    loads = []
    for k in range(groups):
        for ref, i in ((gates[k], k), (ups[k], groups + k)):
            for n, cols in enumerate(spans):
                loads.append(
                    pltpu.make_async_copy(
                        ref.at[:, cols], held_ref.at[i, :, cols], sems.at[n, i]
                    )
                )
    loads.append(pltpu.make_async_copy(back_ref, kept_ref, back_sem.at[0]))
    flying = 3
    for copy in loads[:flying]:
        copy.start()
    place = 0

    def arrived():
        nonlocal place
        loads[place].wait()
        if place + flying < len(loads):
            loads[place + flying].start()
        place += 1

    def against(k, i, cols):
        return jnp.dot(
            x_ref[:, k * share : (k + 1) * share],
            held_ref[i, :, cols],
            preferred_element_type=jnp.float32,
        )

    for k in range(groups):
        for cols in spans:
            arrived()
            part = against(k, k, cols)
            gate_sum_ref[:, cols] = part if k == 0 else gate_sum_ref[:, cols] + part
        for cols in spans:
            arrived()
            pre_up = against(k, groups + k, cols)
            if k > 0:
                pre_up += up_sum_ref[:, cols]
            if k < groups - 1:
                up_sum_ref[:, cols] = pre_up
                continue
            pre_gate = gate_sum_ref[:, cols]
            sig = jax.nn.sigmoid(pre_gate)
            act = pre_gate * sig
            hidden_f = act * pre_up
            act_ref[:, cols] = act
            slope_ref[:, cols] = pre_up * (sig * (1.0 + pre_gate * (1.0 - sig)))
            value_ref[:, cols] = hidden_f
            hidden_ref[:, cols] = hidden_f.astype(hidden_ref.dtype)
    arrived()


def backward_kernel(groups, cap, place_ref, act_ref, slope_ref, value_ref, held_ref, *refs):
    parts, (out_ref, d_gate_ref, d_up_ref, rows_ref, out_sems) = refs[:groups], refs[groups:]
    share = held_ref.shape[1]
    width = groups * share
    block = tile_of(share, 512)
    half = place_ref[1]
    back = sum(part[...].astype(jnp.float32) for part in parts)
    score = jnp.sum(back * value_ref[...], axis=1, keepdims=True)
    d_gate_ref[...] = by_half(back * slope_ref[...], cap, half, True).astype(jnp.bfloat16)
    d_up_ref[...] = by_half(back * act_ref[...], cap, half, True).astype(jnp.bfloat16)
    score = by_half(jnp.broadcast_to(score, (score.shape[0], LANES)), cap, half, True)
    rows_ref[:, width:] = score.astype(rows_ref.dtype)
    outs = []

    def send(cols):
        copy = pltpu.make_async_copy(
            rows_ref.at[:, cols], out_ref.at[:, cols], out_sems.at[len(outs)]
        )
        copy.start()
        outs.append(copy)

    send(slice(width, width + LANES))
    for k in range(groups):
        for at in range(0, share, block):
            cols = slice(k * share + at, k * share + at + block)
            grad = contract_last(d_gate_ref[...], held_ref[k, at : at + block])
            grad += contract_last(d_up_ref[...], held_ref[groups + k, at : at + block])
            rows_ref[:, cols] = grad.astype(rows_ref.dtype)
            send(cols)
    for copy in outs:
        copy.wait()


def combine_kernel(groups, place_ref, pos_ref, gate_ref, rows_ref, tokens_ref, gates_ref):
    top, count = pos_ref.shape
    slots = rows_ref.shape[0]
    width = tokens_ref.shape[1]
    share = width // groups
    places = lax.broadcasted_iota(jnp.int32, (slots, count), 0)
    picks = [
        jnp.where(places == pos_ref[k : k + 1, :], 1.0, 0.0).astype(jnp.bfloat16)
        for k in range(top)
    ]
    both = sum(picks)
    for k in range(groups):
        at = lax.rem(place_ref[0] - k + groups, groups) * share
        tokens_ref[:, pl.ds(pl.multiple_of(at, share), share)] = contract_first(
            both, rows_ref[:, k * share : (k + 1) * share]
        ).astype(tokens_ref.dtype)
    for k in range(top):
        score = contract_first(rows_ref[:, width:], picks[k])
        gates_ref[k : k + 1, :] = score[:1, :] / gate_ref[k : k + 1, :]


def per_device(tokens, routes, gates, grad_out, w_gate, w_up, w_down):
    experts = lax.axis_size("expert")
    groups = lax.axis_size("dp")
    group = lax.axis_index("dp")
    count, width = tokens.shape
    top = routes.shape[1]
    cap = 3 * count * top // (2 * experts)
    slots = experts * cap
    share = width // groups
    hidden = w_gate.shape[2]
    params = pltpu.CompilerParams(vmem_limit_bytes=VMEM_BYTES)
    half = lax.div(lax.axis_index("expert"), experts // 2)
    place = jnp.stack([group, half]).astype(jnp.int32)
    halves = [list(range(experts // 2)), list(range(experts // 2, experts))]

    def shifted(value, by):
        return lax.ppermute(value, "dp", [(i, (i + by) % groups) for i in range(groups)])

    def across(value):
        pairs = [(i, (i + experts // 2) % experts) for i in range(experts)]
        return lax.ppermute(value, "expert", pairs)

    def exchanged(rows, among=None):
        count = experts if among is None else len(among[0])
        split = rows.reshape(count, rows.shape[0] // count, rows.shape[1])
        moved = lax.all_to_all(
            split, "expert", split_axis=0, concat_axis=0, axis_index_groups=among, tiled=True
        )
        return moved.reshape(rows.shape)

    routes_t, gates_t = jnp.transpose(routes), jnp.transpose(gates)
    routes_all = [routes_t] + [shifted(routes_t, k) for k in range(1, groups)]
    gates_all = [gates_t] + [shifted(gates_t, k) for k in range(1, groups)]
    grads = [
        shifted(
            lax.dynamic_slice(grad_out, (0, lax.rem(group + k, groups) * share), (count, share)), k
        )
        for k in range(1, groups)
    ]
    both = jnp.concatenate([w_gate[0], w_up[0]], axis=0)
    both, gates_own = lax.optimization_barrier((both, gates_t))
    both, grads, routes_all, gates_all = lax.optimization_barrier(
        (both, grads, routes_all, gates_all)
    )
    tokens_across, routes_across = across(tokens), across(routes_t)
    weights_moved = [shifted(both, k) for k in range(1, groups)]

    def in_hbm(value):
        return pltpu.with_memory_space_constraint(value, pltpu.HBM)

    block = tile_of(share, 512)
    steps = share // block
    small_spec = pl.BlockSpec((top, count), lambda c, g: (0, 0))
    scaled = pl.pallas_call(
        functools.partial(dispatch_scaled, experts, cap, groups),
        out_shape=pltpu.HBM((groups * slots, share), jnp.bfloat16),
        grid_spec=pltpu.PrefetchScalarGridSpec(
            num_scalar_prefetch=1,
            grid=(steps,),
            in_specs=[small_spec] * (2 * groups)
            + [pl.BlockSpec((count, block), lambda c, g: (0, g[0] * steps + c))]
            + [pl.BlockSpec((count, block), lambda c, g: (0, c))] * (groups - 1),
            out_specs=pl.BlockSpec((groups * slots, block), lambda c, g: (0, c)),
            scratch_shapes=[
                pltpu.VMEM((groups * slots, groups * count), jnp.bfloat16),
                pltpu.VMEM((groups * slots, LANES), jnp.float32),
            ],
        ),
        compiler_params=params,
        name="dispatch_scaled",
    )(place, in_hbm(routes_t), *routes_all[1:], in_hbm(gates_own), *gates_all[1:], in_hbm(grad_out), *grads)
    scaled, tokens_across, routes_across = lax.optimization_barrier(
        (scaled, tokens_across, routes_across)
    )
    scaled_rows = exchanged(scaled)

    sent, pos = pl.pallas_call(
        functools.partial(dispatch_tokens, experts, cap),
        out_shape=(
            pltpu.HBM((slots, width), jnp.bfloat16),
            jax.ShapeDtypeStruct((top, count), jnp.int32),
        ),
        grid_spec=pltpu.PrefetchScalarGridSpec(
            num_scalar_prefetch=1,
            grid=(groups,),
            in_specs=[small_spec] * 2
            + [
                pl.BlockSpec(
                    (count, share), lambda k, g: (0, lax.rem(g[0] - k + groups, groups))
                )
            ]
            * 2,
            out_specs=(pl.BlockSpec((slots, share), lambda k, g: (0, k)), small_spec),
            scratch_shapes=[pltpu.VMEM((slots, 2 * count), jnp.bfloat16)],
        ),
        compiler_params=params,
        name="dispatch_tokens",
    )(place, in_hbm(routes_t), routes_across, in_hbm(tokens), in_hbm(tokens_across))
    x_rows = exchanged(sent, halves)

    scaled_rows, weights_moved = lax.optimization_barrier((scaled_rows, weights_moved))
    weights = [w_gate[0], w_up[0], *weights_moved]

    place_spec = pl.BlockSpec(memory_space=pltpu.SMEM)

    back_own, *rest = pl.pallas_call(
        functools.partial(back_kernel, groups, cap),
        out_shape=[pltpu.HBM((slots, hidden), jnp.float32)]
        + [pltpu.HBM((slots, hidden), jnp.bfloat16)] * (groups - 1)
        + [pltpu.HBM((groups * slots, share), jnp.bfloat16)],
        in_specs=[place_spec, pl.BlockSpec(), pl.BlockSpec()],
        cost_estimate=pl.CostEstimate(
            flops=BACK_COST_US * 10**9, bytes_accessed=BACK_COST_US * 10**6, transcendentals=0
        ),
        compiler_params=params,
        name="back",
    )(place, scaled_rows, in_hbm(w_down[0]))
    scaled_all = rest[-1]
    back_parts = [shifted(rest[k - 1], -k) for k in range(1, groups)]

    whole_spec = pl.BlockSpec(memory_space=pltpu.VMEM)
    any_spec = pl.BlockSpec(memory_space=pl.ANY)
    *factors, hidden_own, held, back_kept = pl.pallas_call(
        functools.partial(forward_kernel, groups),
        out_shape=[pltpu.VMEM((slots, hidden), jnp.float32)] * 3
        + [
            pltpu.HBM((slots, hidden), jnp.bfloat16),
            pltpu.VMEM((2 * groups, share, hidden), jnp.bfloat16),
            pltpu.VMEM((slots, hidden), jnp.float32),
        ],
        in_specs=[whole_spec] + [any_spec] * (groups + 2),
        scratch_shapes=[
            pltpu.VMEM((slots, hidden), jnp.float32),
            pltpu.VMEM((slots, hidden), jnp.float32),
            pltpu.SemaphoreType.DMA((hidden // tile_of(hidden, 384), 2 * groups)),
            pltpu.SemaphoreType.DMA((1,)),
        ],
        compiler_params=params,
        name="forward",
    )(x_rows, in_hbm(back_own), *[in_hbm(value) for value in weights])

    pieces = groups * (share // tile_of(share, 512))
    returning = pl.pallas_call(
        functools.partial(backward_kernel, groups, cap),
        out_shape=pltpu.HBM((slots, width + LANES), jnp.bfloat16),
        in_specs=[place_spec] + [whole_spec] * (4 + groups),
        out_specs=any_spec,
        scratch_shapes=[
            pltpu.VMEM((slots, hidden), jnp.bfloat16),
            pltpu.VMEM((slots, hidden), jnp.bfloat16),
            pltpu.VMEM((slots, width + LANES), jnp.bfloat16),
            pltpu.SemaphoreType.DMA((pieces + 1,)),
        ],
        compiler_params=params,
        name="backward",
    )(place, *factors, held, back_kept, *back_parts)
    returned = exchanged(returning)

    hiddens = [hidden_own] + [shifted(hidden_own, k) for k in range(1, groups)]
    grad_down = contract_first(jnp.concatenate(hiddens, axis=0), scaled_all)[None]

    grad_tokens, grad_gates = pl.pallas_call(
        functools.partial(combine_kernel, groups),
        out_shape=(
            jax.ShapeDtypeStruct((count, width), jnp.bfloat16),
            jax.ShapeDtypeStruct((top, count), jnp.float32),
        ),
        in_specs=[pl.BlockSpec(memory_space=pltpu.SMEM)] + [whole_spec] * 3,
        compiler_params=params,
        name="combine",
    )(place, pos, gates_t, returned)
    return (grad_tokens, jnp.transpose(grad_gates), grad_down)


def solution(mesh):
    placed = (
        P(("dp", "expert"), None),
        P(("dp", "expert"), None),
        P(("dp", "expert"), None),
        P(("dp", "expert"), None),
        P("expert", "dp", None),
        P("expert", "dp", None),
        P("expert", None, "dp"),
    )
    return jax.shard_map(
        per_device,
        mesh=mesh,
        in_specs=placed,
        out_specs=(P(("dp", "expert"), None), P(("dp", "expert"), None), P("expert", None, "dp")),
        check_vma=False,
    )
```

```python
import functools

import jax
import jax.numpy as jnp
from jax import lax
from jax.experimental import pallas as pl
from jax.experimental.pallas import tpu as pltpu
from jax.sharding import PartitionSpec as P

LANES = 128
VMEM_BYTES = 24 * 1024 * 1024
TAIL = 16
BACK_COST_US = 30
TOKENS_COST_US = 30


def contract_last(left, right):
    return lax.dot_general(
        left, right, (((1,), (1,)), ((), ())), preferred_element_type=jnp.float32
    )


def contract_first(left, right):
    return lax.dot_general(
        left, right, (((0,), (0,)), ((), ())), preferred_element_type=jnp.float32
    )


def tile_of(extent, most):
    return most if extent % most == 0 else extent


def slot_positions(routes, experts, stride, base):
    top, count = routes.shape
    labels = lax.broadcasted_iota(jnp.int32, (experts, count), 0)
    named = [labels == routes[k : k + 1, :] for k in range(top)]
    marks = sum(jnp.where(m, 1.0, 0.0) for m in named)
    earlier = lax.broadcasted_iota(jnp.int32, (count, count), 0) < lax.broadcasted_iota(
        jnp.int32, (count, count), 1
    )
    rank = jnp.dot(
        marks.astype(jnp.bfloat16),
        jnp.where(earlier, 1.0, 0.0).astype(jnp.bfloat16),
        preferred_element_type=jnp.float32,
    )
    slot = rank + (labels * stride + base + 1).astype(jnp.float32)
    return [
        jnp.sum(jnp.where(m, slot, 0.0), axis=0, keepdims=True).astype(jnp.int32) - 1
        for m in named
    ]


def by_half(value, cap, half, paired):
    count, width = value.shape
    if paired:
        value = value.reshape(count // (2 * cap), 2, cap, width)
        own, other = value[:, 0], value[:, 1]
    else:
        value = value.reshape(2, count // (2 * cap), cap, width)
        own, other = value[0], value[1]
    first = jnp.where(half == 0, own, other)
    second = jnp.where(half == 0, other, own)
    return jnp.stack([first, second], axis=0 if paired else 1).reshape(count, width)


def dispatch_tokens(experts, cap, place_ref, *refs):
    routes_refs, tokens_refs, (out_ref, pos_ref, pick_ref) = refs[:2], refs[2:4], refs[4:]
    count = tokens_refs[0].shape[0]
    top = pos_ref.shape[0]

    @pl.when(pl.program_id(0) == 0)
    def _():
        rows = lax.broadcasted_iota(jnp.int32, (pick_ref.shape[0], count), 0)
        for c, ref in enumerate(routes_refs):
            routes = ref[...].astype(jnp.float32).astype(jnp.int32)[:top, :count]
            near = routes - place_ref[1] * (experts // 2)
            pos = slot_positions(near, experts // 2, 2 * cap, c * cap)
            pick_ref[:, c * count : (c + 1) * count] = sum(
                jnp.where(rows == p, 1.0, 0.0) for p in pos
            ).astype(jnp.bfloat16)
        for k, p in enumerate(slot_positions(routes_refs[0][...], experts, cap, 0)):
            pos_ref[k : k + 1, :] = p

    values = jnp.concatenate([ref[...] for ref in tokens_refs], axis=0)
    out_ref[...] = jnp.dot(
        pick_ref[...], values, preferred_element_type=jnp.float32
    ).astype(out_ref.dtype)


def dispatch_scaled(experts, cap, groups, place_ref, *refs):
    routes_refs, gate_refs = refs[:groups], refs[groups : 2 * groups]
    grad_refs, (out_ref, pick_ref, scale_ref) = refs[2 * groups : 3 * groups], refs[3 * groups :]
    count = grad_refs[0].shape[0]
    slots = out_ref.shape[0]

    @pl.when(pl.program_id(0) == 0)
    def _():
        rows = lax.broadcasted_iota(jnp.int32, (slots, count), 0)
        total = jnp.zeros((slots, 1), jnp.float32)
        for q in range(groups):
            pos = slot_positions(routes_refs[q][...], experts, groups * cap, q * cap)
            hit = jnp.zeros((slots, count), jnp.float32)
            weight = jnp.zeros((slots, count), jnp.float32)
            for k, p in enumerate(pos):
                here = rows == p
                hit = hit + jnp.where(here, 1.0, 0.0)
                weight = weight + jnp.where(here, gate_refs[q][k : k + 1, :], 0.0)
            pick_ref[:, q * count : (q + 1) * count] = hit.astype(jnp.bfloat16)
            total = total + jnp.sum(weight, axis=1, keepdims=True)
        scale_ref[...] = jnp.broadcast_to(total, scale_ref.shape)

    grads = jnp.concatenate([ref[...] for ref in grad_refs], axis=0)
    rows = jnp.dot(pick_ref[...], grads, preferred_element_type=jnp.float32)
    out_ref[...] = (scale_ref[:, :1] * rows).astype(out_ref.dtype)


def back_kernel(groups, cap, place_ref, rows_ref, down_ref, own_ref, *rest):
    others, all_ref = rest[: groups - 1], rest[groups - 1]
    slots, hidden = own_ref.shape
    count, share = rows_ref.shape
    rows = rows_ref[...].astype(jnp.float32).reshape(count // (groups * cap), groups, cap, share)
    for q in range(groups):
        ordered = by_half(rows[:, q].reshape(slots, share), cap, place_ref[1], False)
        all_ref[q * slots : (q + 1) * slots, :] = ordered.astype(all_ref.dtype)
    step = tile_of(hidden, 256)

    @pl.loop(0, hidden // step)
    def _(j):
        cols = pl.ds(pl.multiple_of(j * step, step), step)
        for q, ref in enumerate((own_ref, *others)):
            part = contract_last(all_ref[q * slots : (q + 1) * slots, :], down_ref[cols, :])
            ref[:, cols] = part.astype(ref.dtype)


def forward_kernel(groups, x_ref, back_ref, *refs):
    (own_gate, own_up), others = refs[:2], refs[2 : groups + 1]
    act_ref, slope_ref, value_ref, hidden_ref, held_ref, kept_ref = refs[groups + 1 : groups + 7]
    gate_sum_ref, up_sum_ref, sems, back_sem = refs[groups + 7 :]
    share, hidden = held_ref.shape[1:]
    step = tile_of(hidden, 384)
    gates = [own_gate, *[ref.at[:share] for ref in others]]
    ups = [own_up, *[ref.at[share:] for ref in others]]
    spans = [slice(at, at + step) for at in range(0, hidden, step)]

    loads = []
    for k in range(groups):
        for ref, i in ((gates[k], k), (ups[k], groups + k)):
            for n, cols in enumerate(spans):
                loads.append(
                    pltpu.make_async_copy(
                        ref.at[:, cols], held_ref.at[i, :, cols], sems.at[n, i]
                    )
                )
    loads.append(pltpu.make_async_copy(back_ref, kept_ref, back_sem.at[0]))
    flying = 3
    for copy in loads[:flying]:
        copy.start()
    place = 0

    def arrived():
        nonlocal place
        loads[place].wait()
        if place + flying < len(loads):
            loads[place + flying].start()
        place += 1

    def against(k, i, cols):
        return jnp.dot(
            x_ref[:, k * share : (k + 1) * share],
            held_ref[i, :, cols],
            preferred_element_type=jnp.float32,
        )

    for k in range(groups):
        for cols in spans:
            arrived()
            part = against(k, k, cols)
            gate_sum_ref[:, cols] = part if k == 0 else gate_sum_ref[:, cols] + part
        for cols in spans:
            arrived()
            pre_up = against(k, groups + k, cols)
            if k > 0:
                pre_up += up_sum_ref[:, cols]
            if k < groups - 1:
                up_sum_ref[:, cols] = pre_up
                continue
            pre_gate = gate_sum_ref[:, cols]
            sig = jax.nn.sigmoid(pre_gate)
            act = pre_gate * sig
            hidden_f = act * pre_up
            act_ref[:, cols] = act
            slope_ref[:, cols] = pre_up * (sig * (1.0 + pre_gate * (1.0 - sig)))
            value_ref[:, cols] = hidden_f
            hidden_ref[:, cols] = hidden_f.astype(hidden_ref.dtype)
    arrived()


def backward_kernel(groups, cap, place_ref, act_ref, slope_ref, value_ref, held_ref, *refs):
    parts, (out_ref, d_gate_ref, d_up_ref, rows_ref, out_sems) = refs[:groups], refs[groups:]
    share = held_ref.shape[1]
    width = groups * share
    block = tile_of(share, 512)
    half = place_ref[1]
    back = sum(part[...].astype(jnp.float32) for part in parts)
    score = jnp.sum(back * value_ref[...], axis=1, keepdims=True)
    d_gate_ref[...] = by_half(back * slope_ref[...], cap, half, True).astype(jnp.bfloat16)
    d_up_ref[...] = by_half(back * act_ref[...], cap, half, True).astype(jnp.bfloat16)
    score = by_half(jnp.broadcast_to(score, (score.shape[0], LANES)), cap, half, True)
    rows_ref[:, width:] = score.astype(rows_ref.dtype)
    outs = []

    def send(cols):
        copy = pltpu.make_async_copy(
            rows_ref.at[:, cols], out_ref.at[:, cols], out_sems.at[len(outs)]
        )
        copy.start()
        outs.append(copy)

    send(slice(width, width + LANES))
    for k in range(groups):
        for at in range(0, share, block):
            cols = slice(k * share + at, k * share + at + block)
            grad = contract_last(d_gate_ref[...], held_ref[k, at : at + block])
            grad += contract_last(d_up_ref[...], held_ref[groups + k, at : at + block])
            rows_ref[:, cols] = grad.astype(rows_ref.dtype)
            send(cols)
    for copy in outs:
        copy.wait()


def combine_kernel(groups, place_ref, pos_ref, gate_ref, rows_ref, tokens_ref, gates_ref):
    top, count = pos_ref.shape
    slots = rows_ref.shape[0]
    width = tokens_ref.shape[1]
    share = width // groups
    places = lax.broadcasted_iota(jnp.int32, (slots, count), 0)
    picks = [
        jnp.where(places == pos_ref[k : k + 1, :], 1.0, 0.0).astype(jnp.bfloat16)
        for k in range(top)
    ]
    both = sum(picks)
    for k in range(groups):
        at = lax.rem(place_ref[0] - k + groups, groups) * share
        tokens_ref[:, pl.ds(pl.multiple_of(at, share), share)] = contract_first(
            both, rows_ref[:, k * share : (k + 1) * share]
        ).astype(tokens_ref.dtype)
    for k in range(top):
        score = contract_first(rows_ref[:, width:], picks[k])
        gates_ref[k : k + 1, :] = score[:1, :] / gate_ref[k : k + 1, :]


def per_device(tokens, routes, gates, grad_out, w_gate, w_up, w_down):
    experts = lax.axis_size("expert")
    groups = lax.axis_size("dp")
    group = lax.axis_index("dp")
    count, width = tokens.shape
    top = routes.shape[1]
    cap = 3 * count * top // (2 * experts)
    slots = experts * cap
    share = width // groups
    hidden = w_gate.shape[2]
    params = pltpu.CompilerParams(vmem_limit_bytes=VMEM_BYTES)
    half = lax.div(lax.axis_index("expert"), experts // 2)
    place = jnp.stack([group, half]).astype(jnp.int32)
    halves = [list(range(experts // 2)), list(range(experts // 2, experts))]

    def shifted(value, by):
        return lax.ppermute(value, "dp", [(i, (i + by) % groups) for i in range(groups)])

    def across(value):
        pairs = [(i, (i + experts // 2) % experts) for i in range(experts)]
        return lax.ppermute(value, "expert", pairs)

    def exchanged(rows, among=None):
        count = experts if among is None else len(among[0])
        split = rows.reshape(count, rows.shape[0] // count, rows.shape[1])
        moved = lax.all_to_all(
            split, "expert", split_axis=0, concat_axis=0, axis_index_groups=among, tiled=True
        )
        return moved.reshape(rows.shape)

    routes_t, gates_t = jnp.transpose(routes), jnp.transpose(gates)
    routes_all = [routes_t] + [shifted(routes_t, k) for k in range(1, groups)]
    gates_all = [gates_t] + [shifted(gates_t, k) for k in range(1, groups)]
    grads = [
        shifted(
            lax.dynamic_slice(grad_out, (0, lax.rem(group + k, groups) * share), (count, share)), k
        )
        for k in range(1, groups)
    ]
    both = jnp.concatenate([w_gate[0], w_up[0]], axis=0)
    both, gates_own = lax.optimization_barrier((both, gates_t))
    both, grads, routes_all, gates_all = lax.optimization_barrier(
        (both, grads, routes_all, gates_all)
    )
    tail = jnp.pad(routes_t.astype(tokens.dtype), ((0, TAIL - top), (0, width - count)))
    tokens_across = across(jnp.concatenate([tokens, tail], axis=0))
    weights_moved = [shifted(both, k) for k in range(1, groups)]

    def in_hbm(value):
        return pltpu.with_memory_space_constraint(value, pltpu.HBM)

    block = tile_of(share, 512)
    steps = share // block
    small_spec = pl.BlockSpec((top, count), lambda c, g: (0, 0))
    scaled = pl.pallas_call(
        functools.partial(dispatch_scaled, experts, cap, groups),
        out_shape=pltpu.HBM((groups * slots, share), jnp.bfloat16),
        grid_spec=pltpu.PrefetchScalarGridSpec(
            num_scalar_prefetch=1,
            grid=(steps,),
            in_specs=[small_spec] * (2 * groups)
            + [pl.BlockSpec((count, block), lambda c, g: (0, g[0] * steps + c))]
            + [pl.BlockSpec((count, block), lambda c, g: (0, c))] * (groups - 1),
            out_specs=pl.BlockSpec((groups * slots, block), lambda c, g: (0, c)),
            scratch_shapes=[
                pltpu.VMEM((groups * slots, groups * count), jnp.bfloat16),
                pltpu.VMEM((groups * slots, LANES), jnp.float32),
            ],
        ),
        compiler_params=params,
        name="dispatch_scaled",
    )(place, in_hbm(routes_t), *routes_all[1:], in_hbm(gates_own), *gates_all[1:], in_hbm(grad_out), *grads)
    scaled_rows = exchanged(scaled)

    sent, pos = pl.pallas_call(
        functools.partial(dispatch_tokens, experts, cap),
        out_shape=(
            pltpu.HBM((slots, width), jnp.bfloat16),
            jax.ShapeDtypeStruct((top, count), jnp.int32),
        ),
        grid_spec=pltpu.PrefetchScalarGridSpec(
            num_scalar_prefetch=1,
            grid=(groups,),
            in_specs=[small_spec, pl.BlockSpec((TAIL, LANES), lambda k, g: (count // TAIL, 0))]
            + [
                pl.BlockSpec(
                    (count, share), lambda k, g: (0, lax.rem(g[0] - k + groups, groups))
                )
            ]
            * 2,
            out_specs=(pl.BlockSpec((slots, share), lambda k, g: (0, k)), small_spec),
            scratch_shapes=[pltpu.VMEM((slots, 2 * count), jnp.bfloat16)],
        ),
        cost_estimate=pl.CostEstimate(
            flops=TOKENS_COST_US * 10**9, bytes_accessed=TOKENS_COST_US * 10**6, transcendentals=0
        ),
        compiler_params=params,
        name="dispatch_tokens",
    )(place, in_hbm(routes_t), tokens_across, in_hbm(tokens), in_hbm(tokens_across))
    x_rows = exchanged(sent, halves)

    scaled_rows, weights_moved = lax.optimization_barrier((scaled_rows, weights_moved))
    weights = [w_gate[0], w_up[0], *weights_moved]

    place_spec = pl.BlockSpec(memory_space=pltpu.SMEM)

    back_own, *rest = pl.pallas_call(
        functools.partial(back_kernel, groups, cap),
        out_shape=[pltpu.HBM((slots, hidden), jnp.float32)]
        + [pltpu.HBM((slots, hidden), jnp.bfloat16)] * (groups - 1)
        + [pltpu.HBM((groups * slots, share), jnp.bfloat16)],
        in_specs=[place_spec, pl.BlockSpec(), pl.BlockSpec()],
        cost_estimate=pl.CostEstimate(
            flops=BACK_COST_US * 10**9, bytes_accessed=BACK_COST_US * 10**6, transcendentals=0
        ),
        compiler_params=params,
        name="back",
    )(place, scaled_rows, in_hbm(w_down[0]))
    scaled_all = rest[-1]
    back_parts = [shifted(rest[k - 1], -k) for k in range(1, groups)]

    whole_spec = pl.BlockSpec(memory_space=pltpu.VMEM)
    any_spec = pl.BlockSpec(memory_space=pl.ANY)
    *factors, hidden_own, held, back_kept = pl.pallas_call(
        functools.partial(forward_kernel, groups),
        out_shape=[pltpu.VMEM((slots, hidden), jnp.float32)] * 3
        + [
            pltpu.HBM((slots, hidden), jnp.bfloat16),
            pltpu.VMEM((2 * groups, share, hidden), jnp.bfloat16),
            pltpu.VMEM((slots, hidden), jnp.float32),
        ],
        in_specs=[whole_spec] + [any_spec] * (groups + 2),
        scratch_shapes=[
            pltpu.VMEM((slots, hidden), jnp.float32),
            pltpu.VMEM((slots, hidden), jnp.float32),
            pltpu.SemaphoreType.DMA((hidden // tile_of(hidden, 384), 2 * groups)),
            pltpu.SemaphoreType.DMA((1,)),
        ],
        compiler_params=params,
        name="forward",
    )(x_rows, in_hbm(back_own), *[in_hbm(value) for value in weights])

    pieces = groups * (share // tile_of(share, 512))
    returning = pl.pallas_call(
        functools.partial(backward_kernel, groups, cap),
        out_shape=pltpu.HBM((slots, width + LANES), jnp.bfloat16),
        in_specs=[place_spec] + [whole_spec] * (4 + groups),
        out_specs=any_spec,
        scratch_shapes=[
            pltpu.VMEM((slots, hidden), jnp.bfloat16),
            pltpu.VMEM((slots, hidden), jnp.bfloat16),
            pltpu.VMEM((slots, width + LANES), jnp.bfloat16),
            pltpu.SemaphoreType.DMA((pieces + 1,)),
        ],
        compiler_params=params,
        name="backward",
    )(place, *factors, held, back_kept, *back_parts)
    returned = exchanged(returning)

    hiddens = [hidden_own] + [shifted(hidden_own, k) for k in range(1, groups)]
    grad_down = contract_first(jnp.concatenate(hiddens, axis=0), scaled_all)[None]

    grad_tokens, grad_gates = pl.pallas_call(
        functools.partial(combine_kernel, groups),
        out_shape=(
            jax.ShapeDtypeStruct((count, width), jnp.bfloat16),
            jax.ShapeDtypeStruct((top, count), jnp.float32),
        ),
        in_specs=[pl.BlockSpec(memory_space=pltpu.SMEM)] + [whole_spec] * 3,
        compiler_params=params,
        name="combine",
    )(place, pos, gates_t, returned)
    return (grad_tokens, jnp.transpose(grad_gates), grad_down)


def solution(mesh):
    placed = (
        P(("dp", "expert"), None),
        P(("dp", "expert"), None),
        P(("dp", "expert"), None),
        P(("dp", "expert"), None),
        P("expert", "dp", None),
        P("expert", "dp", None),
        P("expert", None, "dp"),
    )
    return jax.shard_map(
        per_device,
        mesh=mesh,
        in_specs=placed,
        out_specs=(P(("dp", "expert"), None), P(("dp", "expert"), None), P("expert", None, "dp")),
        check_vma=False,
    )
```

```python
import functools

import jax
import jax.numpy as jnp
from jax import lax
from jax.experimental import pallas as pl
from jax.experimental.pallas import tpu as pltpu
from jax.sharding import PartitionSpec as P

LANES = 128
VMEM_BYTES = 24 * 1024 * 1024
TAIL = 16
READY_COST_US = 30
TOKENS_COST_US = 30


def contract_last(left, right):
    return lax.dot_general(
        left, right, (((1,), (1,)), ((), ())), preferred_element_type=jnp.float32
    )


def contract_first(left, right):
    return lax.dot_general(
        left, right, (((0,), (0,)), ((), ())), preferred_element_type=jnp.float32
    )


def tile_of(extent, most):
    return most if extent % most == 0 else extent


def slot_positions(routes, experts, stride, base):
    top, count = routes.shape
    labels = lax.broadcasted_iota(jnp.int32, (experts, count), 0)
    named = [labels == routes[k : k + 1, :] for k in range(top)]
    marks = sum(jnp.where(m, 1.0, 0.0) for m in named)
    earlier = lax.broadcasted_iota(jnp.int32, (count, count), 0) < lax.broadcasted_iota(
        jnp.int32, (count, count), 1
    )
    rank = jnp.dot(
        marks.astype(jnp.bfloat16),
        jnp.where(earlier, 1.0, 0.0).astype(jnp.bfloat16),
        preferred_element_type=jnp.float32,
    )
    slot = rank + (labels * stride + base + 1).astype(jnp.float32)
    return [
        jnp.sum(jnp.where(m, slot, 0.0), axis=0, keepdims=True).astype(jnp.int32) - 1
        for m in named
    ]


def by_half(value, cap, half, paired):
    count, width = value.shape
    if paired:
        value = value.reshape(count // (2 * cap), 2, cap, width)
        own, other = value[:, 0], value[:, 1]
    else:
        value = value.reshape(2, count // (2 * cap), cap, width)
        own, other = value[0], value[1]
    first = jnp.where(half == 0, own, other)
    second = jnp.where(half == 0, other, own)
    return jnp.stack([first, second], axis=0 if paired else 1).reshape(count, width)


def dispatch_tokens(experts, cap, place_ref, *refs):
    routes_refs, tokens_refs, (out_ref, pos_ref, pick_ref) = refs[:2], refs[2:4], refs[4:]
    count = tokens_refs[0].shape[0]
    top = pos_ref.shape[0]

    @pl.when(pl.program_id(0) == 0)
    def _():
        rows = lax.broadcasted_iota(jnp.int32, (pick_ref.shape[0], count), 0)
        for c, ref in enumerate(routes_refs):
            routes = ref[...].astype(jnp.float32).astype(jnp.int32)[:top, :count]
            near = routes - place_ref[1] * (experts // 2)
            pos = slot_positions(near, experts // 2, 2 * cap, c * cap)
            pick_ref[:, c * count : (c + 1) * count] = sum(
                jnp.where(rows == p, 1.0, 0.0) for p in pos
            ).astype(jnp.bfloat16)
        for k, p in enumerate(slot_positions(routes_refs[0][...], experts, cap, 0)):
            pos_ref[k : k + 1, :] = p

    values = jnp.concatenate([ref[...] for ref in tokens_refs], axis=0)
    out_ref[...] = jnp.dot(
        pick_ref[...], values, preferred_element_type=jnp.float32
    ).astype(out_ref.dtype)


def pick_scaled(experts, cap, groups, *refs):
    routes_refs, gate_refs = refs[:groups], refs[groups : 2 * groups]
    pick_ref, scale_ref = refs[2 * groups :]
    slots, count = pick_ref.shape[0], routes_refs[0].shape[1]
    rows = lax.broadcasted_iota(jnp.int32, (slots, count), 0)
    total = jnp.zeros((slots, 1), jnp.float32)
    for q in range(groups):
        pos = slot_positions(routes_refs[q][...], experts, groups * cap, q * cap)
        hit = jnp.zeros((slots, count), jnp.float32)
        weight = jnp.zeros((slots, count), jnp.float32)
        for k, p in enumerate(pos):
            here = rows == p
            hit = hit + jnp.where(here, 1.0, 0.0)
            weight = weight + jnp.where(here, gate_refs[q][k : k + 1, :], 0.0)
        pick_ref[:, q * count : (q + 1) * count] = hit.astype(jnp.bfloat16)
        total = total + jnp.sum(weight, axis=1, keepdims=True)
    scale_ref[...] = jnp.broadcast_to(total, scale_ref.shape)


def dispatch_scaled(place_ref, pick_ref, scale_ref, *refs):
    grad_refs, out_ref = refs[:-1], refs[-1]
    grads = jnp.concatenate([ref[...] for ref in grad_refs], axis=0)
    rows = jnp.dot(pick_ref[...], grads, preferred_element_type=jnp.float32)
    out_ref[...] = (scale_ref[:, :1] * rows).astype(out_ref.dtype)


def ready_kernel(*refs):
    del refs


def back_kernel(groups, cap, place_ref, rows_ref, down_ref, own_ref, *rest):
    others, all_ref = rest[: groups - 1], rest[groups - 1]
    slots, hidden = own_ref.shape
    count, share = rows_ref.shape
    rows = rows_ref[...].astype(jnp.float32).reshape(count // (groups * cap), groups, cap, share)
    for q in range(groups):
        ordered = by_half(rows[:, q].reshape(slots, share), cap, place_ref[1], False)
        all_ref[q * slots : (q + 1) * slots, :] = ordered.astype(all_ref.dtype)
    step = tile_of(hidden, 256)

    @pl.loop(0, hidden // step)
    def _(j):
        cols = pl.ds(pl.multiple_of(j * step, step), step)
        for q, ref in enumerate((own_ref, *others)):
            part = contract_last(all_ref[q * slots : (q + 1) * slots, :], down_ref[cols, :])
            ref[:, cols] = part.astype(ref.dtype)


def forward_kernel(groups, x_ref, back_ref, *refs):
    (own_gate, own_up), others = refs[:2], refs[2 : groups + 1]
    act_ref, slope_ref, value_ref, hidden_ref, held_ref, kept_ref = refs[groups + 1 : groups + 7]
    gate_sum_ref, up_sum_ref, sems, back_sem = refs[groups + 7 :]
    share, hidden = held_ref.shape[1:]
    step = tile_of(hidden, 256)
    gates = [own_gate, *[ref.at[:share] for ref in others]]
    ups = [own_up, *[ref.at[share:] for ref in others]]
    spans = [slice(at, at + step) for at in range(0, hidden, step)]

    uses = [(k, cols, i) for k in range(groups) for cols in spans for i in (k, groups + k)]
    sources = gates + ups
    loads = [
        pltpu.make_async_copy(
            sources[i].at[:, cols], held_ref.at[i, :, cols], sems.at[cols.start // step, i]
        )
        for _, cols, i in uses
    ]
    loads.append(pltpu.make_async_copy(back_ref, kept_ref, back_sem.at[0]))
    flying = 3
    for copy in loads[:flying]:
        copy.start()

    def finish(cols):
        pre_gate, pre_up = gate_sum_ref[:, cols], up_sum_ref[:, cols]
        sig = jax.nn.sigmoid(pre_gate)
        act = pre_gate * sig
        hidden_f = act * pre_up
        act_ref[:, cols] = act
        slope_ref[:, cols] = pre_up * (sig * (1.0 + pre_gate * (1.0 - sig)))
        value_ref[:, cols] = hidden_f
        hidden_ref[:, cols] = hidden_f.astype(hidden_ref.dtype)

    complete = None
    for n, (k, cols, i) in enumerate(uses):
        loads[n].wait()
        if n + flying < len(loads):
            loads[n + flying].start()
        part = jnp.dot(
            x_ref[:, k * share : (k + 1) * share],
            held_ref[i, :, cols],
            preferred_element_type=jnp.float32,
        )
        sum_ref = gate_sum_ref if i < groups else up_sum_ref
        if complete is not None:
            finish(complete)
            complete = None
        sum_ref[:, cols] = part if k == 0 else sum_ref[:, cols] + part
        if k == groups - 1 and i >= groups:
            complete = cols
    finish(complete)
    loads[-1].wait()


def backward_kernel(groups, cap, place_ref, act_ref, slope_ref, value_ref, held_ref, *refs):
    parts, (out_ref, d_gate_ref, d_up_ref, rows_ref, out_sems) = refs[:groups], refs[groups:]
    share = held_ref.shape[1]
    width = groups * share
    block = tile_of(share, 512)
    half = place_ref[1]
    back = sum(part[...].astype(jnp.float32) for part in parts)
    score = jnp.sum(back * value_ref[...], axis=1, keepdims=True)
    d_gate_ref[...] = by_half(back * slope_ref[...], cap, half, True).astype(jnp.bfloat16)
    d_up_ref[...] = by_half(back * act_ref[...], cap, half, True).astype(jnp.bfloat16)
    score = by_half(jnp.broadcast_to(score, (score.shape[0], LANES)), cap, half, True)
    rows_ref[:, width:] = score.astype(rows_ref.dtype)
    outs = []

    def send(cols):
        copy = pltpu.make_async_copy(
            rows_ref.at[:, cols], out_ref.at[:, cols], out_sems.at[len(outs)]
        )
        copy.start()
        outs.append(copy)

    send(slice(width, width + LANES))
    for k in range(groups):
        for at in range(0, share, block):
            cols = slice(k * share + at, k * share + at + block)
            grad = contract_last(d_gate_ref[...], held_ref[k, at : at + block])
            grad += contract_last(d_up_ref[...], held_ref[groups + k, at : at + block])
            rows_ref[:, cols] = grad.astype(rows_ref.dtype)
            send(cols)
    for copy in outs:
        copy.wait()


def combine_kernel(groups, place_ref, pos_ref, gate_ref, rows_ref, tokens_ref, gates_ref):
    top, count = pos_ref.shape
    slots = rows_ref.shape[0]
    width = tokens_ref.shape[1]
    share = width // groups
    places = lax.broadcasted_iota(jnp.int32, (slots, count), 0)
    picks = [
        jnp.where(places == pos_ref[k : k + 1, :], 1.0, 0.0).astype(jnp.bfloat16)
        for k in range(top)
    ]
    both = sum(picks)
    for k in range(groups):
        at = lax.rem(place_ref[0] - k + groups, groups) * share
        tokens_ref[:, pl.ds(pl.multiple_of(at, share), share)] = contract_first(
            both, rows_ref[:, k * share : (k + 1) * share]
        ).astype(tokens_ref.dtype)
    for k in range(top):
        score = contract_first(rows_ref[:, width:], picks[k])
        gates_ref[k : k + 1, :] = score[:1, :] / gate_ref[k : k + 1, :]


def per_device(tokens, routes, gates, grad_out, w_gate, w_up, w_down):
    experts = lax.axis_size("expert")
    groups = lax.axis_size("dp")
    group = lax.axis_index("dp")
    count, width = tokens.shape
    top = routes.shape[1]
    cap = 3 * count * top // (2 * experts)
    slots = experts * cap
    share = width // groups
    hidden = w_gate.shape[2]
    params = pltpu.CompilerParams(vmem_limit_bytes=VMEM_BYTES)
    half = lax.div(lax.axis_index("expert"), experts // 2)
    place = jnp.stack([group, half]).astype(jnp.int32)
    halves = [list(range(experts // 2)), list(range(experts // 2, experts))]

    def shifted(value, by):
        return lax.ppermute(value, "dp", [(i, (i + by) % groups) for i in range(groups)])

    def across(value):
        pairs = [(i, (i + experts // 2) % experts) for i in range(experts)]
        return lax.ppermute(value, "expert", pairs)

    def exchanged(rows, among=None):
        count = experts if among is None else len(among[0])
        split = rows.reshape(count, rows.shape[0] // count, rows.shape[1])
        moved = lax.all_to_all(
            split, "expert", split_axis=0, concat_axis=0, axis_index_groups=among, tiled=True
        )
        return moved.reshape(rows.shape)

    routes_t, gates_t = jnp.transpose(routes), jnp.transpose(gates)
    routes_all = [routes_t] + [shifted(routes_t, k) for k in range(1, groups)]
    gates_all = [gates_t] + [shifted(gates_t, k) for k in range(1, groups)]
    grads = [
        shifted(
            lax.dynamic_slice(grad_out, (0, lax.rem(group + k, groups) * share), (count, share)), k
        )
        for k in range(1, groups)
    ]
    both = jnp.concatenate([w_gate[0], w_up[0]], axis=0)
    both, gates_own = lax.optimization_barrier((both, gates_t))
    both, grads, routes_all, gates_all = lax.optimization_barrier(
        (both, grads, routes_all, gates_all)
    )
    tail = jnp.pad(routes_t.astype(tokens.dtype), ((0, TAIL - top), (0, width - count)))
    tokens_across = across(jnp.concatenate([tokens, tail], axis=0))
    weights_moved = [shifted(both, k) for k in range(1, groups)]

    def in_hbm(value):
        return pltpu.with_memory_space_constraint(value, pltpu.HBM)

    block = tile_of(share, 512)
    steps = share // block
    small_spec = pl.BlockSpec((top, count), lambda c, g: (0, 0))
    picks = pl.pallas_call(
        functools.partial(pick_scaled, experts, cap, groups),
        out_shape=(
            pltpu.VMEM((groups * slots, groups * count), jnp.bfloat16),
            pltpu.VMEM((groups * slots, LANES), jnp.float32),
        ),
        compiler_params=params,
        name="pick_scaled",
    )(in_hbm(routes_t), *routes_all[1:], in_hbm(gates_own), *gates_all[1:])
    scaled = pl.pallas_call(
        dispatch_scaled,
        out_shape=pltpu.HBM((groups * slots, share), jnp.bfloat16),
        grid_spec=pltpu.PrefetchScalarGridSpec(
            num_scalar_prefetch=1,
            grid=(steps,),
            in_specs=[pl.BlockSpec(memory_space=pltpu.VMEM)] * 2
            + [pl.BlockSpec((count, block), lambda c, g: (0, g[0] * steps + c))]
            + [pl.BlockSpec((count, block), lambda c, g: (0, c))] * (groups - 1),
            out_specs=pl.BlockSpec((groups * slots, block), lambda c, g: (0, c)),
        ),
        compiler_params=params,
        name="dispatch_scaled",
    )(place, *picks, in_hbm(grad_out), *grads)
    scaled_rows = exchanged(scaled)

    sent, pos = pl.pallas_call(
        functools.partial(dispatch_tokens, experts, cap),
        out_shape=(
            pltpu.HBM((slots, width), jnp.bfloat16),
            jax.ShapeDtypeStruct((top, count), jnp.int32),
        ),
        grid_spec=pltpu.PrefetchScalarGridSpec(
            num_scalar_prefetch=1,
            grid=(groups,),
            in_specs=[small_spec, pl.BlockSpec((TAIL, LANES), lambda k, g: (count // TAIL, 0))]
            + [
                pl.BlockSpec(
                    (count, share), lambda k, g: (0, lax.rem(g[0] - k + groups, groups))
                )
            ]
            * 2,
            out_specs=(pl.BlockSpec((slots, share), lambda k, g: (0, k)), small_spec),
            scratch_shapes=[pltpu.VMEM((slots, 2 * count), jnp.bfloat16)],
        ),
        cost_estimate=pl.CostEstimate(
            flops=TOKENS_COST_US * 10**9, bytes_accessed=TOKENS_COST_US * 10**6, transcendentals=0
        ),
        compiler_params=params,
        name="dispatch_tokens",
    )(place, in_hbm(routes_t), tokens_across, in_hbm(tokens), in_hbm(tokens_across))
    x_rows = exchanged(sent, halves)

    weights_moved = pl.pallas_call(
        ready_kernel,
        out_shape=[pltpu.HBM(value.shape, value.dtype) for value in weights_moved],
        in_specs=[pl.BlockSpec(memory_space=pl.ANY)] * (groups - 1),
        out_specs=[pl.BlockSpec(memory_space=pl.ANY)] * (groups - 1),
        input_output_aliases={k: k for k in range(groups - 1)},
        cost_estimate=pl.CostEstimate(
            flops=READY_COST_US * 10**9, bytes_accessed=READY_COST_US * 10**6, transcendentals=0
        ),
        compiler_params=params,
        name="ready",
    )(*[in_hbm(value) for value in weights_moved])
    weights = [w_gate[0], w_up[0], *weights_moved]

    place_spec = pl.BlockSpec(memory_space=pltpu.SMEM)

    back_own, *rest = pl.pallas_call(
        functools.partial(back_kernel, groups, cap),
        out_shape=[pltpu.HBM((slots, hidden), jnp.float32)]
        + [pltpu.HBM((slots, hidden), jnp.bfloat16)] * (groups - 1)
        + [pltpu.HBM((groups * slots, share), jnp.bfloat16)],
        in_specs=[place_spec, pl.BlockSpec(), pl.BlockSpec()],
        compiler_params=params,
        name="back",
    )(place, scaled_rows, in_hbm(w_down[0]))
    scaled_all = rest[-1]
    back_parts = [shifted(rest[k - 1], -k) for k in range(1, groups)]

    whole_spec = pl.BlockSpec(memory_space=pltpu.VMEM)
    any_spec = pl.BlockSpec(memory_space=pl.ANY)
    *factors, hidden_own, held, back_kept = pl.pallas_call(
        functools.partial(forward_kernel, groups),
        out_shape=[pltpu.VMEM((slots, hidden), jnp.float32)] * 3
        + [
            pltpu.HBM((slots, hidden), jnp.bfloat16),
            pltpu.VMEM((2 * groups, share, hidden), jnp.bfloat16),
            pltpu.VMEM((slots, hidden), jnp.float32),
        ],
        in_specs=[whole_spec] + [any_spec] * (groups + 2),
        scratch_shapes=[
            pltpu.VMEM((slots, hidden), jnp.float32),
            pltpu.VMEM((slots, hidden), jnp.float32),
            pltpu.SemaphoreType.DMA((hidden // tile_of(hidden, 256), 2 * groups)),
            pltpu.SemaphoreType.DMA((1,)),
        ],
        compiler_params=params,
        name="forward",
    )(x_rows, in_hbm(back_own), *[in_hbm(value) for value in weights])

    pieces = groups * (share // tile_of(share, 512))
    returning = pl.pallas_call(
        functools.partial(backward_kernel, groups, cap),
        out_shape=pltpu.HBM((slots, width + LANES), jnp.bfloat16),
        in_specs=[place_spec] + [whole_spec] * (4 + groups),
        out_specs=any_spec,
        scratch_shapes=[
            pltpu.VMEM((slots, hidden), jnp.bfloat16),
            pltpu.VMEM((slots, hidden), jnp.bfloat16),
            pltpu.VMEM((slots, width + LANES), jnp.bfloat16),
            pltpu.SemaphoreType.DMA((pieces + 1,)),
        ],
        compiler_params=params,
        name="backward",
    )(place, *factors, held, back_kept, *back_parts)
    returned = exchanged(returning)

    hiddens = [hidden_own] + [shifted(hidden_own, k) for k in range(1, groups)]
    grad_down = contract_first(jnp.concatenate(hiddens, axis=0), scaled_all)[None]

    grad_tokens, grad_gates = pl.pallas_call(
        functools.partial(combine_kernel, groups),
        out_shape=(
            jax.ShapeDtypeStruct((count, width), jnp.bfloat16),
            jax.ShapeDtypeStruct((top, count), jnp.float32),
        ),
        in_specs=[pl.BlockSpec(memory_space=pltpu.SMEM)] + [whole_spec] * 3,
        compiler_params=params,
        name="combine",
    )(place, pos, gates_t, returned)
    return (grad_tokens, jnp.transpose(grad_gates), grad_down)


def solution(mesh):
    placed = (
        P(("dp", "expert"), None),
        P(("dp", "expert"), None),
        P(("dp", "expert"), None),
        P(("dp", "expert"), None),
        P("expert", "dp", None),
        P("expert", "dp", None),
        P("expert", None, "dp"),
    )
    return jax.shard_map(
        per_device,
        mesh=mesh,
        in_specs=placed,
        out_specs=(P(("dp", "expert"), None), P(("dp", "expert"), None), P("expert", None, "dp")),
        check_vma=False,
    )
```

```python
import functools

import jax
import jax.numpy as jnp
from jax import lax
from jax.experimental import pallas as pl
from jax.experimental.pallas import tpu as pltpu
from jax.sharding import PartitionSpec as P

LANES = 128
VMEM_BYTES = 24 * 1024 * 1024
TAIL = 16
READY_COST_US = 30
TOKENS_COST_US = 30


def contract_last(left, right):
    return lax.dot_general(
        left, right, (((1,), (1,)), ((), ())), preferred_element_type=jnp.float32
    )


def contract_first(left, right):
    return lax.dot_general(
        left, right, (((0,), (0,)), ((), ())), preferred_element_type=jnp.float32
    )


def tile_of(extent, most):
    return most if extent % most == 0 else extent


def slot_positions(routes, experts, stride, base):
    top, count = routes.shape
    labels = lax.broadcasted_iota(jnp.int32, (experts, count), 0)
    named = [labels == routes[k : k + 1, :] for k in range(top)]
    marks = sum(jnp.where(m, 1.0, 0.0) for m in named)
    earlier = lax.broadcasted_iota(jnp.int32, (count, count), 0) < lax.broadcasted_iota(
        jnp.int32, (count, count), 1
    )
    rank = jnp.dot(
        marks.astype(jnp.bfloat16),
        jnp.where(earlier, 1.0, 0.0).astype(jnp.bfloat16),
        preferred_element_type=jnp.float32,
    )
    slot = rank + (labels * stride + base + 1).astype(jnp.float32)
    return [
        jnp.sum(jnp.where(m, slot, 0.0), axis=0, keepdims=True).astype(jnp.int32) - 1
        for m in named
    ]


def by_half(value, cap, half, paired):
    count, width = value.shape
    if paired:
        value = value.reshape(count // (2 * cap), 2, cap, width)
        own, other = value[:, 0], value[:, 1]
    else:
        value = value.reshape(2, count // (2 * cap), cap, width)
        own, other = value[0], value[1]
    first = jnp.where(half == 0, own, other)
    second = jnp.where(half == 0, other, own)
    return jnp.stack([first, second], axis=0 if paired else 1).reshape(count, width)


def dispatch_tokens(experts, cap, place_ref, *refs):
    routes_refs, tokens_refs, (out_ref, pos_ref, pick_ref) = refs[:2], refs[2:4], refs[4:]
    count = tokens_refs[0].shape[0]
    top = pos_ref.shape[0]

    @pl.when(pl.program_id(0) == 0)
    def _():
        rows = lax.broadcasted_iota(jnp.int32, (pick_ref.shape[0], count), 0)
        for c, ref in enumerate(routes_refs):
            routes = ref[...].astype(jnp.float32).astype(jnp.int32)[:top, :count]
            near = routes - place_ref[1] * (experts // 2)
            pos = slot_positions(near, experts // 2, 2 * cap, c * cap)
            pick_ref[:, c * count : (c + 1) * count] = sum(
                jnp.where(rows == p, 1.0, 0.0) for p in pos
            ).astype(jnp.bfloat16)
        for k, p in enumerate(slot_positions(routes_refs[0][...], experts, cap, 0)):
            pos_ref[k : k + 1, :] = p

    values = jnp.concatenate([ref[...] for ref in tokens_refs], axis=0)
    out_ref[...] = jnp.dot(
        pick_ref[...], values, preferred_element_type=jnp.float32
    ).astype(out_ref.dtype)


def dispatch_scaled(experts, cap, groups, place_ref, *refs):
    routes_refs, gate_refs = refs[:groups], refs[groups : 2 * groups]
    grad_refs, (out_ref, pick_ref, scale_ref) = refs[2 * groups : 3 * groups], refs[3 * groups :]
    count = grad_refs[0].shape[0]
    slots = out_ref.shape[0]

    @pl.when(pl.program_id(0) == 0)
    def _():
        rows = lax.broadcasted_iota(jnp.int32, (slots, count), 0)
        total = jnp.zeros((slots, 1), jnp.float32)
        for q in range(groups):
            pos = slot_positions(routes_refs[q][...], experts, groups * cap, q * cap)
            hit = jnp.zeros((slots, count), jnp.float32)
            weight = jnp.zeros((slots, count), jnp.float32)
            for k, p in enumerate(pos):
                here = rows == p
                hit = hit + jnp.where(here, 1.0, 0.0)
                weight = weight + jnp.where(here, gate_refs[q][k : k + 1, :], 0.0)
            pick_ref[:, q * count : (q + 1) * count] = hit.astype(jnp.bfloat16)
            total = total + jnp.sum(weight, axis=1, keepdims=True)
        scale_ref[...] = jnp.broadcast_to(total, scale_ref.shape)

    grads = jnp.concatenate([ref[...] for ref in grad_refs], axis=0)
    rows = jnp.dot(pick_ref[...], grads, preferred_element_type=jnp.float32)
    out_ref[...] = (scale_ref[:, :1] * rows).astype(out_ref.dtype)


def ready_kernel(*refs):
    del refs


def back_kernel(groups, cap, place_ref, rows_ref, down_ref, own_ref, *rest):
    others, all_ref = rest[: groups - 1], rest[groups - 1]
    slots, hidden = own_ref.shape
    count, share = rows_ref.shape
    rows = rows_ref[...].astype(jnp.float32).reshape(count // (groups * cap), groups, cap, share)
    for q in range(groups):
        ordered = by_half(rows[:, q].reshape(slots, share), cap, place_ref[1], False)
        all_ref[q * slots : (q + 1) * slots, :] = ordered.astype(all_ref.dtype)
    step = tile_of(hidden, 256)

    @pl.loop(0, hidden // step)
    def _(j):
        cols = pl.ds(pl.multiple_of(j * step, step), step)
        for q, ref in enumerate((own_ref, *others)):
            part = contract_last(all_ref[q * slots : (q + 1) * slots, :], down_ref[cols, :])
            ref[:, cols] = part.astype(ref.dtype)


def forward_kernel(groups, x_ref, back_ref, *refs):
    (own_gate, own_up), others = refs[:2], refs[2 : groups + 1]
    act_ref, slope_ref, value_ref, hidden_ref, held_ref, kept_ref = refs[groups + 1 : groups + 7]
    gate_sum_ref, up_sum_ref, sems, back_sem = refs[groups + 7 :]
    share, hidden = held_ref.shape[1:]
    step = tile_of(hidden, 256)
    gates = [own_gate, *[ref.at[:share] for ref in others]]
    ups = [own_up, *[ref.at[share:] for ref in others]]
    spans = [slice(at, at + step) for at in range(0, hidden, step)]

    order = [i for k in range(groups) for i in (k, groups + k)]
    sources, part_rows = gates + ups, share // 2
    loads = [
        pltpu.make_async_copy(
            sources[i].at[n * part_rows : (n + 1) * part_rows],
            held_ref.at[i, n * part_rows : (n + 1) * part_rows],
            sems.at[n, i],
        )
        for i in order
        for n in range(2)
    ]
    loads.append(pltpu.make_async_copy(back_ref, kept_ref, back_sem.at[0]))
    flying = 2
    for copy in loads[:flying]:
        copy.start()

    def finish(cols):
        pre_gate, pre_up = gate_sum_ref[:, cols], up_sum_ref[:, cols]
        sig = jax.nn.sigmoid(pre_gate)
        act = pre_gate * sig
        hidden_f = act * pre_up
        act_ref[:, cols] = act
        slope_ref[:, cols] = pre_up * (sig * (1.0 + pre_gate * (1.0 - sig)))
        value_ref[:, cols] = hidden_f
        hidden_ref[:, cols] = hidden_f.astype(hidden_ref.dtype)

    complete = None
    for at, i in enumerate(order):
        k = i % groups
        for n in (2 * at, 2 * at + 1):
            loads[n].wait()
            if n + flying < len(loads):
                loads[n + flying].start()
        sum_ref = gate_sum_ref if i < groups else up_sum_ref
        for cols in spans:
            part = jnp.dot(
                x_ref[:, k * share : (k + 1) * share],
                held_ref[i, :, cols],
                preferred_element_type=jnp.float32,
            )
            if complete is not None:
                finish(complete)
            sum_ref[:, cols] = part if k == 0 else sum_ref[:, cols] + part
            complete = cols if i == order[-1] else None
    finish(complete)
    loads[-1].wait()


def backward_kernel(groups, cap, place_ref, act_ref, slope_ref, value_ref, held_ref, *refs):
    parts, (out_ref, d_gate_ref, d_up_ref, rows_ref, out_sems) = refs[:groups], refs[groups:]
    share = held_ref.shape[1]
    width = groups * share
    block = tile_of(share, 512)
    half = place_ref[1]
    back = sum(part[...].astype(jnp.float32) for part in parts)
    score = jnp.sum(back * value_ref[...], axis=1, keepdims=True)
    d_gate_ref[...] = by_half(back * slope_ref[...], cap, half, True).astype(jnp.bfloat16)
    d_up_ref[...] = by_half(back * act_ref[...], cap, half, True).astype(jnp.bfloat16)
    score = by_half(jnp.broadcast_to(score, (score.shape[0], LANES)), cap, half, True)
    rows_ref[:, width:] = score.astype(rows_ref.dtype)
    outs = []

    def send(cols):
        copy = pltpu.make_async_copy(
            rows_ref.at[:, cols], out_ref.at[:, cols], out_sems.at[len(outs)]
        )
        copy.start()
        outs.append(copy)

    send(slice(width, width + LANES))
    for k in range(groups):
        for at in range(0, share, block):
            cols = slice(k * share + at, k * share + at + block)
            grad = contract_last(d_gate_ref[...], held_ref[k, at : at + block])
            grad += contract_last(d_up_ref[...], held_ref[groups + k, at : at + block])
            rows_ref[:, cols] = grad.astype(rows_ref.dtype)
            send(cols)
    for copy in outs:
        copy.wait()


def combine_kernel(groups, place_ref, pos_ref, gate_ref, rows_ref, tokens_ref, gates_ref):
    top, count = pos_ref.shape
    slots = rows_ref.shape[0]
    width = tokens_ref.shape[1]
    share = width // groups
    places = lax.broadcasted_iota(jnp.int32, (slots, count), 0)
    picks = [
        jnp.where(places == pos_ref[k : k + 1, :], 1.0, 0.0).astype(jnp.bfloat16)
        for k in range(top)
    ]
    both = sum(picks)
    for k in range(groups):
        at = lax.rem(place_ref[0] - k + groups, groups) * share
        tokens_ref[:, pl.ds(pl.multiple_of(at, share), share)] = contract_first(
            both, rows_ref[:, k * share : (k + 1) * share]
        ).astype(tokens_ref.dtype)
    for k in range(top):
        score = contract_first(rows_ref[:, width:], picks[k])
        gates_ref[k : k + 1, :] = score[:1, :] / gate_ref[k : k + 1, :]


def per_device(tokens, routes, gates, grad_out, w_gate, w_up, w_down):
    experts = lax.axis_size("expert")
    groups = lax.axis_size("dp")
    group = lax.axis_index("dp")
    count, width = tokens.shape
    top = routes.shape[1]
    cap = 3 * count * top // (2 * experts)
    slots = experts * cap
    share = width // groups
    hidden = w_gate.shape[2]
    params = pltpu.CompilerParams(vmem_limit_bytes=VMEM_BYTES)
    half = lax.div(lax.axis_index("expert"), experts // 2)
    place = jnp.stack([group, half]).astype(jnp.int32)
    halves = [list(range(experts // 2)), list(range(experts // 2, experts))]

    def shifted(value, by):
        return lax.ppermute(value, "dp", [(i, (i + by) % groups) for i in range(groups)])

    def across(value):
        pairs = [(i, (i + experts // 2) % experts) for i in range(experts)]
        return lax.ppermute(value, "expert", pairs)

    def exchanged(rows, among=None):
        count = experts if among is None else len(among[0])
        split = rows.reshape(count, rows.shape[0] // count, rows.shape[1])
        moved = lax.all_to_all(
            split, "expert", split_axis=0, concat_axis=0, axis_index_groups=among, tiled=True
        )
        return moved.reshape(rows.shape)

    routes_t, gates_t = jnp.transpose(routes), jnp.transpose(gates)
    routes_all = [routes_t] + [shifted(routes_t, k) for k in range(1, groups)]
    gates_all = [gates_t] + [shifted(gates_t, k) for k in range(1, groups)]
    grads = [
        shifted(
            lax.dynamic_slice(grad_out, (0, lax.rem(group + k, groups) * share), (count, share)), k
        )
        for k in range(1, groups)
    ]
    both = jnp.concatenate([w_gate[0], w_up[0]], axis=0)
    both, gates_own = lax.optimization_barrier((both, gates_t))
    both, grads, routes_all, gates_all = lax.optimization_barrier(
        (both, grads, routes_all, gates_all)
    )
    tail = jnp.pad(routes_t.astype(tokens.dtype), ((0, TAIL - top), (0, width - count)))
    tokens_across = across(jnp.concatenate([tokens, tail], axis=0))
    weights_moved = [shifted(both, k) for k in range(1, groups)]

    def in_hbm(value):
        return pltpu.with_memory_space_constraint(value, pltpu.HBM)

    block = tile_of(share, 512)
    steps = share // block
    small_spec = pl.BlockSpec((top, count), lambda c, g: (0, 0))
    scaled = pl.pallas_call(
        functools.partial(dispatch_scaled, experts, cap, groups),
        out_shape=pltpu.HBM((groups * slots, share), jnp.bfloat16),
        grid_spec=pltpu.PrefetchScalarGridSpec(
            num_scalar_prefetch=1,
            grid=(steps,),
            in_specs=[small_spec] * (2 * groups)
            + [pl.BlockSpec((count, block), lambda c, g: (0, g[0] * steps + c))]
            + [pl.BlockSpec((count, block), lambda c, g: (0, c))] * (groups - 1),
            out_specs=pl.BlockSpec((groups * slots, block), lambda c, g: (0, c)),
            scratch_shapes=[
                pltpu.VMEM((groups * slots, groups * count), jnp.bfloat16),
                pltpu.VMEM((groups * slots, LANES), jnp.float32),
            ],
        ),
        compiler_params=params,
        name="dispatch_scaled",
    )(place, in_hbm(routes_t), *routes_all[1:], in_hbm(gates_own), *gates_all[1:], in_hbm(grad_out), *grads)
    scaled_rows = exchanged(scaled)

    sent, pos = pl.pallas_call(
        functools.partial(dispatch_tokens, experts, cap),
        out_shape=(
            pltpu.HBM((slots, width), jnp.bfloat16),
            jax.ShapeDtypeStruct((top, count), jnp.int32),
        ),
        grid_spec=pltpu.PrefetchScalarGridSpec(
            num_scalar_prefetch=1,
            grid=(groups,),
            in_specs=[small_spec, pl.BlockSpec((TAIL, LANES), lambda k, g: (count // TAIL, 0))]
            + [
                pl.BlockSpec(
                    (count, share), lambda k, g: (0, lax.rem(g[0] - k + groups, groups))
                )
            ]
            * 2,
            out_specs=(pl.BlockSpec((slots, share), lambda k, g: (0, k)), small_spec),
            scratch_shapes=[pltpu.VMEM((slots, 2 * count), jnp.bfloat16)],
        ),
        cost_estimate=pl.CostEstimate(
            flops=TOKENS_COST_US * 10**9, bytes_accessed=TOKENS_COST_US * 10**6, transcendentals=0
        ),
        compiler_params=params,
        name="dispatch_tokens",
    )(place, in_hbm(routes_t), tokens_across, in_hbm(tokens), in_hbm(tokens_across))
    x_rows = exchanged(sent, halves)

    weights_moved = pl.pallas_call(
        ready_kernel,
        out_shape=[pltpu.HBM(value.shape, value.dtype) for value in weights_moved],
        in_specs=[pl.BlockSpec(memory_space=pl.ANY)] * (groups - 1),
        out_specs=[pl.BlockSpec(memory_space=pl.ANY)] * (groups - 1),
        input_output_aliases={k: k for k in range(groups - 1)},
        cost_estimate=pl.CostEstimate(
            flops=READY_COST_US * 10**9, bytes_accessed=READY_COST_US * 10**6, transcendentals=0
        ),
        compiler_params=params,
        name="ready",
    )(*[in_hbm(value) for value in weights_moved])
    weights = [w_gate[0], w_up[0], *weights_moved]

    place_spec = pl.BlockSpec(memory_space=pltpu.SMEM)

    back_own, *rest = pl.pallas_call(
        functools.partial(back_kernel, groups, cap),
        out_shape=[pltpu.HBM((slots, hidden), jnp.float32)]
        + [pltpu.HBM((slots, hidden), jnp.bfloat16)] * (groups - 1)
        + [pltpu.HBM((groups * slots, share), jnp.bfloat16)],
        in_specs=[place_spec, pl.BlockSpec(), pl.BlockSpec()],
        compiler_params=params,
        name="back",
    )(place, scaled_rows, in_hbm(w_down[0]))
    scaled_all = rest[-1]
    back_parts = [shifted(rest[k - 1], -k) for k in range(1, groups)]

    whole_spec = pl.BlockSpec(memory_space=pltpu.VMEM)
    any_spec = pl.BlockSpec(memory_space=pl.ANY)
    *factors, hidden_own, held, back_kept = pl.pallas_call(
        functools.partial(forward_kernel, groups),
        out_shape=[pltpu.VMEM((slots, hidden), jnp.float32)] * 3
        + [
            pltpu.HBM((slots, hidden), jnp.bfloat16),
            pltpu.VMEM((2 * groups, share, hidden), jnp.bfloat16),
            pltpu.VMEM((slots, hidden), jnp.float32),
        ],
        in_specs=[whole_spec] + [any_spec] * (groups + 2),
        scratch_shapes=[
            pltpu.VMEM((slots, hidden), jnp.float32),
            pltpu.VMEM((slots, hidden), jnp.float32),
            pltpu.SemaphoreType.DMA((2, 2 * groups)),
            pltpu.SemaphoreType.DMA((1,)),
        ],
        compiler_params=params,
        name="forward",
    )(x_rows, in_hbm(back_own), *[in_hbm(value) for value in weights])

    pieces = groups * (share // tile_of(share, 512))
    returning = pl.pallas_call(
        functools.partial(backward_kernel, groups, cap),
        out_shape=pltpu.HBM((slots, width + LANES), jnp.bfloat16),
        in_specs=[place_spec] + [whole_spec] * (4 + groups),
        out_specs=any_spec,
        scratch_shapes=[
            pltpu.VMEM((slots, hidden), jnp.bfloat16),
            pltpu.VMEM((slots, hidden), jnp.bfloat16),
            pltpu.VMEM((slots, width + LANES), jnp.bfloat16),
            pltpu.SemaphoreType.DMA((pieces + 1,)),
        ],
        compiler_params=params,
        name="backward",
    )(place, *factors, held, back_kept, *back_parts)
    returned = exchanged(returning)

    hiddens = [hidden_own] + [shifted(hidden_own, k) for k in range(1, groups)]
    grad_down = contract_first(jnp.concatenate(hiddens, axis=0), scaled_all)[None]

    grad_tokens, grad_gates = pl.pallas_call(
        functools.partial(combine_kernel, groups),
        out_shape=(
            jax.ShapeDtypeStruct((count, width), jnp.bfloat16),
            jax.ShapeDtypeStruct((top, count), jnp.float32),
        ),
        in_specs=[pl.BlockSpec(memory_space=pltpu.SMEM)] + [whole_spec] * 3,
        compiler_params=params,
        name="combine",
    )(place, pos, gates_t, returned)
    return (grad_tokens, jnp.transpose(grad_gates), grad_down)


def solution(mesh):
    placed = (
        P(("dp", "expert"), None),
        P(("dp", "expert"), None),
        P(("dp", "expert"), None),
        P(("dp", "expert"), None),
        P("expert", "dp", None),
        P("expert", "dp", None),
        P("expert", None, "dp"),
    )
    return jax.shard_map(
        per_device,
        mesh=mesh,
        in_specs=placed,
        out_specs=(P(("dp", "expert"), None), P(("dp", "expert"), None), P("expert", None, "dp")),
        check_vma=False,
    )
```

```python
import functools

import jax
import jax.numpy as jnp
from jax import lax
from jax.experimental import pallas as pl
from jax.experimental.pallas import tpu as pltpu
from jax.sharding import PartitionSpec as P

LANES = 128
VMEM_BYTES = 24 * 1024 * 1024
READY_COST_US = 30
TOKENS_COST_US = 30


def contract_last(left, right):
    return lax.dot_general(
        left, right, (((1,), (1,)), ((), ())), preferred_element_type=jnp.float32
    )


def contract_first(left, right):
    return lax.dot_general(
        left, right, (((0,), (0,)), ((), ())), preferred_element_type=jnp.float32
    )


def tile_of(extent, most):
    return most if extent % most == 0 else extent


def slot_positions(routes, experts, stride, base):
    top, count = routes.shape
    labels = lax.broadcasted_iota(jnp.int32, (experts, count), 0)
    named = [labels == routes[k : k + 1, :] for k in range(top)]
    marks = sum(jnp.where(m, 1.0, 0.0) for m in named)
    earlier = lax.broadcasted_iota(jnp.int32, (count, count), 0) < lax.broadcasted_iota(
        jnp.int32, (count, count), 1
    )
    rank = jnp.dot(
        marks.astype(jnp.bfloat16),
        jnp.where(earlier, 1.0, 0.0).astype(jnp.bfloat16),
        preferred_element_type=jnp.float32,
    )
    slot = rank + (labels * stride + base + 1).astype(jnp.float32)
    return [
        jnp.sum(jnp.where(m, slot, 0.0), axis=0, keepdims=True).astype(jnp.int32) - 1
        for m in named
    ]


def by_half(value, cap, half, paired):
    count, width = value.shape
    if paired:
        value = value.reshape(count // (2 * cap), 2, cap, width)
        own, other = value[:, 0], value[:, 1]
    else:
        value = value.reshape(2, count // (2 * cap), cap, width)
        own, other = value[0], value[1]
    first = jnp.where(half == 0, own, other)
    second = jnp.where(half == 0, other, own)
    return jnp.stack([first, second], axis=0 if paired else 1).reshape(count, width)


def dispatch_tokens(experts, cap, place_ref, *refs):
    routes_refs, tokens_refs, (out_ref, pos_ref, pick_ref) = refs[:2], refs[2:4], refs[4:]
    count = tokens_refs[0].shape[0]

    @pl.when(pl.program_id(0) == 0)
    def _():
        rows = lax.broadcasted_iota(jnp.int32, (pick_ref.shape[0], count), 0)
        for c, ref in enumerate(routes_refs):
            near = ref[...] - place_ref[1] * (experts // 2)
            pos = slot_positions(near, experts // 2, 2 * cap, c * cap)
            pick_ref[:, c * count : (c + 1) * count] = sum(
                jnp.where(rows == p, 1.0, 0.0) for p in pos
            ).astype(jnp.bfloat16)
        for k, p in enumerate(slot_positions(routes_refs[0][...], experts, cap, 0)):
            pos_ref[k : k + 1, :] = p

    values = jnp.concatenate([ref[...] for ref in tokens_refs], axis=0)
    out_ref[...] = jnp.dot(
        pick_ref[...], values, preferred_element_type=jnp.float32
    ).astype(out_ref.dtype)


def dispatch_scaled(experts, cap, groups, place_ref, *refs):
    routes_refs, gate_refs = refs[:groups], refs[groups : 2 * groups]
    grad_refs, (out_ref, pick_ref, scale_ref) = refs[2 * groups : 3 * groups], refs[3 * groups :]
    count = grad_refs[0].shape[0]
    slots = out_ref.shape[0]

    @pl.when(pl.program_id(0) == 0)
    def _():
        rows = lax.broadcasted_iota(jnp.int32, (slots, count), 0)
        total = jnp.zeros((slots, 1), jnp.float32)
        for q in range(groups):
            pos = slot_positions(routes_refs[q][...], experts, groups * cap, q * cap)
            hit = jnp.zeros((slots, count), jnp.float32)
            weight = jnp.zeros((slots, count), jnp.float32)
            for k, p in enumerate(pos):
                here = rows == p
                hit = hit + jnp.where(here, 1.0, 0.0)
                weight = weight + jnp.where(here, gate_refs[q][k : k + 1, :], 0.0)
            pick_ref[:, q * count : (q + 1) * count] = hit.astype(jnp.bfloat16)
            total = total + jnp.sum(weight, axis=1, keepdims=True)
        scale_ref[...] = jnp.broadcast_to(total, scale_ref.shape)

    grads = jnp.concatenate([ref[...] for ref in grad_refs], axis=0)
    rows = jnp.dot(pick_ref[...], grads, preferred_element_type=jnp.float32)
    out_ref[...] = (scale_ref[:, :1] * rows).astype(out_ref.dtype)


def ready_kernel(gate_ref, *refs):
    held_ref, sems = refs[-2:]
    half = gate_ref.shape[0] // 2
    copies = [
        pltpu.make_async_copy(
            gate_ref.at[n * half : (n + 1) * half],
            held_ref.at[n * half : (n + 1) * half],
            sems.at[n],
        )
        for n in range(2)
    ]
    for copy in copies:
        copy.start()
    for copy in copies:
        copy.wait()


def back_kernel(groups, cap, place_ref, rows_ref, down_ref, own_ref, *rest):
    others, all_ref = rest[: groups - 1], rest[groups - 1]
    slots, hidden = own_ref.shape
    count, share = rows_ref.shape
    rows = rows_ref[...].astype(jnp.float32).reshape(count // (groups * cap), groups, cap, share)
    for q in range(groups):
        ordered = by_half(rows[:, q].reshape(slots, share), cap, place_ref[1], False)
        all_ref[q * slots : (q + 1) * slots, :] = ordered.astype(all_ref.dtype)
    step = tile_of(hidden, 256)

    @pl.loop(0, hidden // step)
    def _(j):
        cols = pl.ds(pl.multiple_of(j * step, step), step)
        for q, ref in enumerate((own_ref, *others)):
            part = contract_last(all_ref[q * slots : (q + 1) * slots, :], down_ref[cols, :])
            ref[:, cols] = part.astype(ref.dtype)


def forward_kernel(groups, x_ref, gate_ref, back_ref, own_up_ref, *refs):
    others = refs[: groups - 1]
    act_ref, slope_ref, value_ref, hidden_ref, held_ref, kept_ref = refs[groups - 1 : groups + 5]
    gate_sum_ref, up_sum_ref, sems, back_sem = refs[groups + 5 :]
    share, hidden = gate_ref.shape
    step = tile_of(hidden, 256)
    sources = [gate_ref, *[ref.at[:share] for ref in others]]
    sources += [own_up_ref, *[ref.at[share:] for ref in others]]
    spans = [slice(at, at + step) for at in range(0, hidden, step)]

    order = [i for k in range(groups) for i in (k, groups + k)]
    part_rows = share // 2
    stages = [
        [
            pltpu.make_async_copy(
                sources[i].at[n * part_rows : (n + 1) * part_rows],
                held_ref.at[i - 1, n * part_rows : (n + 1) * part_rows],
                sems.at[n, i - 1],
            )
            for n in range(2)
        ]
        for i in order[1:]
    ]
    stages[-1].append(pltpu.make_async_copy(back_ref, kept_ref, back_sem.at[0]))

    def finish(cols):
        pre_gate, pre_up = gate_sum_ref[:, cols], up_sum_ref[:, cols]
        sig = jax.nn.sigmoid(pre_gate)
        act = pre_gate * sig
        hidden_f = act * pre_up
        act_ref[:, cols] = act
        slope_ref[:, cols] = pre_up * (sig * (1.0 + pre_gate * (1.0 - sig)))
        value_ref[:, cols] = hidden_f
        hidden_ref[:, cols] = hidden_f.astype(hidden_ref.dtype)

    complete = None
    for at, i in enumerate(order):
        k = i % groups
        if at > 0:
            for copy in stages[at - 1]:
                copy.wait()
        if at < len(stages):
            for copy in stages[at]:
                copy.start()
        sum_ref = gate_sum_ref if i < groups else up_sum_ref
        for cols in spans:
            part = jnp.dot(
                x_ref[:, k * share : (k + 1) * share],
                gate_ref[:, cols] if i == 0 else held_ref[i - 1, :, cols],
                preferred_element_type=jnp.float32,
            )
            if complete is not None:
                finish(complete)
            sum_ref[:, cols] = part if k == 0 else sum_ref[:, cols] + part
            complete = cols if i == order[-1] else None
    finish(complete)


def backward_kernel(
    groups, cap, half_ref, act_ref, slope_ref, value_ref, gate_ref, held_ref, *refs
):
    parts, (out_ref, d_gate_ref, d_up_ref, rows_ref, out_sems) = refs[:groups], refs[groups:]
    share = held_ref.shape[1]
    width = groups * share
    block = tile_of(share, 512)
    half = half_ref[0]
    back = sum(part[...].astype(jnp.float32) for part in parts)
    score = jnp.sum(back * value_ref[...], axis=1, keepdims=True)
    d_gate_ref[...] = by_half(back * slope_ref[...], cap, half, True).astype(jnp.bfloat16)
    d_up_ref[...] = by_half(back * act_ref[...], cap, half, True).astype(jnp.bfloat16)
    score = by_half(jnp.broadcast_to(score, (score.shape[0], LANES)), cap, half, True)
    rows_ref[:, width:] = score.astype(rows_ref.dtype)
    outs = []

    def send(cols):
        copy = pltpu.make_async_copy(
            rows_ref.at[:, cols], out_ref.at[:, cols], out_sems.at[len(outs)]
        )
        copy.start()
        outs.append(copy)

    send(slice(width, width + LANES))
    for k in range(groups):
        for at in range(0, share, block):
            cols = slice(k * share + at, k * share + at + block)
            gate = gate_ref[at : at + block] if k == 0 else held_ref[k - 1, at : at + block]
            grad = contract_last(d_gate_ref[...], gate)
            grad += contract_last(d_up_ref[...], held_ref[groups - 1 + k, at : at + block])
            rows_ref[:, cols] = grad.astype(rows_ref.dtype)
            send(cols)
    for copy in outs:
        copy.wait()


def combine_kernel(groups, place_ref, pos_ref, gate_ref, rows_ref, tokens_ref, gates_ref):
    top, count = pos_ref.shape
    slots = rows_ref.shape[0]
    width = tokens_ref.shape[1]
    share = width // groups
    places = lax.broadcasted_iota(jnp.int32, (slots, count), 0)
    picks = [
        jnp.where(places == pos_ref[k : k + 1, :], 1.0, 0.0).astype(jnp.bfloat16)
        for k in range(top)
    ]
    both = sum(picks)
    for k in range(groups):
        at = lax.rem(place_ref[0] - k + groups, groups) * share
        tokens_ref[:, pl.ds(pl.multiple_of(at, share), share)] = contract_first(
            both, rows_ref[:, k * share : (k + 1) * share]
        ).astype(tokens_ref.dtype)
    for k in range(top):
        score = contract_first(rows_ref[:, width:], picks[k])
        gates_ref[k : k + 1, :] = score[:1, :] / gate_ref[k : k + 1, :]


def per_device(tokens, routes, gates, grad_out, w_gate, w_up, w_down):
    experts = lax.axis_size("expert")
    groups = lax.axis_size("dp")
    group = lax.axis_index("dp")
    count, width = tokens.shape
    top = routes.shape[1]
    cap = 3 * count * top // (2 * experts)
    slots = experts * cap
    share = width // groups
    hidden = w_gate.shape[2]
    params = pltpu.CompilerParams(vmem_limit_bytes=VMEM_BYTES)
    half = lax.div(lax.axis_index("expert"), experts // 2)
    place = jnp.stack([group, half]).astype(jnp.int32)
    place_group, place_half = group.reshape(1), half.reshape(1)
    halves = [list(range(experts // 2)), list(range(experts // 2, experts))]

    def shifted(value, by):
        return lax.ppermute(value, "dp", [(i, (i + by) % groups) for i in range(groups)])

    def across(value):
        pairs = [(i, (i + experts // 2) % experts) for i in range(experts)]
        return lax.ppermute(value, "expert", pairs)

    def exchanged(rows, among=None):
        count = experts if among is None else len(among[0])
        split = rows.reshape(count, rows.shape[0] // count, rows.shape[1])
        moved = lax.all_to_all(
            split, "expert", split_axis=0, concat_axis=0, axis_index_groups=among, tiled=True
        )
        return moved.reshape(rows.shape)

    routes_t, gates_t = jnp.transpose(routes), jnp.transpose(gates)
    routes_all = [routes_t] + [shifted(routes_t, k) for k in range(1, groups)]
    gates_all = [gates_t] + [shifted(gates_t, k) for k in range(1, groups)]
    grads = [
        shifted(
            lax.dynamic_slice(grad_out, (0, lax.rem(group + k, groups) * share), (count, share)), k
        )
        for k in range(1, groups)
    ]
    both = jnp.concatenate([w_gate[0], w_up[0]], axis=0)
    both, gates_own = lax.optimization_barrier((both, gates_t))
    both, grads, routes_all, gates_all = lax.optimization_barrier(
        (both, grads, routes_all, gates_all)
    )
    routes_across = across(routes_t)
    tokens_sent, routes_across = lax.optimization_barrier((tokens, routes_across))
    tokens_across = across(tokens_sent)
    weights_moved = [shifted(both, k) for k in range(1, groups)]

    def in_hbm(value):
        return pltpu.with_memory_space_constraint(value, pltpu.HBM)

    block = tile_of(share, 512)
    steps = share // block
    small_spec = pl.BlockSpec((top, count), lambda c, g: (0, 0))
    scaled = pl.pallas_call(
        functools.partial(dispatch_scaled, experts, cap, groups),
        out_shape=pltpu.HBM((groups * slots, share), jnp.bfloat16),
        grid_spec=pltpu.PrefetchScalarGridSpec(
            num_scalar_prefetch=1,
            grid=(steps,),
            in_specs=[small_spec] * (2 * groups)
            + [pl.BlockSpec((count, block), lambda c, g: (0, g[0] * steps + c))]
            + [pl.BlockSpec((count, block), lambda c, g: (0, c))] * (groups - 1),
            out_specs=pl.BlockSpec((groups * slots, block), lambda c, g: (0, c)),
            scratch_shapes=[
                pltpu.VMEM((groups * slots, groups * count), jnp.bfloat16),
                pltpu.VMEM((groups * slots, LANES), jnp.float32),
            ],
        ),
        compiler_params=params,
        name="dispatch_scaled",
    )(
        place_group,
        in_hbm(routes_t),
        *routes_all[1:],
        in_hbm(gates_own),
        *gates_all[1:],
        in_hbm(grad_out),
        *grads,
    )
    scaled_rows = exchanged(scaled)

    sent, pos = pl.pallas_call(
        functools.partial(dispatch_tokens, experts, cap),
        out_shape=(
            pltpu.HBM((slots, width), jnp.bfloat16),
            jax.ShapeDtypeStruct((top, count), jnp.int32),
        ),
        grid_spec=pltpu.PrefetchScalarGridSpec(
            num_scalar_prefetch=1,
            grid=(groups,),
            in_specs=[small_spec] * 2
            + [
                pl.BlockSpec(
                    (count, share), lambda k, g: (0, lax.rem(g[0] - k + groups, groups))
                )
            ]
            * 2,
            out_specs=(pl.BlockSpec((slots, share), lambda k, g: (0, k)), small_spec),
            scratch_shapes=[pltpu.VMEM((slots, 2 * count), jnp.bfloat16)],
        ),
        cost_estimate=pl.CostEstimate(
            flops=TOKENS_COST_US * 10**9, bytes_accessed=TOKENS_COST_US * 10**6, transcendentals=0
        ),
        compiler_params=params,
        name="dispatch_tokens",
    )(place, in_hbm(routes_t), routes_across, in_hbm(tokens), in_hbm(tokens_across))
    x_rows = exchanged(sent, halves)

    any_spec = pl.BlockSpec(memory_space=pl.ANY)
    whole_spec = pl.BlockSpec(memory_space=pltpu.VMEM)
    *weights_moved, gate_held = pl.pallas_call(
        ready_kernel,
        out_shape=[pltpu.HBM(value.shape, value.dtype) for value in weights_moved]
        + [pltpu.VMEM((share, hidden), jnp.bfloat16)],
        in_specs=[any_spec] * groups,
        out_specs=[any_spec] * (groups - 1) + [whole_spec],
        input_output_aliases={k + 1: k for k in range(groups - 1)},
        scratch_shapes=[pltpu.SemaphoreType.DMA((2,))],
        cost_estimate=pl.CostEstimate(
            flops=READY_COST_US * 10**9, bytes_accessed=READY_COST_US * 10**6, transcendentals=0
        ),
        compiler_params=params,
        name="ready",
    )(in_hbm(w_gate[0]), *[in_hbm(value) for value in weights_moved])

    place_spec = pl.BlockSpec(memory_space=pltpu.SMEM)

    back_own, *rest = pl.pallas_call(
        functools.partial(back_kernel, groups, cap),
        out_shape=[pltpu.HBM((slots, hidden), jnp.float32)]
        + [pltpu.HBM((slots, hidden), jnp.bfloat16)] * (groups - 1)
        + [pltpu.HBM((groups * slots, share), jnp.bfloat16)],
        in_specs=[place_spec, pl.BlockSpec(), pl.BlockSpec()],
        compiler_params=params,
        name="back",
    )(place, scaled_rows, in_hbm(w_down[0]))
    scaled_all = rest[-1]
    back_parts = [shifted(rest[k - 1], -k) for k in range(1, groups)]

    *factors, hidden_own, held, back_kept = pl.pallas_call(
        functools.partial(forward_kernel, groups),
        out_shape=[pltpu.VMEM((slots, hidden), jnp.float32)] * 3
        + [
            pltpu.HBM((slots, hidden), jnp.bfloat16),
            pltpu.VMEM((2 * groups - 1, share, hidden), jnp.bfloat16),
            pltpu.VMEM((slots, hidden), jnp.float32),
        ],
        in_specs=[whole_spec] * 2 + [any_spec] * (groups + 1),
        scratch_shapes=[
            pltpu.VMEM((slots, hidden), jnp.float32),
            pltpu.VMEM((slots, hidden), jnp.float32),
            pltpu.SemaphoreType.DMA((2, 2 * groups - 1)),
            pltpu.SemaphoreType.DMA((1,)),
        ],
        compiler_params=params,
        name="forward",
    )(x_rows, gate_held, in_hbm(back_own), in_hbm(w_up[0]), *[in_hbm(w) for w in weights_moved])

    pieces = groups * (share // tile_of(share, 512))
    returning = pl.pallas_call(
        functools.partial(backward_kernel, groups, cap),
        out_shape=pltpu.HBM((slots, width + LANES), jnp.bfloat16),
        in_specs=[place_spec] + [whole_spec] * (5 + groups),
        out_specs=any_spec,
        scratch_shapes=[
            pltpu.VMEM((slots, hidden), jnp.bfloat16),
            pltpu.VMEM((slots, hidden), jnp.bfloat16),
            pltpu.VMEM((slots, width + LANES), jnp.bfloat16),
            pltpu.SemaphoreType.DMA((pieces + 1,)),
        ],
        compiler_params=params,
        name="backward",
    )(place_half, *factors, gate_held, held, back_kept, *back_parts)
    returned = exchanged(returning)

    hiddens = [hidden_own] + [shifted(hidden_own, k) for k in range(1, groups)]
    grad_down = contract_first(jnp.concatenate(hiddens, axis=0), scaled_all)[None]

    grad_tokens, grad_gates = pl.pallas_call(
        functools.partial(combine_kernel, groups),
        out_shape=(
            jax.ShapeDtypeStruct((count, width), jnp.bfloat16),
            jax.ShapeDtypeStruct((top, count), jnp.float32),
        ),
        in_specs=[pl.BlockSpec(memory_space=pltpu.SMEM)] + [whole_spec] * 3,
        compiler_params=params,
        name="combine",
    )(place_group, pos, gates_t, returned)
    return (grad_tokens, jnp.transpose(grad_gates), grad_down)


def solution(mesh):
    placed = (
        P(("dp", "expert"), None),
        P(("dp", "expert"), None),
        P(("dp", "expert"), None),
        P(("dp", "expert"), None),
        P("expert", "dp", None),
        P("expert", "dp", None),
        P("expert", None, "dp"),
    )
    return jax.shard_map(
        per_device,
        mesh=mesh,
        in_specs=placed,
        out_specs=(P(("dp", "expert"), None), P(("dp", "expert"), None), P("expert", None, "dp")),
        check_vma=False,
    )
```

```python
import functools

import jax
import jax.numpy as jnp
from jax import lax
from jax.experimental import pallas as pl
from jax.experimental.pallas import tpu as pltpu
from jax.sharding import PartitionSpec as P

LANES = 128
VMEM_BYTES = 24 * 1024 * 1024
READY_COST_US = 30
TOKENS_COST_US = 30


def contract_last(left, right):
    return lax.dot_general(
        left, right, (((1,), (1,)), ((), ())), preferred_element_type=jnp.float32
    )


def contract_first(left, right):
    return lax.dot_general(
        left, right, (((0,), (0,)), ((), ())), preferred_element_type=jnp.float32
    )


def tile_of(extent, most):
    return most if extent % most == 0 else extent


def slot_positions(routes, experts, stride, base):
    top, count = routes.shape
    labels = lax.broadcasted_iota(jnp.int32, (experts, count), 0)
    named = [labels == routes[k : k + 1, :] for k in range(top)]
    marks = sum(jnp.where(m, 1.0, 0.0) for m in named)
    earlier = lax.broadcasted_iota(jnp.int32, (count, count), 0) < lax.broadcasted_iota(
        jnp.int32, (count, count), 1
    )
    rank = jnp.dot(
        marks.astype(jnp.bfloat16),
        jnp.where(earlier, 1.0, 0.0).astype(jnp.bfloat16),
        preferred_element_type=jnp.float32,
    )
    slot = rank + (labels * stride + base + 1).astype(jnp.float32)
    return [
        jnp.sum(jnp.where(m, slot, 0.0), axis=0, keepdims=True).astype(jnp.int32) - 1
        for m in named
    ]


def by_half(value, cap, half, paired):
    count, width = value.shape
    if paired:
        value = value.reshape(count // (2 * cap), 2, cap, width)
        own, other = value[:, 0], value[:, 1]
    else:
        value = value.reshape(2, count // (2 * cap), cap, width)
        own, other = value[0], value[1]
    first = jnp.where(half == 0, own, other)
    second = jnp.where(half == 0, other, own)
    return jnp.stack([first, second], axis=0 if paired else 1).reshape(count, width)


def dispatch_tokens(experts, cap, place_ref, *refs):
    routes_refs, tokens_refs, (out_ref, pos_ref, pick_ref) = refs[:2], refs[2:4], refs[4:]
    count = tokens_refs[0].shape[0]

    @pl.when(pl.program_id(0) == 0)
    def _():
        rows = lax.broadcasted_iota(jnp.int32, (pick_ref.shape[0], count), 0)
        for c, ref in enumerate(routes_refs):
            near = ref[...] - place_ref[1] * (experts // 2)
            pos = slot_positions(near, experts // 2, 2 * cap, c * cap)
            pick_ref[:, c * count : (c + 1) * count] = sum(
                jnp.where(rows == p, 1.0, 0.0) for p in pos
            ).astype(jnp.bfloat16)
        for k, p in enumerate(slot_positions(routes_refs[0][...], experts, cap, 0)):
            pos_ref[k : k + 1, :] = p

    values = jnp.concatenate([ref[...] for ref in tokens_refs], axis=0)
    out_ref[...] = jnp.dot(
        pick_ref[...], values, preferred_element_type=jnp.float32
    ).astype(out_ref.dtype)


def dispatch_scaled(experts, cap, groups, place_ref, *refs):
    routes_refs, gate_refs = refs[:groups], refs[groups : 2 * groups]
    grad_refs, (out_ref, pick_ref, scale_ref) = refs[2 * groups : 3 * groups], refs[3 * groups :]
    count = grad_refs[0].shape[0]
    slots = out_ref.shape[0]

    @pl.when(pl.program_id(0) == 0)
    def _():
        rows = lax.broadcasted_iota(jnp.int32, (slots, count), 0)
        total = jnp.zeros((slots, 1), jnp.float32)
        for q in range(groups):
            pos = slot_positions(routes_refs[q][...], experts, groups * cap, q * cap)
            hit = jnp.zeros((slots, count), jnp.float32)
            weight = jnp.zeros((slots, count), jnp.float32)
            for k, p in enumerate(pos):
                here = rows == p
                hit = hit + jnp.where(here, 1.0, 0.0)
                weight = weight + jnp.where(here, gate_refs[q][k : k + 1, :], 0.0)
            pick_ref[:, q * count : (q + 1) * count] = hit.astype(jnp.bfloat16)
            total = total + jnp.sum(weight, axis=1, keepdims=True)
        scale_ref[...] = jnp.broadcast_to(total, scale_ref.shape)

    grads = jnp.concatenate([ref[...] for ref in grad_refs], axis=0)
    rows = jnp.dot(pick_ref[...], grads, preferred_element_type=jnp.float32)
    out_ref[...] = (scale_ref[:, :1] * rows).astype(out_ref.dtype)


def stack_kernel(pieces, top_ref, bottom_ref, out_ref, sems):
    extent = top_ref.shape[0]
    each = extent // pieces
    copies = [
        pltpu.make_async_copy(
            ref.at[n * each : (n + 1) * each],
            out_ref.at[to + n * each : to + (n + 1) * each],
            sems.at[i, n],
        )
        for i, (ref, to) in enumerate(((top_ref, 0), (bottom_ref, extent)))
        for n in range(pieces)
    ]
    for copy in copies:
        copy.start()
    for copy in copies:
        copy.wait()


def ready_kernel(gate_ref, *refs):
    held_ref, sems = refs[-2:]
    half = gate_ref.shape[0] // 2
    copies = [
        pltpu.make_async_copy(
            gate_ref.at[n * half : (n + 1) * half],
            held_ref.at[n * half : (n + 1) * half],
            sems.at[n],
        )
        for n in range(2)
    ]
    for copy in copies:
        copy.start()
    for copy in copies:
        copy.wait()


def back_kernel(groups, cap, place_ref, rows_ref, down_ref, own_ref, *rest):
    others, all_ref = rest[: groups - 1], rest[groups - 1]
    slots, hidden = own_ref.shape
    count, share = rows_ref.shape
    rows = rows_ref[...].astype(jnp.float32).reshape(count // (groups * cap), groups, cap, share)
    for q in range(groups):
        ordered = by_half(rows[:, q].reshape(slots, share), cap, place_ref[1], False)
        all_ref[q * slots : (q + 1) * slots, :] = ordered.astype(all_ref.dtype)
    step = tile_of(hidden, 256)

    @pl.loop(0, hidden // step)
    def _(j):
        cols = pl.ds(pl.multiple_of(j * step, step), step)
        for q, ref in enumerate((own_ref, *others)):
            part = contract_last(all_ref[q * slots : (q + 1) * slots, :], down_ref[cols, :])
            ref[:, cols] = part.astype(ref.dtype)


def forward_kernel(groups, x_ref, gate_ref, back_ref, own_up_ref, *refs):
    others = refs[: groups - 1]
    act_ref, slope_ref, value_ref, hidden_ref, held_ref, kept_ref = refs[groups - 1 : groups + 5]
    gate_sum_ref, up_sum_ref, sems, back_sem = refs[groups + 5 :]
    share, hidden = gate_ref.shape
    step = tile_of(hidden, 256)
    sources = [gate_ref, *[ref.at[:share] for ref in others]]
    sources += [own_up_ref, *[ref.at[share:] for ref in others]]
    spans = [slice(at, at + step) for at in range(0, hidden, step)]

    order = [i for k in range(groups) for i in (k, groups + k)]
    part_rows = share // 2
    stages = [
        [
            pltpu.make_async_copy(
                sources[i].at[n * part_rows : (n + 1) * part_rows],
                held_ref.at[i - 1, n * part_rows : (n + 1) * part_rows],
                sems.at[n, i - 1],
            )
            for n in range(2)
        ]
        for i in order[1:]
    ]
    stages[-1].append(pltpu.make_async_copy(back_ref, kept_ref, back_sem.at[0]))

    def finish(cols):
        pre_gate, pre_up = gate_sum_ref[:, cols], up_sum_ref[:, cols]
        sig = jax.nn.sigmoid(pre_gate)
        act = pre_gate * sig
        hidden_f = act * pre_up
        act_ref[:, cols] = act
        slope_ref[:, cols] = pre_up * (sig * (1.0 + pre_gate * (1.0 - sig)))
        value_ref[:, cols] = hidden_f
        hidden_ref[:, cols] = hidden_f.astype(hidden_ref.dtype)

    ahead = 2
    for copies in stages[:ahead]:
        for copy in copies:
            copy.start()
    complete = None
    for at, i in enumerate(order):
        k = i % groups
        if at > 0:
            for copy in stages[at - 1]:
                copy.wait()
            if at - 1 + ahead < len(stages):
                for copy in stages[at - 1 + ahead]:
                    copy.start()
        sum_ref = gate_sum_ref if i < groups else up_sum_ref
        for cols in spans:
            part = jnp.dot(
                x_ref[:, k * share : (k + 1) * share],
                gate_ref[:, cols] if i == 0 else held_ref[i - 1, :, cols],
                preferred_element_type=jnp.float32,
            )
            if complete is not None:
                finish(complete)
            sum_ref[:, cols] = part if k == 0 else sum_ref[:, cols] + part
            complete = cols if i == order[-1] else None
    finish(complete)


def backward_kernel(
    groups, cap, half_ref, act_ref, slope_ref, value_ref, gate_ref, held_ref, *refs
):
    parts, (out_ref, d_gate_ref, d_up_ref, rows_ref, out_sems) = refs[:groups], refs[groups:]
    share = held_ref.shape[1]
    width = groups * share
    block = tile_of(share, 512)
    half = half_ref[0]
    back = sum(part[...].astype(jnp.float32) for part in parts)
    score = jnp.sum(back * value_ref[...], axis=1, keepdims=True)
    d_gate_ref[...] = by_half(back * slope_ref[...], cap, half, True).astype(jnp.bfloat16)
    d_up_ref[...] = by_half(back * act_ref[...], cap, half, True).astype(jnp.bfloat16)
    score = by_half(jnp.broadcast_to(score, (score.shape[0], LANES)), cap, half, True)
    rows_ref[:, width:] = score.astype(rows_ref.dtype)
    outs = []

    def send(cols):
        copy = pltpu.make_async_copy(
            rows_ref.at[:, cols], out_ref.at[:, cols], out_sems.at[len(outs)]
        )
        copy.start()
        outs.append(copy)

    send(slice(width, width + LANES))
    for k in range(groups):
        for at in range(0, share, block):
            cols = slice(k * share + at, k * share + at + block)
            gate = gate_ref[at : at + block] if k == 0 else held_ref[k - 1, at : at + block]
            grad = contract_last(d_gate_ref[...], gate)
            grad += contract_last(d_up_ref[...], held_ref[groups - 1 + k, at : at + block])
            rows_ref[:, cols] = grad.astype(rows_ref.dtype)
            send(cols)
    for copy in outs:
        copy.wait()


def combine_kernel(groups, place_ref, pos_ref, gate_ref, rows_ref, tokens_ref, gates_ref):
    top, count = pos_ref.shape
    slots = rows_ref.shape[0]
    width = tokens_ref.shape[1]
    share = width // groups
    places = lax.broadcasted_iota(jnp.int32, (slots, count), 0)
    picks = [
        jnp.where(places == pos_ref[k : k + 1, :], 1.0, 0.0).astype(jnp.bfloat16)
        for k in range(top)
    ]
    both = sum(picks)
    for k in range(groups):
        at = lax.rem(place_ref[0] - k + groups, groups) * share
        tokens_ref[:, pl.ds(pl.multiple_of(at, share), share)] = contract_first(
            both, rows_ref[:, k * share : (k + 1) * share]
        ).astype(tokens_ref.dtype)
    for k in range(top):
        score = contract_first(rows_ref[:, width:], picks[k])
        gates_ref[k : k + 1, :] = score[:1, :] / gate_ref[k : k + 1, :]


def per_device(tokens, routes, gates, grad_out, w_gate, w_up, w_down):
    experts = lax.axis_size("expert")
    groups = lax.axis_size("dp")
    group = lax.axis_index("dp")
    count, width = tokens.shape
    top = routes.shape[1]
    cap = 3 * count * top // (2 * experts)
    slots = experts * cap
    share = width // groups
    hidden = w_gate.shape[2]
    params = pltpu.CompilerParams(vmem_limit_bytes=VMEM_BYTES)
    half = lax.div(lax.axis_index("expert"), experts // 2)
    place = jnp.stack([group, half]).astype(jnp.int32)
    place_group, place_half = group.reshape(1), half.reshape(1)
    halves = [list(range(experts // 2)), list(range(experts // 2, experts))]

    def shifted(value, by):
        return lax.ppermute(value, "dp", [(i, (i + by) % groups) for i in range(groups)])

    def across(value):
        pairs = [(i, (i + experts // 2) % experts) for i in range(experts)]
        return lax.ppermute(value, "expert", pairs)

    def exchanged(rows, among=None):
        count = experts if among is None else len(among[0])
        split = rows.reshape(count, rows.shape[0] // count, rows.shape[1])
        moved = lax.all_to_all(
            split, "expert", split_axis=0, concat_axis=0, axis_index_groups=among, tiled=True
        )
        return moved.reshape(rows.shape)

    def in_hbm(value):
        return pltpu.with_memory_space_constraint(value, pltpu.HBM)

    routes_t, gates_t = jnp.transpose(routes), jnp.transpose(gates)
    routes_all = [routes_t] + [shifted(routes_t, k) for k in range(1, groups)]
    gates_all = [gates_t] + [shifted(gates_t, k) for k in range(1, groups)]
    grads = [
        shifted(
            lax.dynamic_slice(grad_out, (0, lax.rem(group + k, groups) * share), (count, share)), k
        )
        for k in range(1, groups)
    ]
    any_spec = pl.BlockSpec(memory_space=pl.ANY)
    both = pl.pallas_call(
        functools.partial(stack_kernel, 4),
        out_shape=pltpu.HBM((2 * share, hidden), jnp.bfloat16),
        in_specs=[any_spec] * 2,
        out_specs=any_spec,
        scratch_shapes=[pltpu.SemaphoreType.DMA((2, 4))],
        compiler_params=params,
        name="stack",
    )(in_hbm(w_gate[0]), in_hbm(w_up[0]))
    both, gates_own = lax.optimization_barrier((both, gates_t))
    both, grads, routes_all, gates_all = lax.optimization_barrier(
        (both, grads, routes_all, gates_all)
    )
    routes_across = across(routes_t)
    tokens_sent, routes_across = lax.optimization_barrier((tokens, routes_across))
    tokens_across = across(tokens_sent)
    weights_moved = [shifted(both, k) for k in range(1, groups)]

    block = tile_of(share, 512)
    steps = share // block
    small_spec = pl.BlockSpec((top, count), lambda c, g: (0, 0))
    scaled = pl.pallas_call(
        functools.partial(dispatch_scaled, experts, cap, groups),
        out_shape=pltpu.HBM((groups * slots, share), jnp.bfloat16),
        grid_spec=pltpu.PrefetchScalarGridSpec(
            num_scalar_prefetch=1,
            grid=(steps,),
            in_specs=[small_spec] * (2 * groups)
            + [pl.BlockSpec((count, block), lambda c, g: (0, g[0] * steps + c))]
            + [pl.BlockSpec((count, block), lambda c, g: (0, c))] * (groups - 1),
            out_specs=pl.BlockSpec((groups * slots, block), lambda c, g: (0, c)),
            scratch_shapes=[
                pltpu.VMEM((groups * slots, groups * count), jnp.bfloat16),
                pltpu.VMEM((groups * slots, LANES), jnp.float32),
            ],
        ),
        compiler_params=params,
        name="dispatch_scaled",
    )(
        place_group,
        in_hbm(routes_t),
        *routes_all[1:],
        in_hbm(gates_own),
        *gates_all[1:],
        in_hbm(grad_out),
        *grads,
    )
    scaled_rows = exchanged(scaled)

    sent, pos = pl.pallas_call(
        functools.partial(dispatch_tokens, experts, cap),
        out_shape=(
            pltpu.HBM((slots, width), jnp.bfloat16),
            jax.ShapeDtypeStruct((top, count), jnp.int32),
        ),
        grid_spec=pltpu.PrefetchScalarGridSpec(
            num_scalar_prefetch=1,
            grid=(groups,),
            in_specs=[small_spec] * 2
            + [
                pl.BlockSpec(
                    (count, share), lambda k, g: (0, lax.rem(g[0] - k + groups, groups))
                )
            ]
            * 2,
            out_specs=(pl.BlockSpec((slots, share), lambda k, g: (0, k)), small_spec),
            scratch_shapes=[pltpu.VMEM((slots, 2 * count), jnp.bfloat16)],
        ),
        cost_estimate=pl.CostEstimate(
            flops=TOKENS_COST_US * 10**9, bytes_accessed=TOKENS_COST_US * 10**6, transcendentals=0
        ),
        compiler_params=params,
        name="dispatch_tokens",
    )(place, in_hbm(routes_t), routes_across, in_hbm(tokens), in_hbm(tokens_across))
    x_rows = exchanged(sent, halves)

    whole_spec = pl.BlockSpec(memory_space=pltpu.VMEM)
    *weights_moved, gate_held = pl.pallas_call(
        ready_kernel,
        out_shape=[pltpu.HBM(value.shape, value.dtype) for value in weights_moved]
        + [pltpu.VMEM((share, hidden), jnp.bfloat16)],
        in_specs=[any_spec] * groups,
        out_specs=[any_spec] * (groups - 1) + [whole_spec],
        input_output_aliases={k + 1: k for k in range(groups - 1)},
        scratch_shapes=[pltpu.SemaphoreType.DMA((2,))],
        cost_estimate=pl.CostEstimate(
            flops=READY_COST_US * 10**9, bytes_accessed=READY_COST_US * 10**6, transcendentals=0
        ),
        compiler_params=params,
        name="ready",
    )(in_hbm(w_gate[0]), *[in_hbm(value) for value in weights_moved])

    place_spec = pl.BlockSpec(memory_space=pltpu.SMEM)

    back_own, *rest = pl.pallas_call(
        functools.partial(back_kernel, groups, cap),
        out_shape=[pltpu.HBM((slots, hidden), jnp.float32)]
        + [pltpu.HBM((slots, hidden), jnp.bfloat16)] * (groups - 1)
        + [pltpu.HBM((groups * slots, share), jnp.bfloat16)],
        in_specs=[place_spec, pl.BlockSpec(), pl.BlockSpec()],
        compiler_params=params,
        name="back",
    )(place, scaled_rows, in_hbm(w_down[0]))
    scaled_all = rest[-1]
    back_parts = [shifted(rest[k - 1], -k) for k in range(1, groups)]

    *factors, hidden_own, held, back_kept = pl.pallas_call(
        functools.partial(forward_kernel, groups),
        out_shape=[pltpu.VMEM((slots, hidden), jnp.float32)] * 3
        + [
            pltpu.HBM((slots, hidden), jnp.bfloat16),
            pltpu.VMEM((2 * groups - 1, share, hidden), jnp.bfloat16),
            pltpu.VMEM((slots, hidden), jnp.float32),
        ],
        in_specs=[whole_spec] * 2 + [any_spec] * (groups + 1),
        scratch_shapes=[
            pltpu.VMEM((slots, hidden), jnp.float32),
            pltpu.VMEM((slots, hidden), jnp.float32),
            pltpu.SemaphoreType.DMA((2, 2 * groups - 1)),
            pltpu.SemaphoreType.DMA((1,)),
        ],
        compiler_params=params,
        name="forward",
    )(x_rows, gate_held, in_hbm(back_own), in_hbm(w_up[0]), *[in_hbm(w) for w in weights_moved])

    pieces = groups * (share // tile_of(share, 512))
    returning = pl.pallas_call(
        functools.partial(backward_kernel, groups, cap),
        out_shape=pltpu.HBM((slots, width + LANES), jnp.bfloat16),
        in_specs=[place_spec] + [whole_spec] * (5 + groups),
        out_specs=any_spec,
        scratch_shapes=[
            pltpu.VMEM((slots, hidden), jnp.bfloat16),
            pltpu.VMEM((slots, hidden), jnp.bfloat16),
            pltpu.VMEM((slots, width + LANES), jnp.bfloat16),
            pltpu.SemaphoreType.DMA((pieces + 1,)),
        ],
        compiler_params=params,
        name="backward",
    )(place_half, *factors, gate_held, held, back_kept, *back_parts)
    returned = exchanged(returning)

    hiddens = [hidden_own] + [shifted(hidden_own, k) for k in range(1, groups)]
    grad_down = contract_first(jnp.concatenate(hiddens, axis=0), scaled_all)[None]

    grad_tokens, grad_gates = pl.pallas_call(
        functools.partial(combine_kernel, groups),
        out_shape=(
            jax.ShapeDtypeStruct((count, width), jnp.bfloat16),
            jax.ShapeDtypeStruct((top, count), jnp.float32),
        ),
        in_specs=[pl.BlockSpec(memory_space=pltpu.SMEM)] + [whole_spec] * 3,
        compiler_params=params,
        name="combine",
    )(place_group, pos, gates_t, returned)
    return (grad_tokens, jnp.transpose(grad_gates), grad_down)


def solution(mesh):
    placed = (
        P(("dp", "expert"), None),
        P(("dp", "expert"), None),
        P(("dp", "expert"), None),
        P(("dp", "expert"), None),
        P("expert", "dp", None),
        P("expert", "dp", None),
        P("expert", None, "dp"),
    )
    return jax.shard_map(
        per_device,
        mesh=mesh,
        in_specs=placed,
        out_specs=(P(("dp", "expert"), None), P(("dp", "expert"), None), P("expert", None, "dp")),
        check_vma=False,
    )
```

```python
import functools

import jax
import jax.numpy as jnp
from jax import lax
from jax.experimental import pallas as pl
from jax.experimental.pallas import tpu as pltpu
from jax.sharding import PartitionSpec as P

LANES = 128
VMEM_BYTES = 24 * 1024 * 1024
READY_COST_US = 30
TOKENS_COST_US = 30


def contract_last(left, right):
    return lax.dot_general(
        left, right, (((1,), (1,)), ((), ())), preferred_element_type=jnp.float32
    )


def contract_first(left, right):
    return lax.dot_general(
        left, right, (((0,), (0,)), ((), ())), preferred_element_type=jnp.float32
    )


def tile_of(extent, most):
    return most if extent % most == 0 else extent


def slot_positions(routes, experts, stride, base):
    top, count = routes.shape
    labels = lax.broadcasted_iota(jnp.int32, (experts, count), 0)
    named = [labels == routes[k : k + 1, :] for k in range(top)]
    marks = sum(jnp.where(m, 1.0, 0.0) for m in named)
    earlier = lax.broadcasted_iota(jnp.int32, (count, count), 0) < lax.broadcasted_iota(
        jnp.int32, (count, count), 1
    )
    rank = jnp.dot(
        marks.astype(jnp.bfloat16),
        jnp.where(earlier, 1.0, 0.0).astype(jnp.bfloat16),
        preferred_element_type=jnp.float32,
    )
    slot = rank + (labels * stride + base + 1).astype(jnp.float32)
    return [
        jnp.sum(jnp.where(m, slot, 0.0), axis=0, keepdims=True).astype(jnp.int32) - 1
        for m in named
    ]


def by_half(value, cap, half, paired):
    count, width = value.shape
    if paired:
        value = value.reshape(count // (2 * cap), 2, cap, width)
        own, other = value[:, 0], value[:, 1]
    else:
        value = value.reshape(2, count // (2 * cap), cap, width)
        own, other = value[0], value[1]
    first = jnp.where(half == 0, own, other)
    second = jnp.where(half == 0, other, own)
    return jnp.stack([first, second], axis=0 if paired else 1).reshape(count, width)


def dispatch_tokens(experts, cap, place_ref, *refs):
    routes_refs, tokens_refs, (out_ref, pos_ref, pick_ref) = refs[:2], refs[2:4], refs[4:]
    count = tokens_refs[0].shape[0]

    @pl.when(pl.program_id(0) == 0)
    def _():
        rows = lax.broadcasted_iota(jnp.int32, (pick_ref.shape[0], count), 0)
        for c, ref in enumerate(routes_refs):
            near = ref[...] - place_ref[1] * (experts // 2)
            pos = slot_positions(near, experts // 2, 2 * cap, c * cap)
            pick_ref[:, c * count : (c + 1) * count] = sum(
                jnp.where(rows == p, 1.0, 0.0) for p in pos
            ).astype(jnp.bfloat16)
        for k, p in enumerate(slot_positions(routes_refs[0][...], experts, cap, 0)):
            pos_ref[k : k + 1, :] = p

    values = jnp.concatenate([ref[...] for ref in tokens_refs], axis=0)
    out_ref[...] = jnp.dot(
        pick_ref[...], values, preferred_element_type=jnp.float32
    ).astype(out_ref.dtype)


def dispatch_scaled(experts, cap, groups, place_ref, *refs):
    routes_refs, gate_refs = refs[:groups], refs[groups : 2 * groups]
    grad_refs, (out_ref, pick_ref, scale_ref) = refs[2 * groups : 3 * groups], refs[3 * groups :]
    count = grad_refs[0].shape[0]
    slots = out_ref.shape[0]

    @pl.when(pl.program_id(0) == 0)
    def _():
        rows = lax.broadcasted_iota(jnp.int32, (slots, count), 0)
        total = jnp.zeros((slots, 1), jnp.float32)
        for q in range(groups):
            pos = slot_positions(routes_refs[q][...], experts, groups * cap, q * cap)
            hit = jnp.zeros((slots, count), jnp.float32)
            weight = jnp.zeros((slots, count), jnp.float32)
            for k, p in enumerate(pos):
                here = rows == p
                hit = hit + jnp.where(here, 1.0, 0.0)
                weight = weight + jnp.where(here, gate_refs[q][k : k + 1, :], 0.0)
            pick_ref[:, q * count : (q + 1) * count] = hit.astype(jnp.bfloat16)
            total = total + jnp.sum(weight, axis=1, keepdims=True)
        scale_ref[...] = jnp.broadcast_to(total, scale_ref.shape)

    grads = jnp.concatenate([ref[...] for ref in grad_refs], axis=0)
    rows = jnp.dot(pick_ref[...], grads, preferred_element_type=jnp.float32)
    out_ref[...] = (scale_ref[:, :1] * rows).astype(out_ref.dtype)


def stack_kernel(pieces, top_ref, bottom_ref, out_ref, held_ref, sems):
    extent = top_ref.shape[0]
    each = extent // pieces
    moves = []
    for i, ref in enumerate((top_ref, bottom_ref)):
        for n in range(pieces):
            to = slice(i * extent + n * each, i * extent + (n + 1) * each)
            number = i * pieces + n
            load = pltpu.make_async_copy(
                ref.at[n * each : (n + 1) * each], held_ref.at[to], sems.at[0, number]
            )
            moves.append(
                (load, pltpu.make_async_copy(held_ref.at[to], out_ref.at[to], sems.at[1, number]))
            )
    for load, _ in moves:
        load.start()
    for load, store in moves:
        load.wait()
        store.start()
    for _, store in moves:
        store.wait()


def ready_kernel(gate_ref, *refs):
    held_ref, sems = refs[-2:]
    half = gate_ref.shape[0] // 2
    copies = [
        pltpu.make_async_copy(
            gate_ref.at[n * half : (n + 1) * half],
            held_ref.at[n * half : (n + 1) * half],
            sems.at[n],
        )
        for n in range(2)
    ]
    for copy in copies:
        copy.start()
    for copy in copies:
        copy.wait()


def back_kernel(groups, cap, place_ref, rows_ref, down_ref, own_ref, *rest):
    others, all_ref = rest[: groups - 1], rest[groups - 1]
    slots, hidden = own_ref.shape
    count, share = rows_ref.shape
    rows = rows_ref[...].astype(jnp.float32).reshape(count // (groups * cap), groups, cap, share)
    for q in range(groups):
        ordered = by_half(rows[:, q].reshape(slots, share), cap, place_ref[1], False)
        all_ref[q * slots : (q + 1) * slots, :] = ordered.astype(all_ref.dtype)
    step = tile_of(hidden, 256)

    @pl.loop(0, hidden // step)
    def _(j):
        cols = pl.ds(pl.multiple_of(j * step, step), step)
        for q, ref in enumerate((own_ref, *others)):
            part = contract_last(all_ref[q * slots : (q + 1) * slots, :], down_ref[cols, :])
            ref[:, cols] = part.astype(ref.dtype)


def forward_kernel(groups, x_ref, gate_ref, back_ref, own_up_ref, *refs):
    others = refs[: groups - 1]
    act_ref, slope_ref, value_ref, hidden_ref, held_ref, kept_ref = refs[groups - 1 : groups + 5]
    gate_sum_ref, up_sum_ref, sems, back_sem = refs[groups + 5 :]
    share, hidden = gate_ref.shape
    step = tile_of(hidden, 256)
    sources = [gate_ref, *[ref.at[:share] for ref in others]]
    sources += [own_up_ref, *[ref.at[share:] for ref in others]]
    spans = [slice(at, at + step) for at in range(0, hidden, step)]

    order = [i for k in range(groups) for i in (k, groups + k)]
    part_rows = share // 2
    stages = [
        [
            pltpu.make_async_copy(
                sources[i].at[n * part_rows : (n + 1) * part_rows],
                held_ref.at[i - 1, n * part_rows : (n + 1) * part_rows],
                sems.at[n, i - 1],
            )
            for n in range(2)
        ]
        for i in order[1:]
    ]
    stages[-1].append(pltpu.make_async_copy(back_ref, kept_ref, back_sem.at[0]))

    def finish(cols):
        pre_gate, pre_up = gate_sum_ref[:, cols], up_sum_ref[:, cols]
        sig = jax.nn.sigmoid(pre_gate)
        act = pre_gate * sig
        hidden_f = act * pre_up
        act_ref[:, cols] = act
        slope_ref[:, cols] = pre_up * (sig * (1.0 + pre_gate * (1.0 - sig)))
        value_ref[:, cols] = hidden_f
        hidden_ref[:, cols] = hidden_f.astype(hidden_ref.dtype)

    ahead = 2
    for copies in stages[:ahead]:
        for copy in copies:
            copy.start()
    complete = None
    for at, i in enumerate(order):
        k = i % groups
        if at > 0:
            for copy in stages[at - 1]:
                copy.wait()
            if at - 1 + ahead < len(stages):
                for copy in stages[at - 1 + ahead]:
                    copy.start()
        sum_ref = gate_sum_ref if i < groups else up_sum_ref
        for cols in spans:
            part = jnp.dot(
                x_ref[:, k * share : (k + 1) * share],
                gate_ref[:, cols] if i == 0 else held_ref[i - 1, :, cols],
                preferred_element_type=jnp.float32,
            )
            if complete is not None:
                finish(complete)
            sum_ref[:, cols] = part if k == 0 else sum_ref[:, cols] + part
            complete = cols if i == order[-1] else None
    finish(complete)


def backward_kernel(
    groups, cap, half_ref, act_ref, slope_ref, value_ref, gate_ref, held_ref, *refs
):
    parts, (out_ref, d_gate_ref, d_up_ref, rows_ref, out_sems) = refs[:groups], refs[groups:]
    share = held_ref.shape[1]
    width = groups * share
    block = tile_of(share, 512)
    half = half_ref[0]
    back = sum(part[...].astype(jnp.float32) for part in parts)
    score = jnp.sum(back * value_ref[...], axis=1, keepdims=True)
    d_gate_ref[...] = by_half(back * slope_ref[...], cap, half, True).astype(jnp.bfloat16)
    d_up_ref[...] = by_half(back * act_ref[...], cap, half, True).astype(jnp.bfloat16)
    score = by_half(jnp.broadcast_to(score, (score.shape[0], LANES)), cap, half, True)
    rows_ref[:, width:] = score.astype(rows_ref.dtype)
    outs = []

    def send(cols):
        copy = pltpu.make_async_copy(
            rows_ref.at[:, cols], out_ref.at[:, cols], out_sems.at[len(outs)]
        )
        copy.start()
        outs.append(copy)

    send(slice(width, width + LANES))
    for k in range(groups):
        for at in range(0, share, block):
            cols = slice(k * share + at, k * share + at + block)
            gate = gate_ref[at : at + block] if k == 0 else held_ref[k - 1, at : at + block]
            grad = contract_last(d_gate_ref[...], gate)
            grad += contract_last(d_up_ref[...], held_ref[groups - 1 + k, at : at + block])
            rows_ref[:, cols] = grad.astype(rows_ref.dtype)
            send(cols)
    for copy in outs:
        copy.wait()


def combine_kernel(groups, place_ref, pos_ref, gate_ref, rows_ref, tokens_ref, gates_ref):
    top, count = pos_ref.shape
    slots = rows_ref.shape[0]
    width = tokens_ref.shape[1]
    share = width // groups
    places = lax.broadcasted_iota(jnp.int32, (slots, count), 0)
    picks = [
        jnp.where(places == pos_ref[k : k + 1, :], 1.0, 0.0).astype(jnp.bfloat16)
        for k in range(top)
    ]
    both = sum(picks)
    for k in range(groups):
        at = lax.rem(place_ref[0] - k + groups, groups) * share
        tokens_ref[:, pl.ds(pl.multiple_of(at, share), share)] = contract_first(
            both, rows_ref[:, k * share : (k + 1) * share]
        ).astype(tokens_ref.dtype)
    for k in range(top):
        score = contract_first(rows_ref[:, width:], picks[k])
        gates_ref[k : k + 1, :] = score[:1, :] / gate_ref[k : k + 1, :]


def per_device(tokens, routes, gates, grad_out, w_gate, w_up, w_down):
    experts = lax.axis_size("expert")
    groups = lax.axis_size("dp")
    group = lax.axis_index("dp")
    count, width = tokens.shape
    top = routes.shape[1]
    cap = 3 * count * top // (2 * experts)
    slots = experts * cap
    share = width // groups
    hidden = w_gate.shape[2]
    params = pltpu.CompilerParams(vmem_limit_bytes=VMEM_BYTES)
    half = lax.div(lax.axis_index("expert"), experts // 2)
    place = jnp.stack([group, half]).astype(jnp.int32)
    place_group, place_half = group.reshape(1), half.reshape(1)
    halves = [list(range(experts // 2)), list(range(experts // 2, experts))]

    def shifted(value, by):
        return lax.ppermute(value, "dp", [(i, (i + by) % groups) for i in range(groups)])

    def across(value):
        pairs = [(i, (i + experts // 2) % experts) for i in range(experts)]
        return lax.ppermute(value, "expert", pairs)

    def exchanged(rows, among=None):
        count = experts if among is None else len(among[0])
        split = rows.reshape(count, rows.shape[0] // count, rows.shape[1])
        moved = lax.all_to_all(
            split, "expert", split_axis=0, concat_axis=0, axis_index_groups=among, tiled=True
        )
        return moved.reshape(rows.shape)

    def in_hbm(value):
        return pltpu.with_memory_space_constraint(value, pltpu.HBM)

    routes_t, gates_t = jnp.transpose(routes), jnp.transpose(gates)
    routes_all = [routes_t] + [shifted(routes_t, k) for k in range(1, groups)]
    gates_all = [gates_t] + [shifted(gates_t, k) for k in range(1, groups)]
    grads = [
        shifted(
            lax.dynamic_slice(grad_out, (0, lax.rem(group + k, groups) * share), (count, share)), k
        )
        for k in range(1, groups)
    ]
    any_spec = pl.BlockSpec(memory_space=pl.ANY)
    both = pl.pallas_call(
        functools.partial(stack_kernel, 4),
        out_shape=pltpu.HBM((2 * share, hidden), jnp.bfloat16),
        in_specs=[any_spec] * 2,
        out_specs=any_spec,
        scratch_shapes=[
            pltpu.VMEM((2 * share, hidden), jnp.bfloat16),
            pltpu.SemaphoreType.DMA((2, 8)),
        ],
        compiler_params=params,
        name="stack",
    )(in_hbm(w_gate[0]), in_hbm(w_up[0]))
    both, gates_own = lax.optimization_barrier((both, gates_t))
    both, grads, routes_all, gates_all = lax.optimization_barrier(
        (both, grads, routes_all, gates_all)
    )
    routes_across = across(routes_t)
    tokens_sent, routes_across = lax.optimization_barrier((tokens, routes_across))
    tokens_across = across(tokens_sent)
    weights_moved = [shifted(both, k) for k in range(1, groups)]

    block = tile_of(share, 512)
    steps = share // block
    small_spec = pl.BlockSpec((top, count), lambda c, g: (0, 0))
    scaled = pl.pallas_call(
        functools.partial(dispatch_scaled, experts, cap, groups),
        out_shape=pltpu.HBM((groups * slots, share), jnp.bfloat16),
        grid_spec=pltpu.PrefetchScalarGridSpec(
            num_scalar_prefetch=1,
            grid=(steps,),
            in_specs=[small_spec] * (2 * groups)
            + [pl.BlockSpec((count, block), lambda c, g: (0, g[0] * steps + c))]
            + [pl.BlockSpec((count, block), lambda c, g: (0, c))] * (groups - 1),
            out_specs=pl.BlockSpec((groups * slots, block), lambda c, g: (0, c)),
            scratch_shapes=[
                pltpu.VMEM((groups * slots, groups * count), jnp.bfloat16),
                pltpu.VMEM((groups * slots, LANES), jnp.float32),
            ],
        ),
        compiler_params=params,
        name="dispatch_scaled",
    )(
        place_group,
        in_hbm(routes_t),
        *routes_all[1:],
        in_hbm(gates_own),
        *gates_all[1:],
        in_hbm(grad_out),
        *grads,
    )
    scaled_rows = exchanged(scaled)

    sent, pos = pl.pallas_call(
        functools.partial(dispatch_tokens, experts, cap),
        out_shape=(
            pltpu.HBM((slots, width), jnp.bfloat16),
            jax.ShapeDtypeStruct((top, count), jnp.int32),
        ),
        grid_spec=pltpu.PrefetchScalarGridSpec(
            num_scalar_prefetch=1,
            grid=(groups,),
            in_specs=[small_spec] * 2
            + [
                pl.BlockSpec(
                    (count, share), lambda k, g: (0, lax.rem(g[0] - k + groups, groups))
                )
            ]
            * 2,
            out_specs=(pl.BlockSpec((slots, share), lambda k, g: (0, k)), small_spec),
            scratch_shapes=[pltpu.VMEM((slots, 2 * count), jnp.bfloat16)],
        ),
        cost_estimate=pl.CostEstimate(
            flops=TOKENS_COST_US * 10**9, bytes_accessed=TOKENS_COST_US * 10**6, transcendentals=0
        ),
        compiler_params=params,
        name="dispatch_tokens",
    )(place, in_hbm(routes_t), routes_across, in_hbm(tokens), in_hbm(tokens_across))
    x_rows = exchanged(sent, halves)

    whole_spec = pl.BlockSpec(memory_space=pltpu.VMEM)
    *weights_moved, gate_held = pl.pallas_call(
        ready_kernel,
        out_shape=[pltpu.HBM(value.shape, value.dtype) for value in weights_moved]
        + [pltpu.VMEM((share, hidden), jnp.bfloat16)],
        in_specs=[any_spec] * groups,
        out_specs=[any_spec] * (groups - 1) + [whole_spec],
        input_output_aliases={k + 1: k for k in range(groups - 1)},
        scratch_shapes=[pltpu.SemaphoreType.DMA((2,))],
        cost_estimate=pl.CostEstimate(
            flops=READY_COST_US * 10**9, bytes_accessed=READY_COST_US * 10**6, transcendentals=0
        ),
        compiler_params=params,
        name="ready",
    )(in_hbm(w_gate[0]), *[in_hbm(value) for value in weights_moved])

    place_spec = pl.BlockSpec(memory_space=pltpu.SMEM)

    back_own, *rest = pl.pallas_call(
        functools.partial(back_kernel, groups, cap),
        out_shape=[pltpu.HBM((slots, hidden), jnp.float32)]
        + [pltpu.HBM((slots, hidden), jnp.bfloat16)] * (groups - 1)
        + [pltpu.HBM((groups * slots, share), jnp.bfloat16)],
        in_specs=[place_spec, pl.BlockSpec(), pl.BlockSpec()],
        compiler_params=params,
        name="back",
    )(place, scaled_rows, in_hbm(w_down[0]))
    scaled_all = rest[-1]
    back_parts = [shifted(rest[k - 1], -k) for k in range(1, groups)]

    *factors, hidden_own, held, back_kept = pl.pallas_call(
        functools.partial(forward_kernel, groups),
        out_shape=[pltpu.VMEM((slots, hidden), jnp.float32)] * 3
        + [
            pltpu.HBM((slots, hidden), jnp.bfloat16),
            pltpu.VMEM((2 * groups - 1, share, hidden), jnp.bfloat16),
            pltpu.VMEM((slots, hidden), jnp.float32),
        ],
        in_specs=[whole_spec] * 2 + [any_spec] * (groups + 1),
        scratch_shapes=[
            pltpu.VMEM((slots, hidden), jnp.float32),
            pltpu.VMEM((slots, hidden), jnp.float32),
            pltpu.SemaphoreType.DMA((2, 2 * groups - 1)),
            pltpu.SemaphoreType.DMA((1,)),
        ],
        compiler_params=params,
        name="forward",
    )(x_rows, gate_held, in_hbm(back_own), in_hbm(w_up[0]), *[in_hbm(w) for w in weights_moved])

    pieces = groups * (share // tile_of(share, 512))
    returning = pl.pallas_call(
        functools.partial(backward_kernel, groups, cap),
        out_shape=pltpu.HBM((slots, width + LANES), jnp.bfloat16),
        in_specs=[place_spec] + [whole_spec] * (5 + groups),
        out_specs=any_spec,
        scratch_shapes=[
            pltpu.VMEM((slots, hidden), jnp.bfloat16),
            pltpu.VMEM((slots, hidden), jnp.bfloat16),
            pltpu.VMEM((slots, width + LANES), jnp.bfloat16),
            pltpu.SemaphoreType.DMA((pieces + 1,)),
        ],
        compiler_params=params,
        name="backward",
    )(place_half, *factors, gate_held, held, back_kept, *back_parts)
    returned = exchanged(returning)

    hiddens = [hidden_own] + [shifted(hidden_own, k) for k in range(1, groups)]
    grad_down = contract_first(jnp.concatenate(hiddens, axis=0), scaled_all)[None]

    grad_tokens, grad_gates = pl.pallas_call(
        functools.partial(combine_kernel, groups),
        out_shape=(
            jax.ShapeDtypeStruct((count, width), jnp.bfloat16),
            jax.ShapeDtypeStruct((top, count), jnp.float32),
        ),
        in_specs=[pl.BlockSpec(memory_space=pltpu.SMEM)] + [whole_spec] * 3,
        compiler_params=params,
        name="combine",
    )(place_group, pos, gates_t, returned)
    return (grad_tokens, jnp.transpose(grad_gates), grad_down)


def solution(mesh):
    placed = (
        P(("dp", "expert"), None),
        P(("dp", "expert"), None),
        P(("dp", "expert"), None),
        P(("dp", "expert"), None),
        P("expert", "dp", None),
        P("expert", "dp", None),
        P("expert", None, "dp"),
    )
    return jax.shard_map(
        per_device,
        mesh=mesh,
        in_specs=placed,
        out_specs=(P(("dp", "expert"), None), P(("dp", "expert"), None), P("expert", None, "dp")),
        check_vma=False,
    )
```

```python
import functools

import jax
import jax.numpy as jnp
from jax import lax
from jax.experimental import pallas as pl
from jax.experimental.pallas import tpu as pltpu
from jax.sharding import PartitionSpec as P

LANES = 128
VMEM_BYTES = 24 * 1024 * 1024
READY_COST_US = 30
TOKENS_COST_US = 30


def contract_last(left, right):
    return lax.dot_general(
        left, right, (((1,), (1,)), ((), ())), preferred_element_type=jnp.float32
    )


def contract_first(left, right):
    return lax.dot_general(
        left, right, (((0,), (0,)), ((), ())), preferred_element_type=jnp.float32
    )


def tile_of(extent, most):
    return most if extent % most == 0 else extent


def slot_positions(routes, experts, stride, base):
    top, count = routes.shape
    labels = lax.broadcasted_iota(jnp.int32, (experts, count), 0)
    named = [labels == routes[k : k + 1, :] for k in range(top)]
    marks = sum(jnp.where(m, 1.0, 0.0) for m in named)
    earlier = lax.broadcasted_iota(jnp.int32, (count, count), 0) < lax.broadcasted_iota(
        jnp.int32, (count, count), 1
    )
    rank = jnp.dot(
        marks.astype(jnp.bfloat16),
        jnp.where(earlier, 1.0, 0.0).astype(jnp.bfloat16),
        preferred_element_type=jnp.float32,
    )
    slot = rank + (labels * stride + base + 1).astype(jnp.float32)
    return [
        jnp.sum(jnp.where(m, slot, 0.0), axis=0, keepdims=True).astype(jnp.int32) - 1
        for m in named
    ]


def by_half(value, cap, half, paired):
    count, width = value.shape
    if paired:
        value = value.reshape(count // (2 * cap), 2, cap, width)
        own, other = value[:, 0], value[:, 1]
    else:
        value = value.reshape(2, count // (2 * cap), cap, width)
        own, other = value[0], value[1]
    first = jnp.where(half == 0, own, other)
    second = jnp.where(half == 0, other, own)
    return jnp.stack([first, second], axis=0 if paired else 1).reshape(count, width)


def dispatch_tokens(experts, cap, place_ref, *refs):
    routes_refs, tokens_refs, (out_ref, pos_ref, pick_ref) = refs[:2], refs[2:4], refs[4:]
    count = tokens_refs[0].shape[0]

    @pl.when(pl.program_id(0) == 0)
    def _():
        rows = lax.broadcasted_iota(jnp.int32, (pick_ref.shape[0], count), 0)
        for c, ref in enumerate(routes_refs):
            near = ref[...] - place_ref[1] * (experts // 2)
            pos = slot_positions(near, experts // 2, 2 * cap, c * cap)
            pick_ref[:, c * count : (c + 1) * count] = sum(
                jnp.where(rows == p, 1.0, 0.0) for p in pos
            ).astype(jnp.bfloat16)
        for k, p in enumerate(slot_positions(routes_refs[0][...], experts, cap, 0)):
            pos_ref[k : k + 1, :] = p

    values = jnp.concatenate([ref[...] for ref in tokens_refs], axis=0)
    out_ref[...] = jnp.dot(
        pick_ref[...], values, preferred_element_type=jnp.float32
    ).astype(out_ref.dtype)


def dispatch_scaled(experts, cap, groups, place_ref, *refs):
    routes_refs, gate_refs = refs[:groups], refs[groups : 2 * groups]
    grad_refs, (out_ref, pick_ref, scale_ref) = refs[2 * groups : 3 * groups], refs[3 * groups :]
    count = grad_refs[0].shape[0]
    slots = out_ref.shape[0]

    @pl.when(pl.program_id(0) == 0)
    def _():
        rows = lax.broadcasted_iota(jnp.int32, (slots, count), 0)
        total = jnp.zeros((slots, 1), jnp.float32)
        for q in range(groups):
            pos = slot_positions(routes_refs[q][...], experts, groups * cap, q * cap)
            hit = jnp.zeros((slots, count), jnp.float32)
            weight = jnp.zeros((slots, count), jnp.float32)
            for k, p in enumerate(pos):
                here = rows == p
                hit = hit + jnp.where(here, 1.0, 0.0)
                weight = weight + jnp.where(here, gate_refs[q][k : k + 1, :], 0.0)
            pick_ref[:, q * count : (q + 1) * count] = hit.astype(jnp.bfloat16)
            total = total + jnp.sum(weight, axis=1, keepdims=True)
        scale_ref[...] = jnp.broadcast_to(total, scale_ref.shape)

    grads = jnp.concatenate([ref[...] for ref in grad_refs], axis=0)
    rows = jnp.dot(pick_ref[...], grads, preferred_element_type=jnp.float32)
    out_ref[...] = (scale_ref[:, :1] * rows).astype(out_ref.dtype)


def stack_kernel(pieces, top_ref, bottom_ref, out_ref, held_ref, sems):
    extent = top_ref.shape[0]
    each = extent // pieces
    moves = []
    for i, ref in enumerate((top_ref, bottom_ref)):
        for n in range(pieces):
            to = slice(i * extent + n * each, i * extent + (n + 1) * each)
            number = i * pieces + n
            load = pltpu.make_async_copy(
                ref.at[n * each : (n + 1) * each], held_ref.at[to], sems.at[0, number]
            )
            moves.append(
                (load, pltpu.make_async_copy(held_ref.at[to], out_ref.at[to], sems.at[1, number]))
            )
    for load, _ in moves:
        load.start()
    for load, store in moves:
        load.wait()
        store.start()
    for _, store in moves:
        store.wait()


def ready_kernel(gate_ref, *refs):
    held_ref, sems = refs[-2:]
    half = gate_ref.shape[0] // 2
    copies = [
        pltpu.make_async_copy(
            gate_ref.at[n * half : (n + 1) * half],
            held_ref.at[n * half : (n + 1) * half],
            sems.at[n],
        )
        for n in range(2)
    ]
    for copy in copies:
        copy.start()
    for copy in copies:
        copy.wait()


def back_kernel(groups, cap, place_ref, rows_ref, down_ref, own_ref, *rest):
    others, all_ref = rest[: groups - 1], rest[groups - 1]
    slots, hidden = own_ref.shape
    count, share = rows_ref.shape
    rows = rows_ref[...].astype(jnp.float32).reshape(count // (groups * cap), groups, cap, share)
    for q in range(groups):
        ordered = by_half(rows[:, q].reshape(slots, share), cap, place_ref[1], False)
        all_ref[q * slots : (q + 1) * slots, :] = ordered.astype(all_ref.dtype)
    step = tile_of(hidden, 256)

    @pl.loop(0, hidden // step)
    def _(j):
        cols = pl.ds(pl.multiple_of(j * step, step), step)
        for q, ref in enumerate((own_ref, *others)):
            part = contract_last(all_ref[q * slots : (q + 1) * slots, :], down_ref[cols, :])
            ref[:, cols] = part.astype(ref.dtype)


def forward_kernel(groups, x_ref, gate_ref, back_ref, own_up_ref, *refs):
    others = refs[: groups - 1]
    act_ref, slope_ref, value_ref, hidden_ref, held_ref, kept_ref = refs[groups - 1 : groups + 5]
    gate_sum_ref, up_sum_ref, sems, back_sem = refs[groups + 5 :]
    share, hidden = gate_ref.shape
    step = tile_of(hidden, 256)
    sources = [gate_ref, *[ref.at[:share] for ref in others]]
    sources += [own_up_ref, *[ref.at[share:] for ref in others]]
    spans = [slice(at, at + step) for at in range(0, hidden, step)]

    order = [i for k in range(groups) for i in (k, groups + k)]
    part_rows = share // 2
    stages = [
        [
            pltpu.make_async_copy(
                sources[i].at[n * part_rows : (n + 1) * part_rows],
                held_ref.at[i - 1, n * part_rows : (n + 1) * part_rows],
                sems.at[n, i - 1],
            )
            for n in range(2)
        ]
        for i in order[1:]
    ]
    stages[-1].append(pltpu.make_async_copy(back_ref, kept_ref, back_sem.at[0]))

    def finish(cols):
        pre_gate, pre_up = gate_sum_ref[:, cols], up_sum_ref[:, cols]
        sig = jax.nn.sigmoid(pre_gate)
        act = pre_gate * sig
        hidden_f = act * pre_up
        act_ref[:, cols] = act
        slope_ref[:, cols] = pre_up * (sig * (1.0 + pre_gate * (1.0 - sig)))
        value_ref[:, cols] = hidden_f
        hidden_ref[:, cols] = hidden_f.astype(hidden_ref.dtype)

    ahead = 2
    for copies in stages[:ahead]:
        for copy in copies:
            copy.start()
    complete = None
    for at, i in enumerate(order):
        k = i % groups
        if at > 0:
            for copy in stages[at - 1]:
                copy.wait()
            if at - 1 + ahead < len(stages):
                for copy in stages[at - 1 + ahead]:
                    copy.start()
        sum_ref = gate_sum_ref if i < groups else up_sum_ref
        for cols in spans:
            part = jnp.dot(
                x_ref[:, k * share : (k + 1) * share],
                gate_ref[:, cols] if i == 0 else held_ref[i - 1, :, cols],
                preferred_element_type=jnp.float32,
            )
            if complete is not None:
                finish(complete)
            sum_ref[:, cols] = part if k == 0 else sum_ref[:, cols] + part
            complete = cols if i == order[-1] else None
    finish(complete)


def backward_kernel(
    groups, cap, half_ref, act_ref, slope_ref, value_ref, gate_ref, held_ref, *refs
):
    kept_ref, others = refs[0], refs[1:groups]
    out_ref, d_gate_ref, d_up_ref, rows_ref, other_ref, out_sems, other_sems = refs[groups:]
    share = held_ref.shape[1]
    width = groups * share
    block = tile_of(share, 512)
    half = half_ref[0]
    pieces = other_sems.shape[1]
    each = kept_ref.shape[0] // pieces
    copies = [
        pltpu.make_async_copy(
            ref.at[n * each : (n + 1) * each],
            other_ref.at[k, n * each : (n + 1) * each],
            other_sems.at[k, n],
        )
        for k, ref in enumerate(others)
        for n in range(pieces)
    ]
    for copy in copies:
        copy.start()
    for copy in copies:
        copy.wait()
    back = kept_ref[...]
    for k in range(groups - 1):
        back += other_ref[k].astype(jnp.float32)
    score = jnp.sum(back * value_ref[...], axis=1, keepdims=True)
    d_gate_ref[...] = by_half(back * slope_ref[...], cap, half, True).astype(jnp.bfloat16)
    d_up_ref[...] = by_half(back * act_ref[...], cap, half, True).astype(jnp.bfloat16)
    score = by_half(jnp.broadcast_to(score, (score.shape[0], LANES)), cap, half, True)
    rows_ref[:, width:] = score.astype(rows_ref.dtype)
    outs = []

    def send(cols):
        copy = pltpu.make_async_copy(
            rows_ref.at[:, cols], out_ref.at[:, cols], out_sems.at[len(outs)]
        )
        copy.start()
        outs.append(copy)

    send(slice(width, width + LANES))
    for k in range(groups):
        for at in range(0, share, block):
            cols = slice(k * share + at, k * share + at + block)
            gate = gate_ref[at : at + block] if k == 0 else held_ref[k - 1, at : at + block]
            grad = contract_last(d_gate_ref[...], gate)
            grad += contract_last(d_up_ref[...], held_ref[groups - 1 + k, at : at + block])
            rows_ref[:, cols] = grad.astype(rows_ref.dtype)
            send(cols)
    for copy in outs:
        copy.wait()


def combine_kernel(groups, place_ref, pos_ref, gate_ref, rows_ref, tokens_ref, gates_ref):
    top, count = pos_ref.shape
    slots = rows_ref.shape[0]
    width = tokens_ref.shape[1]
    share = width // groups
    places = lax.broadcasted_iota(jnp.int32, (slots, count), 0)
    picks = [
        jnp.where(places == pos_ref[k : k + 1, :], 1.0, 0.0).astype(jnp.bfloat16)
        for k in range(top)
    ]
    both = sum(picks)
    for k in range(groups):
        at = lax.rem(place_ref[0] - k + groups, groups) * share
        tokens_ref[:, pl.ds(pl.multiple_of(at, share), share)] = contract_first(
            both, rows_ref[:, k * share : (k + 1) * share]
        ).astype(tokens_ref.dtype)
    for k in range(top):
        score = contract_first(rows_ref[:, width:], picks[k])
        gates_ref[k : k + 1, :] = score[:1, :] / gate_ref[k : k + 1, :]


def per_device(tokens, routes, gates, grad_out, w_gate, w_up, w_down):
    experts = lax.axis_size("expert")
    groups = lax.axis_size("dp")
    group = lax.axis_index("dp")
    count, width = tokens.shape
    top = routes.shape[1]
    cap = 3 * count * top // (2 * experts)
    slots = experts * cap
    share = width // groups
    hidden = w_gate.shape[2]
    params = pltpu.CompilerParams(vmem_limit_bytes=VMEM_BYTES)
    half = lax.div(lax.axis_index("expert"), experts // 2)
    place = jnp.stack([group, half]).astype(jnp.int32)
    place_group, place_half = group.reshape(1), half.reshape(1)
    halves = [list(range(experts // 2)), list(range(experts // 2, experts))]

    def shifted(value, by):
        return lax.ppermute(value, "dp", [(i, (i + by) % groups) for i in range(groups)])

    def across(value):
        pairs = [(i, (i + experts // 2) % experts) for i in range(experts)]
        return lax.ppermute(value, "expert", pairs)

    def exchanged(rows, among=None):
        count = experts if among is None else len(among[0])
        split = rows.reshape(count, rows.shape[0] // count, rows.shape[1])
        moved = lax.all_to_all(
            split, "expert", split_axis=0, concat_axis=0, axis_index_groups=among, tiled=True
        )
        return moved.reshape(rows.shape)

    def in_hbm(value):
        return pltpu.with_memory_space_constraint(value, pltpu.HBM)

    routes_t, gates_t = jnp.transpose(routes), jnp.transpose(gates)
    routes_all = [routes_t] + [shifted(routes_t, k) for k in range(1, groups)]
    gates_all = [gates_t] + [shifted(gates_t, k) for k in range(1, groups)]
    grads = [
        shifted(
            lax.dynamic_slice(grad_out, (0, lax.rem(group + k, groups) * share), (count, share)), k
        )
        for k in range(1, groups)
    ]
    any_spec = pl.BlockSpec(memory_space=pl.ANY)
    both = pl.pallas_call(
        functools.partial(stack_kernel, 4),
        out_shape=pltpu.HBM((2 * share, hidden), jnp.bfloat16),
        in_specs=[any_spec] * 2,
        out_specs=any_spec,
        scratch_shapes=[
            pltpu.VMEM((2 * share, hidden), jnp.bfloat16),
            pltpu.SemaphoreType.DMA((2, 8)),
        ],
        compiler_params=params,
        name="stack",
    )(in_hbm(w_gate[0]), in_hbm(w_up[0]))
    both, gates_own = lax.optimization_barrier((both, gates_t))
    routes_across = across(routes_t)
    tokens_sent, routes_across, both = lax.optimization_barrier((tokens, routes_across, both))
    tokens_across = across(tokens_sent)
    both, grads, routes_all, gates_all = lax.optimization_barrier(
        (both, grads, routes_all, gates_all)
    )
    weights_moved = [shifted(both, k) for k in range(1, groups)]

    block = tile_of(share, 256)
    steps = share // block
    small_spec = pl.BlockSpec((top, count), lambda c, g: (0, 0))
    scaled = pl.pallas_call(
        functools.partial(dispatch_scaled, experts, cap, groups),
        out_shape=pltpu.HBM((groups * slots, share), jnp.bfloat16),
        grid_spec=pltpu.PrefetchScalarGridSpec(
            num_scalar_prefetch=1,
            grid=(steps,),
            in_specs=[small_spec] * (2 * groups)
            + [pl.BlockSpec((count, block), lambda c, g: (0, g[0] * steps + c))]
            + [pl.BlockSpec((count, block), lambda c, g: (0, c))] * (groups - 1),
            out_specs=pl.BlockSpec((groups * slots, block), lambda c, g: (0, c)),
            scratch_shapes=[
                pltpu.VMEM((groups * slots, groups * count), jnp.bfloat16),
                pltpu.VMEM((groups * slots, LANES), jnp.float32),
            ],
        ),
        compiler_params=params,
        name="dispatch_scaled",
    )(
        place_group,
        in_hbm(routes_t),
        *routes_all[1:],
        in_hbm(gates_own),
        *gates_all[1:],
        in_hbm(grad_out),
        *grads,
    )
    scaled_rows = exchanged(scaled)

    sent, pos = pl.pallas_call(
        functools.partial(dispatch_tokens, experts, cap),
        out_shape=(
            pltpu.HBM((slots, width), jnp.bfloat16),
            jax.ShapeDtypeStruct((top, count), jnp.int32),
        ),
        grid_spec=pltpu.PrefetchScalarGridSpec(
            num_scalar_prefetch=1,
            grid=(groups,),
            in_specs=[small_spec] * 2
            + [
                pl.BlockSpec(
                    (count, share), lambda k, g: (0, lax.rem(g[0] - k + groups, groups))
                )
            ]
            * 2,
            out_specs=(pl.BlockSpec((slots, share), lambda k, g: (0, k)), small_spec),
            scratch_shapes=[pltpu.VMEM((slots, 2 * count), jnp.bfloat16)],
        ),
        cost_estimate=pl.CostEstimate(
            flops=TOKENS_COST_US * 10**9, bytes_accessed=TOKENS_COST_US * 10**6, transcendentals=0
        ),
        compiler_params=params,
        name="dispatch_tokens",
    )(place, in_hbm(routes_t), routes_across, in_hbm(tokens), in_hbm(tokens_across))
    x_rows = exchanged(sent, halves)

    whole_spec = pl.BlockSpec(memory_space=pltpu.VMEM)
    *weights_moved, gate_held = pl.pallas_call(
        ready_kernel,
        out_shape=[pltpu.HBM(value.shape, value.dtype) for value in weights_moved]
        + [pltpu.VMEM((share, hidden), jnp.bfloat16)],
        in_specs=[any_spec] * groups,
        out_specs=[any_spec] * (groups - 1) + [whole_spec],
        input_output_aliases={k + 1: k for k in range(groups - 1)},
        scratch_shapes=[pltpu.SemaphoreType.DMA((2,))],
        cost_estimate=pl.CostEstimate(
            flops=READY_COST_US * 10**9, bytes_accessed=READY_COST_US * 10**6, transcendentals=0
        ),
        compiler_params=params,
        name="ready",
    )(in_hbm(w_gate[0]), *[in_hbm(value) for value in weights_moved])

    place_spec = pl.BlockSpec(memory_space=pltpu.SMEM)

    back_own, *rest = pl.pallas_call(
        functools.partial(back_kernel, groups, cap),
        out_shape=[pltpu.HBM((slots, hidden), jnp.float32)]
        + [pltpu.HBM((slots, hidden), jnp.bfloat16)] * (groups - 1)
        + [pltpu.HBM((groups * slots, share), jnp.bfloat16)],
        in_specs=[place_spec, pl.BlockSpec(), pl.BlockSpec()],
        compiler_params=params,
        name="back",
    )(place, scaled_rows, in_hbm(w_down[0]))
    scaled_all = rest[-1]
    back_parts = [shifted(rest[k - 1], -k) for k in range(1, groups)]

    *factors, hidden_own, held, back_kept = pl.pallas_call(
        functools.partial(forward_kernel, groups),
        out_shape=[pltpu.VMEM((slots, hidden), jnp.float32)] * 3
        + [
            pltpu.HBM((slots, hidden), jnp.bfloat16),
            pltpu.VMEM((2 * groups - 1, share, hidden), jnp.bfloat16),
            pltpu.VMEM((slots, hidden), jnp.float32),
        ],
        in_specs=[whole_spec] * 2 + [any_spec] * (groups + 1),
        scratch_shapes=[
            pltpu.VMEM((slots, hidden), jnp.float32),
            pltpu.VMEM((slots, hidden), jnp.float32),
            pltpu.SemaphoreType.DMA((2, 2 * groups - 1)),
            pltpu.SemaphoreType.DMA((1,)),
        ],
        compiler_params=params,
        name="forward",
    )(x_rows, gate_held, in_hbm(back_own), in_hbm(w_up[0]), *[in_hbm(w) for w in weights_moved])

    pieces = groups * (share // tile_of(share, 512))
    returning = pl.pallas_call(
        functools.partial(backward_kernel, groups, cap),
        out_shape=pltpu.HBM((slots, width + LANES), jnp.bfloat16),
        in_specs=[place_spec] + [whole_spec] * 6 + [any_spec] * (groups - 1),
        out_specs=any_spec,
        scratch_shapes=[
            pltpu.VMEM((slots, hidden), jnp.bfloat16),
            pltpu.VMEM((slots, hidden), jnp.bfloat16),
            pltpu.VMEM((slots, width + LANES), jnp.bfloat16),
            pltpu.VMEM((groups - 1, slots, hidden), jnp.bfloat16),
            pltpu.SemaphoreType.DMA((pieces + 1,)),
            pltpu.SemaphoreType.DMA((groups - 1, 4)),
        ],
        compiler_params=params,
        name="backward",
    )(place_half, *factors, gate_held, held, back_kept, *[in_hbm(p) for p in back_parts])
    returned = exchanged(returning)

    hiddens = [hidden_own] + [shifted(hidden_own, k) for k in range(1, groups)]
    grad_down = contract_first(jnp.concatenate(hiddens, axis=0), scaled_all)[None]

    grad_tokens, grad_gates = pl.pallas_call(
        functools.partial(combine_kernel, groups),
        out_shape=(
            jax.ShapeDtypeStruct((count, width), jnp.bfloat16),
            jax.ShapeDtypeStruct((top, count), jnp.float32),
        ),
        in_specs=[pl.BlockSpec(memory_space=pltpu.SMEM)] + [whole_spec] * 3,
        compiler_params=params,
        name="combine",
    )(place_group, pos, gates_t, returned)
    return (grad_tokens, jnp.transpose(grad_gates), grad_down)


def solution(mesh):
    placed = (
        P(("dp", "expert"), None),
        P(("dp", "expert"), None),
        P(("dp", "expert"), None),
        P(("dp", "expert"), None),
        P("expert", "dp", None),
        P("expert", "dp", None),
        P("expert", None, "dp"),
    )
    return jax.shard_map(
        per_device,
        mesh=mesh,
        in_specs=placed,
        out_specs=(P(("dp", "expert"), None), P(("dp", "expert"), None), P("expert", None, "dp")),
        check_vma=False,
    )
```

```python
import functools

import jax
import jax.numpy as jnp
from jax import lax
from jax.experimental import pallas as pl
from jax.experimental.pallas import tpu as pltpu
from jax.sharding import PartitionSpec as P

LANES = 128
VMEM_BYTES = 24 * 1024 * 1024
READY_COST_US = 30
TOKENS_COST_US = 30


def contract_last(left, right):
    return lax.dot_general(
        left, right, (((1,), (1,)), ((), ())), preferred_element_type=jnp.float32
    )


def contract_first(left, right):
    return lax.dot_general(
        left, right, (((0,), (0,)), ((), ())), preferred_element_type=jnp.float32
    )


def tile_of(extent, most):
    return most if extent % most == 0 else extent


def slot_positions(routes, experts, stride, base):
    top, count = routes.shape
    labels = lax.broadcasted_iota(jnp.int32, (experts, count), 0)
    named = [labels == routes[k : k + 1, :] for k in range(top)]
    marks = sum(jnp.where(m, 1.0, 0.0) for m in named)
    earlier = lax.broadcasted_iota(jnp.int32, (count, count), 0) < lax.broadcasted_iota(
        jnp.int32, (count, count), 1
    )
    rank = jnp.dot(
        marks.astype(jnp.bfloat16),
        jnp.where(earlier, 1.0, 0.0).astype(jnp.bfloat16),
        preferred_element_type=jnp.float32,
    )
    slot = rank + (labels * stride + base + 1).astype(jnp.float32)
    return [
        jnp.sum(jnp.where(m, slot, 0.0), axis=0, keepdims=True).astype(jnp.int32) - 1
        for m in named
    ]


def by_half(value, cap, half, paired):
    count, width = value.shape
    if paired:
        value = value.reshape(count // (2 * cap), 2, cap, width)
        own, other = value[:, 0], value[:, 1]
    else:
        value = value.reshape(2, count // (2 * cap), cap, width)
        own, other = value[0], value[1]
    first = jnp.where(half == 0, own, other)
    second = jnp.where(half == 0, other, own)
    return jnp.stack([first, second], axis=0 if paired else 1).reshape(count, width)


def dispatch_tokens(experts, cap, place_ref, *refs):
    routes_refs, tokens_refs, (out_ref, pos_ref, pick_ref) = refs[:2], refs[2:4], refs[4:]
    count = tokens_refs[0].shape[0]

    @pl.when(pl.program_id(0) == 0)
    def _():
        rows = lax.broadcasted_iota(jnp.int32, (pick_ref.shape[0], count), 0)
        for c, ref in enumerate(routes_refs):
            near = ref[...] - place_ref[1] * (experts // 2)
            pos = slot_positions(near, experts // 2, 2 * cap, c * cap)
            pick_ref[:, c * count : (c + 1) * count] = sum(
                jnp.where(rows == p, 1.0, 0.0) for p in pos
            ).astype(jnp.bfloat16)
        for k, p in enumerate(slot_positions(routes_refs[0][...], experts, cap, 0)):
            pos_ref[k : k + 1, :] = p

    values = jnp.concatenate([ref[...] for ref in tokens_refs], axis=0)
    out_ref[...] = jnp.dot(
        pick_ref[...], values, preferred_element_type=jnp.float32
    ).astype(out_ref.dtype)


def dispatch_scaled(experts, cap, groups, place_ref, *refs):
    routes_refs, gate_refs = refs[:groups], refs[groups : 2 * groups]
    grad_refs, (out_ref, pos_ref) = refs[2 * groups : 3 * groups], refs[3 * groups :]
    top, count = routes_refs[0].shape
    step = pl.program_id(0)

    @pl.when(step == 0)
    def _():
        for q in range(groups):
            pos = slot_positions(routes_refs[q][...], experts, groups * cap, q * cap)
            for k, p in enumerate(pos):
                pos_ref[q * top + k : q * top + k + 1, :] = p

    block = out_ref.shape[0]
    rows = lax.broadcasted_iota(jnp.int32, (block, count), 0) + step * block
    total = jnp.zeros((block, 1), jnp.float32)
    picks = []
    for q in range(groups):
        hit = jnp.zeros((block, count), jnp.float32)
        weight = jnp.zeros((block, count), jnp.float32)
        for k in range(top):
            here = rows == pos_ref[q * top + k : q * top + k + 1, :]
            hit = hit + jnp.where(here, 1.0, 0.0)
            weight = weight + jnp.where(here, gate_refs[q][k : k + 1, :], 0.0)
        picks.append(hit.astype(jnp.bfloat16))
        total = total + jnp.sum(weight, axis=1, keepdims=True)
    grads = jnp.concatenate([ref[...] for ref in grad_refs], axis=0)
    picked = jnp.dot(
        jnp.concatenate(picks, axis=1), grads, preferred_element_type=jnp.float32
    )
    out_ref[...] = (total * picked).astype(out_ref.dtype)


def ready_kernel(gate_ref, *refs):
    held_ref, sems = refs[-2:]
    half = gate_ref.shape[0] // 2
    copies = [
        pltpu.make_async_copy(
            gate_ref.at[n * half : (n + 1) * half],
            held_ref.at[n * half : (n + 1) * half],
            sems.at[n],
        )
        for n in range(2)
    ]
    for copy in copies:
        copy.start()
    for copy in copies:
        copy.wait()


def back_kernel(groups, cap, place_ref, rows_ref, down_ref, own_ref, *rest):
    others, all_ref = rest[: groups - 1], rest[groups - 1]
    slots, hidden = own_ref.shape
    count, share = rows_ref.shape
    rows = rows_ref[...].astype(jnp.float32).reshape(count // (groups * cap), groups, cap, share)
    for q in range(groups):
        ordered = by_half(rows[:, q].reshape(slots, share), cap, place_ref[1], False)
        all_ref[q * slots : (q + 1) * slots, :] = ordered.astype(all_ref.dtype)
    step = tile_of(hidden, 256)

    @pl.loop(0, hidden // step)
    def _(j):
        cols = pl.ds(pl.multiple_of(j * step, step), step)
        for q, ref in enumerate((own_ref, *others)):
            part = contract_last(all_ref[q * slots : (q + 1) * slots, :], down_ref[cols, :])
            ref[:, cols] = part.astype(ref.dtype)


def forward_kernel(groups, x_ref, gate_ref, back_ref, own_up_ref, *refs):
    others = refs[: groups - 1]
    act_ref, slope_ref, value_ref, hidden_ref, held_ref, kept_ref = refs[groups - 1 : groups + 5]
    gate_sum_ref, up_sum_ref, sems, back_sem = refs[groups + 5 :]
    share, hidden = gate_ref.shape
    step = tile_of(hidden, 256)
    sources = [gate_ref, *[ref.at[:share] for ref in others]]
    sources += [own_up_ref, *[ref.at[share:] for ref in others]]
    spans = [slice(at, at + step) for at in range(0, hidden, step)]

    order = [i for k in range(groups) for i in (k, groups + k)]
    part_rows = share // 2
    stages = [
        [
            pltpu.make_async_copy(
                sources[i].at[n * part_rows : (n + 1) * part_rows],
                held_ref.at[i - 1, n * part_rows : (n + 1) * part_rows],
                sems.at[n, i - 1],
            )
            for n in range(2)
        ]
        for i in order[1:]
    ]
    stages[-1].append(pltpu.make_async_copy(back_ref, kept_ref, back_sem.at[0]))

    def finish(cols):
        pre_gate, pre_up = gate_sum_ref[:, cols], up_sum_ref[:, cols]
        sig = jax.nn.sigmoid(pre_gate)
        act = pre_gate * sig
        hidden_f = act * pre_up
        act_ref[:, cols] = act
        slope_ref[:, cols] = pre_up * (sig * (1.0 + pre_gate * (1.0 - sig)))
        value_ref[:, cols] = hidden_f
        hidden_ref[:, cols] = hidden_f.astype(hidden_ref.dtype)

    ahead = 2
    for copies in stages[:ahead]:
        for copy in copies:
            copy.start()
    complete = None
    for at, i in enumerate(order):
        k = i % groups
        if at > 0:
            for copy in stages[at - 1]:
                copy.wait()
            if at - 1 + ahead < len(stages):
                for copy in stages[at - 1 + ahead]:
                    copy.start()
        sum_ref = gate_sum_ref if i < groups else up_sum_ref
        for cols in spans:
            part = jnp.dot(
                x_ref[:, k * share : (k + 1) * share],
                gate_ref[:, cols] if i == 0 else held_ref[i - 1, :, cols],
                preferred_element_type=jnp.float32,
            )
            if complete is not None:
                finish(complete)
            sum_ref[:, cols] = part if k == 0 else sum_ref[:, cols] + part
            complete = cols if i == order[-1] else None
    finish(complete)


def backward_kernel(
    groups, cap, half_ref, act_ref, slope_ref, value_ref, gate_ref, held_ref, *refs
):
    parts, (out_ref, d_gate_ref, d_up_ref, rows_ref, out_sems) = refs[:groups], refs[groups:]
    share = held_ref.shape[1]
    width = groups * share
    block = tile_of(share, 512)
    half = half_ref[0]
    back = sum(part[...].astype(jnp.float32) for part in parts)
    score = jnp.sum(back * value_ref[...], axis=1, keepdims=True)
    d_gate_ref[...] = by_half(back * slope_ref[...], cap, half, True).astype(jnp.bfloat16)
    d_up_ref[...] = by_half(back * act_ref[...], cap, half, True).astype(jnp.bfloat16)
    score = by_half(jnp.broadcast_to(score, (score.shape[0], LANES)), cap, half, True)
    rows_ref[:, width:] = score.astype(rows_ref.dtype)
    outs = []

    def send(cols):
        copy = pltpu.make_async_copy(
            rows_ref.at[:, cols], out_ref.at[:, cols], out_sems.at[len(outs)]
        )
        copy.start()
        outs.append(copy)

    send(slice(width, width + LANES))
    for k in range(groups):
        for at in range(0, share, block):
            cols = slice(k * share + at, k * share + at + block)
            gate = gate_ref[at : at + block] if k == 0 else held_ref[k - 1, at : at + block]
            grad = contract_last(d_gate_ref[...], gate)
            grad += contract_last(d_up_ref[...], held_ref[groups - 1 + k, at : at + block])
            rows_ref[:, cols] = grad.astype(rows_ref.dtype)
            send(cols)
    for copy in outs:
        copy.wait()


def combine_kernel(groups, place_ref, pos_ref, gate_ref, rows_ref, tokens_ref, gates_ref):
    top, count = pos_ref.shape
    slots = rows_ref.shape[0]
    width = tokens_ref.shape[1]
    share = width // groups
    places = lax.broadcasted_iota(jnp.int32, (slots, count), 0)
    picks = [
        jnp.where(places == pos_ref[k : k + 1, :], 1.0, 0.0).astype(jnp.bfloat16)
        for k in range(top)
    ]
    both = sum(picks)
    for k in range(groups):
        at = lax.rem(place_ref[0] - k + groups, groups) * share
        tokens_ref[:, pl.ds(pl.multiple_of(at, share), share)] = contract_first(
            both, rows_ref[:, k * share : (k + 1) * share]
        ).astype(tokens_ref.dtype)
    for k in range(top):
        score = contract_first(rows_ref[:, width:], picks[k])
        gates_ref[k : k + 1, :] = score[:1, :] / gate_ref[k : k + 1, :]


def per_device(tokens, routes, gates, grad_out, w_gate, w_up, w_down):
    experts = lax.axis_size("expert")
    groups = lax.axis_size("dp")
    group = lax.axis_index("dp")
    count, width = tokens.shape
    top = routes.shape[1]
    cap = 3 * count * top // (2 * experts)
    slots = experts * cap
    share = width // groups
    hidden = w_gate.shape[2]
    params = pltpu.CompilerParams(vmem_limit_bytes=VMEM_BYTES)
    half = lax.div(lax.axis_index("expert"), experts // 2)
    place = jnp.stack([group, half]).astype(jnp.int32)
    place_group, place_half = group.reshape(1), half.reshape(1)
    halves = [list(range(experts // 2)), list(range(experts // 2, experts))]

    def shifted(value, by):
        return lax.ppermute(value, "dp", [(i, (i + by) % groups) for i in range(groups)])

    def across(value):
        pairs = [(i, (i + experts // 2) % experts) for i in range(experts)]
        return lax.ppermute(value, "expert", pairs)

    def exchanged(rows, among=None):
        count = experts if among is None else len(among[0])
        split = rows.reshape(count, rows.shape[0] // count, rows.shape[1])
        moved = lax.all_to_all(
            split, "expert", split_axis=0, concat_axis=0, axis_index_groups=among, tiled=True
        )
        return moved.reshape(rows.shape)

    routes_t, gates_t = jnp.transpose(routes), jnp.transpose(gates)
    routes_all = [routes_t] + [shifted(routes_t, k) for k in range(1, groups)]
    gates_all = [gates_t] + [shifted(gates_t, k) for k in range(1, groups)]
    grads = [
        shifted(
            lax.dynamic_slice(grad_out, (0, lax.rem(group + k, groups) * share), (count, share)), k
        )
        for k in range(1, groups)
    ]
    both = jnp.concatenate([w_gate[0], w_up[0]], axis=0)
    both, gates_own = lax.optimization_barrier((both, gates_t))
    both, grads, routes_all, gates_all = lax.optimization_barrier(
        (both, grads, routes_all, gates_all)
    )
    routes_across = across(routes_t)
    tokens_sent, routes_across = lax.optimization_barrier((tokens, routes_across))
    tokens_across = across(tokens_sent)
    weights_moved = [shifted(both, k) for k in range(1, groups)]

    def in_hbm(value):
        return pltpu.with_memory_space_constraint(value, pltpu.HBM)

    steps = 4
    block = groups * slots // steps
    small_spec = pl.BlockSpec((top, count), lambda c, g: (0, 0))
    scaled = pl.pallas_call(
        functools.partial(dispatch_scaled, experts, cap, groups),
        out_shape=pltpu.HBM((groups * slots, share), jnp.bfloat16),
        grid_spec=pltpu.PrefetchScalarGridSpec(
            num_scalar_prefetch=1,
            grid=(steps,),
            in_specs=[small_spec] * (2 * groups)
            + [pl.BlockSpec((count, share), lambda c, g: (0, g[0]))]
            + [pl.BlockSpec((count, share), lambda c, g: (0, 0))] * (groups - 1),
            out_specs=pl.BlockSpec((block, share), lambda c, g: (c, 0)),
            scratch_shapes=[pltpu.VMEM((groups * top, count), jnp.int32)],
        ),
        compiler_params=params,
        name="dispatch_scaled",
    )(
        place_group,
        in_hbm(routes_t),
        *routes_all[1:],
        in_hbm(gates_own),
        *gates_all[1:],
        in_hbm(grad_out),
        *grads,
    )
    scaled_rows = exchanged(scaled)

    sent, pos = pl.pallas_call(
        functools.partial(dispatch_tokens, experts, cap),
        out_shape=(
            pltpu.HBM((slots, width), jnp.bfloat16),
            jax.ShapeDtypeStruct((top, count), jnp.int32),
        ),
        grid_spec=pltpu.PrefetchScalarGridSpec(
            num_scalar_prefetch=1,
            grid=(groups,),
            in_specs=[small_spec] * 2
            + [
                pl.BlockSpec(
                    (count, share), lambda k, g: (0, lax.rem(g[0] - k + groups, groups))
                )
            ]
            * 2,
            out_specs=(pl.BlockSpec((slots, share), lambda k, g: (0, k)), small_spec),
            scratch_shapes=[pltpu.VMEM((slots, 2 * count), jnp.bfloat16)],
        ),
        cost_estimate=pl.CostEstimate(
            flops=TOKENS_COST_US * 10**9, bytes_accessed=TOKENS_COST_US * 10**6, transcendentals=0
        ),
        compiler_params=params,
        name="dispatch_tokens",
    )(place, in_hbm(routes_t), routes_across, in_hbm(tokens), in_hbm(tokens_across))
    x_rows = exchanged(sent, halves)

    any_spec = pl.BlockSpec(memory_space=pl.ANY)
    whole_spec = pl.BlockSpec(memory_space=pltpu.VMEM)
    *weights_moved, gate_held = pl.pallas_call(
        ready_kernel,
        out_shape=[pltpu.HBM(value.shape, value.dtype) for value in weights_moved]
        + [pltpu.VMEM((share, hidden), jnp.bfloat16)],
        in_specs=[any_spec] * groups,
        out_specs=[any_spec] * (groups - 1) + [whole_spec],
        input_output_aliases={k + 1: k for k in range(groups - 1)},
        scratch_shapes=[pltpu.SemaphoreType.DMA((2,))],
        cost_estimate=pl.CostEstimate(
            flops=READY_COST_US * 10**9, bytes_accessed=READY_COST_US * 10**6, transcendentals=0
        ),
        compiler_params=params,
        name="ready",
    )(in_hbm(w_gate[0]), *[in_hbm(value) for value in weights_moved])

    place_spec = pl.BlockSpec(memory_space=pltpu.SMEM)

    back_own, *rest = pl.pallas_call(
        functools.partial(back_kernel, groups, cap),
        out_shape=[pltpu.HBM((slots, hidden), jnp.float32)]
        + [pltpu.HBM((slots, hidden), jnp.bfloat16)] * (groups - 1)
        + [pltpu.HBM((groups * slots, share), jnp.bfloat16)],
        in_specs=[place_spec, pl.BlockSpec(), pl.BlockSpec()],
        compiler_params=params,
        name="back",
    )(place, scaled_rows, in_hbm(w_down[0]))
    scaled_all = rest[-1]
    back_parts = [shifted(rest[k - 1], -k) for k in range(1, groups)]

    *factors, hidden_own, held, back_kept = pl.pallas_call(
        functools.partial(forward_kernel, groups),
        out_shape=[pltpu.VMEM((slots, hidden), jnp.float32)] * 3
        + [
            pltpu.HBM((slots, hidden), jnp.bfloat16),
            pltpu.VMEM((2 * groups - 1, share, hidden), jnp.bfloat16),
            pltpu.VMEM((slots, hidden), jnp.float32),
        ],
        in_specs=[whole_spec] * 2 + [any_spec] * (groups + 1),
        scratch_shapes=[
            pltpu.VMEM((slots, hidden), jnp.float32),
            pltpu.VMEM((slots, hidden), jnp.float32),
            pltpu.SemaphoreType.DMA((2, 2 * groups - 1)),
            pltpu.SemaphoreType.DMA((1,)),
        ],
        compiler_params=params,
        name="forward",
    )(x_rows, gate_held, in_hbm(back_own), in_hbm(w_up[0]), *[in_hbm(w) for w in weights_moved])

    pieces = groups * (share // tile_of(share, 512))
    returning = pl.pallas_call(
        functools.partial(backward_kernel, groups, cap),
        out_shape=pltpu.HBM((slots, width + LANES), jnp.bfloat16),
        in_specs=[place_spec] + [whole_spec] * (5 + groups),
        out_specs=any_spec,
        scratch_shapes=[
            pltpu.VMEM((slots, hidden), jnp.bfloat16),
            pltpu.VMEM((slots, hidden), jnp.bfloat16),
            pltpu.VMEM((slots, width + LANES), jnp.bfloat16),
            pltpu.SemaphoreType.DMA((pieces + 1,)),
        ],
        compiler_params=params,
        name="backward",
    )(place_half, *factors, gate_held, held, back_kept, *back_parts)
    returned = exchanged(returning)

    hiddens = [hidden_own] + [shifted(hidden_own, k) for k in range(1, groups)]
    grad_down = contract_first(jnp.concatenate(hiddens, axis=0), scaled_all)[None]

    grad_tokens, grad_gates = pl.pallas_call(
        functools.partial(combine_kernel, groups),
        out_shape=(
            jax.ShapeDtypeStruct((count, width), jnp.bfloat16),
            jax.ShapeDtypeStruct((top, count), jnp.float32),
        ),
        in_specs=[pl.BlockSpec(memory_space=pltpu.SMEM)] + [whole_spec] * 3,
        compiler_params=params,
        name="combine",
    )(place_group, pos, gates_t, returned)
    return (grad_tokens, jnp.transpose(grad_gates), grad_down)


def solution(mesh):
    placed = (
        P(("dp", "expert"), None),
        P(("dp", "expert"), None),
        P(("dp", "expert"), None),
        P(("dp", "expert"), None),
        P("expert", "dp", None),
        P("expert", "dp", None),
        P("expert", None, "dp"),
    )
    return jax.shard_map(
        per_device,
        mesh=mesh,
        in_specs=placed,
        out_specs=(P(("dp", "expert"), None), P(("dp", "expert"), None), P("expert", None, "dp")),
        check_vma=False,
    )
```

```python
import functools

import jax
import jax.numpy as jnp
from jax import lax
from jax.experimental import pallas as pl
from jax.experimental.pallas import tpu as pltpu
from jax.sharding import PartitionSpec as P

LANES = 128
VMEM_BYTES = 24 * 1024 * 1024
READY_COST_US = 30
TOKENS_COST_US = 30


def contract_last(left, right):
    return lax.dot_general(
        left, right, (((1,), (1,)), ((), ())), preferred_element_type=jnp.float32
    )


def contract_first(left, right):
    return lax.dot_general(
        left, right, (((0,), (0,)), ((), ())), preferred_element_type=jnp.float32
    )


def tile_of(extent, most):
    return most if extent % most == 0 else extent


def slot_positions(routes, experts, stride, base):
    top, count = routes.shape
    labels = lax.broadcasted_iota(jnp.int32, (experts, count), 0)
    named = [labels == routes[k : k + 1, :] for k in range(top)]
    marks = sum(jnp.where(m, 1.0, 0.0) for m in named)
    earlier = lax.broadcasted_iota(jnp.int32, (count, count), 0) < lax.broadcasted_iota(
        jnp.int32, (count, count), 1
    )
    rank = jnp.dot(
        marks.astype(jnp.bfloat16),
        jnp.where(earlier, 1.0, 0.0).astype(jnp.bfloat16),
        preferred_element_type=jnp.float32,
    )
    slot = rank + (labels * stride + base + 1).astype(jnp.float32)
    return [
        jnp.sum(jnp.where(m, slot, 0.0), axis=0, keepdims=True).astype(jnp.int32) - 1
        for m in named
    ]


def block_labels(routes, experts):
    half = experts // 2
    return jnp.where(routes < half, 2 * routes, 2 * (routes - half) + 1)


def rows_of(ref, groups, cap, which):
    value = ref[...].astype(jnp.float32)
    count, width = value.shape
    value = value.reshape(count // (groups * cap), groups, cap, width)[:, which]
    return value.reshape(count // groups, width).astype(ref.dtype)


def dispatch_tokens(experts, cap, place_ref, *refs):
    routes_refs, tokens_refs, (out_ref, pos_ref, pick_ref) = refs[:2], refs[2:4], refs[4:]
    count = tokens_refs[0].shape[0]

    @pl.when(pl.program_id(0) == 0)
    def _():
        rows = lax.broadcasted_iota(jnp.int32, (pick_ref.shape[0], count), 0)
        for c, ref in enumerate(routes_refs):
            near = ref[...] - place_ref[1] * (experts // 2)
            side = place_ref[1] if c == 0 else 1 - place_ref[1]
            pos = slot_positions(near, experts // 2, 2 * cap, side * cap)
            pick_ref[:, c * count : (c + 1) * count] = sum(
                jnp.where(rows == p, 1.0, 0.0) for p in pos
            ).astype(jnp.bfloat16)
        labels = block_labels(routes_refs[0][...], experts)
        for k, p in enumerate(slot_positions(labels, experts, cap, 0)):
            pos_ref[k : k + 1, :] = p

    values = jnp.concatenate([ref[...] for ref in tokens_refs], axis=0)
    out_ref[...] = jnp.dot(
        pick_ref[...], values, preferred_element_type=jnp.float32
    ).astype(out_ref.dtype)


def dispatch_scaled(experts, cap, groups, place_ref, *refs):
    routes_refs, gate_refs = refs[:groups], refs[groups : 2 * groups]
    grad_refs, (out_ref, pick_ref, scale_ref) = refs[2 * groups : 3 * groups], refs[3 * groups :]
    count = grad_refs[0].shape[0]
    slots = out_ref.shape[0]

    @pl.when(pl.program_id(0) == 0)
    def _():
        rows = lax.broadcasted_iota(jnp.int32, (slots, count), 0)
        total = jnp.zeros((slots, 1), jnp.float32)
        for q in range(groups):
            labels = block_labels(routes_refs[q][...], experts)
            pos = slot_positions(labels, experts, groups * cap, q * cap)
            hit = jnp.zeros((slots, count), jnp.float32)
            weight = jnp.zeros((slots, count), jnp.float32)
            for k, p in enumerate(pos):
                here = rows == p
                hit = hit + jnp.where(here, 1.0, 0.0)
                weight = weight + jnp.where(here, gate_refs[q][k : k + 1, :], 0.0)
            pick_ref[:, q * count : (q + 1) * count] = hit.astype(jnp.bfloat16)
            total = total + jnp.sum(weight, axis=1, keepdims=True)
        scale_ref[...] = jnp.broadcast_to(total, scale_ref.shape)

    grads = jnp.concatenate([ref[...] for ref in grad_refs], axis=0)
    rows = jnp.dot(pick_ref[...], grads, preferred_element_type=jnp.float32)
    out_ref[...] = (scale_ref[:, :1] * rows).astype(out_ref.dtype)


def ready_kernel(gate_ref, *refs):
    held_ref, sems = refs[-2:]
    half = gate_ref.shape[0] // 2
    copies = [
        pltpu.make_async_copy(
            gate_ref.at[n * half : (n + 1) * half],
            held_ref.at[n * half : (n + 1) * half],
            sems.at[n],
        )
        for n in range(2)
    ]
    for copy in copies:
        copy.start()
    for copy in copies:
        copy.wait()


def back_kernel(groups, cap, rows_ref, down_ref, own_ref, *rest):
    others, all_ref = rest[: groups - 1], rest[groups - 1]
    slots, hidden = own_ref.shape
    for q in range(groups):
        all_ref[q * slots : (q + 1) * slots, :] = rows_of(rows_ref, groups, cap, q)
    step = tile_of(hidden, 256)

    @pl.loop(0, hidden // step)
    def _(j):
        cols = pl.ds(pl.multiple_of(j * step, step), step)
        for q, ref in enumerate((own_ref, *others)):
            part = contract_last(all_ref[q * slots : (q + 1) * slots, :], down_ref[cols, :])
            ref[:, cols] = part.astype(ref.dtype)


def forward_kernel(groups, x_ref, gate_ref, back_ref, own_up_ref, *refs):
    others = refs[: groups - 1]
    act_ref, slope_ref, value_ref, hidden_ref, held_ref, kept_ref = refs[groups - 1 : groups + 5]
    gate_sum_ref, up_sum_ref, sems, back_sem = refs[groups + 5 :]
    share, hidden = gate_ref.shape
    step = tile_of(hidden, 256)
    sources = [gate_ref, *[ref.at[:share] for ref in others]]
    sources += [own_up_ref, *[ref.at[share:] for ref in others]]
    spans = [slice(at, at + step) for at in range(0, hidden, step)]

    order = [i for k in range(groups) for i in (k, groups + k)]
    part_rows = share // 2
    stages = [
        [
            pltpu.make_async_copy(
                sources[i].at[n * part_rows : (n + 1) * part_rows],
                held_ref.at[i - 1, n * part_rows : (n + 1) * part_rows],
                sems.at[n, i - 1],
            )
            for n in range(2)
        ]
        for i in order[1:]
    ]
    stages[-1].append(pltpu.make_async_copy(back_ref, kept_ref, back_sem.at[0]))

    def finish(cols):
        pre_gate, pre_up = gate_sum_ref[:, cols], up_sum_ref[:, cols]
        sig = jax.nn.sigmoid(pre_gate)
        act = pre_gate * sig
        hidden_f = act * pre_up
        act_ref[:, cols] = act
        slope_ref[:, cols] = pre_up * (sig * (1.0 + pre_gate * (1.0 - sig)))
        value_ref[:, cols] = hidden_f
        hidden_ref[:, cols] = hidden_f.astype(hidden_ref.dtype)

    ahead = 2
    for copies in stages[:ahead]:
        for copy in copies:
            copy.start()
    complete = None
    for at, i in enumerate(order):
        k = i % groups
        if at > 0:
            for copy in stages[at - 1]:
                copy.wait()
            if at - 1 + ahead < len(stages):
                for copy in stages[at - 1 + ahead]:
                    copy.start()
        sum_ref = gate_sum_ref if i < groups else up_sum_ref
        for cols in spans:
            part = jnp.dot(
                x_ref[:, k * share : (k + 1) * share],
                gate_ref[:, cols] if i == 0 else held_ref[i - 1, :, cols],
                preferred_element_type=jnp.float32,
            )
            if complete is not None:
                finish(complete)
            sum_ref[:, cols] = part if k == 0 else sum_ref[:, cols] + part
            complete = cols if i == order[-1] else None
    finish(complete)


def backward_kernel(
    groups, act_ref, slope_ref, value_ref, gate_ref, held_ref, *refs
):
    parts, (out_ref, d_gate_ref, d_up_ref, rows_ref, out_sems) = refs[:groups], refs[groups:]
    share = held_ref.shape[1]
    width = groups * share
    block = tile_of(share, 512)
    back = sum(part[...].astype(jnp.float32) for part in parts)
    score = jnp.sum(back * value_ref[...], axis=1, keepdims=True)
    d_gate_ref[...] = (back * slope_ref[...]).astype(jnp.bfloat16)
    d_up_ref[...] = (back * act_ref[...]).astype(jnp.bfloat16)
    score = jnp.broadcast_to(score, (score.shape[0], LANES))
    rows_ref[:, width:] = score.astype(rows_ref.dtype)
    outs = []

    def send(cols):
        copy = pltpu.make_async_copy(
            rows_ref.at[:, cols], out_ref.at[:, cols], out_sems.at[len(outs)]
        )
        copy.start()
        outs.append(copy)

    send(slice(width, width + LANES))
    for k in range(groups):
        for at in range(0, share, block):
            cols = slice(k * share + at, k * share + at + block)
            gate = gate_ref[at : at + block] if k == 0 else held_ref[k - 1, at : at + block]
            grad = contract_last(d_gate_ref[...], gate)
            grad += contract_last(d_up_ref[...], held_ref[groups - 1 + k, at : at + block])
            rows_ref[:, cols] = grad.astype(rows_ref.dtype)
            send(cols)
    for copy in outs:
        copy.wait()


def combine_kernel(groups, place_ref, pos_ref, gate_ref, rows_ref, tokens_ref, gates_ref):
    top, count = pos_ref.shape
    slots = rows_ref.shape[0]
    width = tokens_ref.shape[1]
    share = width // groups
    places = lax.broadcasted_iota(jnp.int32, (slots, count), 0)
    picks = [
        jnp.where(places == pos_ref[k : k + 1, :], 1.0, 0.0).astype(jnp.bfloat16)
        for k in range(top)
    ]
    both = sum(picks)
    for k in range(groups):
        at = lax.rem(place_ref[0] - k + groups, groups) * share
        tokens_ref[:, pl.ds(pl.multiple_of(at, share), share)] = contract_first(
            both, rows_ref[:, k * share : (k + 1) * share]
        ).astype(tokens_ref.dtype)
    for k in range(top):
        score = contract_first(rows_ref[:, width:], picks[k])
        gates_ref[k : k + 1, :] = score[:1, :] / gate_ref[k : k + 1, :]


def per_device(tokens, routes, gates, grad_out, w_gate, w_up, w_down):
    experts = lax.axis_size("expert")
    groups = lax.axis_size("dp")
    group = lax.axis_index("dp")
    count, width = tokens.shape
    top = routes.shape[1]
    cap = 3 * count * top // (2 * experts)
    slots = experts * cap
    share = width // groups
    hidden = w_gate.shape[2]
    params = pltpu.CompilerParams(vmem_limit_bytes=VMEM_BYTES)
    half = lax.div(lax.axis_index("expert"), experts // 2)
    place = jnp.stack([group, half]).astype(jnp.int32)
    place_group = group.reshape(1)
    halves = [list(range(experts // 2)), list(range(experts // 2, experts))]
    pairs = [[expert for pair in zip(*halves) for expert in pair]]

    def shifted(value, by):
        return lax.ppermute(value, "dp", [(i, (i + by) % groups) for i in range(groups)])

    def across(value):
        swaps = [(i, (i + experts // 2) % experts) for i in range(experts)]
        return lax.ppermute(value, "expert", swaps)

    def exchanged(rows, among):
        count = len(among[0])
        split = rows.reshape(count, rows.shape[0] // count, rows.shape[1])
        moved = lax.all_to_all(
            split, "expert", split_axis=0, concat_axis=0, axis_index_groups=among, tiled=True
        )
        return moved.reshape(rows.shape)

    routes_t, gates_t = jnp.transpose(routes), jnp.transpose(gates)
    routes_all = [routes_t] + [shifted(routes_t, k) for k in range(1, groups)]
    gates_all = [gates_t] + [shifted(gates_t, k) for k in range(1, groups)]
    grads = [
        shifted(
            lax.dynamic_slice(grad_out, (0, lax.rem(group + k, groups) * share), (count, share)), k
        )
        for k in range(1, groups)
    ]
    both = jnp.concatenate([w_gate[0], w_up[0]], axis=0)
    both, gates_own = lax.optimization_barrier((both, gates_t))
    both, grads, routes_all, gates_all = lax.optimization_barrier(
        (both, grads, routes_all, gates_all)
    )
    routes_across = across(routes_t)
    tokens_sent, routes_across = lax.optimization_barrier((tokens, routes_across))
    tokens_across = across(tokens_sent)
    weights_moved = [shifted(both, k) for k in range(1, groups)]

    def in_hbm(value):
        return pltpu.with_memory_space_constraint(value, pltpu.HBM)

    block = tile_of(share, 512)
    steps = share // block
    small_spec = pl.BlockSpec((top, count), lambda c, g: (0, 0))
    scaled = pl.pallas_call(
        functools.partial(dispatch_scaled, experts, cap, groups),
        out_shape=pltpu.HBM((groups * slots, share), jnp.bfloat16),
        grid_spec=pltpu.PrefetchScalarGridSpec(
            num_scalar_prefetch=1,
            grid=(steps,),
            in_specs=[small_spec] * (2 * groups)
            + [pl.BlockSpec((count, block), lambda c, g: (0, g[0] * steps + c))]
            + [pl.BlockSpec((count, block), lambda c, g: (0, c))] * (groups - 1),
            out_specs=pl.BlockSpec((groups * slots, block), lambda c, g: (0, c)),
            scratch_shapes=[
                pltpu.VMEM((groups * slots, groups * count), jnp.bfloat16),
                pltpu.VMEM((groups * slots, LANES), jnp.float32),
            ],
        ),
        compiler_params=params,
        name="dispatch_scaled",
    )(
        place_group,
        in_hbm(routes_t),
        *routes_all[1:],
        in_hbm(gates_own),
        *gates_all[1:],
        in_hbm(grad_out),
        *grads,
    )
    scaled_rows = exchanged(scaled, pairs)

    sent, pos = pl.pallas_call(
        functools.partial(dispatch_tokens, experts, cap),
        out_shape=(
            pltpu.HBM((slots, width), jnp.bfloat16),
            jax.ShapeDtypeStruct((top, count), jnp.int32),
        ),
        grid_spec=pltpu.PrefetchScalarGridSpec(
            num_scalar_prefetch=1,
            grid=(groups,),
            in_specs=[small_spec] * 2
            + [
                pl.BlockSpec(
                    (count, share), lambda k, g: (0, lax.rem(g[0] - k + groups, groups))
                )
            ]
            * 2,
            out_specs=(pl.BlockSpec((slots, share), lambda k, g: (0, k)), small_spec),
            scratch_shapes=[pltpu.VMEM((slots, 2 * count), jnp.bfloat16)],
        ),
        cost_estimate=pl.CostEstimate(
            flops=TOKENS_COST_US * 10**9, bytes_accessed=TOKENS_COST_US * 10**6, transcendentals=0
        ),
        compiler_params=params,
        name="dispatch_tokens",
    )(place, in_hbm(routes_t), routes_across, in_hbm(tokens), in_hbm(tokens_across))
    x_rows = exchanged(sent, halves)

    any_spec = pl.BlockSpec(memory_space=pl.ANY)
    whole_spec = pl.BlockSpec(memory_space=pltpu.VMEM)
    *weights_moved, gate_held = pl.pallas_call(
        ready_kernel,
        out_shape=[pltpu.HBM(value.shape, value.dtype) for value in weights_moved]
        + [pltpu.VMEM((share, hidden), jnp.bfloat16)],
        in_specs=[any_spec] * groups,
        out_specs=[any_spec] * (groups - 1) + [whole_spec],
        input_output_aliases={k + 1: k for k in range(groups - 1)},
        scratch_shapes=[pltpu.SemaphoreType.DMA((2,))],
        cost_estimate=pl.CostEstimate(
            flops=READY_COST_US * 10**9, bytes_accessed=READY_COST_US * 10**6, transcendentals=0
        ),
        compiler_params=params,
        name="ready",
    )(in_hbm(w_gate[0]), *[in_hbm(value) for value in weights_moved])

    place_spec = pl.BlockSpec(memory_space=pltpu.SMEM)

    back_own, *rest = pl.pallas_call(
        functools.partial(back_kernel, groups, cap),
        out_shape=[pltpu.HBM((slots, hidden), jnp.float32)]
        + [pltpu.HBM((slots, hidden), jnp.bfloat16)] * (groups - 1)
        + [pltpu.HBM((groups * slots, share), jnp.bfloat16)],
        compiler_params=params,
        name="back",
    )(scaled_rows, in_hbm(w_down[0]))
    scaled_all = rest[-1]
    back_parts = [shifted(rest[k - 1], -k) for k in range(1, groups)]

    *factors, hidden_own, held, back_kept = pl.pallas_call(
        functools.partial(forward_kernel, groups),
        out_shape=[pltpu.VMEM((slots, hidden), jnp.float32)] * 3
        + [
            pltpu.HBM((slots, hidden), jnp.bfloat16),
            pltpu.VMEM((2 * groups - 1, share, hidden), jnp.bfloat16),
            pltpu.VMEM((slots, hidden), jnp.float32),
        ],
        in_specs=[whole_spec] * 2 + [any_spec] * (groups + 1),
        scratch_shapes=[
            pltpu.VMEM((slots, hidden), jnp.float32),
            pltpu.VMEM((slots, hidden), jnp.float32),
            pltpu.SemaphoreType.DMA((2, 2 * groups - 1)),
            pltpu.SemaphoreType.DMA((1,)),
        ],
        compiler_params=params,
        name="forward",
    )(x_rows, gate_held, in_hbm(back_own), in_hbm(w_up[0]), *[in_hbm(w) for w in weights_moved])

    pieces = groups * (share // tile_of(share, 512))
    returning = pl.pallas_call(
        functools.partial(backward_kernel, groups),
        out_shape=pltpu.HBM((slots, width + LANES), jnp.bfloat16),
        in_specs=[whole_spec] * (5 + groups),
        out_specs=any_spec,
        scratch_shapes=[
            pltpu.VMEM((slots, hidden), jnp.bfloat16),
            pltpu.VMEM((slots, hidden), jnp.bfloat16),
            pltpu.VMEM((slots, width + LANES), jnp.bfloat16),
            pltpu.SemaphoreType.DMA((pieces + 1,)),
        ],
        compiler_params=params,
        name="backward",
    )(*factors, gate_held, held, back_kept, *back_parts)
    returned = exchanged(returning, pairs)

    hiddens = [hidden_own] + [shifted(hidden_own, k) for k in range(1, groups)]
    grad_down = contract_first(jnp.concatenate(hiddens, axis=0), scaled_all)[None]

    grad_tokens, grad_gates = pl.pallas_call(
        functools.partial(combine_kernel, groups),
        out_shape=(
            jax.ShapeDtypeStruct((count, width), jnp.bfloat16),
            jax.ShapeDtypeStruct((top, count), jnp.float32),
        ),
        in_specs=[pl.BlockSpec(memory_space=pltpu.SMEM)] + [whole_spec] * 3,
        compiler_params=params,
        name="combine",
    )(place_group, pos, gates_t, returned)
    return (grad_tokens, jnp.transpose(grad_gates), grad_down)


def solution(mesh):
    placed = (
        P(("dp", "expert"), None),
        P(("dp", "expert"), None),
        P(("dp", "expert"), None),
        P(("dp", "expert"), None),
        P("expert", "dp", None),
        P("expert", "dp", None),
        P("expert", None, "dp"),
    )
    return jax.shard_map(
        per_device,
        mesh=mesh,
        in_specs=placed,
        out_specs=(P(("dp", "expert"), None), P(("dp", "expert"), None), P("expert", None, "dp")),
        check_vma=False,
    )
```

```python
import functools

import jax
import jax.numpy as jnp
from jax import lax
from jax.experimental import pallas as pl
from jax.experimental.pallas import tpu as pltpu
from jax.sharding import PartitionSpec as P

LANES = 128
VMEM_BYTES = 24 * 1024 * 1024
READY_COST_US = 30
TOKENS_COST_US = 30


def contract_last(left, right):
    return lax.dot_general(
        left, right, (((1,), (1,)), ((), ())), preferred_element_type=jnp.float32
    )


def contract_first(left, right):
    return lax.dot_general(
        left, right, (((0,), (0,)), ((), ())), preferred_element_type=jnp.float32
    )


def tile_of(extent, most):
    return most if extent % most == 0 else extent


def slot_positions(routes, experts, stride, base):
    top, count = routes.shape
    labels = lax.broadcasted_iota(jnp.int32, (experts, count), 0)
    named = [labels == routes[k : k + 1, :] for k in range(top)]
    marks = sum(jnp.where(m, 1.0, 0.0) for m in named)
    earlier = lax.broadcasted_iota(jnp.int32, (count, count), 0) < lax.broadcasted_iota(
        jnp.int32, (count, count), 1
    )
    rank = jnp.dot(
        marks.astype(jnp.bfloat16),
        jnp.where(earlier, 1.0, 0.0).astype(jnp.bfloat16),
        preferred_element_type=jnp.float32,
    )
    slot = rank + (labels * stride + base + 1).astype(jnp.float32)
    return [
        jnp.sum(jnp.where(m, slot, 0.0), axis=0, keepdims=True).astype(jnp.int32) - 1
        for m in named
    ]


def by_half(value, cap, half, paired):
    count, width = value.shape
    if paired:
        value = value.reshape(count // (2 * cap), 2, cap, width)
        own, other = value[:, 0], value[:, 1]
    else:
        value = value.reshape(2, count // (2 * cap), cap, width)
        own, other = value[0], value[1]
    first = jnp.where(half == 0, own, other)
    second = jnp.where(half == 0, other, own)
    return jnp.stack([first, second], axis=0 if paired else 1).reshape(count, width)


def dispatch_tokens(experts, cap, place_ref, *refs):
    routes_refs, tokens_refs, (out_ref, pos_ref, pick_ref) = refs[:2], refs[2:4], refs[4:]
    count = tokens_refs[0].shape[0]

    @pl.when(pl.program_id(0) == 0)
    def _():
        rows = lax.broadcasted_iota(jnp.int32, (pick_ref.shape[0], count), 0)
        for c, ref in enumerate(routes_refs):
            near = ref[...] - place_ref[1] * (experts // 2)
            pos = slot_positions(near, experts // 2, 2 * cap, c * cap)
            pick_ref[:, c * count : (c + 1) * count] = sum(
                jnp.where(rows == p, 1.0, 0.0) for p in pos
            ).astype(jnp.bfloat16)
        for k, p in enumerate(slot_positions(routes_refs[0][...], experts, cap, 0)):
            pos_ref[k : k + 1, :] = p

    values = jnp.concatenate([ref[...] for ref in tokens_refs], axis=0)
    out_ref[...] = jnp.dot(
        pick_ref[...], values, preferred_element_type=jnp.float32
    ).astype(out_ref.dtype)


def dispatch_scaled(experts, cap, groups, place_ref, *refs):
    routes_refs, gate_refs = refs[:groups], refs[groups : 2 * groups]
    grad_refs, (out_ref, pick_ref, scale_ref) = refs[2 * groups : 3 * groups], refs[3 * groups :]
    count = grad_refs[0].shape[0]
    slots = out_ref.shape[0]

    @pl.when(pl.program_id(0) == 0)
    def _():
        rows = lax.broadcasted_iota(jnp.int32, (slots, count), 0)
        total = jnp.zeros((slots, 1), jnp.float32)
        for q in range(groups):
            pos = slot_positions(routes_refs[q][...], experts, groups * cap, q * cap)
            hit = jnp.zeros((slots, count), jnp.float32)
            weight = jnp.zeros((slots, count), jnp.float32)
            for k, p in enumerate(pos):
                here = rows == p
                hit = hit + jnp.where(here, 1.0, 0.0)
                weight = weight + jnp.where(here, gate_refs[q][k : k + 1, :], 0.0)
            pick_ref[:, q * count : (q + 1) * count] = hit.astype(jnp.bfloat16)
            total = total + jnp.sum(weight, axis=1, keepdims=True)
        scale_ref[...] = jnp.broadcast_to(total, scale_ref.shape)

    grads = jnp.concatenate([ref[...] for ref in grad_refs], axis=0)
    rows = jnp.dot(pick_ref[...], grads, preferred_element_type=jnp.float32)
    out_ref[...] = (scale_ref[:, :1] * rows).astype(out_ref.dtype)


def ready_kernel(gate_ref, *refs):
    held_ref, sems = refs[-2:]
    half = gate_ref.shape[0] // 2
    copies = [
        pltpu.make_async_copy(
            gate_ref.at[n * half : (n + 1) * half],
            held_ref.at[n * half : (n + 1) * half],
            sems.at[n],
        )
        for n in range(2)
    ]
    for copy in copies:
        copy.start()
    for copy in copies:
        copy.wait()


def back_kernel(groups, cap, place_ref, rows_ref, down_ref, own_ref, *rest):
    others, all_ref = rest[: groups - 1], rest[groups - 1]
    slots, hidden = own_ref.shape
    count, share = rows_ref.shape
    rows = rows_ref[...].astype(jnp.float32).reshape(count // (groups * cap), groups, cap, share)
    for q in range(groups):
        ordered = by_half(rows[:, q].reshape(slots, share), cap, place_ref[1], False)
        all_ref[q * slots : (q + 1) * slots, :] = ordered.astype(all_ref.dtype)
    step = tile_of(hidden, 256)

    @pl.loop(0, hidden // step)
    def _(j):
        cols = pl.ds(pl.multiple_of(j * step, step), step)
        for q, ref in enumerate((own_ref, *others)):
            part = contract_last(all_ref[q * slots : (q + 1) * slots, :], down_ref[cols, :])
            ref[:, cols] = part.astype(ref.dtype)


def forward_kernel(groups, x_ref, gate_ref, back_ref, own_up_ref, *refs):
    others = refs[: groups - 1]
    act_ref, slope_ref, value_ref, hidden_ref, held_ref, kept_ref = refs[groups - 1 : groups + 5]
    gate_sum_ref, up_sum_ref, sems, back_sem = refs[groups + 5 :]
    share, hidden = gate_ref.shape
    step = tile_of(hidden, 256)
    sources = [gate_ref, *[ref.at[:share] for ref in others]]
    sources += [own_up_ref, *[ref.at[share:] for ref in others]]
    spans = [slice(at, at + step) for at in range(0, hidden, step)]

    order = [i for k in range(groups) for i in (k, groups + k)]
    part_rows = share // 2
    stages = [
        [
            pltpu.make_async_copy(
                sources[i].at[n * part_rows : (n + 1) * part_rows],
                held_ref.at[i - 1, n * part_rows : (n + 1) * part_rows],
                sems.at[n, i - 1],
            )
            for n in range(2)
        ]
        for i in order[1:]
    ]
    stages[-1].append(pltpu.make_async_copy(back_ref, kept_ref, back_sem.at[0]))

    def finish(cols):
        pre_gate, pre_up = gate_sum_ref[:, cols], up_sum_ref[:, cols]
        sig = jax.nn.sigmoid(pre_gate)
        act = pre_gate * sig
        hidden_f = act * pre_up
        act_ref[:, cols] = act
        slope_ref[:, cols] = pre_up * (sig * (1.0 + pre_gate * (1.0 - sig)))
        value_ref[:, cols] = hidden_f
        hidden_ref[:, cols] = hidden_f.astype(hidden_ref.dtype)

    ahead = 3
    for copies in stages[:ahead]:
        for copy in copies:
            copy.start()
    complete = None
    for at, i in enumerate(order):
        k = i % groups
        if at > 0:
            for copy in stages[at - 1]:
                copy.wait()
            if at - 1 + ahead < len(stages):
                for copy in stages[at - 1 + ahead]:
                    copy.start()
        sum_ref = gate_sum_ref if i < groups else up_sum_ref
        for cols in spans:
            part = jnp.dot(
                x_ref[:, k * share : (k + 1) * share],
                gate_ref[:, cols] if i == 0 else held_ref[i - 1, :, cols],
                preferred_element_type=jnp.float32,
            )
            if complete is not None:
                finish(complete)
            sum_ref[:, cols] = part if k == 0 else sum_ref[:, cols] + part
            complete = cols if i == order[-1] else None
    finish(complete)


def backward_kernel(
    groups, cap, half_ref, act_ref, slope_ref, value_ref, gate_ref, held_ref, *refs
):
    parts, (out_ref, d_gate_ref, d_up_ref, rows_ref, out_sems) = refs[:groups], refs[groups:]
    share = held_ref.shape[1]
    width = groups * share
    block = tile_of(share, 512)
    half = half_ref[0]
    back = sum(part[...].astype(jnp.float32) for part in parts)
    score = jnp.sum(back * value_ref[...], axis=1, keepdims=True)
    d_gate_ref[...] = by_half(back * slope_ref[...], cap, half, True).astype(jnp.bfloat16)
    d_up_ref[...] = by_half(back * act_ref[...], cap, half, True).astype(jnp.bfloat16)
    score = by_half(jnp.broadcast_to(score, (score.shape[0], LANES)), cap, half, True)
    rows_ref[:, width:] = score.astype(rows_ref.dtype)
    outs = []

    def send(cols):
        copy = pltpu.make_async_copy(
            rows_ref.at[:, cols], out_ref.at[:, cols], out_sems.at[len(outs)]
        )
        copy.start()
        outs.append(copy)

    send(slice(width, width + LANES))
    for k in range(groups):
        for at in range(0, share, block):
            cols = slice(k * share + at, k * share + at + block)
            gate = gate_ref[at : at + block] if k == 0 else held_ref[k - 1, at : at + block]
            grad = contract_last(d_gate_ref[...], gate)
            grad += contract_last(d_up_ref[...], held_ref[groups - 1 + k, at : at + block])
            rows_ref[:, cols] = grad.astype(rows_ref.dtype)
            send(cols)
    for copy in outs:
        copy.wait()


def combine_kernel(groups, place_ref, pos_ref, gate_ref, rows_ref, tokens_ref, gates_ref):
    top, count = pos_ref.shape
    slots = rows_ref.shape[0]
    width = tokens_ref.shape[1]
    share = width // groups
    places = lax.broadcasted_iota(jnp.int32, (slots, count), 0)
    picks = [
        jnp.where(places == pos_ref[k : k + 1, :], 1.0, 0.0).astype(jnp.bfloat16)
        for k in range(top)
    ]
    both = sum(picks)
    for k in range(groups):
        at = lax.rem(place_ref[0] - k + groups, groups) * share
        tokens_ref[:, pl.ds(pl.multiple_of(at, share), share)] = contract_first(
            both, rows_ref[:, k * share : (k + 1) * share]
        ).astype(tokens_ref.dtype)
    for k in range(top):
        score = contract_first(rows_ref[:, width:], picks[k])
        gates_ref[k : k + 1, :] = score[:1, :] / gate_ref[k : k + 1, :]


def per_device(tokens, routes, gates, grad_out, w_gate, w_up, w_down):
    experts = lax.axis_size("expert")
    groups = lax.axis_size("dp")
    group = lax.axis_index("dp")
    count, width = tokens.shape
    top = routes.shape[1]
    cap = 3 * count * top // (2 * experts)
    slots = experts * cap
    share = width // groups
    hidden = w_gate.shape[2]
    params = pltpu.CompilerParams(vmem_limit_bytes=VMEM_BYTES)
    half = lax.div(lax.axis_index("expert"), experts // 2)
    place = jnp.stack([group, half]).astype(jnp.int32)
    place_group, place_half = group.reshape(1), half.reshape(1)
    halves = [list(range(experts // 2)), list(range(experts // 2, experts))]

    def shifted(value, by):
        return lax.ppermute(value, "dp", [(i, (i + by) % groups) for i in range(groups)])

    def across(value):
        pairs = [(i, (i + experts // 2) % experts) for i in range(experts)]
        return lax.ppermute(value, "expert", pairs)

    def exchanged(rows, among=None):
        count = experts if among is None else len(among[0])
        split = rows.reshape(count, rows.shape[0] // count, rows.shape[1])
        moved = lax.all_to_all(
            split, "expert", split_axis=0, concat_axis=0, axis_index_groups=among, tiled=True
        )
        return moved.reshape(rows.shape)

    routes_t, gates_t = jnp.transpose(routes), jnp.transpose(gates)
    routes_all = [routes_t] + [shifted(routes_t, k) for k in range(1, groups)]
    gates_all = [gates_t] + [shifted(gates_t, k) for k in range(1, groups)]
    grads = [
        shifted(
            lax.dynamic_slice(grad_out, (0, lax.rem(group + k, groups) * share), (count, share)), k
        )
        for k in range(1, groups)
    ]
    both = jnp.concatenate([w_gate[0], w_up[0]], axis=0)
    both, gates_own = lax.optimization_barrier((both, gates_t))
    both, grads, routes_all, gates_all = lax.optimization_barrier(
        (both, grads, routes_all, gates_all)
    )
    routes_across = across(routes_t)
    tokens_sent, routes_across = lax.optimization_barrier((tokens, routes_across))
    tokens_across = across(tokens_sent)
    weights_moved = [shifted(both, k) for k in range(1, groups)]

    def in_hbm(value):
        return pltpu.with_memory_space_constraint(value, pltpu.HBM)

    block = tile_of(share, 512)
    steps = share // block
    small_spec = pl.BlockSpec((top, count), lambda c, g: (0, 0))
    scaled = pl.pallas_call(
        functools.partial(dispatch_scaled, experts, cap, groups),
        out_shape=pltpu.HBM((groups * slots, share), jnp.bfloat16),
        grid_spec=pltpu.PrefetchScalarGridSpec(
            num_scalar_prefetch=1,
            grid=(steps,),
            in_specs=[small_spec] * (2 * groups)
            + [pl.BlockSpec((count, block), lambda c, g: (0, g[0] * steps + c))]
            + [pl.BlockSpec((count, block), lambda c, g: (0, c))] * (groups - 1),
            out_specs=pl.BlockSpec((groups * slots, block), lambda c, g: (0, c)),
            scratch_shapes=[
                pltpu.VMEM((groups * slots, groups * count), jnp.bfloat16),
                pltpu.VMEM((groups * slots, LANES), jnp.float32),
            ],
        ),
        compiler_params=params,
        name="dispatch_scaled",
    )(
        place_group,
        in_hbm(routes_t),
        *routes_all[1:],
        in_hbm(gates_own),
        *gates_all[1:],
        in_hbm(grad_out),
        *grads,
    )
    scaled_rows = exchanged(scaled)

    sent, pos = pl.pallas_call(
        functools.partial(dispatch_tokens, experts, cap),
        out_shape=(
            pltpu.HBM((slots, width), jnp.bfloat16),
            jax.ShapeDtypeStruct((top, count), jnp.int32),
        ),
        grid_spec=pltpu.PrefetchScalarGridSpec(
            num_scalar_prefetch=1,
            grid=(groups,),
            in_specs=[small_spec] * 2
            + [
                pl.BlockSpec(
                    (count, share), lambda k, g: (0, lax.rem(g[0] - k + groups, groups))
                )
            ]
            * 2,
            out_specs=(pl.BlockSpec((slots, share), lambda k, g: (0, k)), small_spec),
            scratch_shapes=[pltpu.VMEM((slots, 2 * count), jnp.bfloat16)],
        ),
        cost_estimate=pl.CostEstimate(
            flops=TOKENS_COST_US * 10**9, bytes_accessed=TOKENS_COST_US * 10**6, transcendentals=0
        ),
        compiler_params=params,
        name="dispatch_tokens",
    )(place, in_hbm(routes_t), routes_across, in_hbm(tokens), in_hbm(tokens_across))
    x_rows = exchanged(sent, halves)

    any_spec = pl.BlockSpec(memory_space=pl.ANY)
    whole_spec = pl.BlockSpec(memory_space=pltpu.VMEM)
    *weights_moved, gate_held = pl.pallas_call(
        ready_kernel,
        out_shape=[pltpu.HBM(value.shape, value.dtype) for value in weights_moved]
        + [pltpu.VMEM((share, hidden), jnp.bfloat16)],
        in_specs=[any_spec] * groups,
        out_specs=[any_spec] * (groups - 1) + [whole_spec],
        input_output_aliases={k + 1: k for k in range(groups - 1)},
        scratch_shapes=[pltpu.SemaphoreType.DMA((2,))],
        cost_estimate=pl.CostEstimate(
            flops=READY_COST_US * 10**9, bytes_accessed=READY_COST_US * 10**6, transcendentals=0
        ),
        compiler_params=params,
        name="ready",
    )(in_hbm(w_gate[0]), *[in_hbm(value) for value in weights_moved])

    place_spec = pl.BlockSpec(memory_space=pltpu.SMEM)

    back_own, *rest = pl.pallas_call(
        functools.partial(back_kernel, groups, cap),
        out_shape=[pltpu.HBM((slots, hidden), jnp.float32)]
        + [pltpu.HBM((slots, hidden), jnp.bfloat16)] * (groups - 1)
        + [pltpu.HBM((groups * slots, share), jnp.bfloat16)],
        in_specs=[place_spec, pl.BlockSpec(), pl.BlockSpec()],
        compiler_params=params,
        name="back",
    )(place, scaled_rows, in_hbm(w_down[0]))
    scaled_all = rest[-1]
    back_parts = [shifted(rest[k - 1], -k) for k in range(1, groups)]

    *factors, hidden_own, held, back_kept = pl.pallas_call(
        functools.partial(forward_kernel, groups),
        out_shape=[pltpu.VMEM((slots, hidden), jnp.float32)] * 3
        + [
            pltpu.HBM((slots, hidden), jnp.bfloat16),
            pltpu.VMEM((2 * groups - 1, share, hidden), jnp.bfloat16),
            pltpu.VMEM((slots, hidden), jnp.float32),
        ],
        in_specs=[whole_spec] * 2 + [any_spec] * (groups + 1),
        scratch_shapes=[
            pltpu.VMEM((slots, hidden), jnp.float32),
            pltpu.VMEM((slots, hidden), jnp.float32),
            pltpu.SemaphoreType.DMA((2, 2 * groups - 1)),
            pltpu.SemaphoreType.DMA((1,)),
        ],
        compiler_params=params,
        name="forward",
    )(x_rows, gate_held, in_hbm(back_own), in_hbm(w_up[0]), *[in_hbm(w) for w in weights_moved])

    pieces = groups * (share // tile_of(share, 512))
    returning = pl.pallas_call(
        functools.partial(backward_kernel, groups, cap),
        out_shape=pltpu.HBM((slots, width + LANES), jnp.bfloat16),
        in_specs=[place_spec] + [whole_spec] * (5 + groups),
        out_specs=any_spec,
        scratch_shapes=[
            pltpu.VMEM((slots, hidden), jnp.bfloat16),
            pltpu.VMEM((slots, hidden), jnp.bfloat16),
            pltpu.VMEM((slots, width + LANES), jnp.bfloat16),
            pltpu.SemaphoreType.DMA((pieces + 1,)),
        ],
        compiler_params=params,
        name="backward",
    )(place_half, *factors, gate_held, held, back_kept, *back_parts)
    returned = exchanged(returning)

    hiddens = [hidden_own] + [shifted(hidden_own, k) for k in range(1, groups)]
    grad_down = contract_first(jnp.concatenate(hiddens, axis=0), scaled_all)[None]

    grad_tokens, grad_gates = pl.pallas_call(
        functools.partial(combine_kernel, groups),
        out_shape=(
            jax.ShapeDtypeStruct((count, width), jnp.bfloat16),
            jax.ShapeDtypeStruct((top, count), jnp.float32),
        ),
        in_specs=[pl.BlockSpec(memory_space=pltpu.SMEM)] + [whole_spec] * 3,
        compiler_params=params,
        name="combine",
    )(place_group, pos, gates_t, returned)
    return (grad_tokens, jnp.transpose(grad_gates), grad_down)


def solution(mesh):
    placed = (
        P(("dp", "expert"), None),
        P(("dp", "expert"), None),
        P(("dp", "expert"), None),
        P(("dp", "expert"), None),
        P("expert", "dp", None),
        P("expert", "dp", None),
        P("expert", None, "dp"),
    )
    return jax.shard_map(
        per_device,
        mesh=mesh,
        in_specs=placed,
        out_specs=(P(("dp", "expert"), None), P(("dp", "expert"), None), P("expert", None, "dp")),
        check_vma=False,
    )
```

```python
import functools

import jax
import jax.numpy as jnp
from jax import lax
from jax.experimental import pallas as pl
from jax.experimental.pallas import tpu as pltpu
from jax.sharding import PartitionSpec as P

LANES = 128
VMEM_BYTES = 24 * 1024 * 1024
READY_COST_US = 30
TOKENS_COST_US = 30


def contract_last(left, right):
    return lax.dot_general(
        left, right, (((1,), (1,)), ((), ())), preferred_element_type=jnp.float32
    )


def contract_first(left, right):
    return lax.dot_general(
        left, right, (((0,), (0,)), ((), ())), preferred_element_type=jnp.float32
    )


def tile_of(extent, most):
    return most if extent % most == 0 else extent


def slot_positions(routes, experts, stride, base):
    top, count = routes.shape
    labels = lax.broadcasted_iota(jnp.int32, (experts, count), 0)
    named = [labels == routes[k : k + 1, :] for k in range(top)]
    marks = sum(jnp.where(m, 1.0, 0.0) for m in named)
    earlier = lax.broadcasted_iota(jnp.int32, (count, count), 0) < lax.broadcasted_iota(
        jnp.int32, (count, count), 1
    )
    rank = jnp.dot(
        marks.astype(jnp.bfloat16),
        jnp.where(earlier, 1.0, 0.0).astype(jnp.bfloat16),
        preferred_element_type=jnp.float32,
    )
    slot = rank + (labels * stride + base + 1).astype(jnp.float32)
    return [
        jnp.sum(jnp.where(m, slot, 0.0), axis=0, keepdims=True).astype(jnp.int32) - 1
        for m in named
    ]


def by_half(value, cap, half, paired):
    count, width = value.shape
    if paired:
        value = value.reshape(count // (2 * cap), 2, cap, width)
        own, other = value[:, 0], value[:, 1]
    else:
        value = value.reshape(2, count // (2 * cap), cap, width)
        own, other = value[0], value[1]
    first = jnp.where(half == 0, own, other)
    second = jnp.where(half == 0, other, own)
    return jnp.stack([first, second], axis=0 if paired else 1).reshape(count, width)


def dispatch_tokens(experts, cap, place_ref, *refs):
    routes_refs, tokens_refs, (out_ref, pos_ref, pick_ref) = refs[:2], refs[2:4], refs[4:]
    count = tokens_refs[0].shape[0]

    @pl.when(pl.program_id(0) == 0)
    def _():
        rows = lax.broadcasted_iota(jnp.int32, (pick_ref.shape[0], count), 0)
        for c, ref in enumerate(routes_refs):
            near = ref[...] - place_ref[1] * (experts // 2)
            pos = slot_positions(near, experts // 2, 2 * cap, c * cap)
            pick_ref[:, c * count : (c + 1) * count] = sum(
                jnp.where(rows == p, 1.0, 0.0) for p in pos
            ).astype(jnp.bfloat16)
        for k, p in enumerate(slot_positions(routes_refs[0][...], experts, cap, 0)):
            pos_ref[k : k + 1, :] = p

    values = jnp.concatenate([ref[...] for ref in tokens_refs], axis=0)
    out_ref[...] = jnp.dot(
        pick_ref[...], values, preferred_element_type=jnp.float32
    ).astype(out_ref.dtype)


def dispatch_scaled(experts, cap, groups, place_ref, *refs):
    routes_refs, gate_refs = refs[:groups], refs[groups : 2 * groups]
    grad_refs, (out_ref, pick_ref, scale_ref) = refs[2 * groups : 3 * groups], refs[3 * groups :]
    count = grad_refs[0].shape[0]
    slots = out_ref.shape[0]

    @pl.when(pl.program_id(0) == 0)
    def _():
        rows = lax.broadcasted_iota(jnp.int32, (slots, count), 0)
        total = jnp.zeros((slots, 1), jnp.float32)
        for q in range(groups):
            pos = slot_positions(routes_refs[q][...], experts, groups * cap, q * cap)
            hit = jnp.zeros((slots, count), jnp.float32)
            weight = jnp.zeros((slots, count), jnp.float32)
            for k, p in enumerate(pos):
                here = rows == p
                hit = hit + jnp.where(here, 1.0, 0.0)
                weight = weight + jnp.where(here, gate_refs[q][k : k + 1, :], 0.0)
            pick_ref[:, q * count : (q + 1) * count] = hit.astype(jnp.bfloat16)
            total = total + jnp.sum(weight, axis=1, keepdims=True)
        scale_ref[...] = jnp.broadcast_to(total, scale_ref.shape)

    grads = jnp.concatenate([ref[...] for ref in grad_refs], axis=0)
    rows = jnp.dot(pick_ref[...], grads, preferred_element_type=jnp.float32)
    out_ref[...] = (scale_ref[:, :1] * rows).astype(out_ref.dtype)


def stack_kernel(pieces, top_ref, bottom_ref, out_ref, held_ref, sems):
    extent = top_ref.shape[0]
    each = extent // pieces
    moves = []
    for i, ref in enumerate((top_ref, bottom_ref)):
        for n in range(pieces):
            to = slice(i * extent + n * each, i * extent + (n + 1) * each)
            number = i * pieces + n
            load = pltpu.make_async_copy(
                ref.at[n * each : (n + 1) * each], held_ref.at[to], sems.at[0, number]
            )
            moves.append(
                (load, pltpu.make_async_copy(held_ref.at[to], out_ref.at[to], sems.at[1, number]))
            )
    for load, _ in moves:
        load.start()
    for load, store in moves:
        load.wait()
        store.start()
    for _, store in moves:
        store.wait()


def ready_kernel(gate_ref, *refs):
    held_ref, sems = refs[-2:]
    half = gate_ref.shape[0] // 2
    copies = [
        pltpu.make_async_copy(
            gate_ref.at[n * half : (n + 1) * half],
            held_ref.at[n * half : (n + 1) * half],
            sems.at[n],
        )
        for n in range(2)
    ]
    for copy in copies:
        copy.start()
    for copy in copies:
        copy.wait()


def back_kernel(groups, cap, place_ref, rows_ref, down_ref, own_ref, *rest):
    others, all_ref = rest[: groups - 1], rest[groups - 1]
    slots, hidden = own_ref.shape
    count, share = rows_ref.shape
    rows = rows_ref[...].astype(jnp.float32).reshape(count // (groups * cap), groups, cap, share)
    for q in range(groups):
        ordered = by_half(rows[:, q].reshape(slots, share), cap, place_ref[1], False)
        all_ref[q * slots : (q + 1) * slots, :] = ordered.astype(all_ref.dtype)
    step = tile_of(hidden, 256)

    @pl.loop(0, hidden // step)
    def _(j):
        cols = pl.ds(pl.multiple_of(j * step, step), step)
        for q, ref in enumerate((own_ref, *others)):
            part = contract_last(all_ref[q * slots : (q + 1) * slots, :], down_ref[cols, :])
            ref[:, cols] = part.astype(ref.dtype)


def forward_kernel(groups, x_ref, gate_ref, back_ref, own_up_ref, *refs):
    others = refs[: groups - 1]
    act_ref, slope_ref, value_ref, hidden_ref, held_ref, kept_ref = refs[groups - 1 : groups + 5]
    gate_sum_ref, up_sum_ref, sems, back_sem = refs[groups + 5 :]
    share, hidden = gate_ref.shape
    step = tile_of(hidden, 256)
    sources = [gate_ref, *[ref.at[:share] for ref in others]]
    sources += [own_up_ref, *[ref.at[share:] for ref in others]]
    spans = [slice(at, at + step) for at in range(0, hidden, step)]

    order = [i for k in range(groups) for i in (k, groups + k)]
    part_rows = share // 2
    stages = [
        [
            pltpu.make_async_copy(
                sources[i].at[n * part_rows : (n + 1) * part_rows],
                held_ref.at[i - 1, n * part_rows : (n + 1) * part_rows],
                sems.at[n, i - 1],
            )
            for n in range(2)
        ]
        for i in order[1:]
    ]
    stages[-1].append(pltpu.make_async_copy(back_ref, kept_ref, back_sem.at[0]))

    def finish(cols):
        pre_gate, pre_up = gate_sum_ref[:, cols], up_sum_ref[:, cols]
        sig = jax.nn.sigmoid(pre_gate)
        act = pre_gate * sig
        hidden_f = act * pre_up
        act_ref[:, cols] = act
        slope_ref[:, cols] = pre_up * (sig * (1.0 + pre_gate * (1.0 - sig)))
        value_ref[:, cols] = hidden_f
        hidden_ref[:, cols] = hidden_f.astype(hidden_ref.dtype)

    ahead = 3
    for copies in stages[:ahead]:
        for copy in copies:
            copy.start()
    complete = None
    for at, i in enumerate(order):
        k = i % groups
        if at > 0:
            for copy in stages[at - 1]:
                copy.wait()
            if at - 1 + ahead < len(stages):
                for copy in stages[at - 1 + ahead]:
                    copy.start()
        sum_ref = gate_sum_ref if i < groups else up_sum_ref
        for cols in spans:
            part = jnp.dot(
                x_ref[:, k * share : (k + 1) * share],
                gate_ref[:, cols] if i == 0 else held_ref[i - 1, :, cols],
                preferred_element_type=jnp.float32,
            )
            if complete is not None:
                finish(complete)
            sum_ref[:, cols] = part if k == 0 else sum_ref[:, cols] + part
            complete = cols if i == order[-1] else None
    finish(complete)


def backward_kernel(
    groups, cap, half_ref, act_ref, slope_ref, value_ref, gate_ref, held_ref, *refs
):
    parts, (out_ref, d_gate_ref, d_up_ref, rows_ref, out_sems) = refs[:groups], refs[groups:]
    share = held_ref.shape[1]
    width = groups * share
    block = tile_of(share, 512)
    half = half_ref[0]
    back = sum(part[...].astype(jnp.float32) for part in parts)
    score = jnp.sum(back * value_ref[...], axis=1, keepdims=True)
    d_gate_ref[...] = by_half(back * slope_ref[...], cap, half, True).astype(jnp.bfloat16)
    d_up_ref[...] = by_half(back * act_ref[...], cap, half, True).astype(jnp.bfloat16)
    score = by_half(jnp.broadcast_to(score, (score.shape[0], LANES)), cap, half, True)
    rows_ref[:, width:] = score.astype(rows_ref.dtype)
    outs = []

    def send(cols):
        copy = pltpu.make_async_copy(
            rows_ref.at[:, cols], out_ref.at[:, cols], out_sems.at[len(outs)]
        )
        copy.start()
        outs.append(copy)

    send(slice(width, width + LANES))
    for k in range(groups):
        for at in range(0, share, block):
            cols = slice(k * share + at, k * share + at + block)
            gate = gate_ref[at : at + block] if k == 0 else held_ref[k - 1, at : at + block]
            grad = contract_last(d_gate_ref[...], gate)
            grad += contract_last(d_up_ref[...], held_ref[groups - 1 + k, at : at + block])
            rows_ref[:, cols] = grad.astype(rows_ref.dtype)
            send(cols)
    for copy in outs:
        copy.wait()


def combine_kernel(groups, place_ref, pos_ref, gate_ref, rows_ref, tokens_ref, gates_ref):
    top, count = pos_ref.shape
    slots = rows_ref.shape[0]
    width = tokens_ref.shape[1]
    share = width // groups
    places = lax.broadcasted_iota(jnp.int32, (slots, count), 0)
    picks = [
        jnp.where(places == pos_ref[k : k + 1, :], 1.0, 0.0).astype(jnp.bfloat16)
        for k in range(top)
    ]
    both = sum(picks)
    for k in range(groups):
        at = lax.rem(place_ref[0] - k + groups, groups) * share
        tokens_ref[:, pl.ds(pl.multiple_of(at, share), share)] = contract_first(
            both, rows_ref[:, k * share : (k + 1) * share]
        ).astype(tokens_ref.dtype)
    for k in range(top):
        score = contract_first(rows_ref[:, width:], picks[k])
        gates_ref[k : k + 1, :] = score[:1, :] / gate_ref[k : k + 1, :]


def per_device(tokens, routes, gates, grad_out, w_gate, w_up, w_down):
    experts = lax.axis_size("expert")
    groups = lax.axis_size("dp")
    group = lax.axis_index("dp")
    count, width = tokens.shape
    top = routes.shape[1]
    cap = 3 * count * top // (2 * experts)
    slots = experts * cap
    share = width // groups
    hidden = w_gate.shape[2]
    params = pltpu.CompilerParams(vmem_limit_bytes=VMEM_BYTES)
    half = lax.div(lax.axis_index("expert"), experts // 2)
    place = jnp.stack([group, half]).astype(jnp.int32)
    place_group, place_half = group.reshape(1), half.reshape(1)
    halves = [list(range(experts // 2)), list(range(experts // 2, experts))]

    def shifted(value, by):
        return lax.ppermute(value, "dp", [(i, (i + by) % groups) for i in range(groups)])

    def across(value):
        pairs = [(i, (i + experts // 2) % experts) for i in range(experts)]
        return lax.ppermute(value, "expert", pairs)

    def exchanged(rows, among=None):
        count = experts if among is None else len(among[0])
        split = rows.reshape(count, rows.shape[0] // count, rows.shape[1])
        moved = lax.all_to_all(
            split, "expert", split_axis=0, concat_axis=0, axis_index_groups=among, tiled=True
        )
        return moved.reshape(rows.shape)

    def in_hbm(value):
        return pltpu.with_memory_space_constraint(value, pltpu.HBM)

    routes_t, gates_t = jnp.transpose(routes), jnp.transpose(gates)
    routes_all = [routes_t] + [shifted(routes_t, k) for k in range(1, groups)]
    gates_all = [gates_t] + [shifted(gates_t, k) for k in range(1, groups)]
    grads = [
        shifted(
            lax.dynamic_slice(grad_out, (0, lax.rem(group + k, groups) * share), (count, share)), k
        )
        for k in range(1, groups)
    ]
    any_spec = pl.BlockSpec(memory_space=pl.ANY)
    both = pl.pallas_call(
        functools.partial(stack_kernel, 4),
        out_shape=pltpu.HBM((2 * share, hidden), jnp.bfloat16),
        in_specs=[any_spec] * 2,
        out_specs=any_spec,
        scratch_shapes=[
            pltpu.VMEM((2 * share, hidden), jnp.bfloat16),
            pltpu.SemaphoreType.DMA((2, 8)),
        ],
        cost_estimate=pl.CostEstimate(
            flops=4 * 10**9, bytes_accessed=8 * share * hidden, transcendentals=0
        ),
        compiler_params=params,
        name="stack",
    )(in_hbm(w_gate[0]), in_hbm(w_up[0]))
    both, gates_own = lax.optimization_barrier((both, gates_t))
    both, grads, routes_all, gates_all = lax.optimization_barrier(
        (both, grads, routes_all, gates_all)
    )
    routes_across = across(routes_t)
    tokens_sent, routes_across = lax.optimization_barrier((tokens, routes_across))
    tokens_across = across(tokens_sent)
    weights_moved = [shifted(both, k) for k in range(1, groups)]

    block = tile_of(share, 512)
    steps = share // block
    small_spec = pl.BlockSpec((top, count), lambda c, g: (0, 0))
    scaled = pl.pallas_call(
        functools.partial(dispatch_scaled, experts, cap, groups),
        out_shape=pltpu.HBM((groups * slots, share), jnp.bfloat16),
        grid_spec=pltpu.PrefetchScalarGridSpec(
            num_scalar_prefetch=1,
            grid=(steps,),
            in_specs=[small_spec] * (2 * groups)
            + [pl.BlockSpec((count, block), lambda c, g: (0, g[0] * steps + c))]
            + [pl.BlockSpec((count, block), lambda c, g: (0, c))] * (groups - 1),
            out_specs=pl.BlockSpec((groups * slots, block), lambda c, g: (0, c)),
            scratch_shapes=[
                pltpu.VMEM((groups * slots, groups * count), jnp.bfloat16),
                pltpu.VMEM((groups * slots, LANES), jnp.float32),
            ],
        ),
        compiler_params=params,
        name="dispatch_scaled",
    )(
        place_group,
        in_hbm(routes_t),
        *routes_all[1:],
        in_hbm(gates_own),
        *gates_all[1:],
        in_hbm(grad_out),
        *grads,
    )
    scaled_rows = exchanged(scaled)

    sent, pos = pl.pallas_call(
        functools.partial(dispatch_tokens, experts, cap),
        out_shape=(
            pltpu.HBM((slots, width), jnp.bfloat16),
            jax.ShapeDtypeStruct((top, count), jnp.int32),
        ),
        grid_spec=pltpu.PrefetchScalarGridSpec(
            num_scalar_prefetch=1,
            grid=(groups,),
            in_specs=[small_spec] * 2
            + [
                pl.BlockSpec(
                    (count, share), lambda k, g: (0, lax.rem(g[0] - k + groups, groups))
                )
            ]
            * 2,
            out_specs=(pl.BlockSpec((slots, share), lambda k, g: (0, k)), small_spec),
            scratch_shapes=[pltpu.VMEM((slots, 2 * count), jnp.bfloat16)],
        ),
        cost_estimate=pl.CostEstimate(
            flops=TOKENS_COST_US * 10**9, bytes_accessed=TOKENS_COST_US * 10**6, transcendentals=0
        ),
        compiler_params=params,
        name="dispatch_tokens",
    )(place, in_hbm(routes_t), routes_across, in_hbm(tokens), in_hbm(tokens_across))
    x_rows = exchanged(sent, halves)

    whole_spec = pl.BlockSpec(memory_space=pltpu.VMEM)
    *weights_moved, gate_held = pl.pallas_call(
        ready_kernel,
        out_shape=[pltpu.HBM(value.shape, value.dtype) for value in weights_moved]
        + [pltpu.VMEM((share, hidden), jnp.bfloat16)],
        in_specs=[any_spec] * groups,
        out_specs=[any_spec] * (groups - 1) + [whole_spec],
        input_output_aliases={k + 1: k for k in range(groups - 1)},
        scratch_shapes=[pltpu.SemaphoreType.DMA((2,))],
        cost_estimate=pl.CostEstimate(
            flops=READY_COST_US * 10**9, bytes_accessed=READY_COST_US * 10**6, transcendentals=0
        ),
        compiler_params=params,
        name="ready",
    )(in_hbm(w_gate[0]), *[in_hbm(value) for value in weights_moved])

    place_spec = pl.BlockSpec(memory_space=pltpu.SMEM)

    back_own, *rest = pl.pallas_call(
        functools.partial(back_kernel, groups, cap),
        out_shape=[pltpu.HBM((slots, hidden), jnp.float32)]
        + [pltpu.HBM((slots, hidden), jnp.bfloat16)] * (groups - 1)
        + [pltpu.HBM((groups * slots, share), jnp.bfloat16)],
        in_specs=[place_spec, pl.BlockSpec(), pl.BlockSpec()],
        compiler_params=params,
        name="back",
    )(place, scaled_rows, in_hbm(w_down[0]))
    scaled_all = rest[-1]
    back_parts = [shifted(rest[k - 1], -k) for k in range(1, groups)]

    *factors, hidden_own, held, back_kept = pl.pallas_call(
        functools.partial(forward_kernel, groups),
        out_shape=[pltpu.VMEM((slots, hidden), jnp.float32)] * 3
        + [
            pltpu.HBM((slots, hidden), jnp.bfloat16),
            pltpu.VMEM((2 * groups - 1, share, hidden), jnp.bfloat16),
            pltpu.VMEM((slots, hidden), jnp.float32),
        ],
        in_specs=[whole_spec] * 2 + [any_spec] * (groups + 1),
        scratch_shapes=[
            pltpu.VMEM((slots, hidden), jnp.float32),
            pltpu.VMEM((slots, hidden), jnp.float32),
            pltpu.SemaphoreType.DMA((2, 2 * groups - 1)),
            pltpu.SemaphoreType.DMA((1,)),
        ],
        compiler_params=params,
        name="forward",
    )(x_rows, gate_held, in_hbm(back_own), in_hbm(w_up[0]), *[in_hbm(w) for w in weights_moved])

    pieces = groups * (share // tile_of(share, 512))
    returning = pl.pallas_call(
        functools.partial(backward_kernel, groups, cap),
        out_shape=pltpu.HBM((slots, width + LANES), jnp.bfloat16),
        in_specs=[place_spec] + [whole_spec] * (5 + groups),
        out_specs=any_spec,
        scratch_shapes=[
            pltpu.VMEM((slots, hidden), jnp.bfloat16),
            pltpu.VMEM((slots, hidden), jnp.bfloat16),
            pltpu.VMEM((slots, width + LANES), jnp.bfloat16),
            pltpu.SemaphoreType.DMA((pieces + 1,)),
        ],
        compiler_params=params,
        name="backward",
    )(place_half, *factors, gate_held, held, back_kept, *back_parts)
    returned = exchanged(returning)

    hiddens = [hidden_own] + [shifted(hidden_own, k) for k in range(1, groups)]
    grad_down = contract_first(jnp.concatenate(hiddens, axis=0), scaled_all)[None]

    grad_tokens, grad_gates = pl.pallas_call(
        functools.partial(combine_kernel, groups),
        out_shape=(
            jax.ShapeDtypeStruct((count, width), jnp.bfloat16),
            jax.ShapeDtypeStruct((top, count), jnp.float32),
        ),
        in_specs=[pl.BlockSpec(memory_space=pltpu.SMEM)] + [whole_spec] * 3,
        compiler_params=params,
        name="combine",
    )(place_group, pos, gates_t, returned)
    return (grad_tokens, jnp.transpose(grad_gates), grad_down)


def solution(mesh):
    placed = (
        P(("dp", "expert"), None),
        P(("dp", "expert"), None),
        P(("dp", "expert"), None),
        P(("dp", "expert"), None),
        P("expert", "dp", None),
        P("expert", "dp", None),
        P("expert", None, "dp"),
    )
    return jax.shard_map(
        per_device,
        mesh=mesh,
        in_specs=placed,
        out_specs=(P(("dp", "expert"), None), P(("dp", "expert"), None), P("expert", None, "dp")),
        check_vma=False,
    )
```

```python
import functools

import jax
import jax.numpy as jnp
from jax import lax
from jax.experimental import pallas as pl
from jax.experimental.pallas import tpu as pltpu
from jax.sharding import PartitionSpec as P

LANES = 128
VMEM_BYTES = 24 * 1024 * 1024
READY_COST_US = 30
TOKENS_COST_US = 30


def contract_last(left, right):
    return lax.dot_general(
        left, right, (((1,), (1,)), ((), ())), preferred_element_type=jnp.float32
    )


def contract_first(left, right):
    return lax.dot_general(
        left, right, (((0,), (0,)), ((), ())), preferred_element_type=jnp.float32
    )


def tile_of(extent, most):
    return most if extent % most == 0 else extent


def slot_positions(routes, experts, stride, base):
    top, count = routes.shape
    labels = lax.broadcasted_iota(jnp.int32, (experts, count), 0)
    named = [labels == routes[k : k + 1, :] for k in range(top)]
    marks = sum(jnp.where(m, 1.0, 0.0) for m in named)
    earlier = lax.broadcasted_iota(jnp.int32, (count, count), 0) < lax.broadcasted_iota(
        jnp.int32, (count, count), 1
    )
    rank = jnp.dot(
        marks.astype(jnp.bfloat16),
        jnp.where(earlier, 1.0, 0.0).astype(jnp.bfloat16),
        preferred_element_type=jnp.float32,
    )
    slot = rank + (labels * stride + base + 1).astype(jnp.float32)
    return [
        jnp.sum(jnp.where(m, slot, 0.0), axis=0, keepdims=True).astype(jnp.int32) - 1
        for m in named
    ]


def by_half(value, cap, half, paired):
    count, width = value.shape
    if paired:
        value = value.reshape(count // (2 * cap), 2, cap, width)
        own, other = value[:, 0], value[:, 1]
    else:
        value = value.reshape(2, count // (2 * cap), cap, width)
        own, other = value[0], value[1]
    first = jnp.where(half == 0, own, other)
    second = jnp.where(half == 0, other, own)
    return jnp.stack([first, second], axis=0 if paired else 1).reshape(count, width)


def dispatch_tokens(experts, cap, place_ref, *refs):
    routes_refs, tokens_refs, (out_ref, pos_ref, pick_ref) = refs[:2], refs[2:4], refs[4:]
    count = tokens_refs[0].shape[0]

    @pl.when(pl.program_id(0) == 0)
    def _():
        rows = lax.broadcasted_iota(jnp.int32, (pick_ref.shape[0], count), 0)
        for c, ref in enumerate(routes_refs):
            near = ref[...] - place_ref[1] * (experts // 2)
            pos = slot_positions(near, experts // 2, 2 * cap, c * cap)
            pick_ref[:, c * count : (c + 1) * count] = sum(
                jnp.where(rows == p, 1.0, 0.0) for p in pos
            ).astype(jnp.bfloat16)
        for k, p in enumerate(slot_positions(routes_refs[0][...], experts, cap, 0)):
            pos_ref[k : k + 1, :] = p

    values = jnp.concatenate([ref[...] for ref in tokens_refs], axis=0)
    out_ref[...] = jnp.dot(
        pick_ref[...], values, preferred_element_type=jnp.float32
    ).astype(out_ref.dtype)


def dispatch_scaled(experts, cap, groups, place_ref, *refs):
    routes_refs, gate_refs = refs[:groups], refs[groups : 2 * groups]
    grad_refs, (out_ref, pick_ref, scale_ref) = refs[2 * groups : 3 * groups], refs[3 * groups :]
    count = grad_refs[0].shape[0]
    slots = out_ref.shape[0]

    @pl.when(pl.program_id(0) == 0)
    def _():
        rows = lax.broadcasted_iota(jnp.int32, (slots, count), 0)
        total = jnp.zeros((slots, 1), jnp.float32)
        for q in range(groups):
            pos = slot_positions(routes_refs[q][...], experts, groups * cap, q * cap)
            hit = jnp.zeros((slots, count), jnp.float32)
            weight = jnp.zeros((slots, count), jnp.float32)
            for k, p in enumerate(pos):
                here = rows == p
                hit = hit + jnp.where(here, 1.0, 0.0)
                weight = weight + jnp.where(here, gate_refs[q][k : k + 1, :], 0.0)
            pick_ref[:, q * count : (q + 1) * count] = hit.astype(jnp.bfloat16)
            total = total + jnp.sum(weight, axis=1, keepdims=True)
        scale_ref[...] = jnp.broadcast_to(total, scale_ref.shape)

    grads = jnp.concatenate([ref[...] for ref in grad_refs], axis=0)
    rows = jnp.dot(pick_ref[...], grads, preferred_element_type=jnp.float32)
    out_ref[...] = (scale_ref[:, :1] * rows).astype(out_ref.dtype)


def ready_kernel(gate_ref, *refs):
    held_ref, sems = refs[-2:]
    half = gate_ref.shape[0] // 2
    copies = [
        pltpu.make_async_copy(
            gate_ref.at[n * half : (n + 1) * half],
            held_ref.at[n * half : (n + 1) * half],
            sems.at[n],
        )
        for n in range(2)
    ]
    for copy in copies:
        copy.start()
    for copy in copies:
        copy.wait()


def back_kernel(groups, cap, place_ref, rows_ref, down_ref, own_ref, *rest):
    others, all_ref = rest[: groups - 1], rest[groups - 1]
    slots, hidden = own_ref.shape
    count, share = rows_ref.shape
    rows = rows_ref[...].astype(jnp.float32).reshape(count // (groups * cap), groups, cap, share)
    for q in range(groups):
        ordered = by_half(rows[:, q].reshape(slots, share), cap, place_ref[1], False)
        all_ref[q * slots : (q + 1) * slots, :] = ordered.astype(all_ref.dtype)
    step = tile_of(hidden, 256)

    @pl.loop(0, hidden // step)
    def _(j):
        cols = pl.ds(pl.multiple_of(j * step, step), step)
        for q, ref in enumerate((own_ref, *others)):
            part = contract_last(all_ref[q * slots : (q + 1) * slots, :], down_ref[cols, :])
            ref[:, cols] = part.astype(ref.dtype)


def forward_kernel(groups, x_ref, gate_ref, back_ref, own_up_ref, *refs):
    others = refs[: groups - 1]
    act_ref, slope_ref, value_ref, hidden_ref, held_ref, kept_ref = refs[groups - 1 : groups + 5]
    gate_sum_ref, up_sum_ref, sems, back_sem = refs[groups + 5 :]
    share, hidden = gate_ref.shape
    step = tile_of(hidden, 256)
    sources = [gate_ref, *[ref.at[:share] for ref in others]]
    sources += [own_up_ref, *[ref.at[share:] for ref in others]]
    spans = [slice(at, at + step) for at in range(0, hidden, step)]

    order = [i for k in range(groups) for i in (k, groups + k)]
    part_rows = share // 2
    stages = [
        [
            pltpu.make_async_copy(
                sources[i].at[n * part_rows : (n + 1) * part_rows],
                held_ref.at[i - 1, n * part_rows : (n + 1) * part_rows],
                sems.at[n, i - 1],
            )
            for n in range(2)
        ]
        for i in order[1:]
    ]
    stages[-1].append(pltpu.make_async_copy(back_ref, kept_ref, back_sem.at[0]))

    def finish(cols):
        pre_gate, pre_up = gate_sum_ref[:, cols], up_sum_ref[:, cols]
        sig = jax.nn.sigmoid(pre_gate)
        act = pre_gate * sig
        hidden_f = act * pre_up
        act_ref[:, cols] = act
        slope_ref[:, cols] = pre_up * (sig * (1.0 + pre_gate * (1.0 - sig)))
        value_ref[:, cols] = hidden_f
        hidden_ref[:, cols] = hidden_f.astype(hidden_ref.dtype)

    ahead = 3
    for copies in stages[:ahead]:
        for copy in copies:
            copy.start()
    complete = None
    for at, i in enumerate(order):
        k = i % groups
        if at > 0:
            for copy in stages[at - 1]:
                copy.wait()
            if at - 1 + ahead < len(stages):
                for copy in stages[at - 1 + ahead]:
                    copy.start()
        sum_ref = gate_sum_ref if i < groups else up_sum_ref
        for cols in spans:
            part = jnp.dot(
                x_ref[:, k * share : (k + 1) * share],
                gate_ref[:, cols] if i == 0 else held_ref[i - 1, :, cols],
                preferred_element_type=jnp.float32,
            )
            if complete is not None:
                finish(complete)
            sum_ref[:, cols] = part if k == 0 else sum_ref[:, cols] + part
            complete = cols if i == order[-1] else None
    finish(complete)


def backward_kernel(
    groups, cap, half_ref, act_ref, slope_ref, value_ref, gate_ref, held_ref, *refs
):
    parts, (out_ref, d_gate_ref, d_up_ref, rows_ref, out_sems) = refs[:groups], refs[groups:]
    share = held_ref.shape[1]
    width = groups * share
    block = tile_of(share, 512)
    half = half_ref[0]
    back = sum(part[...].astype(jnp.float32) for part in parts)
    score = jnp.sum(back * value_ref[...], axis=1, keepdims=True)
    d_gate_ref[...] = by_half(back * slope_ref[...], cap, half, True).astype(jnp.bfloat16)
    d_up_ref[...] = by_half(back * act_ref[...], cap, half, True).astype(jnp.bfloat16)
    score = by_half(jnp.broadcast_to(score, (score.shape[0], LANES)), cap, half, True)
    rows_ref[:, width:] = score.astype(rows_ref.dtype)
    outs = []

    def send(cols):
        copy = pltpu.make_async_copy(
            rows_ref.at[:, cols], out_ref.at[:, cols], out_sems.at[len(outs)]
        )
        copy.start()
        outs.append(copy)

    send(slice(width, width + LANES))
    for k in range(groups):
        for at in range(0, share, block):
            cols = slice(k * share + at, k * share + at + block)
            gate = gate_ref[at : at + block] if k == 0 else held_ref[k - 1, at : at + block]
            grad = contract_last(d_gate_ref[...], gate)
            grad += contract_last(d_up_ref[...], held_ref[groups - 1 + k, at : at + block])
            rows_ref[:, cols] = grad.astype(rows_ref.dtype)
            send(cols)
    for copy in outs:
        copy.wait()


def combine_kernel(groups, place_ref, pos_ref, gate_ref, rows_ref, tokens_ref, gates_ref):
    top, count = pos_ref.shape
    slots = rows_ref.shape[0]
    width = tokens_ref.shape[1]
    share = width // groups
    places = lax.broadcasted_iota(jnp.int32, (slots, count), 0)
    picks = [
        jnp.where(places == pos_ref[k : k + 1, :], 1.0, 0.0).astype(jnp.bfloat16)
        for k in range(top)
    ]
    both = sum(picks)
    for k in range(groups):
        at = lax.rem(place_ref[0] - k + groups, groups) * share
        tokens_ref[:, pl.ds(pl.multiple_of(at, share), share)] = contract_first(
            both, rows_ref[:, k * share : (k + 1) * share]
        ).astype(tokens_ref.dtype)
    for k in range(top):
        score = contract_first(rows_ref[:, width:], picks[k])
        gates_ref[k : k + 1, :] = score[:1, :] / gate_ref[k : k + 1, :]


def per_device(tokens, routes, gates, grad_out, w_gate, w_up, w_down):
    experts = lax.axis_size("expert")
    groups = lax.axis_size("dp")
    group = lax.axis_index("dp")
    count, width = tokens.shape
    top = routes.shape[1]
    cap = 3 * count * top // (2 * experts)
    slots = experts * cap
    share = width // groups
    hidden = w_gate.shape[2]
    params = pltpu.CompilerParams(vmem_limit_bytes=VMEM_BYTES)
    half = lax.div(lax.axis_index("expert"), experts // 2)
    place = jnp.stack([group, half]).astype(jnp.int32)
    place_group, place_half = group.reshape(1), half.reshape(1)
    halves = [list(range(experts // 2)), list(range(experts // 2, experts))]

    def shifted(value, by):
        return lax.ppermute(value, "dp", [(i, (i + by) % groups) for i in range(groups)])

    def across(value):
        pairs = [(i, (i + experts // 2) % experts) for i in range(experts)]
        return lax.ppermute(value, "expert", pairs)

    def exchanged(rows, among=None):
        count = experts if among is None else len(among[0])
        split = rows.reshape(count, rows.shape[0] // count, rows.shape[1])
        moved = lax.all_to_all(
            split, "expert", split_axis=0, concat_axis=0, axis_index_groups=among, tiled=True
        )
        return moved.reshape(rows.shape)

    routes_t, gates_t = jnp.transpose(routes), jnp.transpose(gates)
    routes_all = [routes_t] + [shifted(routes_t, k) for k in range(1, groups)]
    gates_all = [gates_t] + [shifted(gates_t, k) for k in range(1, groups)]
    grads = [
        shifted(
            lax.dynamic_slice(grad_out, (0, lax.rem(group + k, groups) * share), (count, share)), k
        )
        for k in range(1, groups)
    ]
    both = jnp.concatenate([w_gate[0], w_up[0]], axis=0)
    both, gates_own = lax.optimization_barrier((both, gates_t))
    both, grads, routes_all, gates_all = lax.optimization_barrier(
        (both, grads, routes_all, gates_all)
    )
    routes_across = across(routes_t)
    tokens_sent, routes_across = lax.optimization_barrier((tokens, routes_across))
    tokens_across = across(tokens_sent)
    weights_moved = [shifted(both, k) for k in range(1, groups)]

    def in_hbm(value):
        return pltpu.with_memory_space_constraint(value, pltpu.HBM)

    block = tile_of(share, 1024)
    steps = share // block
    small_spec = pl.BlockSpec((top, count), lambda c, g: (0, 0))
    scaled = pl.pallas_call(
        functools.partial(dispatch_scaled, experts, cap, groups),
        out_shape=pltpu.HBM((groups * slots, share), jnp.bfloat16),
        grid_spec=pltpu.PrefetchScalarGridSpec(
            num_scalar_prefetch=1,
            grid=(steps,),
            in_specs=[small_spec] * (2 * groups)
            + [pl.BlockSpec((count, block), lambda c, g: (0, g[0] * steps + c))]
            + [pl.BlockSpec((count, block), lambda c, g: (0, c))] * (groups - 1),
            out_specs=pl.BlockSpec((groups * slots, block), lambda c, g: (0, c)),
            scratch_shapes=[
                pltpu.VMEM((groups * slots, groups * count), jnp.bfloat16),
                pltpu.VMEM((groups * slots, LANES), jnp.float32),
            ],
        ),
        compiler_params=params,
        name="dispatch_scaled",
    )(
        place_group,
        in_hbm(routes_t),
        *routes_all[1:],
        in_hbm(gates_own),
        *gates_all[1:],
        in_hbm(grad_out),
        *grads,
    )
    scaled_rows = exchanged(scaled)

    sent, pos = pl.pallas_call(
        functools.partial(dispatch_tokens, experts, cap),
        out_shape=(
            pltpu.HBM((slots, width), jnp.bfloat16),
            jax.ShapeDtypeStruct((top, count), jnp.int32),
        ),
        grid_spec=pltpu.PrefetchScalarGridSpec(
            num_scalar_prefetch=1,
            grid=(groups,),
            in_specs=[small_spec] * 2
            + [
                pl.BlockSpec(
                    (count, share), lambda k, g: (0, lax.rem(g[0] - k + groups, groups))
                )
            ]
            * 2,
            out_specs=(pl.BlockSpec((slots, share), lambda k, g: (0, k)), small_spec),
            scratch_shapes=[pltpu.VMEM((slots, 2 * count), jnp.bfloat16)],
        ),
        cost_estimate=pl.CostEstimate(
            flops=TOKENS_COST_US * 10**9, bytes_accessed=TOKENS_COST_US * 10**6, transcendentals=0
        ),
        compiler_params=params,
        name="dispatch_tokens",
    )(place, in_hbm(routes_t), routes_across, in_hbm(tokens), in_hbm(tokens_across))
    x_rows = exchanged(sent, halves)

    any_spec = pl.BlockSpec(memory_space=pl.ANY)
    whole_spec = pl.BlockSpec(memory_space=pltpu.VMEM)
    *weights_moved, gate_held = pl.pallas_call(
        ready_kernel,
        out_shape=[pltpu.HBM(value.shape, value.dtype) for value in weights_moved]
        + [pltpu.VMEM((share, hidden), jnp.bfloat16)],
        in_specs=[any_spec] * groups,
        out_specs=[any_spec] * (groups - 1) + [whole_spec],
        input_output_aliases={k + 1: k for k in range(groups - 1)},
        scratch_shapes=[pltpu.SemaphoreType.DMA((2,))],
        cost_estimate=pl.CostEstimate(
            flops=READY_COST_US * 10**9, bytes_accessed=READY_COST_US * 10**6, transcendentals=0
        ),
        compiler_params=params,
        name="ready",
    )(in_hbm(w_gate[0]), *[in_hbm(value) for value in weights_moved])

    place_spec = pl.BlockSpec(memory_space=pltpu.SMEM)

    back_own, *rest = pl.pallas_call(
        functools.partial(back_kernel, groups, cap),
        out_shape=[pltpu.HBM((slots, hidden), jnp.float32)]
        + [pltpu.HBM((slots, hidden), jnp.bfloat16)] * (groups - 1)
        + [pltpu.HBM((groups * slots, share), jnp.bfloat16)],
        in_specs=[place_spec, pl.BlockSpec(), pl.BlockSpec()],
        compiler_params=params,
        name="back",
    )(place, scaled_rows, in_hbm(w_down[0]))
    scaled_all = rest[-1]
    back_parts = [shifted(rest[k - 1], -k) for k in range(1, groups)]

    *factors, hidden_own, held, back_kept = pl.pallas_call(
        functools.partial(forward_kernel, groups),
        out_shape=[pltpu.VMEM((slots, hidden), jnp.float32)] * 3
        + [
            pltpu.HBM((slots, hidden), jnp.bfloat16),
            pltpu.VMEM((2 * groups - 1, share, hidden), jnp.bfloat16),
            pltpu.VMEM((slots, hidden), jnp.float32),
        ],
        in_specs=[whole_spec] * 2 + [any_spec] * (groups + 1),
        scratch_shapes=[
            pltpu.VMEM((slots, hidden), jnp.float32),
            pltpu.VMEM((slots, hidden), jnp.float32),
            pltpu.SemaphoreType.DMA((2, 2 * groups - 1)),
            pltpu.SemaphoreType.DMA((1,)),
        ],
        compiler_params=params,
        name="forward",
    )(x_rows, gate_held, in_hbm(back_own), in_hbm(w_up[0]), *[in_hbm(w) for w in weights_moved])

    pieces = groups * (share // tile_of(share, 512))
    returning = pl.pallas_call(
        functools.partial(backward_kernel, groups, cap),
        out_shape=pltpu.HBM((slots, width + LANES), jnp.bfloat16),
        in_specs=[place_spec] + [whole_spec] * (5 + groups),
        out_specs=any_spec,
        scratch_shapes=[
            pltpu.VMEM((slots, hidden), jnp.bfloat16),
            pltpu.VMEM((slots, hidden), jnp.bfloat16),
            pltpu.VMEM((slots, width + LANES), jnp.bfloat16),
            pltpu.SemaphoreType.DMA((pieces + 1,)),
        ],
        compiler_params=params,
        name="backward",
    )(place_half, *factors, gate_held, held, back_kept, *back_parts)
    returned = exchanged(returning)

    hiddens = [hidden_own] + [shifted(hidden_own, k) for k in range(1, groups)]
    grad_down = contract_first(jnp.concatenate(hiddens, axis=0), scaled_all)[None]

    grad_tokens, grad_gates = pl.pallas_call(
        functools.partial(combine_kernel, groups),
        out_shape=(
            jax.ShapeDtypeStruct((count, width), jnp.bfloat16),
            jax.ShapeDtypeStruct((top, count), jnp.float32),
        ),
        in_specs=[pl.BlockSpec(memory_space=pltpu.SMEM)] + [whole_spec] * 3,
        compiler_params=params,
        name="combine",
    )(place_group, pos, gates_t, returned)
    return (grad_tokens, jnp.transpose(grad_gates), grad_down)


def solution(mesh):
    placed = (
        P(("dp", "expert"), None),
        P(("dp", "expert"), None),
        P(("dp", "expert"), None),
        P(("dp", "expert"), None),
        P("expert", "dp", None),
        P("expert", "dp", None),
        P("expert", None, "dp"),
    )
    return jax.shard_map(
        per_device,
        mesh=mesh,
        in_specs=placed,
        out_specs=(P(("dp", "expert"), None), P(("dp", "expert"), None), P("expert", None, "dp")),
        check_vma=False,
    )
```
